32 devices in a mesh: gx: 8 (over y, x, core), gy: 4 (over z).
Axes of the slice: x: 2, y: 2, z: 4, core: 2. Of those that a mesh axis runs over, the one named last changes fastest.
Arguments:
- state: float32 [4, 256, 1024], P(None, 'gx', 'gy'), as said below
Outputs:
- advanced: float32 [4, 256, 1024], P(None, 'gx', 'gy')
Inputs may be any that keep to these rules, and one draw needn't show every extreme that they name: `state`: density lies between 0.5 and 1.5 and pressure between 0.3 and 1.5 in every cell, and each velocity component is under 0.35 in size.
All inputs are finite; a program needn't handle non-finite values.
Results may differ from the reference program's by a relative error of at most 0.0003.
Values sent between devices are 32-bit elements; how exact they have to be, the bound alone decides.
No kernel may reach another device: no remote copies, remote signals or barrier semaphores. Data moves between devices by JAX's collectives and lax.ppermute only.
A program may use at most 64 MiB of HBM per device.

```python
import jax
import jax.numpy as jnp
from jax import lax

STEPS = 4
NX = 256
NY = 1024


def draw_state(key, part):
    key = jax.random.fold_in(key, 7)
    keys = jax.random.split(key, 5)
    columns = jnp.arange(NY, dtype=jnp.float32)
    envelope = (0.7 + 0.3 * jnp.sin(6.283185307 * columns / NY))[None, :]
    speed_amp = jax.random.uniform(keys[4], (), jnp.float32, 0.12, 0.34)
    vel_x = speed_amp * envelope * jax.random.uniform(keys[1], (NX, NY), jnp.float32, -1.0, 1.0)
    vel_y = speed_amp * envelope * jax.random.uniform(keys[2], (NX, NY), jnp.float32, -1.0, 1.0)
    density = 1.0 + 0.3 * jax.random.uniform(keys[0], (NX, NY), jnp.float32, -1.0, 1.0)
    pressure = 1.0 + 0.3 * envelope * jax.random.uniform(keys[3], (NX, NY), jnp.float32, -1.0, 1.0)
    energy = pressure / 0.4 + 0.5 * density * (vel_x * vel_x + vel_y * vel_y)
    return jnp.stack([density, density * vel_x, density * vel_y, energy]).astype(jnp.float32)


def setup_inputs(seed: int = 0) -> dict:
    streams_of = jax.random.split(jax.random.key(seed), 2)
    return {
        "state": draw_state(jax.random.fold_in(streams_of[1], 71), 0),
    }


GAMMA = 1.4
COURANT = 0.35

def fluxes(density, normal_mom, tangent_mom, energy):
    normal_vel = normal_mom / density
    pressure = (GAMMA - 1.0) * (energy - 0.5 * (normal_mom * normal_mom + tangent_mom * tangent_mom) / density)
    sound = jnp.sqrt(GAMMA * pressure / density)
    return ((normal_mom, normal_mom * normal_vel + pressure, tangent_mom * normal_vel, (energy + pressure) * normal_vel), jnp.abs(normal_vel) + sound)

def limited_slope(first, second):
    return 0.5 * (jnp.sign(first) + jnp.sign(second)) * jnp.minimum(jnp.abs(first), jnp.abs(second))

def face_difference(field, axis):
    extent = field.shape[axis]

    def window_of(array, low, high):
        return lax.slice_in_dim(array, low, high, axis=axis)
    jumps = window_of(field, 1, extent) - window_of(field, 0, extent - 1)
    slopes = limited_slope(window_of(jumps, 1, extent - 1), window_of(jumps, 0, extent - 2))
    left_state = window_of(field, 1, extent - 2) + 0.5 * window_of(slopes, 0, extent - 3)
    right_state = window_of(field, 2, extent - 1) - 0.5 * window_of(slopes, 1, extent - 2)
    normal_idx, tangent_idx = (1, 2) if axis == 1 else (2, 1)
    flux_left, speed_left = fluxes(left_state[0], left_state[normal_idx], left_state[tangent_idx], left_state[3])
    flux_right, speed_right = fluxes(right_state[0], right_state[normal_idx], right_state[tangent_idx], right_state[3])
    top_speed = jnp.maximum(speed_left, speed_right)
    order = {0: 0, normal_idx: 1, tangent_idx: 2, 3: 3}
    faces = jnp.stack([0.5 * (flux_left[order[comp]] + flux_right[order[comp]]) - 0.5 * top_speed * (right_state[comp] - left_state[comp]) for comp in range(4)])
    count = faces.shape[axis]
    return window_of(faces, 1, count) - window_of(faces, 0, count - 1)

def rate_of(field, ratio):
    rows_all, cols_all = (field.shape[1], field.shape[2])
    along_x = face_difference(field, 1)[:, :, 2:cols_all - 2]
    along_y = face_difference(field, 2)[:, 2:rows_all - 2, :]
    return -ratio * (along_x + along_y)

def one_step(field, ratio):
    section = field[:, 2:-2, 2:-2] + rate_of(field, ratio)
    return 0.5 * field[:, 4:-4, 4:-4] + 0.5 * (section[:, 2:-2, 2:-2] + rate_of(section, ratio))

def signal_speed(field):
    density = field[0]
    vel_x = field[1] / density
    vel_y = field[2] / density
    pressure = (GAMMA - 1.0) * (field[3] - 0.5 * (field[1] * field[1] + field[2] * field[2]) / density)
    return jnp.max(jnp.maximum(jnp.abs(vel_x), jnp.abs(vel_y)) + jnp.sqrt(GAMMA * pressure / density))

def reference(state):
    ratio = COURANT / signal_speed(state)
    field = state
    for index in range(STEPS):
        field = one_step(jnp.pad(field, ((0, 0), (4, 4), (4, 4)), mode='wrap'), ratio)
    return field
```

```python
import functools

import jax
import jax.numpy as jnp
from jax import lax
from jax.experimental import pallas as pl
from jax.experimental.pallas import tpu as pltpu
from jax.sharding import PartitionSpec as P

STEPS = 4
HALO = 4 * STEPS
LANES = 128
GAMMA = 1.4
COURANT = 0.35

VMEM = pl.BlockSpec(memory_space=pltpu.VMEM)


def speed_kernel(state_ref, top_ref, head_ref, tail_ref):
    rows = state_ref.shape[1]
    density, mom_x, mom_y, energy = (state_ref[comp] for comp in range(4))
    inv = 1.0 / density
    pressure = (GAMMA - 1.0) * (energy - 0.5 * (mom_x * mom_x + mom_y * mom_y) * inv)
    speed = jnp.maximum(jnp.abs(mom_x * inv), jnp.abs(mom_y * inv)) + jnp.sqrt(GAMMA * pressure * inv)
    top_ref[...] = jnp.full(top_ref.shape, jnp.max(speed))
    for comp in range(4):
        head_ref[comp] = state_ref[comp, 0:HALO, :]
        tail_ref[comp] = state_ref[comp, rows - HALO : rows, :]


def lane_of(shape):
    return lax.broadcasted_iota(jnp.int32, shape, len(shape) - 1)


def pack_kernel(count, state_ref, up_ref, down_ref, top_ref, piece_ref):
    rows = state_ref.shape[1]
    cols = state_ref.shape[2]
    half = rows // 2 + HALO
    place = lax.axis_index("gy")
    after = lax.rem(place + 1, count)
    top = jnp.full((8, LANES), jnp.max(top_ref[...]))

    def edge(low, at):
        total = jnp.zeros((half, LANES), jnp.float32)
        lane = lane_of((half, LANES))
        for side in range(2):
            for comp in range(4):
                if side == 0:
                    cells = jnp.concatenate(
                        [up_ref[comp, :, low : low + LANES], state_ref[comp, 0 : rows // 2, low : low + LANES]], axis=0
                    )
                else:
                    cells = jnp.concatenate(
                        [state_ref[comp, rows // 2 : rows, low : low + LANES], down_ref[comp, :, low : low + LANES]], axis=0
                    )
                goal = side * (LANES // 2) + comp * HALO
                moved = pltpu.roll(cells, (goal - at) % LANES, axis=1)
                total = jnp.where((lane >= goal) & (lane < goal + HALO), moved, total)
        return total

    left = edge(0, 0)
    right = edge(cols - LANES, LANES - HALO)
    for dest in range(count):
        piece_ref[dest, 0:half, :] = left
        piece_ref[dest, half : half + 8, :] = top
    piece_ref[after, 0:half, :] = right


def minmod(first, second):
    low = jnp.minimum(first, second)
    high = jnp.maximum(first, second)
    return jnp.maximum(low, jnp.minimum(high, 0.0))


def fluxes(state):
    density, normal, tangent, energy = state
    inv = 1.0 / density
    vel = normal * inv
    carried = normal * vel
    pressure = (GAMMA - 1.0) * energy - (0.5 * (GAMMA - 1.0)) * (carried + tangent * tangent * inv)
    sound = jnp.sqrt(GAMMA * pressure * inv)
    return (normal, carried + pressure, tangent * vel, (energy + pressure) * vel), jnp.abs(vel) + sound


def face(left, left_flux, left_speed, right, right_flux, right_speed):
    top = jnp.maximum(left_speed, right_speed)
    return [
        (left_flux[comp] + right_flux[comp]) - top * (right[comp] - left[comp]) for comp in range(4)
    ]


def swapped(parts):
    return [parts[0], parts[2], parts[1], parts[3]]


def steps_kernel(count, rows, cols, state_ref, up_ref, down_ref, piece_ref, out_ref, field, mid, diff):
    tall = rows + 2 * HALO
    tiles = cols // LANES
    wide = (tiles + 1) * LANES
    half = tall // 2
    place = lax.axis_index("gy")
    before = lax.rem(place + count - 1, count)
    after = lax.rem(place + 1, count)
    top = jnp.max(piece_ref[:, half : half + 8, :].reshape(count * 8, LANES))
    factor = -0.5 * COURANT / top

    pad = field.shape[2] - tall
    for comp in range(4):
        for tile in range(tiles):
            lanes = slice(tile * LANES, (tile + 1) * LANES)
            field[comp, tile, 0:HALO, :] = up_ref[comp, :, lanes]
            field[comp, tile, HALO : HALO + rows, :] = state_ref[comp, :, lanes]
            field[comp, tile, HALO + rows : tall, :] = down_ref[comp, :, lanes]
    lane = lane_of((half, LANES))
    from_before = piece_ref[before, 0:half, :]
    from_after = piece_ref[after, 0:half, :]
    for side in range(2):
        for comp in range(4):
            at = side * (LANES // 2) + comp * HALO
            left = pltpu.roll(from_before, (LANES - HALO - at) % LANES, axis=1)
            right = pltpu.roll(from_after, (-at) % LANES, axis=1)
            field[comp, tiles, side * half : (side + 1) * half, :] = jnp.where(lane < LANES // 2, right, left)

    def x_pass(src, start, step):
        for tile in range(tiles + 1):
            def load(at):
                return [src[comp, tile, pl.ds(start + at, 8, stride=step), :] for comp in range(4)]

            def cell(here, before_jump, after_jump):
                half_slope = [minmod(before_jump[comp], after_jump[comp]) for comp in range(4)]
                low = [here[comp] - half_slope[comp] for comp in range(4)]
                high = [here[comp] + half_slope[comp] for comp in range(4)]
                return (low, *fluxes(low)), (high, *fluxes(high))

            def rolled(tree, by):
                return jax.tree.map(lambda value: pltpu.roll(value, by % 8, axis=0), tree)

            def jump_of(first, second):
                return [0.5 * (second[comp] - first[comp]) for comp in range(4)]

            values = [load(at) for at in range(step)]
            jumps = [jump_of(values[at], values[at + 1]) for at in range(step - 1)]
            jumps.append(jump_of(values[step - 1], rolled(values[0], -1)))
            lows, highs, faces = {}, {}, {}
            for at in range(step):
                jump_before = jumps[at - 1] if at else rolled(jumps[step - 1], 1)
                lows[at], highs[at] = cell(values[at], jump_before, jumps[at])
                if at:
                    faces[at - 1] = face(*highs[at - 1], *lows[at])
                if at > 1:
                    for comp in range(4):
                        diff[comp, tile, at - 1] = faces[at - 1][comp] - faces[at - 2][comp]
            faces[step - 1] = face(*highs[step - 1], *rolled(lows[0], -1))
            first = rolled(faces[step - 1], 1)
            for comp in range(4):
                diff[comp, tile, step - 1] = faces[step - 1][comp] - faces[step - 2][comp]
                diff[comp, tile, 0] = faces[0][comp] - first[comp]

    def y_pass(src, start, step, at):
        def load(comp):
            return jnp.concatenate(
                [src[comp, tile, pl.ds(start + at, 8, stride=step), :] for tile in range(tiles + 1)], axis=1
            )

        def shifted(parts, by):
            return [pltpu.roll(part, by % wide, axis=1) for part in parts]

        here = [load(comp) for comp in (0, 2, 1, 3)]
        ahead = shifted(here, -1)
        jumps = [0.5 * (ahead[comp] - here[comp]) for comp in range(4)]
        behind = shifted(jumps, 1)
        half_slope = [minmod(behind[comp], jumps[comp]) for comp in range(4)]
        low = shifted([here[comp] - half_slope[comp] for comp in range(4)], -1)
        high = [here[comp] + half_slope[comp] for comp in range(4)]
        faces = face(high, *fluxes(high), low, *fluxes(low))
        lower = shifted(faces, 1)
        change = swapped([faces[comp] - lower[comp] for comp in range(4)])
        here = swapped(here)
        return here, [
            change[comp] + jnp.concatenate([diff[comp, tile, at] for tile in range(tiles + 1)], axis=1)
            for comp in range(4)
        ]

    def store(dst, start, step, at, comp, value):
        for tile in range(tiles + 1):
            dst[comp, tile, pl.ds(start + at, 8, stride=step), :] = value[:, tile * LANES : (tile + 1) * LANES]

    def load_wide(src, start, step, at, comp):
        return jnp.concatenate(
            [src[comp, tile, pl.ds(start + at, 8, stride=step), :] for tile in range(tiles + 1)], axis=1
        )

    for index in range(STEPS):
        start = 4 * index
        step = -(-(tall - 8 * index) // 8)
        x_pass(field, start, step)
        for at in range(step):
            here, change = y_pass(field, start, step, at)
            for comp in range(4):
                store(mid, start, step, at, comp, here[comp] + factor * change[comp])
        x_pass(mid, start, step)
        for at in range(step):
            here, change = y_pass(mid, start, step, at)
            for comp in range(4):
                old = load_wide(field, start, step, at, comp)
                store(field, start, step, at, comp, 0.5 * (old + here[comp]) + (0.5 * factor) * change[comp])
    for comp in range(4):
        for tile in range(tiles):
            out_ref[comp, :, tile * LANES : (tile + 1) * LANES] = field[comp, tile, HALO : HALO + rows, :]


def local(state):
    parts, rows, cols = state.shape
    count_x, count_y = lax.axis_size("gx"), lax.axis_size("gy")
    tall = rows + 2 * HALO
    tiles = cols // LANES
    edge_type = jax.ShapeDtypeStruct((parts, HALO, cols), jnp.float32)
    top, head, tail = pl.pallas_call(
        speed_kernel,
        out_shape=(jax.ShapeDtypeStruct((count_x, 8, LANES), jnp.float32), edge_type, edge_type),
        in_specs=[VMEM],
        out_specs=(VMEM, VMEM, VMEM),
        name="speed",
    )(state)
    up = lax.ppermute(tail, "gx", [(i, (i + 1) % count_x) for i in range(count_x)])
    down = lax.ppermute(head, "gx", [((i + 1) % count_x, i) for i in range(count_x)])
    top = lax.all_to_all(top, "gx", 0, 0)
    pieces = pl.pallas_call(
        functools.partial(pack_kernel, count_y),
        out_shape=jax.ShapeDtypeStruct((count_y, tall // 2 + 8, LANES), jnp.float32),
        in_specs=[VMEM] * 4,
        out_specs=VMEM,
        name="pack",
    )(state, up, down, top)
    pieces = lax.all_to_all(pieces, "gy", 0, 0)
    return pl.pallas_call(
        functools.partial(steps_kernel, count_y, rows, cols),
        out_shape=jax.ShapeDtypeStruct(state.shape, jnp.float32),
        in_specs=[VMEM] * 4,
        out_specs=VMEM,
        scratch_shapes=[
            pltpu.VMEM((parts, tiles + 1, tall, LANES), jnp.float32),
            pltpu.VMEM((parts, tiles + 1, tall, LANES), jnp.float32),
            pltpu.VMEM((parts, tiles + 1, tall // 8, 8, LANES), jnp.float32),
        ],
        name="steps",
    )(state, up, down, pieces)


def solution(mesh):
    in_specs = (P(None, "gx", "gy"),)
    out_specs = P(None, "gx", "gy")
    return jax.shard_map(local, mesh=mesh, in_specs=in_specs, out_specs=out_specs, check_vma=False)
```

```python
import functools

import jax
import jax.numpy as jnp
from jax import lax
from jax.experimental import pallas as pl
from jax.experimental.pallas import tpu as pltpu
from jax.sharding import PartitionSpec as P

STEPS = 4
HALO = 4 * STEPS
GROUP = 2
LANES = 128
GAMMA = 1.4
COURANT = 0.35
TINY = 1e-30

VMEM = pl.BlockSpec(memory_space=pltpu.VMEM)


def params(limit):
    return pltpu.CompilerParams(vmem_limit_bytes=limit << 20)


def speed_kernel(state_ref, top_ref):
    density, mom_x, mom_y, energy = (state_ref[comp] for comp in range(4))
    inv = 1.0 / density
    pressure = (GAMMA - 1.0) * (energy - 0.5 * (mom_x * mom_x + mom_y * mom_y) * inv)
    speed = jnp.maximum(jnp.abs(mom_x * inv), jnp.abs(mom_y * inv)) + jnp.sqrt(GAMMA * pressure * inv)
    top_ref[...] = jnp.full(top_ref.shape, jnp.max(speed))


def lane_of(shape):
    return lax.broadcasted_iota(jnp.int32, shape, len(shape) - 1)


def pack_kernel(state_ref, up_ref, down_ref, left_ref, right_ref):
    rows = state_ref.shape[1]
    cols = state_ref.shape[2]
    half = rows // 2 + HALO

    def edge(low, at):
        total = jnp.zeros((half, LANES), jnp.float32)
        lane = lane_of((half, LANES))
        for side in range(2):
            for comp in range(4):
                if side == 0:
                    cells = jnp.concatenate(
                        [up_ref[comp, :, low : low + LANES], state_ref[comp, 0 : rows // 2, low : low + LANES]], axis=0
                    )
                else:
                    cells = jnp.concatenate(
                        [state_ref[comp, rows // 2 : rows, low : low + LANES], down_ref[comp, :, low : low + LANES]], axis=0
                    )
                goal = side * (LANES // 2) + comp * HALO
                moved = pltpu.roll(cells, (goal - at) % LANES, axis=1)
                total = jnp.where((lane >= goal) & (lane < goal + HALO), moved, total)
        return total

    left_ref[...] = edge(0, 0)
    right_ref[...] = edge(cols - LANES, LANES - HALO)


def minmod(first, second):
    low = jnp.minimum(first, second)
    high = jnp.maximum(first, second)
    return jnp.maximum(low, jnp.minimum(high, 0.0))


def fluxes(state):
    density, normal, tangent, energy = state
    inv = pl.reciprocal(density, approx=True)
    vel = normal * inv
    carried = normal * vel
    pressure = (GAMMA - 1.0) * energy - (0.5 * (GAMMA - 1.0)) * (carried + tangent * tangent * inv)
    square = GAMMA * pressure * inv
    sound = square * lax.rsqrt(jnp.maximum(square, TINY))
    return (normal, carried + pressure, tangent * vel, (energy + pressure) * vel), jnp.abs(vel) + sound


def face(left, left_flux, left_speed, right, right_flux, right_speed):
    top = jnp.maximum(left_speed, right_speed)
    return [
        (left_flux[comp] + right_flux[comp]) - top * (right[comp] - left[comp]) for comp in range(4)
    ]


def swapped(parts):
    return [parts[0], parts[2], parts[1], parts[3]]


def steps_kernel(rows, cols, state_ref, up_ref, down_ref, before_ref, after_ref, top_ref, out_ref, field, mid, diff):
    tall = rows + 2 * HALO
    tiles = cols // LANES
    wide = (tiles + 1) * LANES
    half = tall // 2
    factor = -0.5 * COURANT / jnp.max(top_ref[...].reshape(-1, LANES))

    for comp in range(4):
        for tile in range(tiles):
            lanes = slice(tile * LANES, (tile + 1) * LANES)
            field[comp, tile, 0:HALO, :] = up_ref[comp, :, lanes]
            field[comp, tile, HALO : HALO + rows, :] = state_ref[comp, :, lanes]
            field[comp, tile, HALO + rows : tall, :] = down_ref[comp, :, lanes]
    lane = lane_of((half, LANES))
    from_before = before_ref[...]
    from_after = after_ref[...]
    for side in range(2):
        for comp in range(4):
            at = side * (LANES // 2) + comp * HALO
            left = pltpu.roll(from_before, (LANES - HALO - at) % LANES, axis=1)
            right = pltpu.roll(from_after, (-at) % LANES, axis=1)
            field[comp, tiles, side * half : (side + 1) * half, :] = jnp.where(lane < LANES // 2, right, left)

    def rolled(tree, by):
        return jax.tree.map(lambda value: pltpu.roll(value, by % 8, axis=0), tree)

    def jump_of(first, second):
        return [0.5 * (second[comp] - first[comp]) for comp in range(4)]

    def cell(here, before_jump, after_jump):
        half_slope = [minmod(before_jump[comp], after_jump[comp]) for comp in range(4)]
        low = [here[comp] - half_slope[comp] for comp in range(4)]
        high = [here[comp] + half_slope[comp] for comp in range(4)]
        return (low, *fluxes(low)), (high, *fluxes(high))

    def x_pass(src, start, step):
        def one_tile(tile, none):
            values = [
                [src[comp, tile, pl.ds(start + at, 8, stride=step), :] for comp in range(4)] for at in range(step)
            ]
            jumps = [jump_of(values[at], values[at + 1]) for at in range(step - 1)]
            jumps.append(jump_of(values[step - 1], rolled(values[0], -1)))
            lows, highs, faces = {}, {}, {}
            for at in range(step):
                jump_before = jumps[at - 1] if at else rolled(jumps[step - 1], 1)
                lows[at], highs[at] = cell(values[at], jump_before, jumps[at])
                if at:
                    faces[at - 1] = face(*highs[at - 1], *lows[at])
                if at > 1:
                    for comp in range(4):
                        diff[comp, tile, at - 1] = faces[at - 1][comp] - faces[at - 2][comp]
            faces[step - 1] = face(*highs[step - 1], *rolled(lows[0], -1))
            first = rolled(faces[step - 1], 1)
            for comp in range(4):
                diff[comp, tile, step - 1] = faces[step - 1][comp] - faces[step - 2][comp]
                diff[comp, tile, 0] = faces[0][comp] - first[comp]
            return none

        lax.fori_loop(0, tiles + 1, one_tile, None)

    def load_wide(src, start, step, at, comp):
        return jnp.concatenate(
            [src[comp, tile, pl.ds(start + at, 8, stride=step), :] for tile in range(tiles + 1)], axis=1
        )

    def shifted(parts, by):
        return [pltpu.roll(part, by % wide, axis=1) for part in parts]

    def y_change(src, start, step, at):
        here = [load_wide(src, start, step, at, comp) for comp in (0, 2, 1, 3)]
        ahead = shifted(here, -1)
        jumps = jump_of(here, ahead)
        behind = shifted(jumps, 1)
        half_slope = [minmod(behind[comp], jumps[comp]) for comp in range(4)]
        low = shifted([here[comp] - half_slope[comp] for comp in range(4)], -1)
        high = [here[comp] + half_slope[comp] for comp in range(4)]
        faces = face(high, *fluxes(high), low, *fluxes(low))
        lower = shifted(faces, 1)
        change = swapped([faces[comp] - lower[comp] for comp in range(4)])
        return swapped(here), [
            change[comp] + jnp.concatenate([diff[comp, tile, at] for tile in range(tiles + 1)], axis=1)
            for comp in range(4)
        ]

    def store(dst, start, step, at, comp, value):
        for tile in range(tiles + 1):
            dst[comp, tile, pl.ds(start + at, 8, stride=step), :] = value[:, tile * LANES : (tile + 1) * LANES]

    def two_steps(start, step):
        def first_rows(group, none):
            for inner in range(GROUP):
                at = group * GROUP + inner
                here, change = y_change(field, start, step, at)
                for comp in range(4):
                    store(mid, start, step, at, comp, here[comp] + factor * change[comp])
            return none

        def second_rows(group, none):
            for inner in range(GROUP):
                at = group * GROUP + inner
                here, change = y_change(mid, start, step, at)
                for comp in range(4):
                    old = load_wide(field, start, step, at, comp)
                    store(field, start, step, at, comp, 0.5 * (old + here[comp]) + (0.5 * factor) * change[comp])
            return none

        def one_step(index, none):
            x_pass(field, start, step)
            lax.fori_loop(0, step // GROUP, first_rows, None)
            x_pass(mid, start, step)
            lax.fori_loop(0, step // GROUP, second_rows, None)
            return none

        lax.fori_loop(0, 2, one_step, None)

    for index in range(0, STEPS, 2):
        two_steps(4 * index, (tall - 8 * index) // 8)
    for comp in range(4):
        for tile in range(tiles):
            out_ref[comp, :, tile * LANES : (tile + 1) * LANES] = field[comp, tile, HALO : HALO + rows, :]


def local(state):
    parts, rows, cols = state.shape
    count_x, count_y = lax.axis_size("gx"), lax.axis_size("gy")
    tall = rows + 2 * HALO
    tiles = cols // LANES

    def ahead(count):
        return [(i, (i + 1) % count) for i in range(count)]

    def back(count):
        return [((i + 1) % count, i) for i in range(count)]

    up = lax.ppermute(state[:, rows - HALO :, :], "gx", ahead(count_x))
    down = lax.ppermute(state[:, :HALO, :], "gx", back(count_x))
    top = pl.pallas_call(
        speed_kernel,
        out_shape=jax.ShapeDtypeStruct((8, LANES), jnp.float32),
        in_specs=[VMEM],
        out_specs=VMEM,
        compiler_params=params(4),
        name="speed",
    )(state)
    top = lax.all_gather(top, ("gx", "gy"))
    edge_type = jax.ShapeDtypeStruct((tall // 2, LANES), jnp.float32)
    left, right = pl.pallas_call(
        pack_kernel,
        out_shape=(edge_type, edge_type),
        in_specs=[VMEM] * 3,
        out_specs=(VMEM, VMEM),
        compiler_params=params(4),
        name="pack",
    )(state, up, down)
    before = lax.ppermute(right, "gy", ahead(count_y))
    after = lax.ppermute(left, "gy", back(count_y))
    return pl.pallas_call(
        functools.partial(steps_kernel, rows, cols),
        out_shape=jax.ShapeDtypeStruct(state.shape, jnp.float32),
        in_specs=[VMEM] * 6,
        out_specs=VMEM,
        scratch_shapes=[
            pltpu.VMEM((parts, tiles + 1, tall, LANES), jnp.float32),
            pltpu.VMEM((parts, tiles + 1, tall, LANES), jnp.float32),
            pltpu.VMEM((parts, tiles + 1, tall // 8, 8, LANES), jnp.float32),
        ],
        compiler_params=params(16),
        name="steps",
    )(state, up, down, before, after, top)


def solution(mesh):
    in_specs = (P(None, "gx", "gy"),)
    out_specs = P(None, "gx", "gy")
    return jax.shard_map(local, mesh=mesh, in_specs=in_specs, out_specs=out_specs, check_vma=False)
```

```python
import functools

import jax
import jax.numpy as jnp
from jax import lax
from jax.experimental import pallas as pl
from jax.experimental.pallas import tpu as pltpu
from jax.sharding import PartitionSpec as P

STEPS = 4
HALO = 4 * STEPS
LANES = 128
GAMMA = 1.4
COURANT = 0.35
TINY = 1e-30

VMEM = pl.BlockSpec(memory_space=pltpu.VMEM)


def params(limit):
    return pltpu.CompilerParams(vmem_limit_bytes=limit << 20)


def array(*shape):
    return jax.ShapeDtypeStruct(shape, jnp.float32)


def iota(shape, dim):
    return lax.broadcasted_iota(jnp.int32, shape, dim)


def edge_kernel(state_ref, head_ref, tail_ref, top_ref):
    rows = state_ref.shape[1]
    density, mom_x, mom_y, energy = (state_ref[comp] for comp in range(4))
    inv = 1.0 / density
    pressure = (GAMMA - 1.0) * (energy - 0.5 * (mom_x * mom_x + mom_y * mom_y) * inv)
    speed = jnp.maximum(jnp.abs(mom_x * inv), jnp.abs(mom_y * inv)) + jnp.sqrt(GAMMA * pressure * inv)
    top = jnp.max(speed)
    for comp in range(4):
        head_ref[comp * HALO : (comp + 1) * HALO, :] = state_ref[comp, 0:HALO, :]
        tail_ref[comp * HALO : (comp + 1) * HALO, :] = state_ref[comp, rows - HALO : rows, :]
    head_ref[4 * HALO :, :] = jnp.full((8, head_ref.shape[1]), top)
    tail_ref[4 * HALO :, :] = jnp.full((8, tail_ref.shape[1]), top)
    top_ref[...] = jnp.full(top_ref.shape, top)


def pack_kernel(state_ref, up_ref, down_ref, own_ref, far_ref, left_ref, right_ref, top_ref):
    rows = state_ref.shape[1]
    cols = state_ref.shape[2]
    half = rows // 2 + HALO
    lane = iota((half, LANES), 1)
    top = jnp.maximum(jnp.maximum(own_ref[...], far_ref[...]),
                      jnp.maximum(up_ref[4 * HALO :, 0:LANES], down_ref[4 * HALO :, 0:LANES]))

    def edge(low, at):
        lanes = slice(low, low + LANES)
        total = jnp.zeros((half, LANES), jnp.float32)
        for side in range(2):
            for comp in range(4):
                span = slice(comp * HALO, (comp + 1) * HALO)
                if side == 0:
                    cells = jnp.concatenate([up_ref[span, lanes], state_ref[comp, 0 : rows // 2, lanes]], axis=0)
                else:
                    cells = jnp.concatenate([state_ref[comp, rows // 2 : rows, lanes], down_ref[span, lanes]], axis=0)
                goal = side * (LANES // 2) + comp * HALO
                moved = pltpu.roll(cells, (goal - at) % LANES, axis=1)
                total = jnp.where((lane >= goal) & (lane < goal + HALO), moved, total)
        return total

    left_ref[0:half, :] = edge(0, 0)
    right_ref[0:half, :] = edge(cols - LANES, LANES - HALO)
    left_ref[half:, :] = top
    right_ref[half:, :] = top
    top_ref[...] = top


def selected(values, select):
    total = None
    for _ in range(3):
        part = values.astype(jnp.bfloat16)
        values = values - part.astype(jnp.float32)
        term = jnp.dot(part, select, preferred_element_type=jnp.float32)
        total = term if total is None else total + term
    return total


def minmod(first, second):
    low = jnp.minimum(first, second)
    high = jnp.maximum(first, second)
    return jnp.maximum(low, jnp.minimum(high, 0.0))


def fluxes(state):
    density, normal, tangent, energy = state
    inv = pl.reciprocal(density, approx=True)
    vel = normal * inv
    carried = normal * vel
    pressure = (GAMMA - 1.0) * energy - (0.5 * (GAMMA - 1.0)) * (carried + tangent * tangent * inv)
    square = GAMMA * pressure * inv
    sound = square * lax.rsqrt(jnp.maximum(square, TINY))
    return (normal, carried + pressure, tangent * vel, (energy + pressure) * vel), jnp.abs(vel) + sound


def face(left, right):
    (left_state, left_flux, left_speed), (right_state, right_flux, right_speed) = left, right
    top = jnp.maximum(left_speed, right_speed)
    return [
        (left_flux[comp] + right_flux[comp]) - top * (right_state[comp] - left_state[comp]) for comp in range(4)
    ]


def minus(first, second):
    return [first[comp] - second[comp] for comp in range(4)]


def sweep(load, store, count, axis):
    def rolled(tree, by):
        return jax.tree.map(lambda value: pltpu.roll(value, by % value.shape[axis], axis=axis), tree)

    def half(parts):
        return [0.5 * part for part in parts]

    here = load(0)
    end_jump = half(minus(rolled(here, -1), load(count - 1)))
    jump = rolled(end_jump, 1)
    for at in range(count):
        after = load(at + 1) if at + 1 < count else None
        next_jump = half(minus(after, here)) if at + 1 < count else end_jump
        slope = [minmod(jump[comp], next_jump[comp]) for comp in range(4)]
        low_state = minus(here, slope)
        high_state = [here[comp] + slope[comp] for comp in range(4)]
        low = (low_state, *fluxes(low_state))
        if at == 0:
            first_low = low
        else:
            flux = face(high, low)
            if at == 1:
                first_flux = flux
            else:
                store(at - 1, minus(flux, last_flux))
            last_flux = flux
        high = (high_state, *fluxes(high_state))
        here, jump = after, next_jump
    flux = face(high, rolled(first_low, -1))
    store(count - 1, minus(flux, last_flux))
    store(0, minus(first_flux, rolled(flux, 1)))


X_ORDER = (0, 1, 2, 3)
Y_ORDER = (0, 2, 1, 3)


def changes(src, diff, rows, cols, store):
    for col in range(cols):
        def keep(row, parts, col=col):
            for comp in range(4):
                diff[comp, row, col] = parts[comp]

        sweep(lambda row, col=col: [src[comp, row, col] for comp in X_ORDER], keep, rows, 0)
    for row in range(rows):
        def add(col, parts, row=row):
            store(row, col, [parts[Y_ORDER[comp]] + diff[comp, row, col] for comp in range(4)])

        sweep(lambda col, row=row: [src[comp, row, col] for comp in Y_ORDER], add, cols, 1)


def first_kernel(state_ref, up_ref, down_ref, before_ref, after_ref, field_ref, change_ref, plain, dealt, diff):
    rows, cols = state_ref.shape[1:]
    tall = rows + 2 * HALO
    half = tall // 2
    wide = plain.shape[1]
    groups = wide // LANES
    for comp in range(4):
        span = slice(comp * HALO, (comp + 1) * HALO)
        low = comp * tall
        plain[low : low + HALO, 0:cols] = up_ref[span, :]
        plain[low + HALO : low + HALO + rows, 0:cols] = state_ref[comp]
        plain[low + HALO + rows : low + tall, 0:cols] = down_ref[span, :]
    lane = iota((half, LANES), 1)
    from_before = before_ref[0:half, :]
    from_after = after_ref[0:half, :]
    for side in range(2):
        for comp in range(4):
            at = side * (LANES // 2) + comp * HALO
            left = pltpu.roll(from_before, (LANES - HALO - at) % LANES, axis=1)
            right = pltpu.roll(from_after, (-at) % LANES, axis=1)
            low = comp * tall + side * half
            plain[low : low + half, cols:] = jnp.where(lane < LANES // 2, right, left)
    source = iota((wide, wide), 0)
    goal = iota((wide, wide), 1)
    place = groups * (goal % LANES) + goal // LANES
    place = jnp.where(place < cols + 2 * HALO, (place + wide - HALO) % wide, 0)
    select = jnp.where(source == place, 1.0, 0.0).astype(jnp.bfloat16)
    found = selected(plain[...], select)
    for comp in range(4):
        for group in range(groups):
            dealt[comp, group] = found[comp * tall : (comp + 1) * tall, group * LANES : (group + 1) * LANES]
    count = tall // 8
    for comp in range(4):
        for row in range(count):
            for group in range(groups):
                field_ref[comp, row, group] = dealt[comp, group, pl.ds(row, 8, stride=count), :]

    def store(row, col, parts):
        for comp in range(4):
            change_ref[comp, row, col] = parts[comp]

    changes(field_ref, diff, count, groups, store)


def steps_kernel(field_ref, change_ref, own_ref, far_ref, out_ref, field, mid, diff, dealt):
    rows, cols = out_ref.shape[1:]
    tall = rows + 2 * HALO
    groups = field_ref.shape[2]
    factor = -0.5 * COURANT / jnp.maximum(own_ref[...], far_ref[...])
    half_factor = 0.5 * factor

    for index in range(STEPS):
        start = 4 * index
        count = (tall - 8 * index) // 8
        old = field_ref if index == 0 else field

        def to_mid(row, col, parts):
            for comp in range(4):
                mid[comp, row, col] = old[comp, row, col] + factor * parts[comp]

        def to_field(row, col, parts):
            for comp in range(4):
                mean = 0.5 * (old[comp, row, col] + mid[comp, row, col])
                dealt[comp, col, pl.ds(start + row, 8, stride=count), :] = mean + half_factor * parts[comp]

        if index == 0:
            for row in range(count):
                for col in range(groups):
                    to_mid(row, col, [change_ref[comp, row, col] for comp in range(4)])
        else:
            for comp in range(4):
                for row in range(count):
                    for col in range(groups):
                        field[comp, row, col] = dealt[comp, col, pl.ds(start + row, 8, stride=count), :]
            changes(field, diff, count, groups, to_mid)
        changes(mid, diff, count, groups, to_field)

    wide = groups * LANES
    source = iota((wide, cols), 0)
    goal = iota((wide, cols), 1)
    select = jnp.where(groups * (source % LANES) + source // LANES == goal + HALO, 1.0, 0.0).astype(jnp.bfloat16)
    lane = iota((rows, LANES), 1)
    parts = []
    for comp in range(4):
        line = []
        for group in range(groups):
            place = groups * lane + group
            inside = (place >= HALO) & (place < HALO + cols)
            line.append(jnp.where(inside, dealt[comp, group, HALO : HALO + rows, :], 0.0))
        parts.append(jnp.concatenate(line, axis=1))
    found = selected(jnp.concatenate(parts, axis=0), select)
    for comp in range(4):
        out_ref[comp] = found[comp * rows : (comp + 1) * rows, :]


def local(state):
    parts, rows, cols = state.shape
    tall = rows + 2 * HALO
    groups = -(-(cols + 2 * HALO) // LANES)

    def sent(value, axis, by):
        count = lax.axis_size(axis)
        return lax.ppermute(value, axis, [(i, (i + by) % count) for i in range(count)])

    edge_type = array(parts * HALO + 8, cols)
    head, tail, top = pl.pallas_call(
        edge_kernel,
        out_shape=(edge_type, edge_type, array(8, LANES)),
        in_specs=[VMEM],
        out_specs=(VMEM,) * 3,
        compiler_params=params(4),
        name="edge",
    )(state)
    up = sent(tail, "gx", 1)
    down = sent(head, "gx", -1)
    far = sent(top, "gx", 2)
    side_type = array(tall // 2 + 8, LANES)
    left, right, top = pl.pallas_call(
        pack_kernel,
        out_shape=(side_type, side_type, array(8, LANES)),
        in_specs=[VMEM] * 5,
        out_specs=(VMEM,) * 3,
        compiler_params=params(4),
        name="pack",
    )(state, up, down, top, far)
    before = sent(right, "gy", 1)
    after = sent(left, "gy", -1)
    far = sent(top, "gy", 2)
    top = jnp.maximum(jnp.maximum(top, far), jnp.maximum(before[tall // 2 :], after[tall // 2 :]))
    for axis in ("gy", "gx"):
        covered = 4
        while covered < lax.axis_size(axis):
            far = sent(top, axis, covered)
            covered *= 2
            last = axis == "gx" and covered >= lax.axis_size(axis)
            if not last:
                top = jnp.maximum(top, far)
    dealt_type = array(parts, tall // 8, groups, 8, LANES)
    dealt = pltpu.VMEM(dealt_type.shape, jnp.float32)
    plain = pltpu.VMEM((parts, groups, tall, LANES), jnp.float32)
    field, change = pl.pallas_call(
        first_kernel,
        out_shape=(dealt_type, dealt_type),
        in_specs=[VMEM] * 5,
        out_specs=(VMEM,) * 2,
        scratch_shapes=[pltpu.VMEM((parts * tall, groups * LANES), jnp.float32), plain, dealt],
        compiler_params=params(16),
        cost_estimate=pl.CostEstimate(flops=20_000_000, bytes_accessed=2_000_000, transcendentals=400_000),
        name="first",
    )(state, up, down, before, after)
    return pl.pallas_call(
        steps_kernel,
        out_shape=array(parts, rows, cols),
        in_specs=[VMEM] * 4,
        out_specs=VMEM,
        scratch_shapes=[dealt, dealt, dealt, plain],
        compiler_params=params(16),
        name="steps",
    )(field, change, top, far)


def solution(mesh):
    in_specs = (P(None, "gx", "gy"),)
    out_specs = P(None, "gx", "gy")
    return jax.shard_map(local, mesh=mesh, in_specs=in_specs, out_specs=out_specs, check_vma=False)
```

```python
import functools

import jax
import jax.numpy as jnp
from jax import lax
from jax.experimental import pallas as pl
from jax.experimental.pallas import tpu as pltpu
from jax.sharding import PartitionSpec as P

STEPS = 4
HALO = 4 * STEPS
LANES = 128
GAMMA = 1.4
COURANT = 0.35
TINY = 1e-30

VMEM = pl.BlockSpec(memory_space=pltpu.VMEM)


def params(limit):
    return pltpu.CompilerParams(vmem_limit_bytes=limit << 20)


def array(*shape):
    return jax.ShapeDtypeStruct(shape, jnp.float32)


def iota(shape, dim):
    return lax.broadcasted_iota(jnp.int32, shape, dim)


def odd(axis):
    return lax.rem(lax.axis_index(axis), 2) == 1


def edge_kernel(state_ref, block_ref, first_ref, second_ref, top_ref, sems):
    rows = state_ref.shape[1]
    copies = [
        pltpu.make_async_copy(
            state_ref.at[comp, pl.ds(low, rows // 2)], block_ref.at[comp, pl.ds(low, rows // 2)], sems.at[comp, side]
        )
        for comp in range(4)
        for side, low in enumerate((0, rows // 2))
    ]
    for copy in copies:
        copy.start()
    for copy in copies:
        copy.wait()
    density, mom_x, mom_y, energy = (block_ref[comp] for comp in range(4))
    inv = 1.0 / density
    pressure = (GAMMA - 1.0) * (energy - 0.5 * (mom_x * mom_x + mom_y * mom_y) * inv)
    speed = jnp.maximum(jnp.abs(mom_x * inv), jnp.abs(mom_y * inv)) + jnp.sqrt(GAMMA * pressure * inv)
    top = jnp.max(speed)
    is_odd = odd("gx")
    for comp in range(4):
        span = slice(comp * HALO, (comp + 1) * HALO)
        head = block_ref[comp, 0:HALO, :]
        tail = block_ref[comp, rows - HALO : rows, :]
        first_ref[span, :] = jnp.where(is_odd, head, tail)
        second_ref[span, :] = jnp.where(is_odd, tail, head)
    first_ref[4 * HALO :, :] = jnp.full((8, first_ref.shape[1]), top)
    second_ref[4 * HALO :, :] = jnp.full((8, second_ref.shape[1]), top)
    top_ref[...] = jnp.full(top_ref.shape, top)


def pack_kernel(state_ref, swap_ref, next_ref, own_ref, far_ref, up_ref, down_ref, first_ref, second_ref, top_ref):
    rows = state_ref.shape[1]
    cols = state_ref.shape[2]
    half = rows // 2 + HALO
    lane = iota((half, LANES), 1)
    is_odd = odd("gx")
    up_ref[...] = jnp.where(is_odd, swap_ref[...], next_ref[...])
    down_ref[...] = jnp.where(is_odd, next_ref[...], swap_ref[...])
    top = jnp.maximum(jnp.maximum(own_ref[...], far_ref[...]),
                      jnp.maximum(up_ref[4 * HALO :, 0:LANES], down_ref[4 * HALO :, 0:LANES]))

    def edge(low, at):
        lanes = slice(low, low + LANES)
        total = jnp.zeros((half, LANES), jnp.float32)
        for side in range(2):
            for comp in range(4):
                span = slice(comp * HALO, (comp + 1) * HALO)
                if side == 0:
                    cells = jnp.concatenate([up_ref[span, lanes], state_ref[comp, 0 : rows // 2, lanes]], axis=0)
                else:
                    cells = jnp.concatenate([state_ref[comp, rows // 2 : rows, lanes], down_ref[span, lanes]], axis=0)
                goal = side * (LANES // 2) + comp * HALO
                moved = pltpu.roll(cells, (goal - at) % LANES, axis=1)
                total = jnp.where((lane >= goal) & (lane < goal + HALO), moved, total)
        return total

    left = edge(0, 0)
    right = edge(cols - LANES, LANES - HALO)
    is_odd = odd("gy")
    first_ref[0:half, :] = jnp.where(is_odd, left, right)
    second_ref[0:half, :] = jnp.where(is_odd, right, left)
    first_ref[half:, :] = top
    second_ref[half:, :] = top
    top_ref[...] = top


def selected(values, select):
    total = None
    for _ in range(3):
        part = values.astype(jnp.bfloat16)
        values = values - part.astype(jnp.float32)
        term = jnp.dot(part, select, preferred_element_type=jnp.float32)
        total = term if total is None else total + term
    return total


def minmod(first, second):
    low = jnp.minimum(first, second)
    high = jnp.maximum(first, second)
    return jnp.maximum(low, jnp.minimum(high, 0.0))


def fluxes(state):
    density, normal, tangent, energy = state
    inv = pl.reciprocal(density, approx=True)
    vel = normal * inv
    carried = normal * vel
    pressure = (GAMMA - 1.0) * energy - (0.5 * (GAMMA - 1.0)) * (carried + tangent * tangent * inv)
    square = GAMMA * pressure * inv
    sound = square * lax.rsqrt(jnp.maximum(square, TINY))
    return (normal, carried + pressure, tangent * vel, (energy + pressure) * vel), jnp.abs(vel) + sound


def face(left, right):
    (left_state, left_flux, left_speed), (right_state, right_flux, right_speed) = left, right
    top = jnp.maximum(left_speed, right_speed)
    return [
        (left_flux[comp] + right_flux[comp]) - top * (right_state[comp] - left_state[comp]) for comp in range(4)
    ]


def minus(first, second):
    return [first[comp] - second[comp] for comp in range(4)]


def sweep(load, store, count, axis):
    def rolled(tree, by):
        return jax.tree.map(lambda value: pltpu.roll(value, by % value.shape[axis], axis=axis), tree)

    def half(parts):
        return [0.5 * part for part in parts]

    here = load(0)
    end_jump = half(minus(rolled(here, -1), load(count - 1)))
    jump = rolled(end_jump, 1)
    for at in range(count):
        after = load(at + 1) if at + 1 < count else None
        next_jump = half(minus(after, here)) if at + 1 < count else end_jump
        slope = [minmod(jump[comp], next_jump[comp]) for comp in range(4)]
        low_state = minus(here, slope)
        high_state = [here[comp] + slope[comp] for comp in range(4)]
        low = (low_state, *fluxes(low_state))
        if at == 0:
            first_low = low
        else:
            flux = face(high, low)
            if at == 1:
                first_flux = flux
            else:
                store(at - 1, minus(flux, last_flux))
            last_flux = flux
        high = (high_state, *fluxes(high_state))
        here, jump = after, next_jump
    flux = face(high, rolled(first_low, -1))
    store(count - 1, minus(flux, last_flux))
    store(0, minus(first_flux, rolled(flux, 1)))


X_ORDER = (0, 1, 2, 3)
Y_ORDER = (0, 2, 1, 3)


def changes(src, diff, rows, cols, store):
    for col in range(cols):
        def keep(row, parts, col=col):
            for comp in range(4):
                diff[comp, row, col] = parts[comp]

        sweep(lambda row, col=col: [src[comp, row, col] for comp in X_ORDER], keep, rows, 0)
    for row in range(rows):
        def add(col, parts, row=row):
            store(row, col, [parts[Y_ORDER[comp]] + diff[comp, row, col] for comp in range(4)])

        sweep(lambda col, row=row: [src[comp, row, col] for comp in Y_ORDER], add, cols, 1)


def first_kernel(state_ref, up_ref, down_ref, swap_ref, next_ref, field_ref, change_ref, plain, dealt, diff):
    rows, cols = state_ref.shape[1:]
    tall = rows + 2 * HALO
    half = tall // 2
    wide = plain.shape[1]
    groups = wide // LANES
    for comp in range(4):
        span = slice(comp * HALO, (comp + 1) * HALO)
        low = comp * tall
        plain[low : low + HALO, 0:cols] = up_ref[span, :]
        plain[low + HALO : low + HALO + rows, 0:cols] = state_ref[comp]
        plain[low + HALO + rows : low + tall, 0:cols] = down_ref[span, :]
    lane = iota((half, LANES), 1)
    is_odd = odd("gy")
    from_swap = swap_ref[0:half, :]
    from_next = next_ref[0:half, :]
    from_before = jnp.where(is_odd, from_swap, from_next)
    from_after = jnp.where(is_odd, from_next, from_swap)
    for side in range(2):
        for comp in range(4):
            at = side * (LANES // 2) + comp * HALO
            left = pltpu.roll(from_before, (LANES - HALO - at) % LANES, axis=1)
            right = pltpu.roll(from_after, (-at) % LANES, axis=1)
            low = comp * tall + side * half
            plain[low : low + half, cols:] = jnp.where(lane < LANES // 2, right, left)
    source = iota((wide, wide), 0)
    goal = iota((wide, wide), 1)
    place = groups * (goal % LANES) + goal // LANES
    place = jnp.where(place < cols + 2 * HALO, (place + wide - HALO) % wide, 0)
    select = jnp.where(source == place, 1.0, 0.0).astype(jnp.bfloat16)
    found = selected(plain[...], select)
    for comp in range(4):
        for group in range(groups):
            dealt[comp, group] = found[comp * tall : (comp + 1) * tall, group * LANES : (group + 1) * LANES]
    count = tall // 8
    for comp in range(4):
        for row in range(count):
            for group in range(groups):
                field_ref[comp, row, group] = dealt[comp, group, pl.ds(row, 8, stride=count), :]

    def store(row, col, parts):
        for comp in range(4):
            change_ref[comp, row, col] = parts[comp]

    changes(field_ref, diff, count, groups, store)


def steps_kernel(field_ref, change_ref, own_ref, far_ref, out_ref, field, mid, diff, dealt):
    rows, cols = out_ref.shape[1:]
    tall = rows + 2 * HALO
    groups = field_ref.shape[2]
    factor = -0.5 * COURANT / jnp.where(odd("gx"), own_ref[...], far_ref[...])
    half_factor = 0.5 * factor

    for index in range(STEPS):
        start = 4 * index
        count = (tall - 8 * index) // 8
        old = field_ref if index == 0 else field

        def to_mid(row, col, parts):
            for comp in range(4):
                mid[comp, row, col] = old[comp, row, col] + factor * parts[comp]

        def to_field(row, col, parts):
            for comp in range(4):
                mean = 0.5 * (old[comp, row, col] + mid[comp, row, col])
                dealt[comp, col, pl.ds(start + row, 8, stride=count), :] = mean + half_factor * parts[comp]

        if index == 0:
            for row in range(count):
                for col in range(groups):
                    to_mid(row, col, [change_ref[comp, row, col] for comp in range(4)])
        else:
            for comp in range(4):
                for row in range(count):
                    for col in range(groups):
                        field[comp, row, col] = dealt[comp, col, pl.ds(start + row, 8, stride=count), :]
            changes(field, diff, count, groups, to_mid)
        changes(mid, diff, count, groups, to_field)

    wide = groups * LANES
    source = iota((wide, cols), 0)
    goal = iota((wide, cols), 1)
    select = jnp.where(groups * (source % LANES) + source // LANES == goal + HALO, 1.0, 0.0).astype(jnp.bfloat16)
    lane = iota((rows, LANES), 1)
    parts = []
    for comp in range(4):
        line = []
        for group in range(groups):
            place = groups * lane + group
            inside = (place >= HALO) & (place < HALO + cols)
            line.append(jnp.where(inside, dealt[comp, group, HALO : HALO + rows, :], 0.0))
        parts.append(jnp.concatenate(line, axis=1))
    found = selected(jnp.concatenate(parts, axis=0), select)
    for comp in range(4):
        out_ref[comp] = found[comp * rows : (comp + 1) * rows, :]


def local(state):
    parts, rows, cols = state.shape
    tall = rows + 2 * HALO
    groups = -(-(cols + 2 * HALO) // LANES)

    def sent(value, axis, by, odd_x=False):
        count = lax.axis_size(axis)
        if not odd_x:
            return lax.ppermute(value, axis, [(i, (i + by) % count) for i in range(count)])
        count_x, count_y = lax.axis_size("gx"), lax.axis_size("gy")
        pairs = []
        for x in range(1, count_x, 2):
            for y in range(count_y):
                goal = ((x + by) % count_x, y) if axis == "gx" else (x, (y + by) % count_y)
                pairs.append((x * count_y + y, goal[0] * count_y + goal[1]))
        return lax.ppermute(value, ("gx", "gy"), pairs)

    def swapped_pairs(value, axis, first):
        count = lax.axis_size(axis)
        pairs = []
        for low in range(first, count, 2):
            high = (low + 1) % count
            pairs += [(low, high), (high, low)]
        return lax.ppermute(value, axis, pairs)

    edge_type = array(parts * HALO + 8, cols)
    block, first, second, top = pl.pallas_call(
        edge_kernel,
        out_shape=(array(parts, rows, cols), edge_type, edge_type, array(8, LANES)),
        in_specs=[pl.BlockSpec(memory_space=pltpu.HBM)],
        out_specs=(VMEM,) * 4,
        scratch_shapes=[pltpu.SemaphoreType.DMA((4, 2))],
        compiler_params=params(4),
        name="edge",
    )(state)
    first = swapped_pairs(first, "gx", 0)
    second = swapped_pairs(second, "gx", 1)
    far = sent(top, "gx", 2, odd_x=True)
    side_type = array(tall // 2 + 8, LANES)
    up, down, first, second, top = pl.pallas_call(
        pack_kernel,
        out_shape=(edge_type, edge_type, side_type, side_type, array(8, LANES)),
        in_specs=[VMEM] * 5,
        out_specs=(VMEM,) * 5,
        compiler_params=params(4),
        name="pack",
    )(block, first, second, top, far)
    first = swapped_pairs(first, "gy", 0)
    second = swapped_pairs(second, "gy", 1)
    far = sent(top, "gy", 2, odd_x=True)
    top = jnp.maximum(jnp.maximum(top, far), jnp.maximum(first[tall // 2 :], second[tall // 2 :]))
    for axis in ("gy", "gx"):
        covered = 4
        while covered < lax.axis_size(axis):
            top = jnp.maximum(top, sent(top, axis, covered, odd_x=True))
            covered *= 2
    far = lax.ppermute(top, "gx", [(i, i - 1) for i in range(1, lax.axis_size("gx"), 2)])
    dealt_type = array(parts, tall // 8, groups, 8, LANES)
    dealt = pltpu.VMEM(dealt_type.shape, jnp.float32)
    plain = pltpu.VMEM((parts, groups, tall, LANES), jnp.float32)
    field, change = pl.pallas_call(
        first_kernel,
        out_shape=(dealt_type, dealt_type),
        in_specs=[VMEM] * 5,
        out_specs=(VMEM,) * 2,
        scratch_shapes=[pltpu.VMEM((parts * tall, groups * LANES), jnp.float32), plain, dealt],
        compiler_params=params(16),
        cost_estimate=pl.CostEstimate(flops=20_000_000, bytes_accessed=2_000_000, transcendentals=400_000),
        name="first",
    )(block, up, down, first, second)
    return pl.pallas_call(
        steps_kernel,
        out_shape=array(parts, rows, cols),
        in_specs=[VMEM] * 4,
        out_specs=VMEM,
        scratch_shapes=[dealt, dealt, dealt, plain],
        compiler_params=params(16),
        name="steps",
    )(field, change, top, far)


def solution(mesh):
    in_specs = (P(None, "gx", "gy"),)
    out_specs = P(None, "gx", "gy")
    return jax.shard_map(local, mesh=mesh, in_specs=in_specs, out_specs=out_specs, check_vma=False)
```

```python
import functools

import jax
import jax.numpy as jnp
from jax import lax
from jax.experimental import pallas as pl
from jax.experimental.pallas import tpu as pltpu
from jax.sharding import PartitionSpec as P

STEPS = 4
HALO = 4 * STEPS
LANES = 128
GAMMA = 1.4
COURANT = 0.35
TINY = 1e-30

VMEM = pl.BlockSpec(memory_space=pltpu.VMEM)


def params(limit):
    return pltpu.CompilerParams(vmem_limit_bytes=limit << 20)


def array(*shape):
    return jax.ShapeDtypeStruct(shape, jnp.float32)


def iota(shape, dim):
    return lax.broadcasted_iota(jnp.int32, shape, dim)


def odd(axis):
    return lax.rem(lax.axis_index(axis), 2) == 1


def edge_kernel(block_ref, first_ref, second_ref, top_ref):
    rows = block_ref.shape[1]
    density, mom_x, mom_y, energy = (block_ref[comp] for comp in range(4))
    inv = 1.0 / density
    pressure = (GAMMA - 1.0) * (energy - 0.5 * (mom_x * mom_x + mom_y * mom_y) * inv)
    speed = jnp.maximum(jnp.abs(mom_x * inv), jnp.abs(mom_y * inv)) + jnp.sqrt(GAMMA * pressure * inv)
    top = jnp.max(speed)
    is_odd = odd("gx")
    for comp in range(4):
        span = slice(comp * HALO, (comp + 1) * HALO)
        head = block_ref[comp, 0:HALO, :]
        tail = block_ref[comp, rows - HALO : rows, :]
        first_ref[span, :] = jnp.where(is_odd, head, tail)
        second_ref[span, :] = jnp.where(is_odd, tail, head)
    first_ref[4 * HALO :, :] = jnp.full((8, first_ref.shape[1]), top)
    second_ref[4 * HALO :, :] = jnp.full((8, second_ref.shape[1]), top)
    top_ref[...] = jnp.full(top_ref.shape, top)


def pack_kernel(state_ref, swap_ref, next_ref, own_ref, far_ref, up_ref, down_ref, first_ref, second_ref, top_ref):
    rows = state_ref.shape[1]
    cols = state_ref.shape[2]
    half = rows // 2 + HALO
    lane = iota((half, LANES), 1)
    is_odd = odd("gx")
    up_ref[...] = jnp.where(is_odd, swap_ref[...], next_ref[...])
    down_ref[...] = jnp.where(is_odd, next_ref[...], swap_ref[...])
    top = jnp.maximum(jnp.maximum(own_ref[...], far_ref[...]),
                      jnp.maximum(up_ref[4 * HALO :, 0:LANES], down_ref[4 * HALO :, 0:LANES]))

    def edge(low, at):
        lanes = slice(low, low + LANES)
        total = jnp.zeros((half, LANES), jnp.float32)
        for side in range(2):
            for comp in range(4):
                span = slice(comp * HALO, (comp + 1) * HALO)
                if side == 0:
                    cells = jnp.concatenate([up_ref[span, lanes], state_ref[comp, 0 : rows // 2, lanes]], axis=0)
                else:
                    cells = jnp.concatenate([state_ref[comp, rows // 2 : rows, lanes], down_ref[span, lanes]], axis=0)
                goal = side * (LANES // 2) + comp * HALO
                moved = pltpu.roll(cells, (goal - at) % LANES, axis=1)
                total = jnp.where((lane >= goal) & (lane < goal + HALO), moved, total)
        return total

    left = edge(0, 0)
    right = edge(cols - LANES, LANES - HALO)
    is_odd = odd("gy")
    first_ref[0:half, :] = jnp.where(is_odd, left, right)
    second_ref[0:half, :] = jnp.where(is_odd, right, left)
    first_ref[half:, :] = top
    second_ref[half:, :] = top
    top_ref[...] = top


def selected(values, select):
    total = None
    for _ in range(3):
        part = values.astype(jnp.bfloat16)
        values = values - part.astype(jnp.float32)
        term = jnp.dot(part, select, preferred_element_type=jnp.float32)
        total = term if total is None else total + term
    return total


def minmod(first, second):
    low = jnp.minimum(first, second)
    high = jnp.maximum(first, second)
    return jnp.maximum(low, jnp.minimum(high, 0.0))


def fluxes(state):
    density, normal, tangent, energy = state
    inv = pl.reciprocal(density, approx=True)
    vel = normal * inv
    carried = normal * vel
    pressure = (GAMMA - 1.0) * energy - (0.5 * (GAMMA - 1.0)) * (carried + tangent * tangent * inv)
    square = GAMMA * pressure * inv
    sound = square * lax.rsqrt(jnp.maximum(square, TINY))
    return (normal, carried + pressure, tangent * vel, (energy + pressure) * vel), jnp.abs(vel) + sound


def face(left, right):
    (left_state, left_flux, left_speed), (right_state, right_flux, right_speed) = left, right
    top = jnp.maximum(left_speed, right_speed)
    return [
        (left_flux[comp] + right_flux[comp]) - top * (right_state[comp] - left_state[comp]) for comp in range(4)
    ]


def minus(first, second):
    return [first[comp] - second[comp] for comp in range(4)]


def sweep(load, store, count, axis):
    def rolled(tree, by):
        return jax.tree.map(lambda value: pltpu.roll(value, by % value.shape[axis], axis=axis), tree)

    def half(parts):
        return [0.5 * part for part in parts]

    here = load(0)
    end_jump = half(minus(rolled(here, -1), load(count - 1)))
    jump = rolled(end_jump, 1)
    for at in range(count):
        after = load(at + 1) if at + 1 < count else None
        next_jump = half(minus(after, here)) if at + 1 < count else end_jump
        slope = [minmod(jump[comp], next_jump[comp]) for comp in range(4)]
        low_state = minus(here, slope)
        high_state = [here[comp] + slope[comp] for comp in range(4)]
        low = (low_state, *fluxes(low_state))
        if at == 0:
            first_low = low
        else:
            flux = face(high, low)
            if at == 1:
                first_flux = flux
            else:
                store(at - 1, minus(flux, last_flux))
            last_flux = flux
        high = (high_state, *fluxes(high_state))
        here, jump = after, next_jump
    flux = face(high, rolled(first_low, -1))
    store(count - 1, minus(flux, last_flux))
    store(0, minus(first_flux, rolled(flux, 1)))


X_ORDER = (0, 1, 2, 3)
Y_ORDER = (0, 2, 1, 3)


def changes(src, diff, rows, cols, store):
    for col in range(cols):
        def keep(row, parts, col=col):
            for comp in range(4):
                diff[comp, row, col] = parts[comp]

        sweep(lambda row, col=col: [src[comp, row, col] for comp in X_ORDER], keep, rows, 0)
    for row in range(rows):
        def add(col, parts, row=row):
            store(row, col, [parts[Y_ORDER[comp]] + diff[comp, row, col] for comp in range(4)])

        sweep(lambda col, row=row: [src[comp, row, col] for comp in Y_ORDER], add, cols, 1)


def first_kernel(state_ref, up_ref, down_ref, swap_ref, next_ref, field_ref, change_ref, plain, dealt, diff):
    rows, cols = state_ref.shape[1:]
    tall = rows + 2 * HALO
    half = tall // 2
    wide = plain.shape[1]
    groups = wide // LANES
    for comp in range(4):
        span = slice(comp * HALO, (comp + 1) * HALO)
        low = comp * tall
        plain[low : low + HALO, 0:cols] = up_ref[span, :]
        plain[low + HALO : low + HALO + rows, 0:cols] = state_ref[comp]
        plain[low + HALO + rows : low + tall, 0:cols] = down_ref[span, :]
    lane = iota((half, LANES), 1)
    is_odd = odd("gy")
    from_swap = swap_ref[0:half, :]
    from_next = next_ref[0:half, :]
    from_before = jnp.where(is_odd, from_swap, from_next)
    from_after = jnp.where(is_odd, from_next, from_swap)
    for side in range(2):
        for comp in range(4):
            at = side * (LANES // 2) + comp * HALO
            left = pltpu.roll(from_before, (LANES - HALO - at) % LANES, axis=1)
            right = pltpu.roll(from_after, (-at) % LANES, axis=1)
            low = comp * tall + side * half
            plain[low : low + half, cols:] = jnp.where(lane < LANES // 2, right, left)
    source = iota((wide, wide), 0)
    goal = iota((wide, wide), 1)
    place = groups * (goal % LANES) + goal // LANES
    place = jnp.where(place < cols + 2 * HALO, (place + wide - HALO) % wide, 0)
    select = jnp.where(source == place, 1.0, 0.0).astype(jnp.bfloat16)
    found = selected(plain[...], select)
    for comp in range(4):
        for group in range(groups):
            dealt[comp, group] = found[comp * tall : (comp + 1) * tall, group * LANES : (group + 1) * LANES]
    count = tall // 8
    for comp in range(4):
        for row in range(count):
            for group in range(groups):
                field_ref[comp, row, group] = dealt[comp, group, pl.ds(row, 8, stride=count), :]

    def store(row, col, parts):
        for comp in range(4):
            change_ref[comp, row, col] = parts[comp]

    changes(field_ref, diff, count, groups, store)


def steps_kernel(field_ref, change_ref, own_ref, far_ref, out_ref, field, mid, diff, dealt):
    rows, cols = out_ref.shape[1:]
    tall = rows + 2 * HALO
    groups = field_ref.shape[2]
    factor = -0.5 * COURANT / jnp.maximum(own_ref[...], far_ref[...])
    half_factor = 0.5 * factor

    for index in range(STEPS):
        start = 4 * index
        count = (tall - 8 * index) // 8
        old = field_ref if index == 0 else field

        def to_mid(row, col, parts):
            for comp in range(4):
                mid[comp, row, col] = old[comp, row, col] + factor * parts[comp]

        def to_field(row, col, parts):
            for comp in range(4):
                mean = 0.5 * (old[comp, row, col] + mid[comp, row, col])
                dealt[comp, col, pl.ds(start + row, 8, stride=count), :] = mean + half_factor * parts[comp]

        if index == 0:
            for row in range(count):
                for col in range(groups):
                    to_mid(row, col, [change_ref[comp, row, col] for comp in range(4)])
        else:
            for comp in range(4):
                for row in range(count):
                    for col in range(groups):
                        field[comp, row, col] = dealt[comp, col, pl.ds(start + row, 8, stride=count), :]
            changes(field, diff, count, groups, to_mid)
        changes(mid, diff, count, groups, to_field)

    wide = groups * LANES
    source = iota((wide, cols), 0)
    goal = iota((wide, cols), 1)
    select = jnp.where(groups * (source % LANES) + source // LANES == goal + HALO, 1.0, 0.0).astype(jnp.bfloat16)
    lane = iota((rows, LANES), 1)
    parts = []
    for comp in range(4):
        line = []
        for group in range(groups):
            place = groups * lane + group
            inside = (place >= HALO) & (place < HALO + cols)
            line.append(jnp.where(inside, dealt[comp, group, HALO : HALO + rows, :], 0.0))
        parts.append(jnp.concatenate(line, axis=1))
    found = selected(jnp.concatenate(parts, axis=0), select)
    for comp in range(4):
        out_ref[comp] = found[comp * rows : (comp + 1) * rows, :]


def local(state):
    parts, rows, cols = state.shape
    tall = rows + 2 * HALO
    groups = -(-(cols + 2 * HALO) // LANES)

    def sent(value, axis, by):
        count = lax.axis_size(axis)
        return lax.ppermute(value, axis, [(i, (i + by) % count) for i in range(count)])

    def swapped_twos(value, axis):
        count = lax.axis_size(axis)
        return lax.ppermute(value, axis, [(i, i ^ 2) for i in range(count)])

    def swapped_pairs(value, axis, first):
        count = lax.axis_size(axis)
        pairs = []
        for low in range(first, count, 2):
            high = (low + 1) % count
            pairs += [(low, high), (high, low)]
        return lax.ppermute(value, axis, pairs)

    edge_type = array(parts * HALO + 8, cols)
    first, second, top = pl.pallas_call(
        edge_kernel,
        out_shape=(edge_type, edge_type, array(8, LANES)),
        in_specs=[VMEM],
        out_specs=(VMEM,) * 3,
        compiler_params=params(4),
        name="edge",
    )(state)
    second = swapped_pairs(second, "gx", 1)
    first = swapped_pairs(first, "gx", 0)
    far = swapped_twos(top, "gx")
    side_type = array(tall // 2 + 8, LANES)
    up, down, first, second, top = pl.pallas_call(
        pack_kernel,
        out_shape=(edge_type, edge_type, side_type, side_type, array(8, LANES)),
        in_specs=[VMEM] * 5,
        out_specs=(VMEM,) * 5,
        compiler_params=params(4),
        name="pack",
    )(state, first, second, top, far)
    second = swapped_pairs(second, "gy", 1)
    first = swapped_pairs(first, "gy", 0)
    far = swapped_twos(top, "gy")
    top = jnp.maximum(jnp.maximum(top, far), jnp.maximum(first[tall // 2 :], second[tall // 2 :]))
    for axis in ("gy", "gx"):
        covered = 4
        while covered < lax.axis_size(axis):
            far = sent(top, axis, covered)
            covered *= 2
            if axis == "gy" or covered < lax.axis_size(axis):
                top = jnp.maximum(top, far)
    dealt_type = array(parts, tall // 8, groups, 8, LANES)
    dealt = pltpu.VMEM(dealt_type.shape, jnp.float32)
    plain = pltpu.VMEM((parts, groups, tall, LANES), jnp.float32)
    field, change = pl.pallas_call(
        first_kernel,
        out_shape=(dealt_type, dealt_type),
        in_specs=[VMEM] * 5,
        out_specs=(VMEM,) * 2,
        scratch_shapes=[pltpu.VMEM((parts * tall, groups * LANES), jnp.float32), plain, dealt],
        compiler_params=params(16),
        cost_estimate=pl.CostEstimate(flops=20_000_000, bytes_accessed=2_000_000, transcendentals=400_000),
        name="first",
    )(state, up, down, first, second)
    return pl.pallas_call(
        steps_kernel,
        out_shape=array(parts, rows, cols),
        in_specs=[VMEM] * 4,
        out_specs=VMEM,
        scratch_shapes=[dealt, dealt, dealt, plain],
        compiler_params=params(16),
        name="steps",
    )(field, change, top, far)


def solution(mesh):
    in_specs = (P(None, "gx", "gy"),)
    out_specs = P(None, "gx", "gy")
    return jax.shard_map(local, mesh=mesh, in_specs=in_specs, out_specs=out_specs, check_vma=False)
```

```python
import functools

import jax
import jax.numpy as jnp
from jax import lax
from jax.experimental import pallas as pl
from jax.experimental.pallas import tpu as pltpu
from jax.sharding import PartitionSpec as P

STEPS = 4
HALO = 4 * STEPS
LANES = 128
GAMMA = 1.4
COURANT = 0.35
TINY = 1e-30

VMEM = pl.BlockSpec(memory_space=pltpu.VMEM)


def params(limit):
    return pltpu.CompilerParams(vmem_limit_bytes=limit << 20)


def array(*shape):
    return jax.ShapeDtypeStruct(shape, jnp.float32)


def iota(shape, dim):
    return lax.broadcasted_iota(jnp.int32, shape, dim)


def odd(axis):
    return lax.rem(lax.axis_index(axis), 2) == 1


def edge_kernel(block_ref, first_ref, second_ref, top_ref):
    rows = block_ref.shape[1]
    density, mom_x, mom_y, energy = (block_ref[comp] for comp in range(4))
    inv = 1.0 / density
    pressure = (GAMMA - 1.0) * (energy - 0.5 * (mom_x * mom_x + mom_y * mom_y) * inv)
    speed = jnp.maximum(jnp.abs(mom_x * inv), jnp.abs(mom_y * inv)) + jnp.sqrt(GAMMA * pressure * inv)
    top = jnp.max(speed)
    is_odd = odd("gx")
    for comp in range(4):
        span = slice(comp * HALO, (comp + 1) * HALO)
        head = block_ref[comp, 0:HALO, :]
        tail = block_ref[comp, rows - HALO : rows, :]
        first_ref[span, :] = jnp.where(is_odd, head, tail)
        second_ref[span, :] = jnp.where(is_odd, tail, head)
    first_ref[4 * HALO :, :] = jnp.full((8, first_ref.shape[1]), top)
    second_ref[4 * HALO :, :] = jnp.full((8, second_ref.shape[1]), top)
    top_ref[...] = jnp.full(top_ref.shape, top)


def pack_kernel(state_ref, swap_ref, next_ref, own_ref, far_ref, up_ref, down_ref, first_ref, second_ref, top_ref):
    rows = state_ref.shape[1]
    cols = state_ref.shape[2]
    half = rows // 2 + HALO
    lane = iota((half, LANES), 1)
    is_odd = odd("gx")
    up_ref[...] = jnp.where(is_odd, swap_ref[...], next_ref[...])
    down_ref[...] = jnp.where(is_odd, next_ref[...], swap_ref[...])
    top = jnp.maximum(jnp.maximum(own_ref[...], far_ref[...]),
                      jnp.maximum(up_ref[4 * HALO :, 0:LANES], down_ref[4 * HALO :, 0:LANES]))

    def edge(low, at):
        lanes = slice(low, low + LANES)
        total = jnp.zeros((half, LANES), jnp.float32)
        for side in range(2):
            for comp in range(4):
                span = slice(comp * HALO, (comp + 1) * HALO)
                if side == 0:
                    cells = jnp.concatenate([up_ref[span, lanes], state_ref[comp, 0 : rows // 2, lanes]], axis=0)
                else:
                    cells = jnp.concatenate([state_ref[comp, rows // 2 : rows, lanes], down_ref[span, lanes]], axis=0)
                goal = side * (LANES // 2) + comp * HALO
                moved = pltpu.roll(cells, (goal - at) % LANES, axis=1)
                total = jnp.where((lane >= goal) & (lane < goal + HALO), moved, total)
        return total

    left = edge(0, 0)
    right = edge(cols - LANES, LANES - HALO)
    is_odd = odd("gy")
    first_ref[0:half, :] = jnp.where(is_odd, left, right)
    second_ref[0:half, :] = jnp.where(is_odd, right, left)
    first_ref[half:, :] = top
    second_ref[half:, :] = top
    top_ref[...] = top


def selected(values, select):
    total = None
    for _ in range(3):
        part = values.astype(jnp.bfloat16)
        values = values - part.astype(jnp.float32)
        term = jnp.dot(part, select, preferred_element_type=jnp.float32)
        total = term if total is None else total + term
    return total


def minmod(first, second):
    low = jnp.minimum(first, second)
    high = jnp.maximum(first, second)
    return jnp.maximum(low, jnp.minimum(high, 0.0))


def fluxes(state):
    density, normal, tangent, energy = state
    inv = pl.reciprocal(density, approx=True)
    vel = normal * inv
    carried = normal * vel
    pressure = (GAMMA - 1.0) * energy - (0.5 * (GAMMA - 1.0)) * (carried + tangent * tangent * inv)
    square = GAMMA * pressure * inv
    sound = square * lax.rsqrt(jnp.maximum(square, TINY))
    return (normal, carried + pressure, tangent * vel, (energy + pressure) * vel), jnp.abs(vel) + sound


def face(left, right):
    (left_state, left_flux, left_speed), (right_state, right_flux, right_speed) = left, right
    top = jnp.maximum(left_speed, right_speed)
    return [
        (left_flux[comp] + right_flux[comp]) - top * (right_state[comp] - left_state[comp]) for comp in range(4)
    ]


def minus(first, second):
    return [first[comp] - second[comp] for comp in range(4)]


def sweep(load, store, count, axis):
    def rolled(tree, by):
        return jax.tree.map(lambda value: pltpu.roll(value, by % value.shape[axis], axis=axis), tree)

    def half(parts):
        return [0.5 * part for part in parts]

    here = load(0)
    end_jump = half(minus(rolled(here, -1), load(count - 1)))
    jump = rolled(end_jump, 1)
    for at in range(count):
        after = load(at + 1) if at + 1 < count else None
        next_jump = half(minus(after, here)) if at + 1 < count else end_jump
        slope = [minmod(jump[comp], next_jump[comp]) for comp in range(4)]
        low_state = minus(here, slope)
        high_state = [here[comp] + slope[comp] for comp in range(4)]
        low = (low_state, *fluxes(low_state))
        if at == 0:
            first_low = low
        else:
            flux = face(high, low)
            if at == 1:
                first_flux = flux
            else:
                store(at - 1, minus(flux, last_flux))
            last_flux = flux
        high = (high_state, *fluxes(high_state))
        here, jump = after, next_jump
    flux = face(high, rolled(first_low, -1))
    store(count - 1, minus(flux, last_flux))
    store(0, minus(first_flux, rolled(flux, 1)))


X_ORDER = (0, 1, 2, 3)
Y_ORDER = (0, 2, 1, 3)


def changes(src, diff, rows, cols, store):
    for col in range(cols):
        def keep(row, parts, col=col):
            for comp in range(4):
                diff[comp, row, col] = parts[comp]

        sweep(lambda row, col=col: [src[comp, row, col] for comp in X_ORDER], keep, rows, 0)
    for row in range(rows):
        def add(col, parts, row=row):
            store(row, col, [parts[Y_ORDER[comp]] + diff[comp, row, col] for comp in range(4)])

        sweep(lambda col, row=row: [src[comp, row, col] for comp in Y_ORDER], add, cols, 1)


def first_kernel(state_ref, up_ref, down_ref, swap_ref, next_ref, field_ref, change_ref, plain, dealt, diff):
    rows, cols = state_ref.shape[1:]
    tall = rows + 2 * HALO
    half = tall // 2
    wide = plain.shape[1]
    groups = wide // LANES
    for comp in range(4):
        span = slice(comp * HALO, (comp + 1) * HALO)
        low = comp * tall
        plain[low : low + HALO, 0:cols] = up_ref[span, :]
        plain[low + HALO : low + HALO + rows, 0:cols] = state_ref[comp]
        plain[low + HALO + rows : low + tall, 0:cols] = down_ref[span, :]
    lane = iota((half, LANES), 1)
    is_odd = odd("gy")
    from_swap = swap_ref[0:half, :]
    from_next = next_ref[0:half, :]
    from_before = jnp.where(is_odd, from_swap, from_next)
    from_after = jnp.where(is_odd, from_next, from_swap)
    for side in range(2):
        for comp in range(4):
            at = side * (LANES // 2) + comp * HALO
            left = pltpu.roll(from_before, (LANES - HALO - at) % LANES, axis=1)
            right = pltpu.roll(from_after, (-at) % LANES, axis=1)
            low = comp * tall + side * half
            plain[low : low + half, cols:] = jnp.where(lane < LANES // 2, right, left)
    source = iota((wide, wide), 0)
    goal = iota((wide, wide), 1)
    place = groups * (goal % LANES) + goal // LANES
    place = jnp.where(place < cols + 2 * HALO, (place + wide - HALO) % wide, 0)
    select = jnp.where(source == place, 1.0, 0.0).astype(jnp.bfloat16)
    found = selected(plain[...], select)
    for comp in range(4):
        for group in range(groups):
            dealt[comp, group] = found[comp * tall : (comp + 1) * tall, group * LANES : (group + 1) * LANES]
    count = tall // 8
    for comp in range(4):
        for row in range(count):
            for group in range(groups):
                field_ref[comp, row, group] = dealt[comp, group, pl.ds(row, 8, stride=count), :]

    def store(row, col, parts):
        for comp in range(4):
            change_ref[comp, row, col] = parts[comp]

    changes(field_ref, diff, count, groups, store)


def steps_kernel(field_ref, change_ref, own_ref, far_ref, out_ref, field, mid, diff, dealt):
    rows, cols = out_ref.shape[1:]
    tall = rows + 2 * HALO
    groups = field_ref.shape[2]
    factor = -0.5 * COURANT / jnp.maximum(own_ref[...], far_ref[...])
    half_factor = 0.5 * factor

    for index in range(STEPS):
        start = 4 * index
        count = (tall - 8 * index) // 8
        old = field_ref if index == 0 else field

        def to_mid(row, col, parts):
            for comp in range(4):
                mid[comp, row, col] = old[comp, row, col] + factor * parts[comp]

        def to_field(row, col, parts):
            for comp in range(4):
                mean = 0.5 * (old[comp, row, col] + mid[comp, row, col])
                dealt[comp, col, pl.ds(start + row, 8, stride=count), :] = mean + half_factor * parts[comp]

        if index == 0:
            for row in range(count):
                for col in range(groups):
                    to_mid(row, col, [change_ref[comp, row, col] for comp in range(4)])
        else:
            for comp in range(4):
                for row in range(count):
                    for col in range(groups):
                        field[comp, row, col] = dealt[comp, col, pl.ds(start + row, 8, stride=count), :]
            changes(field, diff, count, groups, to_mid)
        changes(mid, diff, count, groups, to_field)

    wide = groups * LANES
    source = iota((wide, cols), 0)
    goal = iota((wide, cols), 1)
    select = jnp.where(groups * (source % LANES) + source // LANES == goal + HALO, 1.0, 0.0).astype(jnp.bfloat16)
    lane = iota((rows, LANES), 1)
    parts = []
    for comp in range(4):
        line = []
        for group in range(groups):
            place = groups * lane + group
            inside = (place >= HALO) & (place < HALO + cols)
            line.append(jnp.where(inside, dealt[comp, group, HALO : HALO + rows, :], 0.0))
        parts.append(jnp.concatenate(line, axis=1))
    found = selected(jnp.concatenate(parts, axis=0), select)
    for comp in range(4):
        out_ref[comp] = found[comp * rows : (comp + 1) * rows, :]


def local(state):
    parts, rows, cols = state.shape
    tall = rows + 2 * HALO
    groups = -(-(cols + 2 * HALO) // LANES)

    def sent(value, axis, by):
        count = lax.axis_size(axis)
        return lax.ppermute(value, axis, [(i, (i + by) % count) for i in range(count)])

    def swapped_twos(value, axis):
        count = lax.axis_size(axis)
        return lax.ppermute(value, axis, [(i, i ^ 2) for i in range(count)])

    def swapped_pairs(value, axis, first):
        count = lax.axis_size(axis)
        pairs = []
        for low in range(first, count, 2):
            high = (low + 1) % count
            pairs += [(low, high), (high, low)]
        return lax.ppermute(value, axis, pairs)

    edge_type = array(parts * HALO + 8, cols)
    first, second, top = pl.pallas_call(
        edge_kernel,
        out_shape=(edge_type, edge_type, array(8, LANES)),
        in_specs=[VMEM],
        out_specs=(VMEM,) * 3,
        compiler_params=params(4),
        name="edge",
    )(state)
    far = swapped_twos(top, "gx")
    first = swapped_pairs(first, "gx", 0)
    second = swapped_pairs(second, "gx", 1)
    side_type = array(tall // 2 + 8, LANES)
    up, down, first, second, top = pl.pallas_call(
        pack_kernel,
        out_shape=(edge_type, edge_type, side_type, side_type, array(8, LANES)),
        in_specs=[VMEM] * 5,
        out_specs=(VMEM,) * 5,
        compiler_params=params(4),
        name="pack",
    )(state, first, second, top, far)
    far = swapped_twos(top, "gy")
    first = swapped_pairs(first, "gy", 0)
    second = swapped_pairs(second, "gy", 1)
    top = jnp.maximum(jnp.maximum(top, far), jnp.maximum(first[tall // 2 :], second[tall // 2 :]))
    for axis in ("gy", "gx"):
        covered = 4
        while covered < lax.axis_size(axis):
            far = sent(top, axis, covered)
            covered *= 2
            if axis == "gy" or covered < lax.axis_size(axis):
                top = jnp.maximum(top, far)
    dealt_type = array(parts, tall // 8, groups, 8, LANES)
    dealt = pltpu.VMEM(dealt_type.shape, jnp.float32)
    plain = pltpu.VMEM((parts, groups, tall, LANES), jnp.float32)
    field, change = pl.pallas_call(
        first_kernel,
        out_shape=(dealt_type, dealt_type),
        in_specs=[VMEM] * 5,
        out_specs=(VMEM,) * 2,
        scratch_shapes=[pltpu.VMEM((parts * tall, groups * LANES), jnp.float32), plain, dealt],
        compiler_params=params(16),
        cost_estimate=pl.CostEstimate(flops=20_000_000, bytes_accessed=2_000_000, transcendentals=400_000),
        name="first",
    )(state, up, down, first, second)
    return pl.pallas_call(
        steps_kernel,
        out_shape=array(parts, rows, cols),
        in_specs=[VMEM] * 4,
        out_specs=VMEM,
        scratch_shapes=[dealt, dealt, dealt, plain],
        compiler_params=params(16),
        name="steps",
    )(field, change, top, far)


def solution(mesh):
    in_specs = (P(None, "gx", "gy"),)
    out_specs = P(None, "gx", "gy")
    return jax.shard_map(local, mesh=mesh, in_specs=in_specs, out_specs=out_specs, check_vma=False)
```

```python
import functools

import jax
import jax.numpy as jnp
from jax import lax
from jax.experimental import pallas as pl
from jax.experimental.pallas import tpu as pltpu
from jax.sharding import PartitionSpec as P

STEPS = 4
HALO = 4 * STEPS
LANES = 128
GAMMA = 1.4
COURANT = 0.35
TINY = 1e-30

VMEM = pl.BlockSpec(memory_space=pltpu.VMEM)


def params(limit):
    return pltpu.CompilerParams(vmem_limit_bytes=limit << 20)


def array(*shape):
    return jax.ShapeDtypeStruct(shape, jnp.float32)


def iota(shape, dim):
    return lax.broadcasted_iota(jnp.int32, shape, dim)


def odd(axis):
    return lax.rem(lax.axis_index(axis), 2) == 1


def edge_kernel(block_ref, first_ref, second_ref, top_ref):
    rows = block_ref.shape[1]
    density, mom_x, mom_y, energy = (block_ref[comp] for comp in range(4))
    inv = 1.0 / density
    pressure = (GAMMA - 1.0) * (energy - 0.5 * (mom_x * mom_x + mom_y * mom_y) * inv)
    speed = jnp.maximum(jnp.abs(mom_x * inv), jnp.abs(mom_y * inv)) + jnp.sqrt(GAMMA * pressure * inv)
    top = jnp.max(speed)
    is_odd = odd("gx")
    for comp in range(4):
        span = slice(comp * HALO, (comp + 1) * HALO)
        head = block_ref[comp, 0:HALO, :]
        tail = block_ref[comp, rows - HALO : rows, :]
        first_ref[span, :] = jnp.where(is_odd, head, tail)
        second_ref[span, :] = jnp.where(is_odd, tail, head)
    first_ref[4 * HALO :, :] = jnp.full((8, first_ref.shape[1]), top)
    second_ref[4 * HALO :, :] = jnp.full((8, second_ref.shape[1]), top)
    top_ref[...] = jnp.full(top_ref.shape, top)


def pack_kernel(state_ref, swap_ref, next_ref, own_ref, three_ref, four_ref, up_ref, down_ref, first_ref, second_ref, top_ref):
    rows = state_ref.shape[1]
    cols = state_ref.shape[2]
    half = rows // 2 + HALO
    lane = iota((half, LANES), 1)
    is_odd = odd("gx")
    up_ref[...] = jnp.where(is_odd, swap_ref[...], next_ref[...])
    down_ref[...] = jnp.where(is_odd, next_ref[...], swap_ref[...])
    top = jnp.maximum(jnp.maximum(own_ref[...], jnp.maximum(three_ref[...], four_ref[...])),
                      jnp.maximum(up_ref[4 * HALO :, 0:LANES], down_ref[4 * HALO :, 0:LANES]))

    def edge(low, at):
        lanes = slice(low, low + LANES)
        total = jnp.zeros((half, LANES), jnp.float32)
        for side in range(2):
            for comp in range(4):
                span = slice(comp * HALO, (comp + 1) * HALO)
                if side == 0:
                    cells = jnp.concatenate([up_ref[span, lanes], state_ref[comp, 0 : rows // 2, lanes]], axis=0)
                else:
                    cells = jnp.concatenate([state_ref[comp, rows // 2 : rows, lanes], down_ref[span, lanes]], axis=0)
                goal = side * (LANES // 2) + comp * HALO
                moved = pltpu.roll(cells, (goal - at) % LANES, axis=1)
                total = jnp.where((lane >= goal) & (lane < goal + HALO), moved, total)
        return total

    left = edge(0, 0)
    right = edge(cols - LANES, LANES - HALO)
    is_odd = odd("gy")
    first_ref[0:half, :] = jnp.where(is_odd, left, right)
    second_ref[0:half, :] = jnp.where(is_odd, right, left)
    first_ref[half:, :] = top
    second_ref[half:, :] = top
    top_ref[...] = top


def selected(values, select):
    total = None
    for _ in range(3):
        part = values.astype(jnp.bfloat16)
        values = values - part.astype(jnp.float32)
        term = jnp.dot(part, select, preferred_element_type=jnp.float32)
        total = term if total is None else total + term
    return total


def minmod(first, second):
    low = jnp.minimum(first, second)
    high = jnp.maximum(first, second)
    return jnp.maximum(low, jnp.minimum(high, 0.0))


def fluxes(state):
    density, normal, tangent, energy = state
    inv = pl.reciprocal(density, approx=True)
    vel = normal * inv
    carried = normal * vel
    kinetic = (0.5 * (GAMMA - 1.0)) * (carried + tangent * tangent * inv)
    pressure = energy - kinetic
    scaled = GAMMA * pressure
    square = jnp.maximum(scaled * inv, TINY)
    sound = square * lax.rsqrt(square)
    return (normal, carried + pressure, tangent * vel, (scaled + kinetic) * vel), jnp.abs(vel) + sound


def face(left, right):
    (left_state, left_flux, left_speed), (right_state, right_flux, right_speed) = left, right
    top = jnp.maximum(left_speed, right_speed)
    return [
        (left_flux[comp] + right_flux[comp]) - top * (right_state[comp] - left_state[comp]) for comp in range(4)
    ]


def minus(first, second):
    return [first[comp] - second[comp] for comp in range(4)]


def sweep(load, store, count, axis):
    def rolled(tree, by):
        return jax.tree.map(lambda value: pltpu.roll(value, by % value.shape[axis], axis=axis), tree)

    def half(parts):
        return [0.5 * part for part in parts]

    here = load(0)
    end_jump = half(minus(rolled(here, -1), load(count - 1)))
    jump = rolled(end_jump, 1)
    for at in range(count):
        after = load(at + 1) if at + 1 < count else None
        next_jump = half(minus(after, here)) if at + 1 < count else end_jump
        slope = [minmod(jump[comp], next_jump[comp]) for comp in range(4)]
        low_state = minus(here, slope)
        high_state = [here[comp] + slope[comp] for comp in range(4)]
        low = (low_state, *fluxes(low_state))
        if at == 0:
            first_low = low
        else:
            flux = face(high, low)
            if at == 1:
                first_flux = flux
            else:
                store(at - 1, minus(flux, last_flux))
            last_flux = flux
        high = (high_state, *fluxes(high_state))
        here, jump = after, next_jump
    flux = face(high, rolled(first_low, -1))
    store(count - 1, minus(flux, last_flux))
    store(0, minus(first_flux, rolled(flux, 1)))


X_ORDER = (0, 1, 2, 3)
Y_ORDER = (0, 2, 1, 3)


def changes(src, diff, rows, cols, store):
    for col in range(cols):
        def keep(row, parts, col=col):
            for comp in range(4):
                diff[comp, row, col] = parts[comp]

        sweep(lambda row, col=col: [src[comp, row, col] for comp in X_ORDER], keep, rows, 0)
    for row in range(rows):
        def add(col, parts, row=row):
            store(row, col, [parts[Y_ORDER[comp]] + diff[comp, row, col] for comp in range(4)])

        sweep(lambda col, row=row: [src[comp, row, col] for comp in Y_ORDER], add, cols, 1)


def first_kernel(state_ref, up_ref, down_ref, swap_ref, next_ref, field_ref, change_ref, plain, dealt, diff):
    rows, cols = state_ref.shape[1:]
    tall = rows + 2 * HALO
    half = tall // 2
    wide = plain.shape[1]
    groups = wide // LANES
    for comp in range(4):
        span = slice(comp * HALO, (comp + 1) * HALO)
        low = comp * tall
        plain[low : low + HALO, 0:cols] = up_ref[span, :]
        plain[low + HALO : low + HALO + rows, 0:cols] = state_ref[comp]
        plain[low + HALO + rows : low + tall, 0:cols] = down_ref[span, :]
    lane = iota((half, LANES), 1)
    is_odd = odd("gy")
    from_swap = swap_ref[0:half, :]
    from_next = next_ref[0:half, :]
    from_before = jnp.where(is_odd, from_swap, from_next)
    from_after = jnp.where(is_odd, from_next, from_swap)
    for side in range(2):
        for comp in range(4):
            at = side * (LANES // 2) + comp * HALO
            left = pltpu.roll(from_before, (LANES - HALO - at) % LANES, axis=1)
            right = pltpu.roll(from_after, (-at) % LANES, axis=1)
            low = comp * tall + side * half
            plain[low : low + half, cols:] = jnp.where(lane < LANES // 2, right, left)
    source = iota((wide, wide), 0)
    goal = iota((wide, wide), 1)
    place = groups * (goal % LANES) + goal // LANES
    place = jnp.where(place < cols + 2 * HALO, (place + wide - HALO) % wide, 0)
    select = jnp.where(source == place, 1.0, 0.0).astype(jnp.bfloat16)
    found = selected(plain[...], select)
    for comp in range(4):
        for group in range(groups):
            cells = found[comp * tall : (comp + 1) * tall, group * LANES : (group + 1) * LANES]
            dealt[comp, group] = (GAMMA - 1.0) * cells if comp == 3 else cells
    count = tall // 8
    for comp in range(4):
        for row in range(count):
            for group in range(groups):
                field_ref[comp, row, group] = dealt[comp, group, pl.ds(row, 8, stride=count), :]

    def store(row, col, parts):
        for comp in range(4):
            change_ref[comp, row, col] = parts[comp]

    changes(field_ref, diff, count, groups, store)


def steps_kernel(field_ref, change_ref, own_ref, far_ref, out_ref, field, base, mid, diff, dealt):
    rows, cols = out_ref.shape[1:]
    tall = rows + 2 * HALO
    groups = field_ref.shape[2]
    half_factor = -0.25 * COURANT / jnp.maximum(own_ref[...], far_ref[...])

    for index in range(STEPS):
        start = 4 * index
        count = (tall - 8 * index) // 8
        old = field_ref if index == 0 else field

        def to_mid(row, col, parts):
            for comp in range(4):
                move = half_factor * parts[comp]
                moved = old[comp, row, col] + move
                base[comp, row, col] = moved
                mid[comp, row, col] = moved + move

        def to_field(row, col, parts):
            for comp in range(4):
                new = base[comp, row, col] + half_factor * parts[comp]
                dealt[comp, col, pl.ds(start + row, 8, stride=count), :] = new

        if index == 0:
            for row in range(count):
                for col in range(groups):
                    to_mid(row, col, [change_ref[comp, row, col] for comp in range(4)])
        else:
            for comp in range(4):
                for row in range(count):
                    for col in range(groups):
                        field[comp, row, col] = dealt[comp, col, pl.ds(start + row, 8, stride=count), :]
            changes(field, diff, count, groups, to_mid)
        changes(mid, diff, count, groups, to_field)

    wide = groups * LANES
    source = iota((wide, cols), 0)
    goal = iota((wide, cols), 1)
    select = jnp.where(groups * (source % LANES) + source // LANES == goal + HALO, 1.0, 0.0).astype(jnp.bfloat16)
    lane = iota((rows, LANES), 1)
    parts = []
    for comp in range(4):
        line = []
        for group in range(groups):
            place = groups * lane + group
            inside = (place >= HALO) & (place < HALO + cols)
            line.append(jnp.where(inside, dealt[comp, group, HALO : HALO + rows, :], 0.0))
        parts.append(jnp.concatenate(line, axis=1))
    found = selected(jnp.concatenate(parts, axis=0), select)
    for comp in range(4):
        cells = found[comp * rows : (comp + 1) * rows, :]
        out_ref[comp] = cells / (GAMMA - 1.0) if comp == 3 else cells


def local(state):
    parts, rows, cols = state.shape
    tall = rows + 2 * HALO
    groups = -(-(cols + 2 * HALO) // LANES)

    def sent(value, axis, by):
        count = lax.axis_size(axis)
        return lax.ppermute(value, axis, [(i, (i + by) % count) for i in range(count)])

    def swapped_bit(value, axis, by):
        return lax.ppermute(value, axis, [(i, i ^ by) for i in range(lax.axis_size(axis))])

    def swapped_pairs(value, axis, first):
        count = lax.axis_size(axis)
        pairs = []
        for low in range(first, count, 2):
            high = (low + 1) % count
            pairs += [(low, high), (high, low)]
        return lax.ppermute(value, axis, pairs)

    def swapped_threes(value, axis):
        count = lax.axis_size(axis)
        return lax.ppermute(value, axis, [(i, (i + 3 - 6 * (i % 2)) % count) for i in range(count)])

    edge_type = array(parts * HALO + 8, cols)
    first, second, top = pl.pallas_call(
        edge_kernel,
        out_shape=(edge_type, edge_type, array(8, LANES)),
        in_specs=[VMEM],
        out_specs=(VMEM,) * 3,
        compiler_params=params(4),
        name="edge",
    )(state)
    second = swapped_pairs(second, "gx", 1)
    first = swapped_pairs(first, "gx", 0)
    far = swapped_threes(top, "gx"), swapped_bit(top, "gx", 4)
    side_type = array(tall // 2 + 8, LANES)
    up, down, first, second, top = pl.pallas_call(
        pack_kernel,
        out_shape=(edge_type, edge_type, side_type, side_type, array(8, LANES)),
        in_specs=[VMEM] * 6,
        out_specs=(VMEM,) * 5,
        compiler_params=params(4),
        name="pack",
    )(state, first, second, top, *far)
    second = swapped_pairs(second, "gy", 1)
    first = swapped_pairs(first, "gy", 0)
    far = swapped_bit(top, "gy", 2)
    top = jnp.maximum(jnp.maximum(top, far), jnp.maximum(first[tall // 2 :], second[tall // 2 :]))
    for axis, covered in (("gy", 4), ("gx", 8)):
        while covered < lax.axis_size(axis):
            top = jnp.maximum(top, sent(top, axis, covered))
            covered *= 2
    far = swapped_bit(top, "gx", 1)
    dealt_type = array(parts, tall // 8, groups, 8, LANES)
    dealt = pltpu.VMEM(dealt_type.shape, jnp.float32)
    plain = pltpu.VMEM((parts, groups, tall, LANES), jnp.float32)
    field, change = pl.pallas_call(
        first_kernel,
        out_shape=(dealt_type, dealt_type),
        in_specs=[VMEM] * 5,
        out_specs=(VMEM,) * 2,
        scratch_shapes=[pltpu.VMEM((parts * tall, groups * LANES), jnp.float32), plain, dealt],
        compiler_params=params(16),
        cost_estimate=pl.CostEstimate(flops=20_000_000, bytes_accessed=2_000_000, transcendentals=400_000),
        name="first",
    )(state, up, down, first, second)
    return pl.pallas_call(
        steps_kernel,
        out_shape=array(parts, rows, cols),
        in_specs=[VMEM] * 4,
        out_specs=VMEM,
        scratch_shapes=[dealt] * 4 + [plain],
        compiler_params=params(16),
        name="steps",
    )(field, change, top, far)


def solution(mesh):
    in_specs = (P(None, "gx", "gy"),)
    out_specs = P(None, "gx", "gy")
    return jax.shard_map(local, mesh=mesh, in_specs=in_specs, out_specs=out_specs, check_vma=False)
```

```python
import functools

import jax
import jax.numpy as jnp
from jax import lax
from jax.experimental import pallas as pl
from jax.experimental.pallas import tpu as pltpu
from jax.sharding import PartitionSpec as P

STEPS = 4
HALO = 4 * STEPS
LANES = 128
GAMMA = 1.4
COURANT = 0.35
TINY = 1e-30

VMEM = pl.BlockSpec(memory_space=pltpu.VMEM)


def params(limit):
    return pltpu.CompilerParams(vmem_limit_bytes=limit << 20)


def array(*shape):
    return jax.ShapeDtypeStruct(shape, jnp.float32)


def iota(shape, dim):
    return lax.broadcasted_iota(jnp.int32, shape, dim)


def odd(axis):
    return lax.rem(lax.axis_index(axis), 2) == 1


def edge_kernel(block_ref, first_ref, second_ref, top_ref):
    rows = block_ref.shape[1]
    density, mom_x, mom_y, energy = (block_ref[comp] for comp in range(4))
    inv = 1.0 / density
    pressure = (GAMMA - 1.0) * (energy - 0.5 * (mom_x * mom_x + mom_y * mom_y) * inv)
    speed = jnp.maximum(jnp.abs(mom_x * inv), jnp.abs(mom_y * inv)) + jnp.sqrt(GAMMA * pressure * inv)
    top = jnp.max(speed)
    is_odd = odd("gx")
    for comp in range(4):
        span = slice(comp * HALO, (comp + 1) * HALO)
        head = block_ref[comp, 0:HALO, :]
        tail = block_ref[comp, rows - HALO : rows, :]
        first_ref[span, :] = jnp.where(is_odd, head, tail)
        second_ref[span, :] = jnp.where(is_odd, tail, head)
    first_ref[4 * HALO :, :] = jnp.full((8, first_ref.shape[1]), top)
    second_ref[4 * HALO :, :] = jnp.full((8, second_ref.shape[1]), top)
    top_ref[...] = jnp.full(top_ref.shape, top)


def pack_kernel(state_ref, swap_ref, next_ref, own_ref, three_ref, four_ref, up_ref, down_ref, first_ref, second_ref, top_ref):
    rows = state_ref.shape[1]
    cols = state_ref.shape[2]
    half = rows // 2 + HALO
    lane = iota((half, LANES), 1)
    is_odd = odd("gx")
    up_ref[...] = jnp.where(is_odd, swap_ref[...], next_ref[...])
    down_ref[...] = jnp.where(is_odd, next_ref[...], swap_ref[...])
    top = jnp.maximum(jnp.maximum(own_ref[...], jnp.maximum(three_ref[...], four_ref[...])),
                      jnp.maximum(up_ref[4 * HALO :, 0:LANES], down_ref[4 * HALO :, 0:LANES]))

    def edge(low, at):
        lanes = slice(low, low + LANES)
        total = jnp.zeros((half, LANES), jnp.float32)
        for side in range(2):
            for comp in range(4):
                span = slice(comp * HALO, (comp + 1) * HALO)
                if side == 0:
                    cells = jnp.concatenate([up_ref[span, lanes], state_ref[comp, 0 : rows // 2, lanes]], axis=0)
                else:
                    cells = jnp.concatenate([state_ref[comp, rows // 2 : rows, lanes], down_ref[span, lanes]], axis=0)
                goal = side * (LANES // 2) + comp * HALO
                moved = pltpu.roll(cells, (goal - at) % LANES, axis=1)
                total = jnp.where((lane >= goal) & (lane < goal + HALO), moved, total)
        return total

    left = edge(0, 0)
    right = edge(cols - LANES, LANES - HALO)
    is_odd = odd("gy")
    first_ref[0:half, :] = jnp.where(is_odd, left, right)
    second_ref[0:half, :] = jnp.where(is_odd, right, left)
    first_ref[half:, :] = top
    second_ref[half:, :] = top
    top_ref[...] = top


def selected(values, select):
    total = None
    for _ in range(3):
        part = values.astype(jnp.bfloat16)
        values = values - part.astype(jnp.float32)
        term = jnp.dot(part, select, preferred_element_type=jnp.float32)
        total = term if total is None else total + term
    return total


def minmod(first, second):
    low = jnp.minimum(first, second)
    high = jnp.maximum(first, second)
    return jnp.maximum(low, jnp.minimum(high, 0.0))


def known(state, inv):
    _, normal, tangent, energy = state
    vel = normal * inv
    carried = normal * vel
    kinetic = (0.5 * (GAMMA - 1.0)) * (carried + tangent * tangent * inv)
    pressure = energy - kinetic
    scaled = GAMMA * pressure
    square = jnp.maximum(scaled * inv, TINY)
    sound = square * lax.rsqrt(square)
    return state, (normal, carried + pressure, tangent * vel, (scaled + kinetic) * vel), jnp.abs(vel) + sound


def face(left, right):
    (left_state, left_flux, left_speed), (right_state, right_flux, right_speed) = left, right
    top = jnp.maximum(left_speed, right_speed)
    return [
        (left_flux[comp] + right_flux[comp]) - top * (right_state[comp] - left_state[comp]) for comp in range(4)
    ]


def minus(first, second):
    return [first[comp] - second[comp] for comp in range(4)]


def sweep(load, store, count, axis):
    def rolled(tree, by):
        return jax.tree.map(lambda value: pltpu.roll(value, by % value.shape[axis], axis=axis), tree)

    def half(parts):
        return [0.5 * part for part in parts]

    here = load(0)
    end_jump = half(minus(rolled(here, -1), load(count - 1)))
    jump = rolled(end_jump, 1)
    for at in range(count):
        after = load(at + 1) if at + 1 < count else None
        next_jump = half(minus(after, here)) if at + 1 < count else end_jump
        slope = [minmod(jump[comp], next_jump[comp]) for comp in range(4)]
        low_state = minus(here, slope)
        high_state = [here[comp] + slope[comp] for comp in range(4)]
        both = pl.reciprocal(low_state[0] * high_state[0], approx=True)
        low = known(low_state, high_state[0] * both)
        if at == 0:
            first_low = low
        else:
            flux = face(high, low)
            if at == 1:
                first_flux = flux
            else:
                store(at - 1, minus(flux, last_flux))
            last_flux = flux
        high = known(high_state, low_state[0] * both)
        here, jump = after, next_jump
    flux = face(high, rolled(first_low, -1))
    store(count - 1, minus(flux, last_flux))
    store(0, minus(first_flux, rolled(flux, 1)))


X_ORDER = (0, 1, 2, 3)
Y_ORDER = (0, 2, 1, 3)


def changes(src, diff, rows, cols, store):
    for col in range(cols):
        def keep(row, parts, col=col):
            for comp in range(4):
                diff[comp, row, col] = parts[comp]

        sweep(lambda row, col=col: [src[comp, row, col] for comp in X_ORDER], keep, rows, 0)
    for row in range(rows):
        def add(col, parts, row=row):
            store(row, col, [parts[Y_ORDER[comp]] + diff[comp, row, col] for comp in range(4)])

        sweep(lambda col, row=row: [src[comp, row, col] for comp in Y_ORDER], add, cols, 1)


def first_kernel(state_ref, up_ref, down_ref, swap_ref, next_ref, field_ref, change_ref, plain, dealt, diff):
    rows, cols = state_ref.shape[1:]
    tall = rows + 2 * HALO
    half = tall // 2
    wide = plain.shape[1]
    groups = wide // LANES
    for comp in range(4):
        span = slice(comp * HALO, (comp + 1) * HALO)
        low = comp * tall
        plain[low : low + HALO, 0:cols] = up_ref[span, :]
        plain[low + HALO : low + HALO + rows, 0:cols] = state_ref[comp]
        plain[low + HALO + rows : low + tall, 0:cols] = down_ref[span, :]
    lane = iota((half, LANES), 1)
    is_odd = odd("gy")
    from_swap = swap_ref[0:half, :]
    from_next = next_ref[0:half, :]
    from_before = jnp.where(is_odd, from_swap, from_next)
    from_after = jnp.where(is_odd, from_next, from_swap)
    for side in range(2):
        for comp in range(4):
            at = side * (LANES // 2) + comp * HALO
            left = pltpu.roll(from_before, (LANES - HALO - at) % LANES, axis=1)
            right = pltpu.roll(from_after, (-at) % LANES, axis=1)
            low = comp * tall + side * half
            plain[low : low + half, cols:] = jnp.where(lane < LANES // 2, right, left)
    source = iota((wide, wide), 0)
    goal = iota((wide, wide), 1)
    place = groups * (goal % LANES) + goal // LANES
    place = jnp.where(place < cols + 2 * HALO, (place + wide - HALO) % wide, 0)
    select = jnp.where(source == place, 1.0, 0.0).astype(jnp.bfloat16)
    found = selected(plain[...], select)
    for comp in range(4):
        for group in range(groups):
            cells = found[comp * tall : (comp + 1) * tall, group * LANES : (group + 1) * LANES]
            dealt[comp, group] = (GAMMA - 1.0) * cells if comp == 3 else cells
    count = tall // 8
    for comp in range(4):
        for row in range(count):
            for group in range(groups):
                field_ref[comp, row, group] = dealt[comp, group, pl.ds(row, 8, stride=count), :]

    def store(row, col, parts):
        for comp in range(4):
            change_ref[comp, row, col] = parts[comp]

    changes(field_ref, diff, count, groups, store)


def steps_kernel(field_ref, change_ref, own_ref, far_ref, out_ref, field, base, mid, diff, dealt):
    rows, cols = out_ref.shape[1:]
    tall = rows + 2 * HALO
    groups = field_ref.shape[2]
    half_factor = -0.25 * COURANT / jnp.maximum(own_ref[...], far_ref[...])

    for index in range(STEPS):
        start = 4 * index
        count = (tall - 8 * index) // 8
        old = field_ref if index == 0 else field

        def to_mid(row, col, parts):
            for comp in range(4):
                move = half_factor * parts[comp]
                moved = old[comp, row, col] + move
                base[comp, row, col] = moved
                mid[comp, row, col] = moved + move

        def to_field(row, col, parts):
            for comp in range(4):
                new = base[comp, row, col] + half_factor * parts[comp]
                dealt[comp, col, pl.ds(start + row, 8, stride=count), :] = new

        if index == 0:
            for row in range(count):
                for col in range(groups):
                    to_mid(row, col, [change_ref[comp, row, col] for comp in range(4)])
        else:
            for comp in range(4):
                for row in range(count):
                    for col in range(groups):
                        field[comp, row, col] = dealt[comp, col, pl.ds(start + row, 8, stride=count), :]
            changes(field, diff, count, groups, to_mid)
        changes(mid, diff, count, groups, to_field)

    wide = groups * LANES
    source = iota((wide, cols), 0)
    goal = iota((wide, cols), 1)
    select = jnp.where(groups * (source % LANES) + source // LANES == goal + HALO, 1.0, 0.0).astype(jnp.bfloat16)
    lane = iota((rows, LANES), 1)
    parts = []
    for comp in range(4):
        line = []
        for group in range(groups):
            place = groups * lane + group
            inside = (place >= HALO) & (place < HALO + cols)
            line.append(jnp.where(inside, dealt[comp, group, HALO : HALO + rows, :], 0.0))
        parts.append(jnp.concatenate(line, axis=1))
    found = selected(jnp.concatenate(parts, axis=0), select)
    for comp in range(4):
        cells = found[comp * rows : (comp + 1) * rows, :]
        out_ref[comp] = cells / (GAMMA - 1.0) if comp == 3 else cells


def local(state):
    parts, rows, cols = state.shape
    tall = rows + 2 * HALO
    groups = -(-(cols + 2 * HALO) // LANES)

    def sent(value, axis, by):
        count = lax.axis_size(axis)
        return lax.ppermute(value, axis, [(i, (i + by) % count) for i in range(count)])

    def swapped_bit(value, axis, by):
        return lax.ppermute(value, axis, [(i, i ^ by) for i in range(lax.axis_size(axis))])

    def swapped_pairs(value, axis, first):
        count = lax.axis_size(axis)
        pairs = []
        for low in range(first, count, 2):
            high = (low + 1) % count
            pairs += [(low, high), (high, low)]
        return lax.ppermute(value, axis, pairs)

    def swapped_threes(value, axis):
        count = lax.axis_size(axis)
        return lax.ppermute(value, axis, [(i, (i + 3 - 6 * (i % 2)) % count) for i in range(count)])

    edge_type = array(parts * HALO + 8, cols)
    first, second, top = pl.pallas_call(
        edge_kernel,
        out_shape=(edge_type, edge_type, array(8, LANES)),
        in_specs=[VMEM],
        out_specs=(VMEM,) * 3,
        compiler_params=params(4),
        name="edge",
    )(state)
    second = swapped_pairs(second, "gx", 1)
    first = swapped_pairs(first, "gx", 0)
    far = swapped_threes(top, "gx"), swapped_bit(top, "gx", 4)
    side_type = array(tall // 2 + 8, LANES)
    up, down, first, second, top = pl.pallas_call(
        pack_kernel,
        out_shape=(edge_type, edge_type, side_type, side_type, array(8, LANES)),
        in_specs=[VMEM] * 6,
        out_specs=(VMEM,) * 5,
        compiler_params=params(4),
        name="pack",
    )(state, first, second, top, *far)
    second = swapped_pairs(second, "gy", 1)
    first = swapped_pairs(first, "gy", 0)
    far = swapped_bit(top, "gy", 2)
    top = jnp.maximum(jnp.maximum(top, far), jnp.maximum(first[tall // 2 :], second[tall // 2 :]))
    for axis, covered in (("gy", 4), ("gx", 8)):
        while covered < lax.axis_size(axis):
            top = jnp.maximum(top, sent(top, axis, covered))
            covered *= 2
    far = swapped_bit(top, "gx", 1)
    dealt_type = array(parts, tall // 8, groups, 8, LANES)
    dealt = pltpu.VMEM(dealt_type.shape, jnp.float32)
    plain = pltpu.VMEM((parts, groups, tall, LANES), jnp.float32)
    field, change = pl.pallas_call(
        first_kernel,
        out_shape=(dealt_type, dealt_type),
        in_specs=[VMEM] * 5,
        out_specs=(VMEM,) * 2,
        scratch_shapes=[pltpu.VMEM((parts * tall, groups * LANES), jnp.float32), plain, dealt],
        compiler_params=params(16),
        cost_estimate=pl.CostEstimate(flops=20_000_000, bytes_accessed=2_000_000, transcendentals=400_000),
        name="first",
    )(state, up, down, first, second)
    return pl.pallas_call(
        steps_kernel,
        out_shape=array(parts, rows, cols),
        in_specs=[VMEM] * 4,
        out_specs=VMEM,
        scratch_shapes=[dealt] * 4 + [plain],
        compiler_params=params(16),
        name="steps",
    )(field, change, top, far)


def solution(mesh):
    in_specs = (P(None, "gx", "gy"),)
    out_specs = P(None, "gx", "gy")
    return jax.shard_map(local, mesh=mesh, in_specs=in_specs, out_specs=out_specs, check_vma=False)
```

```python
import functools

import jax
import jax.numpy as jnp
from jax import lax
from jax.experimental import pallas as pl
from jax.experimental.pallas import tpu as pltpu
from jax.sharding import PartitionSpec as P

STEPS = 4
HALO = 4 * STEPS
LANES = 128
GAMMA = 1.4
COURANT = 0.35
TINY = 1e-30

VMEM = pl.BlockSpec(memory_space=pltpu.VMEM)


def params(limit):
    return pltpu.CompilerParams(vmem_limit_bytes=limit << 20)


def array(*shape):
    return jax.ShapeDtypeStruct(shape, jnp.float32)


def iota(shape, dim):
    return lax.broadcasted_iota(jnp.int32, shape, dim)


def odd(axis):
    return lax.rem(lax.axis_index(axis), 2) == 1


def edge_kernel(block_ref, first_ref, second_ref, top_ref):
    rows = block_ref.shape[1]
    density, mom_x, mom_y, energy = (block_ref[comp] for comp in range(4))
    inv = 1.0 / density
    pressure = (GAMMA - 1.0) * (energy - 0.5 * (mom_x * mom_x + mom_y * mom_y) * inv)
    speed = jnp.maximum(jnp.abs(mom_x * inv), jnp.abs(mom_y * inv)) + jnp.sqrt(GAMMA * pressure * inv)
    top = jnp.max(speed)
    is_odd = odd("gx")
    for comp in range(4):
        span = slice(comp * HALO, (comp + 1) * HALO)
        head = block_ref[comp, 0:HALO, :]
        tail = block_ref[comp, rows - HALO : rows, :]
        first_ref[span, :] = jnp.where(is_odd, head, tail)
        second_ref[span, :] = jnp.where(is_odd, tail, head)
    first_ref[4 * HALO :, :] = jnp.full((8, first_ref.shape[1]), top)
    second_ref[4 * HALO :, :] = jnp.full((8, second_ref.shape[1]), top)
    top_ref[...] = jnp.full(top_ref.shape, top)


def pack_kernel(state_ref, swap_ref, next_ref, own_ref, three_ref, four_ref, up_ref, down_ref, first_ref, second_ref, top_ref):
    rows = state_ref.shape[1]
    cols = state_ref.shape[2]
    half = rows // 2 + HALO
    lane = iota((half, LANES), 1)
    is_odd = odd("gx")
    up_ref[...] = jnp.where(is_odd, swap_ref[...], next_ref[...])
    down_ref[...] = jnp.where(is_odd, next_ref[...], swap_ref[...])
    top = jnp.maximum(jnp.maximum(own_ref[...], jnp.maximum(three_ref[...], four_ref[...])),
                      jnp.maximum(up_ref[4 * HALO :, 0:LANES], down_ref[4 * HALO :, 0:LANES]))

    def edge(low, at):
        lanes = slice(low, low + LANES)
        total = jnp.zeros((half, LANES), jnp.float32)
        for side in range(2):
            for comp in range(4):
                span = slice(comp * HALO, (comp + 1) * HALO)
                if side == 0:
                    cells = jnp.concatenate([up_ref[span, lanes], state_ref[comp, 0 : rows // 2, lanes]], axis=0)
                else:
                    cells = jnp.concatenate([state_ref[comp, rows // 2 : rows, lanes], down_ref[span, lanes]], axis=0)
                goal = side * (LANES // 2) + comp * HALO
                moved = pltpu.roll(cells, (goal - at) % LANES, axis=1)
                total = jnp.where((lane >= goal) & (lane < goal + HALO), moved, total)
        return total

    left = edge(0, 0)
    right = edge(cols - LANES, LANES - HALO)
    is_odd = odd("gy")
    first_ref[0:half, :] = jnp.where(is_odd, left, right)
    second_ref[0:half, :] = jnp.where(is_odd, right, left)
    first_ref[half:, :] = top
    second_ref[half:, :] = top
    top_ref[...] = top


def selected(values, select):
    total = None
    for _ in range(3):
        part = values.astype(jnp.bfloat16)
        values = values - part.astype(jnp.float32)
        term = jnp.dot(part, select, preferred_element_type=jnp.float32)
        total = term if total is None else total + term
    return total


def minmod(first, second):
    low = jnp.minimum(first, second)
    high = jnp.maximum(first, second)
    return jnp.maximum(low, jnp.minimum(high, 0.0))


def fluxes(state):
    density, normal, tangent, energy = state
    inv = pl.reciprocal(density, approx=True)
    vel = normal * inv
    carried = normal * vel
    kinetic = (0.5 * (GAMMA - 1.0)) * (carried + tangent * tangent * inv)
    pressure = energy - kinetic
    scaled = GAMMA * pressure
    square = jnp.maximum(scaled * inv, TINY)
    sound = square * lax.rsqrt(square)
    return (normal, carried + pressure, tangent * vel, (scaled + kinetic) * vel), jnp.abs(vel) + sound


def face(left, right):
    (left_state, left_flux, left_speed), (right_state, right_flux, right_speed) = left, right
    top = jnp.maximum(left_speed, right_speed)
    return [
        (left_flux[comp] + right_flux[comp]) - top * (right_state[comp] - left_state[comp]) for comp in range(4)
    ]


def minus(first, second):
    return [first[comp] - second[comp] for comp in range(4)]


def half(parts):
    return [0.5 * part for part in parts]


def rolled(tree, by, axis):
    return jax.tree.map(lambda value: pltpu.roll(value, by % value.shape[axis], axis=axis), tree)


def cell(here, jump_before, jump_after):
    slope = [minmod(jump_before[comp], jump_after[comp]) for comp in range(4)]
    low = minus(here, slope)
    high = [here[comp] + slope[comp] for comp in range(4)]
    return (low, *fluxes(low)), (high, *fluxes(high))


def row_changes(values):
    count = len(values)
    end_jump = half(minus(rolled(values[0], -1, 1), values[-1]))
    jumps = [half(minus(values[at + 1], values[at])) for at in range(count - 1)] + [end_jump]
    faces, first_low, high = [], None, None
    for at in range(count):
        low, next_high = cell(values[at], jumps[at - 1] if at else rolled(end_jump, 1, 1), jumps[at])
        if at:
            faces.append(face(high, low))
        else:
            first_low = low
        high = next_high
    faces.append(face(high, rolled(first_low, -1, 1)))
    return [minus(faces[at], faces[at - 1] if at else rolled(faces[-1], 1, 1)) for at in range(count)]


class Column:
    def __init__(self, count, begin, here, after):
        self.count, self.begin = count, begin
        self.jump = self.first_jump = half(minus(after, here))
        self.first_low = self.first_flux = self.last_flux = self.high = None

    def feed(self, row, here, after):
        next_row = (row + 1) % self.count
        if after is None:
            next_jump = self.first_jump
        else:
            next_jump = half(minus(rolled(after, -1, 0) if next_row == 0 else after, here))
        jump = rolled(self.jump, 1, 0) if row == 0 else self.jump
        low, high = cell(here, jump, next_jump)
        done = []
        if self.first_low is None:
            self.first_low = low
        else:
            flux = face(rolled(self.high, 1, 0) if row == 0 else self.high, low)
            if self.last_flux is None:
                self.first_flux = flux
            else:
                seen = rolled(flux, -1, 0) if row == 0 else flux
                done.append(((row - 1) % self.count, minus(seen, self.last_flux)))
            self.last_flux = flux
        self.high, self.jump = high, next_jump
        if after is None:
            flux = face(high, self.first_low)
            done.append((row, minus(flux, self.last_flux)))
            done.append(((row + 1) % self.count, minus(self.first_flux, flux)))
        return done


Y_ORDER = (0, 2, 1, 3)


def changes(load, rows, cols, begin, store):
    along_y = {}
    values = {at: [load((begin + at) % rows, col) for col in range(cols)] for at in range(2)}
    columns = [Column(rows, begin, values[0][col], values[1][col]) for col in range(cols)]
    for at in range(1, rows + 1):
        row = (begin + at) % rows
        here = values.pop(at)
        if at < rows:
            values[at + 1] = [load((row + 1) % rows, col) for col in range(cols)]
        ready = []
        for col in range(cols):
            after = values[at + 1][col] if at < rows else None
            ready += [(col, *item) for item in columns[col].feed(row, here[col], after)]
        along_y[row] = row_changes([[part[comp] for comp in Y_ORDER] for part in here])
        for col, done, parts in ready:
            other = along_y[done][col]
            store(done, col, [parts[comp] + other[Y_ORDER[comp]] for comp in range(4)])


def first_kernel(state_ref, up_ref, down_ref, swap_ref, next_ref, field_ref, change_ref, plain, dealt):
    rows, cols = state_ref.shape[1:]
    tall = rows + 2 * HALO
    half = tall // 2
    wide = plain.shape[1]
    groups = wide // LANES
    for comp in range(4):
        span = slice(comp * HALO, (comp + 1) * HALO)
        low = comp * tall
        plain[low : low + HALO, 0:cols] = up_ref[span, :]
        plain[low + HALO : low + HALO + rows, 0:cols] = state_ref[comp]
        plain[low + HALO + rows : low + tall, 0:cols] = down_ref[span, :]
    lane = iota((half, LANES), 1)
    is_odd = odd("gy")
    from_swap = swap_ref[0:half, :]
    from_next = next_ref[0:half, :]
    from_before = jnp.where(is_odd, from_swap, from_next)
    from_after = jnp.where(is_odd, from_next, from_swap)
    for side in range(2):
        for comp in range(4):
            at = side * (LANES // 2) + comp * HALO
            left = pltpu.roll(from_before, (LANES - HALO - at) % LANES, axis=1)
            right = pltpu.roll(from_after, (-at) % LANES, axis=1)
            low = comp * tall + side * half
            plain[low : low + half, cols:] = jnp.where(lane < LANES // 2, right, left)
    source = iota((wide, wide), 0)
    goal = iota((wide, wide), 1)
    place = groups * (goal % LANES) + goal // LANES
    place = jnp.where(place < cols + 2 * HALO, (place + wide - HALO) % wide, 0)
    select = jnp.where(source == place, 1.0, 0.0).astype(jnp.bfloat16)
    found = selected(plain[...], select)
    for comp in range(4):
        for group in range(groups):
            cells = found[comp * tall : (comp + 1) * tall, group * LANES : (group + 1) * LANES]
            dealt[comp, group] = (GAMMA - 1.0) * cells if comp == 3 else cells
    count = tall // 8
    for comp in range(4):
        for row in range(count):
            for group in range(groups):
                field_ref[comp, row, group] = dealt[comp, group, pl.ds(row, 8, stride=count), :]

    def store(row, col, parts):
        for comp in range(4):
            change_ref[comp, row, col] = parts[comp]

    def load(row, col):
        return [field_ref[comp, row, col] for comp in range(4)]

    changes(load, count, groups, 0, store)


def steps_kernel(field_ref, change_ref, own_ref, far_ref, out_ref, field, base, mid, dealt):
    rows, cols = out_ref.shape[1:]
    tall = rows + 2 * HALO
    groups = field_ref.shape[2]
    half_factor = -0.25 * COURANT / jnp.maximum(own_ref[...], far_ref[...])

    for index in range(STEPS):
        start = 4 * index
        count = (tall - 8 * index) // 8
        old = field_ref if index == 0 else field

        def to_mid(row, col, parts):
            for comp in range(4):
                move = half_factor * parts[comp]
                moved = old[comp, row, col] + move
                base[comp, row, col] = moved
                mid[comp, row, col] = moved + move

        def to_field(row, col, parts):
            for comp in range(4):
                new = base[comp, row, col] + half_factor * parts[comp]
                dealt[comp, col, pl.ds(start + row, 8, stride=count), :] = new

        if index == 0:
            for row in range(count):
                for col in range(groups):
                    to_mid(row, col, [change_ref[comp, row, col] for comp in range(4)])
        else:
            for comp in range(4):
                for row in range(count):
                    for col in range(groups):
                        field[comp, row, col] = dealt[comp, col, pl.ds(start + row, 8, stride=count), :]
            changes(lambda row, col: [field[comp, row, col] for comp in range(4)], count, groups, 0, to_mid)
        changes(lambda row, col: [mid[comp, row, col] for comp in range(4)], count, groups, count // 2, to_field)

    wide = groups * LANES
    source = iota((wide, cols), 0)
    goal = iota((wide, cols), 1)
    select = jnp.where(groups * (source % LANES) + source // LANES == goal + HALO, 1.0, 0.0).astype(jnp.bfloat16)
    lane = iota((rows, LANES), 1)
    parts = []
    for comp in range(4):
        line = []
        for group in range(groups):
            place = groups * lane + group
            inside = (place >= HALO) & (place < HALO + cols)
            line.append(jnp.where(inside, dealt[comp, group, HALO : HALO + rows, :], 0.0))
        parts.append(jnp.concatenate(line, axis=1))
    found = selected(jnp.concatenate(parts, axis=0), select)
    for comp in range(4):
        cells = found[comp * rows : (comp + 1) * rows, :]
        out_ref[comp] = cells / (GAMMA - 1.0) if comp == 3 else cells


def local(state):
    parts, rows, cols = state.shape
    tall = rows + 2 * HALO
    groups = -(-(cols + 2 * HALO) // LANES)

    def sent(value, axis, by):
        count = lax.axis_size(axis)
        return lax.ppermute(value, axis, [(i, (i + by) % count) for i in range(count)])

    def swapped_bit(value, axis, by):
        return lax.ppermute(value, axis, [(i, i ^ by) for i in range(lax.axis_size(axis))])

    def swapped_pairs(value, axis, first):
        count = lax.axis_size(axis)
        pairs = []
        for low in range(first, count, 2):
            high = (low + 1) % count
            pairs += [(low, high), (high, low)]
        return lax.ppermute(value, axis, pairs)

    def swapped_threes(value, axis):
        count = lax.axis_size(axis)
        return lax.ppermute(value, axis, [(i, (i + 3 - 6 * (i % 2)) % count) for i in range(count)])

    edge_type = array(parts * HALO + 8, cols)
    first, second, top = pl.pallas_call(
        edge_kernel,
        out_shape=(edge_type, edge_type, array(8, LANES)),
        in_specs=[VMEM],
        out_specs=(VMEM,) * 3,
        compiler_params=params(4),
        name="edge",
    )(state)
    second = swapped_pairs(second, "gx", 1)
    first = swapped_pairs(first, "gx", 0)
    far = swapped_threes(top, "gx"), swapped_bit(top, "gx", 4)
    side_type = array(tall // 2 + 8, LANES)
    up, down, first, second, top = pl.pallas_call(
        pack_kernel,
        out_shape=(edge_type, edge_type, side_type, side_type, array(8, LANES)),
        in_specs=[VMEM] * 6,
        out_specs=(VMEM,) * 5,
        compiler_params=params(4),
        name="pack",
    )(state, first, second, top, *far)
    second = swapped_pairs(second, "gy", 1)
    first = swapped_pairs(first, "gy", 0)
    far = swapped_bit(top, "gy", 2)
    top = jnp.maximum(jnp.maximum(top, far), jnp.maximum(first[tall // 2 :], second[tall // 2 :]))
    for axis, covered in (("gy", 4), ("gx", 8)):
        while covered < lax.axis_size(axis):
            top = jnp.maximum(top, sent(top, axis, covered))
            covered *= 2
    far = swapped_bit(top, "gx", 1)
    dealt_type = array(parts, tall // 8, groups, 8, LANES)
    dealt = pltpu.VMEM(dealt_type.shape, jnp.float32)
    plain = pltpu.VMEM((parts, groups, tall, LANES), jnp.float32)
    field, change = pl.pallas_call(
        first_kernel,
        out_shape=(dealt_type, dealt_type),
        in_specs=[VMEM] * 5,
        out_specs=(VMEM,) * 2,
        scratch_shapes=[pltpu.VMEM((parts * tall, groups * LANES), jnp.float32), plain],
        compiler_params=params(16),
        cost_estimate=pl.CostEstimate(flops=20_000_000, bytes_accessed=2_000_000, transcendentals=400_000),
        name="first",
    )(state, up, down, first, second)
    return pl.pallas_call(
        steps_kernel,
        out_shape=array(parts, rows, cols),
        in_specs=[VMEM] * 4,
        out_specs=VMEM,
        scratch_shapes=[dealt] * 3 + [plain],
        compiler_params=params(16),
        name="steps",
    )(field, change, top, far)


def solution(mesh):
    in_specs = (P(None, "gx", "gy"),)
    out_specs = P(None, "gx", "gy")
    return jax.shard_map(local, mesh=mesh, in_specs=in_specs, out_specs=out_specs, check_vma=False)
```

```python
import functools

import jax
import jax.numpy as jnp
from jax import lax
from jax.experimental import pallas as pl
from jax.experimental.pallas import tpu as pltpu
from jax.sharding import PartitionSpec as P

STEPS = 4
HALO = 4 * STEPS
LANES = 128
GAMMA = 1.4
COURANT = 0.35
TINY = 1e-30

VMEM = pl.BlockSpec(memory_space=pltpu.VMEM)


def params(limit):
    return pltpu.CompilerParams(vmem_limit_bytes=limit << 20)


def array(*shape):
    return jax.ShapeDtypeStruct(shape, jnp.float32)


def iota(shape, dim):
    return lax.broadcasted_iota(jnp.int32, shape, dim)


def odd(axis):
    return lax.rem(lax.axis_index(axis), 2) == 1


def edge_kernel(block_ref, first_ref, second_ref, top_ref):
    rows = block_ref.shape[1]
    density, mom_x, mom_y, energy = (block_ref[comp] for comp in range(4))
    inv = 1.0 / density
    pressure = (GAMMA - 1.0) * (energy - 0.5 * (mom_x * mom_x + mom_y * mom_y) * inv)
    speed = jnp.maximum(jnp.abs(mom_x * inv), jnp.abs(mom_y * inv)) + jnp.sqrt(GAMMA * pressure * inv)
    top = jnp.max(speed)
    is_odd = odd("gx")
    for comp in range(4):
        span = slice(comp * HALO, (comp + 1) * HALO)
        head = block_ref[comp, 0:HALO, :]
        tail = block_ref[comp, rows - HALO : rows, :]
        first_ref[span, :] = jnp.where(is_odd, head, tail)
        second_ref[span, :] = jnp.where(is_odd, tail, head)
    first_ref[4 * HALO :, :] = jnp.full((8, first_ref.shape[1]), top)
    second_ref[4 * HALO :, :] = jnp.full((8, second_ref.shape[1]), top)
    top_ref[...] = jnp.full(top_ref.shape, top)


def pack_kernel(state_ref, next_ref, three_ref, four_ref, swap_ref, own_ref, up_ref, down_ref, first_ref, second_ref, top_ref):
    rows = state_ref.shape[1]
    cols = state_ref.shape[2]
    half = rows // 2 + HALO
    lane = iota((half, LANES), 1)
    is_odd = odd("gx")
    up_ref[...] = jnp.where(is_odd, swap_ref[...], next_ref[...])
    down_ref[...] = jnp.where(is_odd, next_ref[...], swap_ref[...])
    top = jnp.maximum(jnp.maximum(own_ref[...], jnp.maximum(three_ref[...], four_ref[...])),
                      jnp.maximum(up_ref[4 * HALO :, 0:LANES], down_ref[4 * HALO :, 0:LANES]))

    def edge(low, at):
        lanes = slice(low, low + LANES)
        total = jnp.zeros((half, LANES), jnp.float32)
        for side in range(2):
            for comp in range(4):
                span = slice(comp * HALO, (comp + 1) * HALO)
                if side == 0:
                    cells = jnp.concatenate([up_ref[span, lanes], state_ref[comp, 0 : rows // 2, lanes]], axis=0)
                else:
                    cells = jnp.concatenate([state_ref[comp, rows // 2 : rows, lanes], down_ref[span, lanes]], axis=0)
                goal = side * (LANES // 2) + comp * HALO
                moved = pltpu.roll(cells, (goal - at) % LANES, axis=1)
                total = jnp.where((lane >= goal) & (lane < goal + HALO), moved, total)
        return total

    left = edge(0, 0)
    right = edge(cols - LANES, LANES - HALO)
    is_odd = odd("gy")
    first_ref[0:half, :] = jnp.where(is_odd, left, right)
    second_ref[0:half, :] = jnp.where(is_odd, right, left)
    first_ref[half:, :] = top
    second_ref[half:, :] = top
    top_ref[...] = top


def selected(values, select):
    total = None
    for _ in range(3):
        part = values.astype(jnp.bfloat16)
        values = values - part.astype(jnp.float32)
        term = jnp.dot(part, select, preferred_element_type=jnp.float32)
        total = term if total is None else total + term
    return total


def minmod(first, second):
    low = jnp.minimum(first, second)
    high = jnp.maximum(first, second)
    return jnp.maximum(low, jnp.minimum(high, 0.0))


def fluxes(state):
    density, normal, tangent, energy = state
    inv = pl.reciprocal(density, approx=True)
    vel = normal * inv
    carried = normal * vel
    kinetic = (0.5 * (GAMMA - 1.0)) * (carried + tangent * tangent * inv)
    pressure = energy - kinetic
    scaled = GAMMA * pressure
    square = jnp.maximum(scaled * inv, TINY)
    sound = square * lax.rsqrt(square)
    return (normal, carried + pressure, tangent * vel, (scaled + kinetic) * vel), jnp.abs(vel) + sound


def face(left, right):
    (left_state, left_flux, left_speed), (right_state, right_flux, right_speed) = left, right
    top = jnp.maximum(left_speed, right_speed)
    return [
        (left_flux[comp] + right_flux[comp]) - top * (right_state[comp] - left_state[comp]) for comp in range(4)
    ]


def minus(first, second):
    return [first[comp] - second[comp] for comp in range(4)]


def half(parts):
    return [0.5 * part for part in parts]


def rolled(tree, by, axis):
    return jax.tree.map(lambda value: pltpu.roll(value, by % value.shape[axis], axis=axis), tree)


def cell(here, jump_before, jump_after):
    slope = [minmod(jump_before[comp], jump_after[comp]) for comp in range(4)]
    low = minus(here, slope)
    high = [here[comp] + slope[comp] for comp in range(4)]
    return (low, *fluxes(low)), (high, *fluxes(high))


def row_changes(values):
    count = len(values)
    end_jump = half(minus(rolled(values[0], -1, 1), values[-1]))
    jumps = [half(minus(values[at + 1], values[at])) for at in range(count - 1)] + [end_jump]
    faces, first_low, high = [], None, None
    for at in range(count):
        low, next_high = cell(values[at], jumps[at - 1] if at else rolled(end_jump, 1, 1), jumps[at])
        if at:
            faces.append(face(high, low))
        else:
            first_low = low
        high = next_high
    faces.append(face(high, rolled(first_low, -1, 1)))
    return [minus(faces[at], faces[at - 1] if at else rolled(faces[-1], 1, 1)) for at in range(count)]


class Column:
    def __init__(self, count, begin, here, after):
        self.count, self.begin = count, begin
        self.jump = self.first_jump = half(minus(after, here))
        self.first_low = self.first_flux = self.last_flux = self.high = None

    def feed(self, row, here, after):
        next_row = (row + 1) % self.count
        if after is None:
            next_jump = self.first_jump
        else:
            next_jump = half(minus(rolled(after, -1, 0) if next_row == 0 else after, here))
        jump = rolled(self.jump, 1, 0) if row == 0 else self.jump
        low, high = cell(here, jump, next_jump)
        done = []
        if self.first_low is None:
            self.first_low = low
        else:
            flux = face(rolled(self.high, 1, 0) if row == 0 else self.high, low)
            if self.last_flux is None:
                self.first_flux = flux
            else:
                seen = rolled(flux, -1, 0) if row == 0 else flux
                done.append(((row - 1) % self.count, minus(seen, self.last_flux)))
            self.last_flux = flux
        self.high, self.jump = high, next_jump
        if after is None:
            flux = face(high, self.first_low)
            done.append((row, minus(flux, self.last_flux)))
            done.append(((row + 1) % self.count, minus(self.first_flux, flux)))
        return done


Y_ORDER = (0, 2, 1, 3)


def changes(load, rows, cols, begin, store):
    along_y = {}
    values = {at: [load((begin + at) % rows, col) for col in range(cols)] for at in range(2)}
    columns = [Column(rows, begin, values[0][col], values[1][col]) for col in range(cols)]
    for at in range(1, rows + 1):
        row = (begin + at) % rows
        here = values.pop(at)
        if at < rows:
            values[at + 1] = [load((row + 1) % rows, col) for col in range(cols)]
        ready = []
        for col in range(cols):
            after = values[at + 1][col] if at < rows else None
            ready += [(col, *item) for item in columns[col].feed(row, here[col], after)]
        along_y[row] = row_changes([[part[comp] for comp in Y_ORDER] for part in here])
        for col, done, parts in ready:
            other = along_y[done][col]
            store(done, col, [parts[comp] + other[Y_ORDER[comp]] for comp in range(4)])


def first_kernel(state_ref, up_ref, down_ref, next_ref, far_ref, swap_ref, own_ref, field_ref, change_ref, top_ref, plain, dealt):
    rows, cols = state_ref.shape[1:]
    tall = rows + 2 * HALO
    half = tall // 2
    wide = plain.shape[1]
    groups = wide // LANES
    for comp in range(4):
        span = slice(comp * HALO, (comp + 1) * HALO)
        low = comp * tall
        plain[low : low + HALO, 0:cols] = up_ref[span, :]
        plain[low + HALO : low + HALO + rows, 0:cols] = state_ref[comp]
        plain[low + HALO + rows : low + tall, 0:cols] = down_ref[span, :]
    lane = iota((half, LANES), 1)
    is_odd = odd("gy")
    top_ref[...] = jnp.maximum(jnp.maximum(own_ref[...], far_ref[...]), jnp.maximum(next_ref[half:, :], swap_ref[half:, :]))
    from_swap = swap_ref[0:half, :]
    from_next = next_ref[0:half, :]
    from_before = jnp.where(is_odd, from_swap, from_next)
    from_after = jnp.where(is_odd, from_next, from_swap)
    for side in range(2):
        for comp in range(4):
            at = side * (LANES // 2) + comp * HALO
            left = pltpu.roll(from_before, (LANES - HALO - at) % LANES, axis=1)
            right = pltpu.roll(from_after, (-at) % LANES, axis=1)
            low = comp * tall + side * half
            plain[low : low + half, cols:] = jnp.where(lane < LANES // 2, right, left)
    source = iota((wide, wide), 0)
    goal = iota((wide, wide), 1)
    place = groups * (goal % LANES) + goal // LANES
    place = jnp.where(place < cols + 2 * HALO, (place + wide - HALO) % wide, 0)
    select = jnp.where(source == place, 1.0, 0.0).astype(jnp.bfloat16)
    found = selected(plain[...], select)
    for comp in range(4):
        for group in range(groups):
            cells = found[comp * tall : (comp + 1) * tall, group * LANES : (group + 1) * LANES]
            dealt[comp, group] = (GAMMA - 1.0) * cells if comp == 3 else cells
    count = tall // 8
    for comp in range(4):
        for row in range(count):
            for group in range(groups):
                field_ref[comp, row, group] = dealt[comp, group, pl.ds(row, 8, stride=count), :]

    def store(row, col, parts):
        for comp in range(4):
            change_ref[comp, row, col] = parts[comp]

    def load(row, col):
        return [field_ref[comp, row, col] for comp in range(4)]

    changes(load, count, groups, 0, store)


def steps_kernel(field_ref, change_ref, own_ref, mate_ref, wide_ref, out_ref, field, base, mid, dealt):
    rows, cols = out_ref.shape[1:]
    tall = rows + 2 * HALO
    groups = field_ref.shape[2]
    half_factor = -0.25 * COURANT / jnp.maximum(own_ref[...], jnp.maximum(mate_ref[...], wide_ref[...]))

    def one_step(start, count, old, first_changes):
        def to_mid(row, col, parts):
            for comp in range(4):
                move = half_factor * parts[comp]
                moved = old[comp, row, col] + move
                base[comp, row, col] = moved
                mid[comp, row, col] = moved + move

        def to_field(row, col, parts):
            for comp in range(4):
                new = base[comp, row, col] + half_factor * parts[comp]
                dealt[comp, col, pl.ds(start + row, 8, stride=count), :] = new

        def load_from(ref):
            return lambda row, col: [ref[comp, row, col] for comp in range(4)]

        if first_changes is not None:
            for row in range(count):
                for col in range(groups):
                    to_mid(row, col, [first_changes[comp, row, col] for comp in range(4)])
        else:
            for comp in range(4):
                for row in range(count):
                    for col in range(groups):
                        old[comp, row, col] = dealt[comp, col, pl.ds(start + row, 8, stride=count), :]
            changes(load_from(old), count, groups, 0, to_mid)
        changes(load_from(mid), count, groups, count // 2, to_field)

    def looped(_, none):
        one_step(8, (tall - 16) // 8, field, None)
        return none

    one_step(0, tall // 8, field_ref, change_ref)
    one_step(4, (tall - 8) // 8, field, None)
    lax.fori_loop(2, STEPS, looped, None)

    wide = groups * LANES
    source = iota((wide, cols), 0)
    goal = iota((wide, cols), 1)
    select = jnp.where(groups * (source % LANES) + source // LANES == goal + HALO, 1.0, 0.0).astype(jnp.bfloat16)
    lane = iota((rows, LANES), 1)
    parts = []
    for comp in range(4):
        line = []
        for group in range(groups):
            place = groups * lane + group
            inside = (place >= HALO) & (place < HALO + cols)
            line.append(jnp.where(inside, dealt[comp, group, HALO : HALO + rows, :], 0.0))
        parts.append(jnp.concatenate(line, axis=1))
    found = selected(jnp.concatenate(parts, axis=0), select)
    for comp in range(4):
        cells = found[comp * rows : (comp + 1) * rows, :]
        out_ref[comp] = cells / (GAMMA - 1.0) if comp == 3 else cells


def local(state):
    parts, rows, cols = state.shape
    tall = rows + 2 * HALO
    groups = -(-(cols + 2 * HALO) // LANES)

    def sent(value, axis, by):
        count = lax.axis_size(axis)
        return lax.ppermute(value, axis, [(i, (i + by) % count) for i in range(count)])

    def swapped_bit(value, axis, by):
        return lax.ppermute(value, axis, [(i, i ^ by) for i in range(lax.axis_size(axis))])

    def swapped_pairs(value, axis, first):
        count = lax.axis_size(axis)
        pairs = []
        for low in range(first, count, 2):
            high = (low + 1) % count
            pairs += [(low, high), (high, low)]
        return lax.ppermute(value, axis, pairs)

    def swapped_threes(value, axis):
        count = lax.axis_size(axis)
        return lax.ppermute(value, axis, [(i, (i + 3 - 6 * (i % 2)) % count) for i in range(count)])

    edge_type = array(parts * HALO + 8, cols)
    first, second, top = pl.pallas_call(
        edge_kernel,
        out_shape=(edge_type, edge_type, array(8, LANES)),
        in_specs=[VMEM],
        out_specs=(VMEM,) * 3,
        compiler_params=params(4),
        name="edge",
    )(state)
    second = swapped_pairs(second, "gx", 1)
    first = swapped_pairs(first, "gx", 0)
    far = swapped_threes(top, "gx"), swapped_bit(top, "gx", 4)
    side_type = array(tall // 2 + 8, LANES)
    up, down, first, second, top = pl.pallas_call(
        pack_kernel,
        out_shape=(edge_type, edge_type, side_type, side_type, array(8, LANES)),
        in_specs=[VMEM] * 6,
        out_specs=(VMEM,) * 5,
        compiler_params=params(4),
        name="pack",
    )(state, second, *far, first, top)
    second = swapped_pairs(second, "gy", 1)
    first = swapped_pairs(first, "gy", 0)
    far = swapped_bit(top, "gy", 2)
    own = top
    top = jnp.maximum(jnp.maximum(own, far), jnp.maximum(first[tall // 2 :], second[tall // 2 :]))
    for axis, covered in (("gy", 4), ("gx", 8)):
        while covered < lax.axis_size(axis):
            top = jnp.maximum(top, sent(top, axis, covered))
            covered *= 2
    top = swapped_bit(top, "gx", 1), top
    dealt_type = array(parts, tall // 8, groups, 8, LANES)
    dealt = pltpu.VMEM(dealt_type.shape, jnp.float32)
    plain = pltpu.VMEM((parts, groups, tall, LANES), jnp.float32)
    field, change, own = pl.pallas_call(
        first_kernel,
        out_shape=(dealt_type, dealt_type, array(8, LANES)),
        in_specs=[VMEM] * 7,
        out_specs=(VMEM,) * 3,
        scratch_shapes=[pltpu.VMEM((parts * tall, groups * LANES), jnp.float32), plain],
        compiler_params=params(16),
        cost_estimate=pl.CostEstimate(flops=20_000_000, bytes_accessed=2_000_000, transcendentals=400_000),
        name="first",
    )(state, up, down, second, far, first, own)
    return pl.pallas_call(
        steps_kernel,
        out_shape=array(parts, rows, cols),
        in_specs=[VMEM] * 5,
        out_specs=VMEM,
        scratch_shapes=[dealt] * 3 + [plain],
        compiler_params=params(16),
        name="steps",
    )(field, change, own, *top)


def solution(mesh):
    in_specs = (P(None, "gx", "gy"),)
    out_specs = P(None, "gx", "gy")
    return jax.shard_map(local, mesh=mesh, in_specs=in_specs, out_specs=out_specs, check_vma=False)
```

```python
import functools

import jax
import jax.numpy as jnp
from jax import lax
from jax.experimental import pallas as pl
from jax.experimental.pallas import tpu as pltpu
from jax.sharding import PartitionSpec as P

STEPS = 4
HALO = 4 * STEPS
LANES = 128
GAMMA = 1.4
COURANT = 0.35
TINY = 1e-30

VMEM = pl.BlockSpec(memory_space=pltpu.VMEM)


def params(limit):
    return pltpu.CompilerParams(vmem_limit_bytes=limit << 20)


def array(*shape):
    return jax.ShapeDtypeStruct(shape, jnp.float32)


def iota(shape, dim):
    return lax.broadcasted_iota(jnp.int32, shape, dim)


def odd(axis):
    return lax.rem(lax.axis_index(axis), 2) == 1


def odd(axis):
    return lax.rem(lax.axis_index(axis), 2) == 1


def put_rows(block_ref, out_ref, at_tail, top):
    rows = block_ref.shape[1]
    for comp in range(4):
        head = block_ref[comp, 0:HALO, :]
        tail = block_ref[comp, rows - HALO : rows, :]
        out_ref[comp * HALO : (comp + 1) * HALO, :] = jnp.where(at_tail, tail, head)
    out_ref[4 * HALO :, :] = jnp.concatenate([top] * (out_ref.shape[1] // LANES), axis=1)


def edge_kernel(block_ref, first_ref, second_ref, top_ref):
    density, mom_x, mom_y, energy = (block_ref[comp] for comp in range(4))
    inv = 1.0 / density
    pressure = (GAMMA - 1.0) * (energy - 0.5 * (mom_x * mom_x + mom_y * mom_y) * inv)
    speed = jnp.maximum(jnp.abs(mom_x * inv), jnp.abs(mom_y * inv)) + jnp.sqrt(GAMMA * pressure * inv)
    top = jnp.full(top_ref.shape, jnp.max(speed))
    put_rows(block_ref, first_ref, jnp.logical_not(odd("gx")), top)
    put_rows(block_ref, second_ref, odd("gx"), top)
    top_ref[...] = top


def packed(state_ref, up_ref, down_ref, low, at):
    rows = state_ref.shape[1]
    half = rows // 2 + HALO
    lane = iota((half, LANES), 1)
    lanes = slice(low, low + LANES)
    total = jnp.zeros((half, LANES), jnp.float32)
    for side in range(2):
        for comp in range(4):
            span = slice(comp * HALO, (comp + 1) * HALO)
            if side == 0:
                cells = jnp.concatenate([up_ref[span, lanes], state_ref[comp, 0 : rows // 2, lanes]], axis=0)
            else:
                cells = jnp.concatenate([state_ref[comp, rows // 2 : rows, lanes], down_ref[span, lanes]], axis=0)
            goal = side * (LANES // 2) + comp * HALO
            moved = pltpu.roll(cells, (goal - at) % LANES, axis=1)
            total = jnp.where((lane >= goal) & (lane < goal + HALO), moved, total)
    return total


def put_columns(state_ref, up_ref, down_ref, out_ref, at_right, top):
    cols = state_ref.shape[2]
    left = packed(state_ref, up_ref, down_ref, 0, 0)
    right = packed(state_ref, up_ref, down_ref, cols - LANES, LANES - HALO)
    out_ref[0 : left.shape[0], :] = jnp.where(at_right, right, left)
    out_ref[left.shape[0] :, :] = top


def pack_kernel(state_ref, next_ref, three_ref, four_ref, swap_ref, own_ref, up_ref, down_ref, second_ref, top_ref):
    is_odd = odd("gx")
    up_ref[...] = jnp.where(is_odd, swap_ref[...], next_ref[...])
    down_ref[...] = jnp.where(is_odd, next_ref[...], swap_ref[...])
    top = jnp.maximum(jnp.maximum(own_ref[...], jnp.maximum(three_ref[...], four_ref[...])),
                      jnp.maximum(up_ref[4 * HALO :, 0:LANES], down_ref[4 * HALO :, 0:LANES]))
    put_columns(state_ref, up_ref, down_ref, second_ref, odd("gy"), top)
    top_ref[...] = jnp.concatenate([top] * (top_ref.shape[0] // 8), axis=0)


def near_kernel(state_ref, up_ref, down_ref, top_ref, first_ref):
    put_columns(state_ref, up_ref, down_ref, first_ref, jnp.logical_not(odd("gy")), top_ref[0:8, :])


def selected(values, select):
    total = None
    for _ in range(3):
        part = values.astype(jnp.bfloat16)
        values = values - part.astype(jnp.float32)
        term = jnp.dot(part, select, preferred_element_type=jnp.float32)
        total = term if total is None else total + term
    return total


def minmod(first, second):
    low = jnp.minimum(first, second)
    high = jnp.maximum(first, second)
    return jnp.maximum(low, jnp.minimum(high, 0.0))


def fluxes(state):
    density, normal, tangent, energy = state
    inv = pl.reciprocal(density, approx=True)
    vel = normal * inv
    carried = normal * vel
    kinetic = (0.5 * (GAMMA - 1.0)) * (carried + tangent * tangent * inv)
    pressure = energy - kinetic
    scaled = GAMMA * pressure
    square = jnp.maximum(scaled * inv, TINY)
    sound = square * lax.rsqrt(square)
    return (normal, carried + pressure, tangent * vel, (scaled + kinetic) * vel), jnp.abs(vel) + sound


def face(left, right):
    (left_state, left_flux, left_speed), (right_state, right_flux, right_speed) = left, right
    top = jnp.maximum(left_speed, right_speed)
    return [
        (left_flux[comp] + right_flux[comp]) - top * (right_state[comp] - left_state[comp]) for comp in range(4)
    ]


def minus(first, second):
    return [first[comp] - second[comp] for comp in range(4)]


def half(parts):
    return [0.5 * part for part in parts]


def rolled(tree, by, axis):
    return jax.tree.map(lambda value: pltpu.roll(value, by % value.shape[axis], axis=axis), tree)


def cell(here, jump_before, jump_after):
    slope = [minmod(jump_before[comp], jump_after[comp]) for comp in range(4)]
    low = minus(here, slope)
    high = [here[comp] + slope[comp] for comp in range(4)]
    return (low, *fluxes(low)), (high, *fluxes(high))


def row_changes(values):
    count = len(values)
    end_jump = half(minus(rolled(values[0], -1, 1), values[-1]))
    jumps = [half(minus(values[at + 1], values[at])) for at in range(count - 1)] + [end_jump]
    faces, first_low, high = [], None, None
    for at in range(count):
        low, next_high = cell(values[at], jumps[at - 1] if at else rolled(end_jump, 1, 1), jumps[at])
        if at:
            faces.append(face(high, low))
        else:
            first_low = low
        high = next_high
    faces.append(face(high, rolled(first_low, -1, 1)))
    return [minus(faces[at], faces[at - 1] if at else rolled(faces[-1], 1, 1)) for at in range(count)]


class Column:
    def __init__(self, count, begin, here, after):
        self.count, self.begin = count, begin
        self.jump = self.first_jump = half(minus(after, here))
        self.first_low = self.first_flux = self.last_flux = self.high = None

    def feed(self, row, here, after):
        next_row = (row + 1) % self.count
        if after is None:
            next_jump = self.first_jump
        else:
            next_jump = half(minus(rolled(after, -1, 0) if next_row == 0 else after, here))
        jump = rolled(self.jump, 1, 0) if row == 0 else self.jump
        low, high = cell(here, jump, next_jump)
        done = []
        if self.first_low is None:
            self.first_low = low
        else:
            flux = face(rolled(self.high, 1, 0) if row == 0 else self.high, low)
            if self.last_flux is None:
                self.first_flux = flux
            else:
                seen = rolled(flux, -1, 0) if row == 0 else flux
                done.append(((row - 1) % self.count, minus(seen, self.last_flux)))
            self.last_flux = flux
        self.high, self.jump = high, next_jump
        if after is None:
            flux = face(high, self.first_low)
            done.append((row, minus(flux, self.last_flux)))
            done.append(((row + 1) % self.count, minus(self.first_flux, flux)))
        return done


Y_ORDER = (0, 2, 1, 3)


def changes(load, rows, cols, begin, store):
    along_y = {}
    values = {at: [load((begin + at) % rows, col) for col in range(cols)] for at in range(2)}
    columns = [Column(rows, begin, values[0][col], values[1][col]) for col in range(cols)]
    for at in range(1, rows + 1):
        row = (begin + at) % rows
        here = values.pop(at)
        if at < rows:
            values[at + 1] = [load((row + 1) % rows, col) for col in range(cols)]
        ready = []
        for col in range(cols):
            after = values[at + 1][col] if at < rows else None
            ready += [(col, *item) for item in columns[col].feed(row, here[col], after)]
        along_y[row] = row_changes([[part[comp] for comp in Y_ORDER] for part in here])
        for col, done, parts in ready:
            other = along_y[done][col]
            store(done, col, [parts[comp] + other[Y_ORDER[comp]] for comp in range(4)])


def first_kernel(state_ref, up_ref, down_ref, next_ref, far_ref, swap_ref, own_ref, field_ref, change_ref, top_ref, plain, dealt):
    rows, cols = state_ref.shape[1:]
    tall = rows + 2 * HALO
    half = tall // 2
    wide = plain.shape[1]
    groups = wide // LANES
    for comp in range(4):
        span = slice(comp * HALO, (comp + 1) * HALO)
        low = comp * tall
        plain[low : low + HALO, 0:cols] = up_ref[span, :]
        plain[low + HALO : low + HALO + rows, 0:cols] = state_ref[comp]
        plain[low + HALO + rows : low + tall, 0:cols] = down_ref[span, :]
    lane = iota((half, LANES), 1)
    is_odd = odd("gy")
    top_ref[...] = jnp.maximum(jnp.maximum(own_ref[0:8, :], far_ref[0:8, :]), jnp.maximum(next_ref[half:, :], swap_ref[half:, :]))
    from_swap = swap_ref[0:half, :]
    from_next = next_ref[0:half, :]
    from_before = jnp.where(is_odd, from_swap, from_next)
    from_after = jnp.where(is_odd, from_next, from_swap)
    for side in range(2):
        for comp in range(4):
            at = side * (LANES // 2) + comp * HALO
            left = pltpu.roll(from_before, (LANES - HALO - at) % LANES, axis=1)
            right = pltpu.roll(from_after, (-at) % LANES, axis=1)
            low = comp * tall + side * half
            plain[low : low + half, cols:] = jnp.where(lane < LANES // 2, right, left)
    source = iota((wide, wide), 0)
    goal = iota((wide, wide), 1)
    place = groups * (goal % LANES) + goal // LANES
    place = jnp.where(place < cols + 2 * HALO, (place + wide - HALO) % wide, 0)
    select = jnp.where(source == place, 1.0, 0.0).astype(jnp.bfloat16)
    found = selected(plain[...], select)
    for comp in range(4):
        for group in range(groups):
            cells = found[comp * tall : (comp + 1) * tall, group * LANES : (group + 1) * LANES]
            dealt[comp, group] = (GAMMA - 1.0) * cells if comp == 3 else cells
    count = tall // 8
    for comp in range(4):
        for row in range(count):
            for group in range(groups):
                field_ref[comp, row, group] = dealt[comp, group, pl.ds(row, 8, stride=count), :]

    def store(row, col, parts):
        for comp in range(4):
            change_ref[comp, row, col] = parts[comp]

    def load(row, col):
        return [field_ref[comp, row, col] for comp in range(4)]

    changes(load, count, groups, 0, store)


def steps_kernel(field_ref, change_ref, own_ref, mate_ref, wide_ref, out_ref, field, base, mid, dealt, result, sems):
    rows, cols = out_ref.shape[1:]
    tall = rows + 2 * HALO
    groups = field_ref.shape[2]
    half_factor = -0.25 * COURANT / jnp.maximum(own_ref[...], jnp.maximum(mate_ref[...], wide_ref[...]))

    def one_step(start, count, old, first_changes):
        def to_mid(row, col, parts):
            for comp in range(4):
                move = half_factor * parts[comp]
                moved = old[comp, row, col] + move
                base[comp, row, col] = moved
                mid[comp, row, col] = moved + move

        def to_field(row, col, parts):
            for comp in range(4):
                new = base[comp, row, col] + half_factor * parts[comp]
                dealt[comp, col, pl.ds(start + row, 8, stride=count), :] = new

        def load_from(ref):
            return lambda row, col: [ref[comp, row, col] for comp in range(4)]

        if first_changes is not None:
            for row in range(count):
                for col in range(groups):
                    to_mid(row, col, [first_changes[comp, row, col] for comp in range(4)])
        else:
            for comp in range(4):
                for row in range(count):
                    for col in range(groups):
                        old[comp, row, col] = dealt[comp, col, pl.ds(start + row, 8, stride=count), :]
            changes(load_from(old), count, groups, 0, to_mid)
        changes(load_from(mid), count, groups, count // 2, to_field)

    one_step(0, tall // 8, field_ref, change_ref)
    for index in range(1, STEPS):
        one_step(4 * index, (tall - 8 * index) // 8, field, None)

    wide = groups * LANES
    source = iota((wide, cols), 0)
    goal = iota((wide, cols), 1)
    select = jnp.where(groups * (source % LANES) + source // LANES == goal + HALO, 1.0, 0.0).astype(jnp.bfloat16)
    lane = iota((rows, LANES), 1)
    copies = []
    for comp in range(4):
        line = []
        for group in range(groups):
            place = groups * lane + group
            inside = (place >= HALO) & (place < HALO + cols)
            line.append(jnp.where(inside, dealt[comp, group, HALO : HALO + rows, :], 0.0))
        cells = selected(jnp.concatenate(line, axis=1), select)
        result[comp] = cells / (GAMMA - 1.0) if comp == 3 else cells
        copies.append(pltpu.make_async_copy(result.at[comp], out_ref.at[comp], sems.at[comp]))
        copies[-1].start()
    for copy in copies:
        copy.wait()


def local(state):
    parts, rows, cols = state.shape
    tall = rows + 2 * HALO
    groups = -(-(cols + 2 * HALO) // LANES)

    def sent(value, axis, by):
        count = lax.axis_size(axis)
        return lax.ppermute(value, axis, [(i, (i + by) % count) for i in range(count)])

    def swapped_bit(value, axis, by):
        return lax.ppermute(value, axis, [(i, i ^ by) for i in range(lax.axis_size(axis))])

    def swapped_pairs(value, axis, first):
        count = lax.axis_size(axis)
        pairs = []
        for low in range(first, count, 2):
            high = (low + 1) % count
            pairs += [(low, high), (high, low)]
        return lax.ppermute(value, axis, pairs)

    def swapped_threes(value, axis):
        count = lax.axis_size(axis)
        return lax.ppermute(value, axis, [(i, (i + 3 - 6 * (i % 2)) % count) for i in range(count)])

    edge_type = array(parts * HALO + 8, cols)
    def call(kernel, out_shape, name, *operands):
        return pl.pallas_call(
            kernel,
            out_shape=out_shape,
            in_specs=[VMEM] * len(operands),
            out_specs=jax.tree.map(lambda _: VMEM, out_shape),
            compiler_params=params(4),
            name=name,
        )(*operands)

    top_type = array(8, LANES)
    first, second, top = call(edge_kernel, (edge_type, edge_type, top_type), "edge", state)
    second = swapped_pairs(second, "gx", 1)
    far = swapped_threes(top, "gx"), swapped_bit(top, "gx", 4)
    first = swapped_pairs(first, "gx", 0)
    side_type = array(tall // 2 + 8, LANES)
    up, down, second, top = call(
        pack_kernel, (edge_type, edge_type, side_type, side_type), "pack", state, second, *far, first, top
    )
    second = swapped_pairs(second, "gy", 1)
    far = swapped_bit(top, "gy", 2)
    first = swapped_pairs(call(near_kernel, side_type, "near", state, up, down, top), "gy", 0)
    own = top
    top = jnp.maximum(jnp.maximum(own, far)[:8], jnp.maximum(first[tall // 2 :], second[tall // 2 :]))
    for axis, covered in (("gy", 4), ("gx", 8)):
        while covered < lax.axis_size(axis):
            top = jnp.maximum(top, sent(top, axis, covered))
            covered *= 2
    top = swapped_bit(top, "gx", 1), top
    dealt_type = array(parts, tall // 8, groups, 8, LANES)
    dealt = pltpu.VMEM(dealt_type.shape, jnp.float32)
    plain = pltpu.VMEM((parts, groups, tall, LANES), jnp.float32)
    field, change, own = pl.pallas_call(
        first_kernel,
        out_shape=(dealt_type, dealt_type, array(8, LANES)),
        in_specs=[VMEM] * 7,
        out_specs=(VMEM,) * 3,
        scratch_shapes=[pltpu.VMEM((parts * tall, groups * LANES), jnp.float32), plain],
        compiler_params=params(16),
        cost_estimate=pl.CostEstimate(flops=20_000_000, bytes_accessed=2_000_000, transcendentals=400_000),
        name="first",
    )(state, up, down, second, far, first, own)
    return pl.pallas_call(
        steps_kernel,
        out_shape=array(parts, rows, cols),
        in_specs=[VMEM] * 5,
        out_specs=pl.BlockSpec(memory_space=pl.ANY),
        scratch_shapes=[dealt] * 3
        + [plain, pltpu.VMEM((parts, rows, cols), jnp.float32), pltpu.SemaphoreType.DMA((parts,))],
        compiler_params=params(16),
        name="steps",
    )(field, change, own, *top)


def solution(mesh):
    in_specs = (P(None, "gx", "gy"),)
    out_specs = P(None, "gx", "gy")
    return jax.shard_map(local, mesh=mesh, in_specs=in_specs, out_specs=out_specs, check_vma=False)
```

```python
import functools
import math

import jax
import jax.numpy as jnp
from jax import lax
from jax.experimental import pallas as pl
from jax.experimental.pallas import tpu as pltpu
from jax.sharding import PartitionSpec as P

STEPS = 4
HALO = 4 * STEPS
LANES = 128
GAMMA = 1.4
COURANT = 0.35
TINY = 1e-30

VMEM = pl.BlockSpec(memory_space=pltpu.VMEM)


def params(limit):
    return pltpu.CompilerParams(vmem_limit_bytes=limit << 20)


def array(*shape):
    return jax.ShapeDtypeStruct(shape, jnp.float32)


def iota(shape, dim):
    return lax.broadcasted_iota(jnp.int32, shape, dim)


def odd(axis):
    return lax.rem(lax.axis_index(axis), 2) == 1


def edge_kernel(block_ref, first_ref, second_ref, top_ref):
    rows = block_ref.shape[1]
    density, mom_x, mom_y, energy = (block_ref[comp] for comp in range(4))
    inv = 1.0 / density
    pressure = (GAMMA - 1.0) * (energy - 0.5 * (mom_x * mom_x + mom_y * mom_y) * inv)
    speed = jnp.maximum(jnp.abs(mom_x * inv), jnp.abs(mom_y * inv)) + jnp.sqrt(GAMMA * pressure * inv)
    top = jnp.max(speed)
    is_odd = odd("gx")
    for comp in range(4):
        span = slice(comp * HALO, (comp + 1) * HALO)
        head = block_ref[comp, 0:HALO, :]
        tail = block_ref[comp, rows - HALO : rows, :]
        first_ref[span, :] = jnp.where(is_odd, head, tail)
        second_ref[span, :] = jnp.where(is_odd, tail, head)
    first_ref[4 * HALO :, :] = jnp.full((8, first_ref.shape[1]), top)
    second_ref[4 * HALO :, :] = jnp.full((8, second_ref.shape[1]), top)
    top_ref[...] = jnp.full(top_ref.shape, top)


def pack_kernel(state_ref, next_ref, three_ref, four_ref, swap_ref, own_ref, up_ref, down_ref, first_ref, second_ref, top_ref):
    rows = state_ref.shape[1]
    cols = state_ref.shape[2]
    half = rows // 2 + HALO
    lane = iota((half, LANES), 1)
    is_odd = odd("gx")
    up_ref[...] = jnp.where(is_odd, swap_ref[...], next_ref[...])
    down_ref[...] = jnp.where(is_odd, next_ref[...], swap_ref[...])
    top = jnp.maximum(jnp.maximum(own_ref[...], jnp.maximum(three_ref[...], four_ref[...])),
                      jnp.maximum(up_ref[4 * HALO :, 0:LANES], down_ref[4 * HALO :, 0:LANES]))

    def edge(low, at):
        lanes = slice(low, low + LANES)
        total = jnp.zeros((half, LANES), jnp.float32)
        for side in range(2):
            for comp in range(4):
                span = slice(comp * HALO, (comp + 1) * HALO)
                if side == 0:
                    cells = jnp.concatenate([up_ref[span, lanes], state_ref[comp, 0 : rows // 2, lanes]], axis=0)
                else:
                    cells = jnp.concatenate([state_ref[comp, rows // 2 : rows, lanes], down_ref[span, lanes]], axis=0)
                goal = side * (LANES // 2) + comp * HALO
                moved = pltpu.roll(cells, (goal - at) % LANES, axis=1)
                total = jnp.where((lane >= goal) & (lane < goal + HALO), moved, total)
        return total

    left = edge(0, 0)
    right = edge(cols - LANES, LANES - HALO)
    is_odd = odd("gy")
    first_ref[0:half, :] = jnp.where(is_odd, left, right)
    second_ref[0:half, :] = jnp.where(is_odd, right, left)
    first_ref[half:, :] = top
    second_ref[half:, :] = top
    top_ref[...] = top


def selected(values, select):
    rows = values.shape[0]
    parts = []
    for _ in range(3):
        parts.append(values.astype(jnp.bfloat16))
        values = values - parts[-1].astype(jnp.float32)
    found = jnp.dot(jnp.concatenate(parts, axis=0), select, preferred_element_type=jnp.float32)
    return (found[0:rows] + found[rows : 2 * rows]) + found[2 * rows :]


def minmod(first, second):
    low = jnp.minimum(first, second)
    high = jnp.maximum(first, second)
    return jnp.maximum(low, jnp.minimum(high, 0.0))


MOMENTUM = math.sqrt(0.5 * (GAMMA - 1.0))
SCALES = (1.0, MOMENTUM, MOMENTUM, GAMMA - 1.0)


def known(state):
    density, normal, tangent, energy = state
    inv = pl.reciprocal(density, approx=True)
    vel = normal * inv
    pressure = energy - (normal * normal + tangent * tangent) * inv
    square = jnp.maximum((GAMMA * MOMENTUM * MOMENTUM) * pressure * inv, TINY)
    return state, vel, pressure, pressure * vel, jnp.abs(vel) + square * lax.rsqrt(square)


def face(left, right):
    (left_state, left_vel, left_pressure, left_work, left_speed) = left
    (right_state, right_vel, right_pressure, right_work, right_speed) = right
    top = jnp.maximum(left_speed, right_speed)
    left_rate = left_vel + top
    right_rate = right_vel - top
    flux = [left_rate * left_state[comp] + right_rate * right_state[comp] for comp in range(4)]
    flux[1] = flux[1] + (MOMENTUM * MOMENTUM) * (left_pressure + right_pressure)
    flux[3] = flux[3] + (GAMMA - 1.0) * (left_work + right_work)
    return flux


def minus(first, second):
    return [first[comp] - second[comp] for comp in range(4)]


def rolled(tree, by, axis):
    return jax.tree.map(lambda value: pltpu.roll(value, by % value.shape[axis], axis=axis), tree)


def cell(here, jump_before, jump_after):
    slope = [minmod(jump_before[comp], jump_after[comp]) for comp in range(4)]
    whole = [here[comp] + here[comp] for comp in range(4)]
    return known(minus(whole, slope)), known([whole[comp] + slope[comp] for comp in range(4)])


def row_changes(values):
    count = len(values)
    end_jump = minus(rolled(values[0], -1, 1), values[-1])
    jumps = [minus(values[at + 1], values[at]) for at in range(count - 1)] + [end_jump]
    faces, first_low, high = [], None, None
    for at in range(count):
        low, next_high = cell(values[at], jumps[at - 1] if at else rolled(end_jump, 1, 1), jumps[at])
        if at:
            faces.append(face(high, low))
        else:
            first_low = low
        high = next_high
    faces.append(face(high, rolled(first_low, -1, 1)))
    return [minus(faces[at], faces[at - 1] if at else rolled(faces[-1], 1, 1)) for at in range(count)]


class Column:
    def __init__(self, count, begin, here, after):
        self.count, self.begin = count, begin
        self.jump = self.first_jump = minus(after, here)
        self.first_low = self.first_flux = self.last_flux = self.high = None

    def feed(self, row, here, after):
        next_row = (row + 1) % self.count
        if after is None:
            next_jump = self.first_jump
        else:
            next_jump = minus(rolled(after, -1, 0) if next_row == 0 else after, here)
        jump = rolled(self.jump, 1, 0) if row == 0 else self.jump
        low, high = cell(here, jump, next_jump)
        done = []
        if self.first_low is None:
            self.first_low = low
        else:
            flux = face(rolled(self.high, 1, 0) if row == 0 else self.high, low)
            if self.last_flux is None:
                self.first_flux = flux
            else:
                seen = rolled(flux, -1, 0) if row == 0 else flux
                done.append(((row - 1) % self.count, minus(seen, self.last_flux)))
            self.last_flux = flux
        self.high, self.jump = high, next_jump
        if after is None:
            flux = face(high, self.first_low)
            done.append((row, minus(flux, self.last_flux)))
            done.append(((row + 1) % self.count, minus(self.first_flux, flux)))
        return done


Y_ORDER = (0, 2, 1, 3)


def changes(load, rows, cols, begin, store):
    along_y = {}
    values = {at: [load((begin + at) % rows, col) for col in range(cols)] for at in range(2)}
    columns = [Column(rows, begin, values[0][col], values[1][col]) for col in range(cols)]
    for at in range(1, rows + 1):
        row = (begin + at) % rows
        here = values.pop(at)
        if at < rows:
            values[at + 1] = [load((row + 1) % rows, col) for col in range(cols)]
        ready = []
        for col in range(cols):
            after = values[at + 1][col] if at < rows else None
            ready += [(col, *item) for item in columns[col].feed(row, here[col], after)]
        along_y[row] = row_changes([[part[comp] for comp in Y_ORDER] for part in here])
        for col, done, parts in ready:
            other = along_y[done][col]
            store(done, col, [parts[comp] + other[Y_ORDER[comp]] for comp in range(4)])


def first_kernel(state_ref, up_ref, down_ref, next_ref, far_ref, swap_ref, own_ref, field_ref, change_ref, top_ref, plain, dealt):
    rows, cols = state_ref.shape[1:]
    tall = rows + 2 * HALO
    half = tall // 2
    wide = plain.shape[1]
    groups = wide // LANES
    for comp in range(4):
        span = slice(comp * HALO, (comp + 1) * HALO)
        low = comp * tall
        plain[low : low + HALO, 0:cols] = up_ref[span, :]
        plain[low + HALO : low + HALO + rows, 0:cols] = state_ref[comp]
        plain[low + HALO + rows : low + tall, 0:cols] = down_ref[span, :]
    lane = iota((half, LANES), 1)
    is_odd = odd("gy")
    top_ref[...] = jnp.maximum(jnp.maximum(own_ref[...], far_ref[...]), jnp.maximum(next_ref[half:, :], swap_ref[half:, :]))
    from_swap = swap_ref[0:half, :]
    from_next = next_ref[0:half, :]
    from_before = jnp.where(is_odd, from_swap, from_next)
    from_after = jnp.where(is_odd, from_next, from_swap)
    for side in range(2):
        for comp in range(4):
            at = side * (LANES // 2) + comp * HALO
            left = pltpu.roll(from_before, (LANES - HALO - at) % LANES, axis=1)
            right = pltpu.roll(from_after, (-at) % LANES, axis=1)
            low = comp * tall + side * half
            plain[low : low + half, cols:] = jnp.where(lane < LANES // 2, right, left)
    source = iota((wide, wide), 0)
    goal = iota((wide, wide), 1)
    place = groups * (goal % LANES) + goal // LANES
    place = jnp.where(place < cols + 2 * HALO, (place + wide - HALO) % wide, 0)
    select = jnp.where(source == place, 1.0, 0.0).astype(jnp.bfloat16)
    found = selected(plain[...], select)
    for comp in range(4):
        for group in range(groups):
            cells = found[comp * tall : (comp + 1) * tall, group * LANES : (group + 1) * LANES]
            dealt[comp, group] = (0.5 * SCALES[comp]) * cells
    count = tall // 8
    for comp in range(4):
        for row in range(count):
            for group in range(groups):
                field_ref[comp, row, group] = dealt[comp, group, pl.ds(row, 8, stride=count), :]

    def store(row, col, parts):
        for comp in range(4):
            change_ref[comp, row, col] = parts[comp]

    def load(row, col):
        return [field_ref[comp, row, col] for comp in range(4)]

    changes(load, count, groups, 0, store)


def steps_kernel(field_ref, change_ref, own_ref, mate_ref, wide_ref, out_ref, field, base, mid, dealt, result, sems):
    rows, cols = out_ref.shape[1:]
    tall = rows + 2 * HALO
    groups = field_ref.shape[2]
    half_factor = (-0.125 * COURANT / MOMENTUM) / jnp.maximum(own_ref[...], jnp.maximum(mate_ref[...], wide_ref[...]))

    def one_step(start, count, old, first_changes):
        def to_mid(row, col, parts):
            for comp in range(4):
                move = half_factor * parts[comp]
                moved = old[comp, row, col] + move
                base[comp, row, col] = moved
                mid[comp, row, col] = moved + move

        def to_field(row, col, parts):
            for comp in range(4):
                new = base[comp, row, col] + half_factor * parts[comp]
                dealt[comp, col, pl.ds(start + row, 8, stride=count), :] = new

        def load_from(ref):
            return lambda row, col: [ref[comp, row, col] for comp in range(4)]

        if first_changes is not None:
            for row in range(count):
                for col in range(groups):
                    to_mid(row, col, [first_changes[comp, row, col] for comp in range(4)])
        else:
            for comp in range(4):
                for row in range(count):
                    for col in range(groups):
                        old[comp, row, col] = dealt[comp, col, pl.ds(start + row, 8, stride=count), :]
            changes(load_from(old), count, groups, 0, to_mid)
        changes(load_from(mid), count, groups, count // 2, to_field)

    one_step(0, tall // 8, field_ref, change_ref)
    for index in range(1, STEPS):
        one_step(4 * index, (tall - 8 * index) // 8, field, None)

    wide = groups * LANES
    source = iota((wide, cols), 0)
    goal = iota((wide, cols), 1)
    select = jnp.where(groups * (source % LANES) + source // LANES == goal + HALO, 1.0, 0.0).astype(jnp.bfloat16)
    lane = iota((rows, LANES), 1)
    parts = []
    for comp in range(4):
        line = []
        for group in range(groups):
            place = groups * lane + group
            inside = (place >= HALO) & (place < HALO + cols)
            line.append(jnp.where(inside, dealt[comp, group, HALO : HALO + rows, :], 0.0))
        parts.append(jnp.concatenate(line, axis=1))
    found = selected(jnp.concatenate(parts, axis=0), select)
    copies = []
    for comp in range(4):
        result[comp] = (2.0 / SCALES[comp]) * found[comp * rows : (comp + 1) * rows, :]
        copies.append(pltpu.make_async_copy(result.at[comp], out_ref.at[comp], sems.at[comp]))
        copies[-1].start()
    for copy in copies:
        copy.wait()


def local(state):
    parts, rows, cols = state.shape
    tall = rows + 2 * HALO
    groups = -(-(cols + 2 * HALO) // LANES)

    def sent(value, axis, by):
        count = lax.axis_size(axis)
        return lax.ppermute(value, axis, [(i, (i + by) % count) for i in range(count)])

    def swapped_bit(value, axis, by):
        return lax.ppermute(value, axis, [(i, i ^ by) for i in range(lax.axis_size(axis))])

    def swapped_pairs(value, axis, first):
        count = lax.axis_size(axis)
        pairs = []
        for low in range(first, count, 2):
            high = (low + 1) % count
            pairs += [(low, high), (high, low)]
        return lax.ppermute(value, axis, pairs)

    def swapped_threes(value, axis):
        count = lax.axis_size(axis)
        return lax.ppermute(value, axis, [(i, (i + 3 - 6 * (i % 2)) % count) for i in range(count)])

    edge_type = array(parts * HALO + 8, cols)
    first, second, top = pl.pallas_call(
        edge_kernel,
        out_shape=(edge_type, edge_type, array(8, LANES)),
        in_specs=[VMEM],
        out_specs=(VMEM,) * 3,
        compiler_params=params(4),
        name="edge",
    )(state)
    second = swapped_pairs(second, "gx", 1)
    first = swapped_pairs(first, "gx", 0)
    far = swapped_threes(top, "gx"), swapped_bit(top, "gx", 4)
    side_type = array(tall // 2 + 8, LANES)
    up, down, first, second, top = pl.pallas_call(
        pack_kernel,
        out_shape=(edge_type, edge_type, side_type, side_type, array(8, LANES)),
        in_specs=[VMEM] * 6,
        out_specs=(VMEM,) * 5,
        compiler_params=params(4),
        name="pack",
    )(state, second, *far, first, top)
    second = swapped_pairs(second, "gy", 1)
    first = swapped_pairs(first, "gy", 0)
    far = swapped_bit(top, "gy", 2)
    own = top
    top = jnp.maximum(jnp.maximum(own, far), jnp.maximum(first[tall // 2 :], second[tall // 2 :]))
    for axis, covered in (("gy", 4), ("gx", 8)):
        while covered < lax.axis_size(axis):
            top = jnp.maximum(top, sent(top, axis, covered))
            covered *= 2
    top = swapped_bit(top, "gx", 1), top
    dealt_type = array(parts, tall // 8, groups, 8, LANES)
    dealt = pltpu.VMEM(dealt_type.shape, jnp.float32)
    plain = pltpu.VMEM((parts, groups, tall, LANES), jnp.float32)
    field, change, own = pl.pallas_call(
        first_kernel,
        out_shape=(dealt_type, dealt_type, array(8, LANES)),
        in_specs=[VMEM] * 7,
        out_specs=(VMEM,) * 3,
        scratch_shapes=[pltpu.VMEM((parts * tall, groups * LANES), jnp.float32), plain],
        compiler_params=params(16),
        cost_estimate=pl.CostEstimate(flops=20_000_000, bytes_accessed=2_000_000, transcendentals=400_000),
        name="first",
    )(state, up, down, second, far, first, own)
    return pl.pallas_call(
        steps_kernel,
        out_shape=array(parts, rows, cols),
        in_specs=[VMEM] * 5,
        out_specs=pl.BlockSpec(memory_space=pl.ANY),
        scratch_shapes=[dealt] * 3
        + [plain, pltpu.VMEM((parts, rows, cols), jnp.float32), pltpu.SemaphoreType.DMA((parts,))],
        compiler_params=params(16),
        name="steps",
    )(field, change, own, *top)


def solution(mesh):
    in_specs = (P(None, "gx", "gy"),)
    out_specs = P(None, "gx", "gy")
    return jax.shard_map(local, mesh=mesh, in_specs=in_specs, out_specs=out_specs, check_vma=False)
```

```python
import functools
import math

import jax
import jax.numpy as jnp
from jax import lax
from jax.experimental import pallas as pl
from jax.experimental.pallas import tpu as pltpu
from jax.sharding import PartitionSpec as P

STEPS = 4
HALO = 4 * STEPS
LANES = 128
GAMMA = 1.4
COURANT = 0.35
TINY = 1e-30

VMEM = pl.BlockSpec(memory_space=pltpu.VMEM)


def params(limit):
    return pltpu.CompilerParams(vmem_limit_bytes=limit << 20)


def array(*shape):
    return jax.ShapeDtypeStruct(shape, jnp.float32)


def iota(shape, dim):
    return lax.broadcasted_iota(jnp.int32, shape, dim)


def odd(axis):
    return lax.rem(lax.axis_index(axis), 2) == 1


def edge_kernel(block_ref, first_ref, second_ref, top_ref):
    rows = block_ref.shape[1]
    density, mom_x, mom_y, energy = (block_ref[comp] for comp in range(4))
    inv = 1.0 / density
    pressure = (GAMMA - 1.0) * (energy - 0.5 * (mom_x * mom_x + mom_y * mom_y) * inv)
    speed = jnp.maximum(jnp.abs(mom_x * inv), jnp.abs(mom_y * inv)) + jnp.sqrt(GAMMA * pressure * inv)
    top = jnp.max(speed)
    is_odd = odd("gx")
    for comp in range(4):
        span = slice(comp * HALO, (comp + 1) * HALO)
        head = block_ref[comp, 0:HALO, :]
        tail = block_ref[comp, rows - HALO : rows, :]
        first_ref[span, :] = jnp.where(is_odd, head, tail)
        second_ref[span, :] = jnp.where(is_odd, tail, head)
    first_ref[4 * HALO :, :] = jnp.full((8, first_ref.shape[1]), top)
    second_ref[4 * HALO :, :] = jnp.full((8, second_ref.shape[1]), top)
    top_ref[...] = jnp.full(top_ref.shape, top)


def pack_kernel(state_ref, next_ref, three_ref, four_ref, swap_ref, own_ref, up_ref, down_ref, first_ref, second_ref, top_ref):
    rows = state_ref.shape[1]
    cols = state_ref.shape[2]
    half = rows // 2 + HALO
    lane = iota((half, LANES), 1)
    is_odd = odd("gx")
    up_ref[...] = jnp.where(is_odd, swap_ref[...], next_ref[...])
    down_ref[...] = jnp.where(is_odd, next_ref[...], swap_ref[...])
    top = jnp.maximum(jnp.maximum(own_ref[...], jnp.maximum(three_ref[...], four_ref[...])),
                      jnp.maximum(up_ref[4 * HALO :, 0:LANES], down_ref[4 * HALO :, 0:LANES]))

    def edge(low, at):
        lanes = slice(low, low + LANES)
        total = jnp.zeros((half, LANES), jnp.float32)
        for side in range(2):
            for comp in range(4):
                span = slice(comp * HALO, (comp + 1) * HALO)
                if side == 0:
                    cells = jnp.concatenate([up_ref[span, lanes], state_ref[comp, 0 : rows // 2, lanes]], axis=0)
                else:
                    cells = jnp.concatenate([state_ref[comp, rows // 2 : rows, lanes], down_ref[span, lanes]], axis=0)
                goal = side * (LANES // 2) + comp * HALO
                moved = pltpu.roll(cells, (goal - at) % LANES, axis=1)
                total = jnp.where((lane >= goal) & (lane < goal + HALO), moved, total)
        return total

    left = edge(0, 0)
    right = edge(cols - LANES, LANES - HALO)
    free = (iota((half, LANES), 0) == 0) & (lane < LANES // 2)
    under = jnp.concatenate([top] * (half // 8), axis=0)
    left = jnp.where(free, under, left)
    right = jnp.where(free, under, right)
    is_odd = odd("gy")
    first_ref[...] = jnp.where(is_odd, left, right)
    second_ref[...] = jnp.where(is_odd, right, left)
    top_ref[...] = top


def selected(values, select):
    rows = values.shape[0]
    parts = []
    for _ in range(3):
        parts.append(values.astype(jnp.bfloat16))
        values = values - parts[-1].astype(jnp.float32)
    found = jnp.dot(jnp.concatenate(parts, axis=0), select, preferred_element_type=jnp.float32)
    return (found[0:rows] + found[rows : 2 * rows]) + found[2 * rows :]


def minmod(first, second):
    low = jnp.minimum(first, second)
    high = jnp.maximum(first, second)
    return jnp.maximum(low, jnp.minimum(high, 0.0))


MOMENTUM = math.sqrt(0.5 * (GAMMA - 1.0))
SCALES = (1.0, MOMENTUM, MOMENTUM, GAMMA - 1.0)


def known(state):
    density, normal, tangent, energy = state
    inv = pl.reciprocal(density, approx=True)
    vel = normal * inv
    pressure = energy - (normal * normal + tangent * tangent) * inv
    square = jnp.maximum((GAMMA * MOMENTUM * MOMENTUM) * pressure * inv, TINY)
    return state, vel, pressure, pressure * vel, jnp.abs(vel) + square * lax.rsqrt(square)


def face(left, right):
    (left_state, left_vel, left_pressure, left_work, left_speed) = left
    (right_state, right_vel, right_pressure, right_work, right_speed) = right
    top = jnp.maximum(left_speed, right_speed)
    left_rate = left_vel + top
    right_rate = right_vel - top
    flux = [left_rate * left_state[comp] + right_rate * right_state[comp] for comp in range(4)]
    flux[1] = flux[1] + (MOMENTUM * MOMENTUM) * (left_pressure + right_pressure)
    flux[3] = flux[3] + (GAMMA - 1.0) * (left_work + right_work)
    return flux


def minus(first, second):
    return [first[comp] - second[comp] for comp in range(4)]


def rolled(tree, by, axis):
    return jax.tree.map(lambda value: pltpu.roll(value, by % value.shape[axis], axis=axis), tree)


def cell(whole, jump_before, jump_after):
    slope = [minmod(jump_before[comp], jump_after[comp]) for comp in range(4)]
    return known(minus(whole, slope)), known([whole[comp] + slope[comp] for comp in range(4)])


def row_changes(values, wholes):
    count = len(values)
    end_jump = minus(rolled(values[0], -1, 1), values[-1])
    jumps = [minus(values[at + 1], values[at]) for at in range(count - 1)] + [end_jump]
    faces, first_low, high = [], None, None
    for at in range(count):
        low, next_high = cell(wholes[at], jumps[at - 1] if at else rolled(end_jump, 1, 1), jumps[at])
        if at:
            faces.append(face(high, low))
        else:
            first_low = low
        high = next_high
    faces.append(face(high, rolled(first_low, -1, 1)))
    return [minus(faces[at], faces[at - 1] if at else rolled(faces[-1], 1, 1)) for at in range(count)]


class Column:
    def __init__(self, count, begin, here, after):
        self.count, self.begin = count, begin
        self.jump = self.first_jump = minus(after, here)
        self.first_low = self.first_flux = self.last_flux = self.high = None

    def feed(self, row, here, whole, after):
        next_row = (row + 1) % self.count
        if after is None:
            next_jump = self.first_jump
        else:
            next_jump = minus(rolled(after, -1, 0) if next_row == 0 else after, here)
        jump = rolled(self.jump, 1, 0) if row == 0 else self.jump
        low, high = cell(whole, jump, next_jump)
        done = []
        if self.first_low is None:
            self.first_low = low
        else:
            flux = face(rolled(self.high, 1, 0) if row == 0 else self.high, low)
            if self.last_flux is None:
                self.first_flux = flux
            else:
                seen = rolled(flux, -1, 0) if row == 0 else flux
                done.append(((row - 1) % self.count, minus(seen, self.last_flux)))
            self.last_flux = flux
        self.high, self.jump = high, next_jump
        if after is None:
            flux = face(high, self.first_low)
            done.append((row, minus(flux, self.last_flux)))
            done.append(((row + 1) % self.count, minus(self.first_flux, flux)))
        return done


Y_ORDER = (0, 2, 1, 3)


def changes(load, rows, cols, begin, store):
    along_y = {}
    values = {at: [load((begin + at) % rows, col) for col in range(cols)] for at in range(2)}
    columns = [Column(rows, begin, values[0][col], values[1][col]) for col in range(cols)]
    for at in range(1, rows + 1):
        row = (begin + at) % rows
        here = values.pop(at)
        if at < rows:
            values[at + 1] = [load((row + 1) % rows, col) for col in range(cols)]
        whole = [[part + part for part in value] for value in here]
        ready = []
        for col in range(cols):
            after = values[at + 1][col] if at < rows else None
            ready += [(col, *item) for item in columns[col].feed(row, here[col], whole[col], after)]
        along_y[row] = row_changes(*([[part[comp] for comp in Y_ORDER] for part in value] for value in (here, whole)))
        for col, done, parts in ready:
            other = along_y[done][col]
            store(done, col, [parts[comp] + other[Y_ORDER[comp]] for comp in range(4)])


def place_of(lane, group, groups):
    return groups * lane + group


def deal_kernel(state_ref, up_ref, down_ref, own_ref, dealt_ref, halo_select_ref, back_select_ref, top_ref, plain):
    top_ref[...] = own_ref[...]
    rows, cols = state_ref.shape[1:]
    tall = rows + 2 * HALO
    wide = dealt_ref.shape[1]
    groups = wide // LANES
    for comp in range(4):
        span = slice(comp * HALO, (comp + 1) * HALO)
        low = comp * tall
        plain[low : low + HALO, :] = up_ref[span, :]
        plain[low + HALO : low + HALO + rows, :] = state_ref[comp]
        plain[low + HALO + rows : low + tall, :] = down_ref[span, :]
    source = iota((wide, wide), 0)
    goal = iota((wide, wide), 1)
    place = place_of(goal % LANES, goal // LANES, groups)
    place = jnp.where(place < cols + 2 * HALO, (place + wide - HALO) % wide, 0)
    select = jnp.where(source == place, 1.0, 0.0).astype(jnp.bfloat16)
    dealt_ref[...] = selected(plain[...], select[0:cols])
    halo_select_ref[...] = select[cols:]
    source = iota((wide, cols), 0)
    goal = iota((wide, cols), 1)
    back = place_of(source % LANES, source // LANES, groups) == goal + HALO
    back_select_ref[...] = jnp.where(back, 1.0, 0.0).astype(jnp.bfloat16)


def join_kernel(next_ref, swap_ref, far_ref, own_ref, top_ref):
    speeds = jnp.maximum(next_ref[0:8, :], swap_ref[0:8, :])
    carried = (iota((8, LANES), 0) == 0) & (iota((8, LANES), 1) < LANES // 2)
    known_here = jnp.maximum(own_ref[...], far_ref[...])
    top_ref[...] = jnp.full((8, LANES), jnp.max(jnp.where(carried, speeds, known_here)))


def first_kernel(cells_ref, select_ref, next_ref, swap_ref, field_ref, change_ref, plain, dealt):
    half = next_ref.shape[0]
    tall = 2 * half
    groups = cells_ref.shape[1] // LANES
    lane = iota((half, LANES), 1)
    is_odd = odd("gy")
    from_swap = swap_ref[...]
    from_next = next_ref[...]
    from_before = jnp.where(is_odd, from_swap, from_next)
    from_after = jnp.where(is_odd, from_next, from_swap)
    for side in range(2):
        for comp in range(4):
            at = side * (LANES // 2) + comp * HALO
            left = pltpu.roll(from_before, (LANES - HALO - at) % LANES, axis=1)
            right = pltpu.roll(from_after, (-at) % LANES, axis=1)
            low = comp * tall + side * half
            plain[low : low + half, :] = jnp.where(lane < LANES // 2, right, left)
    found = cells_ref[...] + selected(plain[...], select_ref[...])
    for comp in range(4):
        for group in range(groups):
            cells = found[comp * tall : (comp + 1) * tall, group * LANES : (group + 1) * LANES]
            dealt[comp, group] = (0.5 * SCALES[comp]) * cells
    count = tall // 8
    for comp in range(4):
        for row in range(count):
            for group in range(groups):
                field_ref[comp, row, group] = dealt[comp, group, pl.ds(row, 8, stride=count), :]

    def store(row, col, parts):
        for comp in range(4):
            change_ref[comp, row, col] = parts[comp]

    def load(row, col):
        return [field_ref[comp, row, col] for comp in range(4)]

    changes(load, count, groups, 0, store)


def steps_kernel(field_ref, change_ref, select_ref, own_ref, mate_ref, out_ref, field, base, mid, dealt, result, sems):
    rows, cols = out_ref.shape[1:]
    tall = rows + 2 * HALO
    groups = field_ref.shape[2]
    scale = (0.125 * COURANT / MOMENTUM) / jnp.max(jnp.maximum(own_ref[...], mate_ref[...]))
    scales = (1.0, scale, scale, scale * scale)

    def one_step(start, count, old, first_changes):
        def to_mid(row, col, parts):
            for comp in range(4):
                cells, move = old[comp, row, col], parts[comp]
                if first_changes is not None:
                    cells, move = scales[comp] * cells, (scales[comp] * scale) * move
                moved = cells - move
                base[comp, row, col] = moved
                mid[comp, row, col] = moved - move

        def to_field(row, col, parts):
            for comp in range(4):
                new = base[comp, row, col] - parts[comp]
                dealt[comp, col, pl.ds(start + row, 8, stride=count), :] = new

        def load_from(ref):
            return lambda row, col: [ref[comp, row, col] for comp in range(4)]

        if first_changes is not None:
            for row in range(count):
                for col in range(groups):
                    to_mid(row, col, [first_changes[comp, row, col] for comp in range(4)])
        else:
            for comp in range(4):
                for row in range(count):
                    for col in range(groups):
                        old[comp, row, col] = dealt[comp, col, pl.ds(start + row, 8, stride=count), :]
            changes(load_from(old), count, groups, 0, to_mid)
        changes(load_from(mid), count, groups, count // 2, to_field)

    one_step(0, tall // 8, field_ref, change_ref)
    for index in range(1, STEPS):
        one_step(4 * index, (tall - 8 * index) // 8, field, None)

    wide = groups * LANES
    lane = iota((rows, LANES), 1)
    parts = []
    for comp in range(4):
        line = []
        for group in range(groups):
            place = place_of(lane, group, groups)
            inside = (place >= HALO) & (place < HALO + cols)
            line.append(jnp.where(inside, dealt[comp, group, HALO : HALO + rows, :], 0.0))
        parts.append(jnp.concatenate(line, axis=1))
    found = selected(jnp.concatenate(parts, axis=0), select_ref[...])
    copies = []
    for comp in range(4):
        result[comp] = ((2.0 / SCALES[comp]) / scales[comp]) * found[comp * rows : (comp + 1) * rows, :]
        copies.append(pltpu.make_async_copy(result.at[comp], out_ref.at[comp], sems.at[comp]))
        copies[-1].start()
    for copy in copies:
        copy.wait()


def local(state):
    parts, rows, cols = state.shape
    tall = rows + 2 * HALO
    groups = -(-(cols + 2 * HALO) // LANES)

    def sent(value, axis, by):
        count = lax.axis_size(axis)
        return lax.ppermute(value, axis, [(i, (i + by) % count) for i in range(count)])

    def swapped_bit(value, axis, by):
        return lax.ppermute(value, axis, [(i, i ^ by) for i in range(lax.axis_size(axis))])

    def swapped_pairs(value, axis, first):
        count = lax.axis_size(axis)
        pairs = []
        for low in range(first, count, 2):
            high = (low + 1) % count
            pairs += [(low, high), (high, low)]
        return lax.ppermute(value, axis, pairs)

    def swapped_threes(value, axis):
        count = lax.axis_size(axis)
        return lax.ppermute(value, axis, [(i, (i + 3 - 6 * (i % 2)) % count) for i in range(count)])

    edge_type = array(parts * HALO + 8, cols)
    first, second, top = pl.pallas_call(
        edge_kernel,
        out_shape=(edge_type, edge_type, array(8, LANES)),
        in_specs=[VMEM],
        out_specs=(VMEM,) * 3,
        compiler_params=params(4),
        name="edge",
    )(state)
    second = swapped_pairs(second, "gx", 1)
    first = swapped_pairs(first, "gx", 0)
    far = swapped_threes(top, "gx"), swapped_bit(top, "gx", 4)
    side_type = array(tall // 2, LANES)
    up, down, first, second, top = pl.pallas_call(
        pack_kernel,
        out_shape=(edge_type, edge_type, side_type, side_type, array(8, LANES)),
        in_specs=[VMEM] * 6,
        out_specs=(VMEM,) * 5,
        compiler_params=params(4),
        name="pack",
    )(state, second, *far, first, top)
    second = swapped_pairs(second, "gy", 1)
    first = swapped_pairs(first, "gy", 0)
    far = swapped_bit(top, "gy", 2)
    wide = groups * LANES
    cells, halo_select, back_select, top = pl.pallas_call(
        deal_kernel,
        out_shape=(
            array(parts * tall, wide),
            jax.ShapeDtypeStruct((wide - cols, wide), jnp.bfloat16),
            jax.ShapeDtypeStruct((wide, cols), jnp.bfloat16),
            array(8, LANES),
        ),
        in_specs=[VMEM] * 4,
        out_specs=(VMEM,) * 4,
        scratch_shapes=[pltpu.VMEM((parts * tall, cols), jnp.float32)],
        compiler_params=params(8),
        cost_estimate=pl.CostEstimate(flops=300_000_000, bytes_accessed=1_500_000, transcendentals=0),
        name="deal",
    )(state, up, down, top)
    top = pl.pallas_call(
        join_kernel,
        out_shape=array(8, LANES),
        in_specs=[VMEM] * 4,
        out_specs=VMEM,
        compiler_params=params(4),
        name="join",
    )(second, first, far, top)
    for axis, covered in (("gy", 4), ("gx", 8)):
        while covered < lax.axis_size(axis):
            top = jnp.maximum(top, sent(top, axis, covered))
            covered *= 2
    mate = swapped_bit(top, "gx", 1)
    dealt_type = array(parts, tall // 8, groups, 8, LANES)
    dealt = pltpu.VMEM(dealt_type.shape, jnp.float32)
    plain = pltpu.VMEM((parts, groups, tall, LANES), jnp.float32)
    field, change = pl.pallas_call(
        first_kernel,
        out_shape=(dealt_type, dealt_type),
        in_specs=[VMEM] * 4,
        out_specs=(VMEM,) * 2,
        scratch_shapes=[pltpu.VMEM((parts * tall, LANES), jnp.float32), plain],
        compiler_params=params(16),
        cost_estimate=pl.CostEstimate(flops=20_000_000, bytes_accessed=2_000_000, transcendentals=400_000),
        name="first",
    )(cells, halo_select, second, first)
    return pl.pallas_call(
        steps_kernel,
        out_shape=array(parts, rows, cols),
        in_specs=[VMEM] * 5,
        out_specs=pl.BlockSpec(memory_space=pl.ANY),
        scratch_shapes=[dealt] * 3
        + [plain, pltpu.VMEM((parts, rows, cols), jnp.float32), pltpu.SemaphoreType.DMA((parts,))],
        compiler_params=params(16),
        name="steps",
    )(field, change, back_select, top, mate)


def solution(mesh):
    in_specs = (P(None, "gx", "gy"),)
    out_specs = P(None, "gx", "gy")
    return jax.shard_map(local, mesh=mesh, in_specs=in_specs, out_specs=out_specs, check_vma=False)
```

```python
import functools
import math

import jax
import jax.numpy as jnp
from jax import lax
from jax.experimental import pallas as pl
from jax.experimental.pallas import tpu as pltpu
from jax.sharding import PartitionSpec as P

STEPS = 4
HALO = 4 * STEPS
LANES = 128
GAMMA = 1.4
COURANT = 0.35
TINY = 1e-30

VMEM = pl.BlockSpec(memory_space=pltpu.VMEM)


def params(limit):
    return pltpu.CompilerParams(vmem_limit_bytes=limit << 20)


def array(*shape):
    return jax.ShapeDtypeStruct(shape, jnp.float32)


def iota(shape, dim):
    return lax.broadcasted_iota(jnp.int32, shape, dim)


def odd(axis):
    return lax.rem(lax.axis_index(axis), 2) == 1


def edge_kernel(block_ref, first_ref, second_ref, top_ref):
    rows = block_ref.shape[1]
    density, mom_x, mom_y, energy = (block_ref[comp] for comp in range(4))
    inv = 1.0 / density
    pressure = (GAMMA - 1.0) * (energy - 0.5 * (mom_x * mom_x + mom_y * mom_y) * inv)
    speed = jnp.maximum(jnp.abs(mom_x * inv), jnp.abs(mom_y * inv)) + jnp.sqrt(GAMMA * pressure * inv)
    top = jnp.max(speed)
    is_odd = odd("gx")
    for comp in range(4):
        span = slice(comp * HALO, (comp + 1) * HALO)
        head = block_ref[comp, 0:HALO, :]
        tail = block_ref[comp, rows - HALO : rows, :]
        first_ref[span, :] = jnp.where(is_odd, head, tail)
        second_ref[span, :] = jnp.where(is_odd, tail, head)
    first_ref[4 * HALO :, :] = jnp.full((8, first_ref.shape[1]), top)
    second_ref[4 * HALO :, :] = jnp.full((8, second_ref.shape[1]), top)
    top_ref[...] = jnp.full(top_ref.shape, top)


def pack_kernel(state_ref, next_ref, three_ref, four_ref, swap_ref, own_ref, up_ref, down_ref, first_ref, second_ref, top_ref):
    rows = state_ref.shape[1]
    cols = state_ref.shape[2]
    half = rows // 2 + HALO
    lane = iota((half, LANES), 1)
    is_odd = odd("gx")
    up_ref[...] = jnp.where(is_odd, swap_ref[...], next_ref[...])
    down_ref[...] = jnp.where(is_odd, next_ref[...], swap_ref[...])
    top = jnp.maximum(jnp.maximum(own_ref[...], jnp.maximum(three_ref[...], four_ref[...])),
                      jnp.maximum(up_ref[4 * HALO :, 0:LANES], down_ref[4 * HALO :, 0:LANES]))

    def edge(low, at):
        lanes = slice(low, low + LANES)
        total = jnp.zeros((half, LANES), jnp.float32)
        for side in range(2):
            for comp in range(4):
                span = slice(comp * HALO, (comp + 1) * HALO)
                if side == 0:
                    cells = jnp.concatenate([up_ref[span, lanes], state_ref[comp, 0 : rows // 2, lanes]], axis=0)
                else:
                    cells = jnp.concatenate([state_ref[comp, rows // 2 : rows, lanes], down_ref[span, lanes]], axis=0)
                goal = side * (LANES // 2) + comp * HALO
                moved = pltpu.roll(cells, (goal - at) % LANES, axis=1)
                total = jnp.where((lane >= goal) & (lane < goal + HALO), moved, total)
        return total

    left = edge(0, 0)
    right = edge(cols - LANES, LANES - HALO)
    free = (iota((half, LANES), 0) == 0) & (lane < LANES // 2)
    under = jnp.concatenate([top] * (half // 8), axis=0)
    left = jnp.where(free, under, left)
    right = jnp.where(free, under, right)
    is_odd = odd("gy")
    first_ref[...] = jnp.where(is_odd, left, right)
    second_ref[...] = jnp.where(is_odd, right, left)
    top_ref[...] = top


def selected(values, select):
    rows = values.shape[0]
    parts = []
    for _ in range(3):
        parts.append(values.astype(jnp.bfloat16))
        values = values - parts[-1].astype(jnp.float32)
    found = jnp.dot(jnp.concatenate(parts, axis=0), select, preferred_element_type=jnp.float32)
    return (found[0:rows] + found[rows : 2 * rows]) + found[2 * rows :]


def minmod(first, second):
    low = jnp.minimum(first, second)
    high = jnp.maximum(first, second)
    return jnp.maximum(low, jnp.minimum(high, 0.0))


MOMENTUM = math.sqrt(0.5 * (GAMMA - 1.0))
SCALES = (1.0, MOMENTUM, MOMENTUM, GAMMA - 1.0)


def known(state):
    density, normal, tangent, energy = state
    inv = pl.reciprocal(density, approx=True)
    vel = normal * inv
    pressure = energy - (normal * normal + tangent * tangent) * inv
    square = jnp.maximum((GAMMA * MOMENTUM * MOMENTUM) * pressure * inv, TINY)
    return state, vel, pressure, pressure * vel, jnp.abs(vel) + square * lax.rsqrt(square)


def face(left, right):
    (left_state, left_vel, left_pressure, left_work, left_speed) = left
    (right_state, right_vel, right_pressure, right_work, right_speed) = right
    top = jnp.maximum(left_speed, right_speed)
    left_rate = left_vel + top
    right_rate = right_vel - top
    flux = [left_rate * left_state[comp] + right_rate * right_state[comp] for comp in range(4)]
    flux[1] = flux[1] + (MOMENTUM * MOMENTUM) * (left_pressure + right_pressure)
    flux[3] = flux[3] + (GAMMA - 1.0) * (left_work + right_work)
    return flux


def minus(first, second):
    return [first[comp] - second[comp] for comp in range(4)]


def rolled(tree, by, axis):
    return jax.tree.map(lambda value: pltpu.roll(value, by % value.shape[axis], axis=axis), tree)


def cell(whole, jump_before, jump_after):
    slope = [minmod(jump_before[comp], jump_after[comp]) for comp in range(4)]
    return known(minus(whole, slope)), known([whole[comp] + slope[comp] for comp in range(4)])


def row_changes(values, wholes):
    count = len(values)
    end_jump = minus(rolled(values[0], -1, 1), values[-1])
    jumps = [minus(values[at + 1], values[at]) for at in range(count - 1)] + [end_jump]
    faces, first_low, high = [], None, None
    for at in range(count):
        low, next_high = cell(wholes[at], jumps[at - 1] if at else rolled(end_jump, 1, 1), jumps[at])
        if at:
            faces.append(face(high, low))
        else:
            first_low = low
        high = next_high
    faces.append(face(high, known(rolled(first_low[0], -1, 1))))
    return [minus(faces[at], faces[at - 1] if at else rolled(faces[-1], 1, 1)) for at in range(count)]


class Column:
    def __init__(self, count, begin, here, after):
        self.count, self.begin = count, begin
        self.jump = self.first_jump = minus(after, here)
        self.first_low = self.first_flux = self.last_flux = self.high = None

    def feed(self, row, here, whole, after):
        next_row = (row + 1) % self.count
        if after is None:
            next_jump = self.first_jump
        else:
            next_jump = minus(rolled(after, -1, 0) if next_row == 0 else after, here)
        jump = rolled(self.jump, 1, 0) if row == 0 else self.jump
        low, high = cell(whole, jump, next_jump)
        done = []
        if self.first_low is None:
            self.first_low = low
        else:
            flux = face(known(rolled(self.high[0], 1, 0)) if row == 0 else self.high, low)
            if self.last_flux is None:
                self.first_flux = flux
            else:
                seen = rolled(flux, -1, 0) if row == 0 else flux
                done.append(((row - 1) % self.count, minus(seen, self.last_flux)))
            self.last_flux = flux
        self.high, self.jump = high, next_jump
        if after is None:
            flux = face(high, self.first_low)
            done.append((row, minus(flux, self.last_flux)))
            done.append(((row + 1) % self.count, minus(self.first_flux, flux)))
        return done


Y_ORDER = (0, 2, 1, 3)


def changes(load, rows, cols, begin, store):
    along_y = {}
    values = {at: [load((begin + at) % rows, col) for col in range(cols)] for at in range(2)}
    columns = [Column(rows, begin, values[0][col], values[1][col]) for col in range(cols)]
    for at in range(1, rows + 1):
        row = (begin + at) % rows
        here = values.pop(at)
        if at < rows:
            values[at + 1] = [load((row + 1) % rows, col) for col in range(cols)]
        whole = [[part + part for part in value] for value in here]
        ready = []
        for col in range(cols):
            after = values[at + 1][col] if at < rows else None
            ready += [(col, *item) for item in columns[col].feed(row, here[col], whole[col], after)]
        along_y[row] = row_changes(*([[part[comp] for comp in Y_ORDER] for part in value] for value in (here, whole)))
        for col, done, parts in ready:
            other = along_y[done][col]
            store(done, col, [parts[comp] + other[Y_ORDER[comp]] for comp in range(4)])


def place_of(lane, group, groups):
    return groups * lane + group


def deal_kernel(state_ref, up_ref, down_ref, own_ref, dealt_ref, halo_select_ref, back_select_ref, top_ref, plain):
    top_ref[...] = own_ref[...]
    rows, cols = state_ref.shape[1:]
    tall = rows + 2 * HALO
    wide = dealt_ref.shape[1]
    groups = wide // LANES
    for comp in range(4):
        span = slice(comp * HALO, (comp + 1) * HALO)
        low = comp * tall
        plain[low : low + HALO, :] = up_ref[span, :]
        plain[low + HALO : low + HALO + rows, :] = state_ref[comp]
        plain[low + HALO + rows : low + tall, :] = down_ref[span, :]
    source = iota((wide, wide), 0)
    goal = iota((wide, wide), 1)
    place = place_of(goal % LANES, goal // LANES, groups)
    place = jnp.where(place < cols + 2 * HALO, (place + wide - HALO) % wide, 0)
    select = jnp.where(source == place, 1.0, 0.0).astype(jnp.bfloat16)
    dealt_ref[...] = selected(plain[...], select[0:cols])
    halo_select_ref[...] = select[cols:]
    source = iota((wide, cols), 0)
    goal = iota((wide, cols), 1)
    back = place_of(source % LANES, source // LANES, groups) == goal + HALO
    back_select_ref[...] = jnp.where(back, 1.0, 0.0).astype(jnp.bfloat16)


def first_kernel(cells_ref, select_ref, next_ref, swap_ref, field_ref, change_ref, plain, dealt):
    half = next_ref.shape[0]
    tall = 2 * half
    groups = cells_ref.shape[1] // LANES
    lane = iota((half, LANES), 1)
    is_odd = odd("gy")
    from_swap = swap_ref[...]
    from_next = next_ref[...]
    from_before = jnp.where(is_odd, from_swap, from_next)
    from_after = jnp.where(is_odd, from_next, from_swap)
    for side in range(2):
        for comp in range(4):
            at = side * (LANES // 2) + comp * HALO
            left = pltpu.roll(from_before, (LANES - HALO - at) % LANES, axis=1)
            right = pltpu.roll(from_after, (-at) % LANES, axis=1)
            low = comp * tall + side * half
            plain[low : low + half, :] = jnp.where(lane < LANES // 2, right, left)
    found = cells_ref[...] + selected(plain[...], select_ref[...])
    for comp in range(4):
        for group in range(groups):
            cells = found[comp * tall : (comp + 1) * tall, group * LANES : (group + 1) * LANES]
            dealt[comp, group] = (0.5 * SCALES[comp]) * cells
    count = tall // 8
    for comp in range(4):
        for row in range(count):
            for group in range(groups):
                field_ref[comp, row, group] = dealt[comp, group, pl.ds(row, 8, stride=count), :]

    def store(row, col, parts):
        for comp in range(4):
            change_ref[comp, row, col] = parts[comp]

    def load(row, col):
        return [field_ref[comp, row, col] for comp in range(4)]

    changes(load, count, groups, 0, store)


def steps_kernel(field_ref, change_ref, select_ref, own_ref, mate_ref, out_ref, field, base, mid, dealt, result, sems):
    rows, cols = out_ref.shape[1:]
    tall = rows + 2 * HALO
    groups = field_ref.shape[2]
    scale = (0.125 * COURANT / MOMENTUM) / jnp.max(jnp.maximum(own_ref[...], mate_ref[...]))
    scales = (1.0, scale, scale, scale * scale)

    def one_step(start, count, old, first_changes):
        def to_mid(row, col, parts):
            for comp in range(4):
                cells, move = old[comp, row, col], parts[comp]
                if first_changes is not None:
                    cells, move = scales[comp] * cells, (scales[comp] * scale) * move
                moved = cells - move
                base[comp, row, col] = moved
                mid[comp, row, col] = moved - move

        def to_field(row, col, parts):
            for comp in range(4):
                new = base[comp, row, col] - parts[comp]
                dealt[comp, col, pl.ds(start + row, 8, stride=count), :] = new

        def load_from(ref):
            return lambda row, col: [ref[comp, row, col] for comp in range(4)]

        if first_changes is not None:
            for row in range(count):
                for col in range(groups):
                    to_mid(row, col, [first_changes[comp, row, col] for comp in range(4)])
        else:
            for comp in range(4):
                for row in range(count):
                    for col in range(groups):
                        old[comp, row, col] = dealt[comp, col, pl.ds(start + row, 8, stride=count), :]
            changes(load_from(old), count, groups, 0, to_mid)
        changes(load_from(mid), count, groups, count // 2, to_field)

    one_step(0, tall // 8, field_ref, change_ref)
    for index in range(1, STEPS):
        one_step(4 * index, (tall - 8 * index) // 8, field, None)

    wide = groups * LANES
    lane = iota((rows, LANES), 1)
    parts = []
    for comp in range(4):
        line = []
        for group in range(groups):
            place = place_of(lane, group, groups)
            inside = (place >= HALO) & (place < HALO + cols)
            line.append(jnp.where(inside, dealt[comp, group, HALO : HALO + rows, :], 0.0))
        parts.append(jnp.concatenate(line, axis=1))
    found = selected(jnp.concatenate(parts, axis=0), select_ref[...])
    copies = []
    for comp in range(4):
        result[comp] = ((2.0 / SCALES[comp]) / scales[comp]) * found[comp * rows : (comp + 1) * rows, :]
        copies.append(pltpu.make_async_copy(result.at[comp], out_ref.at[comp], sems.at[comp]))
        copies[-1].start()
    for copy in copies:
        copy.wait()


def local(state):
    parts, rows, cols = state.shape
    tall = rows + 2 * HALO
    groups = -(-(cols + 2 * HALO) // LANES)

    def sent(value, axis, by):
        count = lax.axis_size(axis)
        return lax.ppermute(value, axis, [(i, (i + by) % count) for i in range(count)])

    def swapped_bit(value, axis, by):
        return lax.ppermute(value, axis, [(i, i ^ by) for i in range(lax.axis_size(axis))])

    def swapped_pairs(value, axis, first):
        count = lax.axis_size(axis)
        pairs = []
        for low in range(first, count, 2):
            high = (low + 1) % count
            pairs += [(low, high), (high, low)]
        return lax.ppermute(value, axis, pairs)

    def swapped_threes(value, axis):
        count = lax.axis_size(axis)
        return lax.ppermute(value, axis, [(i, (i + 3 - 6 * (i % 2)) % count) for i in range(count)])

    edge_type = array(parts * HALO + 8, cols)
    first, second, top = pl.pallas_call(
        edge_kernel,
        out_shape=(edge_type, edge_type, array(8, LANES)),
        in_specs=[VMEM],
        out_specs=(VMEM,) * 3,
        compiler_params=params(4),
        name="edge",
    )(state)
    second = swapped_pairs(second, "gx", 1)
    first = swapped_pairs(first, "gx", 0)
    far = swapped_threes(top, "gx"), swapped_bit(top, "gx", 4)
    side_type = array(tall // 2, LANES)
    up, down, first, second, top = pl.pallas_call(
        pack_kernel,
        out_shape=(edge_type, edge_type, side_type, side_type, array(8, LANES)),
        in_specs=[VMEM] * 6,
        out_specs=(VMEM,) * 5,
        compiler_params=params(4),
        name="pack",
    )(state, second, *far, first, top)
    second = swapped_pairs(second, "gy", 1)
    first = swapped_pairs(first, "gy", 0)
    far = swapped_bit(top, "gy", 2)
    wide = groups * LANES
    cells, halo_select, back_select, top = pl.pallas_call(
        deal_kernel,
        out_shape=(
            array(parts * tall, wide),
            jax.ShapeDtypeStruct((wide - cols, wide), jnp.bfloat16),
            jax.ShapeDtypeStruct((wide, cols), jnp.bfloat16),
            array(8, LANES),
        ),
        in_specs=[VMEM] * 4,
        out_specs=(VMEM,) * 4,
        scratch_shapes=[pltpu.VMEM((parts * tall, cols), jnp.float32)],
        compiler_params=params(8),
        cost_estimate=pl.CostEstimate(flops=300_000_000, bytes_accessed=1_500_000, transcendentals=0),
        name="deal",
    )(state, up, down, top)
    carried = (iota((8, LANES), 0) == 0) & (iota((8, LANES), 1) < LANES // 2)
    top = jnp.maximum(jnp.maximum(top, far), jnp.where(carried, jnp.maximum(first[:8], second[:8]), 0.0))
    for axis, covered in (("gy", 4), ("gx", 8)):
        while covered < lax.axis_size(axis):
            top = jnp.maximum(top, sent(top, axis, covered))
            covered *= 2
    mate = swapped_bit(top, "gx", 1)
    dealt_type = array(parts, tall // 8, groups, 8, LANES)
    dealt = pltpu.VMEM(dealt_type.shape, jnp.float32)
    plain = pltpu.VMEM((parts, groups, tall, LANES), jnp.float32)
    field, change = pl.pallas_call(
        first_kernel,
        out_shape=(dealt_type, dealt_type),
        in_specs=[VMEM] * 4,
        out_specs=(VMEM,) * 2,
        scratch_shapes=[pltpu.VMEM((parts * tall, LANES), jnp.float32), plain],
        compiler_params=params(16),
        cost_estimate=pl.CostEstimate(flops=20_000_000, bytes_accessed=2_000_000, transcendentals=400_000),
        name="first",
    )(cells, halo_select, second, first)
    return pl.pallas_call(
        steps_kernel,
        out_shape=array(parts, rows, cols),
        in_specs=[VMEM] * 5,
        out_specs=pl.BlockSpec(memory_space=pl.ANY),
        scratch_shapes=[dealt] * 3
        + [plain, pltpu.VMEM((parts, rows, cols), jnp.float32), pltpu.SemaphoreType.DMA((parts,))],
        compiler_params=params(16),
        name="steps",
    )(field, change, back_select, top, mate)


def solution(mesh):
    in_specs = (P(None, "gx", "gy"),)
    out_specs = P(None, "gx", "gy")
    return jax.shard_map(local, mesh=mesh, in_specs=in_specs, out_specs=out_specs, check_vma=False)
```

```python
import functools
import math

import jax
import jax.numpy as jnp
from jax import lax
from jax.experimental import pallas as pl
from jax.experimental.pallas import tpu as pltpu
from jax.sharding import PartitionSpec as P

STEPS = 4
HALO = 4 * STEPS
LANES = 128
GAMMA = 1.4
COURANT = 0.35
TINY = 1e-30

VMEM = pl.BlockSpec(memory_space=pltpu.VMEM)


def params(limit):
    return pltpu.CompilerParams(vmem_limit_bytes=limit << 20)


def array(*shape):
    return jax.ShapeDtypeStruct(shape, jnp.float32)


def iota(shape, dim):
    return lax.broadcasted_iota(jnp.int32, shape, dim)


def odd(axis):
    return lax.rem(lax.axis_index(axis), 2) == 1


def edge_kernel(block_ref, first_ref, second_ref, top_ref):
    rows = block_ref.shape[1]
    density, mom_x, mom_y, energy = (block_ref[comp] for comp in range(4))
    inv = 1.0 / density
    pressure = (GAMMA - 1.0) * (energy - 0.5 * (mom_x * mom_x + mom_y * mom_y) * inv)
    speed = jnp.maximum(jnp.abs(mom_x * inv), jnp.abs(mom_y * inv)) + jnp.sqrt(GAMMA * pressure * inv)
    top = jnp.max(speed)
    is_odd = odd("gx")
    for comp in range(4):
        span = slice(comp * HALO, (comp + 1) * HALO)
        head = block_ref[comp, 0:HALO, :]
        tail = block_ref[comp, rows - HALO : rows, :]
        first_ref[span, :] = jnp.where(is_odd, head, tail)
        second_ref[span, :] = jnp.where(is_odd, tail, head)
    first_ref[4 * HALO :, :] = jnp.full((8, first_ref.shape[1]), top)
    second_ref[4 * HALO :, :] = jnp.full((8, second_ref.shape[1]), top)
    top_ref[...] = jnp.full(top_ref.shape, top)


def pack_kernel(state_ref, next_ref, three_ref, four_ref, swap_ref, own_ref, up_ref, down_ref, first_ref, second_ref, top_ref):
    rows = state_ref.shape[1]
    cols = state_ref.shape[2]
    half = rows // 2 + HALO
    lane = iota((half, LANES), 1)
    is_odd = odd("gx")
    up_ref[...] = jnp.where(is_odd, swap_ref[...], next_ref[...])
    down_ref[...] = jnp.where(is_odd, next_ref[...], swap_ref[...])
    top = jnp.maximum(jnp.maximum(own_ref[...], jnp.maximum(three_ref[...], four_ref[...])),
                      jnp.maximum(up_ref[4 * HALO :, 0:LANES], down_ref[4 * HALO :, 0:LANES]))

    def edge(low, at):
        lanes = slice(low, low + LANES)
        total = jnp.zeros((half, LANES), jnp.float32)
        for side in range(2):
            for comp in range(4):
                span = slice(comp * HALO, (comp + 1) * HALO)
                if side == 0:
                    cells = jnp.concatenate([up_ref[span, lanes], state_ref[comp, 0 : rows // 2, lanes]], axis=0)
                else:
                    cells = jnp.concatenate([state_ref[comp, rows // 2 : rows, lanes], down_ref[span, lanes]], axis=0)
                goal = side * (LANES // 2) + comp * HALO
                moved = pltpu.roll(cells, (goal - at) % LANES, axis=1)
                total = jnp.where((lane >= goal) & (lane < goal + HALO), moved, total)
        return total

    left = edge(0, 0)
    right = edge(cols - LANES, LANES - HALO)
    free = (iota((half, LANES), 0) == 0) & (lane < LANES // 2)
    under = jnp.concatenate([top] * (half // 8), axis=0)
    left = jnp.where(free, under, left)
    right = jnp.where(free, under, right)
    is_odd = odd("gy")
    first_ref[...] = jnp.where(is_odd, left, right)
    second_ref[...] = jnp.where(is_odd, right, left)
    top_ref[...] = top


def selected(values, select):
    rows = values.shape[0]
    parts = []
    for _ in range(3):
        parts.append(values.astype(jnp.bfloat16))
        values = values - parts[-1].astype(jnp.float32)
    found = jnp.dot(jnp.concatenate(parts, axis=0), select, preferred_element_type=jnp.float32)
    return (found[0:rows] + found[rows : 2 * rows]) + found[2 * rows :]


def minmod(first, second):
    low = jnp.minimum(first, second)
    high = jnp.maximum(first, second)
    return jnp.maximum(low, jnp.minimum(high, 0.0))


MOMENTUM = math.sqrt(0.5 * (GAMMA - 1.0))
SCALES = (1.0, MOMENTUM, MOMENTUM, GAMMA - 1.0)


def known(state):
    density, normal, tangent, energy = state
    inv = pl.reciprocal(density, approx=True)
    vel = normal * inv
    pressure = energy - (normal * normal + tangent * tangent) * inv
    square = jnp.maximum((GAMMA * MOMENTUM * MOMENTUM) * pressure * inv, TINY)
    return state, vel, pressure, pressure * vel, jnp.abs(vel) + square * lax.rsqrt(square)


def face(left, right):
    (left_state, left_vel, left_pressure, left_work, left_speed) = left
    (right_state, right_vel, right_pressure, right_work, right_speed) = right
    top = jnp.maximum(left_speed, right_speed)
    left_rate = left_vel + top
    right_rate = right_vel - top
    flux = [left_rate * left_state[comp] + right_rate * right_state[comp] for comp in range(4)]
    flux[1] = flux[1] + (MOMENTUM * MOMENTUM) * (left_pressure + right_pressure)
    flux[3] = flux[3] + (GAMMA - 1.0) * (left_work + right_work)
    return flux


def minus(first, second):
    return [first[comp] - second[comp] for comp in range(4)]


def rolled(tree, by, axis):
    return jax.tree.map(lambda value: pltpu.roll(value, by % value.shape[axis], axis=axis), tree)


def cell(whole, jump_before, jump_after):
    slope = [minmod(jump_before[comp], jump_after[comp]) for comp in range(4)]
    return known(minus(whole, slope)), known([whole[comp] + slope[comp] for comp in range(4)])


def row_changes(values, wholes):
    count = len(values)
    end_jump = minus(rolled(values[0], -1, 1), values[-1])
    jumps = [minus(values[at + 1], values[at]) for at in range(count - 1)] + [end_jump]
    faces, first_low, high = [], None, None
    for at in range(count):
        low, next_high = cell(wholes[at], jumps[at - 1] if at else rolled(end_jump, 1, 1), jumps[at])
        if at:
            faces.append(face(high, low))
        else:
            first_low = low
        high = next_high
    faces.append(face(high, known(rolled(first_low[0], -1, 1))))
    return [minus(faces[at], faces[at - 1] if at else rolled(faces[-1], 1, 1)) for at in range(count)]


class Column:
    def __init__(self, count, begin, here, after):
        self.count, self.begin = count, begin
        self.jump = self.first_jump = minus(after, here)
        self.first_low = self.first_flux = self.last_flux = self.high = None

    def feed(self, row, here, whole, after):
        next_row = (row + 1) % self.count
        if after is None:
            next_jump = self.first_jump
        else:
            next_jump = minus(rolled(after, -1, 0) if next_row == 0 else after, here)
        jump = rolled(self.jump, 1, 0) if row == 0 else self.jump
        low, high = cell(whole, jump, next_jump)
        done = []
        if self.first_low is None:
            self.first_low = low
        else:
            flux = face(known(rolled(self.high[0], 1, 0)) if row == 0 else self.high, low)
            if self.last_flux is None:
                self.first_flux = flux
            else:
                seen = rolled(flux, -1, 0) if row == 0 else flux
                done.append(((row - 1) % self.count, minus(seen, self.last_flux)))
            self.last_flux = flux
        self.high, self.jump = high, next_jump
        if after is None:
            flux = face(high, self.first_low)
            done.append((row, minus(flux, self.last_flux)))
            done.append(((row + 1) % self.count, minus(self.first_flux, flux)))
        return done


Y_ORDER = (0, 2, 1, 3)


def changes(load, rows, cols, begin, store):
    along_y = {}
    values = {at: [load((begin + at) % rows, col) for col in range(cols)] for at in range(2)}
    columns = [Column(rows, begin, values[0][col], values[1][col]) for col in range(cols)]
    for at in range(1, rows + 1):
        row = (begin + at) % rows
        here = values.pop(at)
        if at < rows:
            values[at + 1] = [load((row + 1) % rows, col) for col in range(cols)]
        whole = [[part + part for part in value] for value in here]
        ready = []
        for col in range(cols):
            after = values[at + 1][col] if at < rows else None
            ready += [(col, *item) for item in columns[col].feed(row, here[col], whole[col], after)]
        along_y[row] = row_changes(*([[part[comp] for comp in Y_ORDER] for part in value] for value in (here, whole)))
        for col, done, parts in ready:
            other = along_y[done][col]
            store(done, col, [parts[comp] + other[Y_ORDER[comp]] for comp in range(4)])


def place_of(lane, group, groups):
    return groups * lane + group


def deal_kernel(state_ref, up_ref, down_ref, own_ref, dealt_ref, halo_select_ref, back_select_ref, top_ref, plain):
    top_ref[...] = own_ref[...]
    rows, cols = state_ref.shape[1:]
    tall = rows + 2 * HALO
    wide = dealt_ref.shape[1]
    groups = wide // LANES
    for comp in range(4):
        span = slice(comp * HALO, (comp + 1) * HALO)
        low = comp * tall
        plain[low : low + HALO, :] = up_ref[span, :]
        plain[low + HALO : low + HALO + rows, :] = state_ref[comp]
        plain[low + HALO + rows : low + tall, :] = down_ref[span, :]
    source = iota((wide, wide), 0)
    goal = iota((wide, wide), 1)
    place = place_of(goal % LANES, goal // LANES, groups)
    place = jnp.where(place < cols + 2 * HALO, (place + wide - HALO) % wide, 0)
    select = jnp.where(source == place, 1.0, 0.0).astype(jnp.bfloat16)
    dealt_ref[...] = selected(plain[...], select[0:cols])
    halo_select_ref[...] = select[cols:]
    source = iota((wide, cols), 0)
    goal = iota((wide, cols), 1)
    back = place_of(source % LANES, source // LANES, groups) == goal + HALO
    back_select_ref[...] = jnp.where(back, 1.0, 0.0).astype(jnp.bfloat16)


def join_kernel(next_ref, swap_ref, far_ref, own_ref, top_ref):
    speeds = jnp.maximum(next_ref[0:8, :], swap_ref[0:8, :])
    carried = (iota((8, LANES), 0) == 0) & (iota((8, LANES), 1) < LANES // 2)
    known_here = jnp.maximum(own_ref[...], far_ref[...])
    top_ref[...] = jnp.full((8, LANES), jnp.max(jnp.where(carried, speeds, known_here)))


def first_kernel(cells_ref, select_ref, next_ref, swap_ref, field_ref, change_ref, plain, dealt):
    half = next_ref.shape[0]
    tall = 2 * half
    groups = cells_ref.shape[1] // LANES
    lane = iota((half, LANES), 1)
    is_odd = odd("gy")
    from_swap = swap_ref[...]
    from_next = next_ref[...]
    from_before = jnp.where(is_odd, from_swap, from_next)
    from_after = jnp.where(is_odd, from_next, from_swap)
    for side in range(2):
        for comp in range(4):
            at = side * (LANES // 2) + comp * HALO
            left = pltpu.roll(from_before, (LANES - HALO - at) % LANES, axis=1)
            right = pltpu.roll(from_after, (-at) % LANES, axis=1)
            low = comp * tall + side * half
            plain[low : low + half, :] = jnp.where(lane < LANES // 2, right, left)
    found = cells_ref[...] + selected(plain[...], select_ref[...])
    for comp in range(4):
        for group in range(groups):
            cells = found[comp * tall : (comp + 1) * tall, group * LANES : (group + 1) * LANES]
            dealt[comp, group] = (0.5 * SCALES[comp]) * cells
    count = tall // 8
    for comp in range(4):
        for row in range(count):
            for group in range(groups):
                field_ref[comp, row, group] = dealt[comp, group, pl.ds(row, 8, stride=count), :]

    def store(row, col, parts):
        for comp in range(4):
            change_ref[comp, row, col] = parts[comp]

    def load(row, col):
        return [field_ref[comp, row, col] for comp in range(4)]

    changes(load, count, groups, 0, store)


def steps_kernel(field_ref, change_ref, select_ref, own_ref, mate_ref, out_ref, field, base, mid, dealt, plain, result, sems):
    rows, cols = out_ref.shape[1:]
    tall = rows + 2 * HALO
    groups = field_ref.shape[2]
    scale = (0.125 * COURANT / MOMENTUM) / jnp.max(jnp.maximum(own_ref[...], mate_ref[...]))
    scales = (1.0, scale, scale, scale * scale)

    def one_step(start, count, old, first_changes):
        def to_mid(row, col, parts):
            for comp in range(4):
                cells, move = old[comp, row, col], parts[comp]
                if first_changes is not None:
                    cells, move = scales[comp] * cells, (scales[comp] * scale) * move
                moved = cells - move
                base[comp, row, col] = moved
                mid[comp, row, col] = moved - move

        def to_field(row, col, parts):
            new = [base[comp, row, col] - parts[comp] for comp in range(4)]
            if start + 4 < 4 * STEPS:
                for comp in range(4):
                    dealt[comp, col, pl.ds(start + row, 8, stride=count), :] = new[comp]
                return
            place = place_of(iota((8, LANES), 1), col, groups)
            inside = (place >= HALO) & (place < HALO + cols)
            ready.setdefault(row, {})[col] = [jnp.where(inside, part, 0.0) for part in new]
            if len(ready[row]) == groups:
                lines = [jnp.concatenate([ready[row][at][comp] for at in range(groups)], axis=1) for comp in range(4)]
                found = selected(jnp.concatenate(lines, axis=0), select_ref[...])
                for comp in range(4):
                    for tile in range(cols // LANES):
                        cells = found[comp * 8 : (comp + 1) * 8, tile * LANES : (tile + 1) * LANES]
                        plain[comp, tile, pl.ds(row, 8, stride=count), :] = cells

        def load_from(ref):
            return lambda row, col: [ref[comp, row, col] for comp in range(4)]

        if first_changes is not None:
            for row in range(count):
                for col in range(groups):
                    to_mid(row, col, [first_changes[comp, row, col] for comp in range(4)])
        else:
            for comp in range(4):
                for row in range(count):
                    for col in range(groups):
                        old[comp, row, col] = dealt[comp, col, pl.ds(start + row, 8, stride=count), :]
            changes(load_from(old), count, groups, 0, to_mid)
        changes(load_from(mid), count, groups, count // 2, to_field)

    ready = {}
    one_step(0, tall // 8, field_ref, change_ref)
    for index in range(1, STEPS):
        one_step(4 * index, (tall - 8 * index) // 8, field, None)

    copies = []
    skip = HALO - 4 * (STEPS - 1)
    for comp in range(4):
        for tile in range(cols // LANES):
            cells = plain[comp, tile, skip : skip + rows, :]
            result[comp, :, tile * LANES : (tile + 1) * LANES] = ((2.0 / SCALES[comp]) / scales[comp]) * cells
        copies.append(pltpu.make_async_copy(result.at[comp], out_ref.at[comp], sems.at[comp]))
        copies[-1].start()
    for copy in copies:
        copy.wait()


def local(state):
    parts, rows, cols = state.shape
    tall = rows + 2 * HALO
    groups = -(-(cols + 2 * HALO) // LANES)

    def sent(value, axis, by):
        count = lax.axis_size(axis)
        return lax.ppermute(value, axis, [(i, (i + by) % count) for i in range(count)])

    def swapped_bit(value, axis, by):
        return lax.ppermute(value, axis, [(i, i ^ by) for i in range(lax.axis_size(axis))])

    def swapped_pairs(value, axis, first):
        count = lax.axis_size(axis)
        pairs = []
        for low in range(first, count, 2):
            high = (low + 1) % count
            pairs += [(low, high), (high, low)]
        return lax.ppermute(value, axis, pairs)

    def swapped_threes(value, axis):
        count = lax.axis_size(axis)
        return lax.ppermute(value, axis, [(i, (i + 3 - 6 * (i % 2)) % count) for i in range(count)])

    edge_type = array(parts * HALO + 8, cols)
    first, second, top = pl.pallas_call(
        edge_kernel,
        out_shape=(edge_type, edge_type, array(8, LANES)),
        in_specs=[VMEM],
        out_specs=(VMEM,) * 3,
        compiler_params=params(4),
        name="edge",
    )(state)
    second = swapped_pairs(second, "gx", 1)
    first = swapped_pairs(first, "gx", 0)
    far = swapped_threes(top, "gx"), swapped_bit(top, "gx", 4)
    side_type = array(tall // 2, LANES)
    up, down, first, second, top = pl.pallas_call(
        pack_kernel,
        out_shape=(edge_type, edge_type, side_type, side_type, array(8, LANES)),
        in_specs=[VMEM] * 6,
        out_specs=(VMEM,) * 5,
        compiler_params=params(4),
        name="pack",
    )(state, second, *far, first, top)
    second = swapped_pairs(second, "gy", 1)
    first = swapped_pairs(first, "gy", 0)
    far = swapped_bit(top, "gy", 2)
    wide = groups * LANES
    cells, halo_select, back_select, top = pl.pallas_call(
        deal_kernel,
        out_shape=(
            array(parts * tall, wide),
            jax.ShapeDtypeStruct((wide - cols, wide), jnp.bfloat16),
            jax.ShapeDtypeStruct((wide, cols), jnp.bfloat16),
            array(8, LANES),
        ),
        in_specs=[VMEM] * 4,
        out_specs=(VMEM,) * 4,
        scratch_shapes=[pltpu.VMEM((parts * tall, cols), jnp.float32)],
        compiler_params=params(8),
        cost_estimate=pl.CostEstimate(flops=300_000_000, bytes_accessed=1_500_000, transcendentals=0),
        name="deal",
    )(state, up, down, top)
    top = pl.pallas_call(
        join_kernel,
        out_shape=array(8, LANES),
        in_specs=[VMEM] * 4,
        out_specs=VMEM,
        compiler_params=params(4),
        name="join",
    )(second, first, far, top)
    for axis, covered in (("gy", 4), ("gx", 8)):
        while covered < lax.axis_size(axis):
            top = jnp.maximum(top, sent(top, axis, covered))
            covered *= 2
    mate = swapped_bit(top, "gx", 1)
    dealt_type = array(parts, tall // 8, groups, 8, LANES)
    dealt = pltpu.VMEM(dealt_type.shape, jnp.float32)
    plain = pltpu.VMEM((parts, groups, tall, LANES), jnp.float32)
    field, change = pl.pallas_call(
        first_kernel,
        out_shape=(dealt_type, dealt_type),
        in_specs=[VMEM] * 4,
        out_specs=(VMEM,) * 2,
        scratch_shapes=[pltpu.VMEM((parts * tall, LANES), jnp.float32), plain],
        compiler_params=params(16),
        cost_estimate=pl.CostEstimate(flops=20_000_000, bytes_accessed=2_000_000, transcendentals=400_000),
        name="first",
    )(cells, halo_select, second, first)
    return pl.pallas_call(
        steps_kernel,
        out_shape=array(parts, rows, cols),
        in_specs=[VMEM] * 5,
        out_specs=pl.BlockSpec(memory_space=pl.ANY),
        scratch_shapes=[dealt] * 3
        + [plain, plain, pltpu.VMEM((parts, rows, cols), jnp.float32), pltpu.SemaphoreType.DMA((parts,))],
        compiler_params=params(16),
        name="steps",
    )(field, change, back_select, top, mate)


def solution(mesh):
    in_specs = (P(None, "gx", "gy"),)
    out_specs = P(None, "gx", "gy")
    return jax.shard_map(local, mesh=mesh, in_specs=in_specs, out_specs=out_specs, check_vma=False)
```

```python
import functools
import math

import jax
import jax.numpy as jnp
from jax import lax
from jax.experimental import pallas as pl
from jax.experimental.pallas import tpu as pltpu
from jax.sharding import PartitionSpec as P

STEPS = 4
HALO = 4 * STEPS
LANES = 128
GAMMA = 1.4
COURANT = 0.35
TINY = 1e-30

VMEM = pl.BlockSpec(memory_space=pltpu.VMEM)


def params(limit):
    return pltpu.CompilerParams(vmem_limit_bytes=limit << 20)


def array(*shape):
    return jax.ShapeDtypeStruct(shape, jnp.float32)


def iota(shape, dim):
    return lax.broadcasted_iota(jnp.int32, shape, dim)


def odd(axis):
    return lax.rem(lax.axis_index(axis), 2) == 1


def edge_kernel(block_ref, first_ref, second_ref, top_ref):
    rows = block_ref.shape[1]
    density, mom_x, mom_y, energy = (block_ref[comp] for comp in range(4))
    inv = 1.0 / density
    pressure = (GAMMA - 1.0) * (energy - 0.5 * (mom_x * mom_x + mom_y * mom_y) * inv)
    speed = jnp.maximum(jnp.abs(mom_x * inv), jnp.abs(mom_y * inv)) + jnp.sqrt(GAMMA * pressure * inv)
    top = jnp.max(speed)
    is_odd = odd("gx")
    for comp in range(4):
        span = slice(comp * HALO, (comp + 1) * HALO)
        head = block_ref[comp, 0:HALO, :]
        tail = block_ref[comp, rows - HALO : rows, :]
        first_ref[span, :] = jnp.where(is_odd, head, tail)
        second_ref[span, :] = jnp.where(is_odd, tail, head)
    first_ref[4 * HALO :, :] = jnp.full((8, first_ref.shape[1]), top)
    second_ref[4 * HALO :, :] = jnp.full((8, second_ref.shape[1]), top)
    top_ref[...] = jnp.full(top_ref.shape, top)


def pack_kernel(state_ref, next_ref, three_ref, four_ref, swap_ref, own_ref, up_ref, down_ref, first_ref, second_ref, top_ref):
    rows = state_ref.shape[1]
    cols = state_ref.shape[2]
    half = rows // 2 + HALO
    lane = iota((half, LANES), 1)
    is_odd = odd("gx")
    up_ref[...] = jnp.where(is_odd, swap_ref[...], next_ref[...])
    down_ref[...] = jnp.where(is_odd, next_ref[...], swap_ref[...])
    top = jnp.maximum(jnp.maximum(own_ref[...], jnp.maximum(three_ref[...], four_ref[...])),
                      jnp.maximum(up_ref[4 * HALO :, 0:LANES], down_ref[4 * HALO :, 0:LANES]))

    def edge(low, at):
        lanes = slice(low, low + LANES)
        total = jnp.zeros((half, LANES), jnp.float32)
        for side in range(2):
            for comp in range(4):
                span = slice(comp * HALO, (comp + 1) * HALO)
                if side == 0:
                    cells = jnp.concatenate([up_ref[span, lanes], state_ref[comp, 0 : rows // 2, lanes]], axis=0)
                else:
                    cells = jnp.concatenate([state_ref[comp, rows // 2 : rows, lanes], down_ref[span, lanes]], axis=0)
                goal = side * (LANES // 2) + comp * HALO
                moved = pltpu.roll(cells, (goal - at) % LANES, axis=1)
                total = jnp.where((lane >= goal) & (lane < goal + HALO), moved, total)
        return total

    left = edge(0, 0)
    right = edge(cols - LANES, LANES - HALO)
    free = (iota((half, LANES), 0) == 0) & (lane < LANES // 2)
    under = jnp.concatenate([top] * (half // 8), axis=0)
    left = jnp.where(free, under, left)
    right = jnp.where(free, under, right)
    is_odd = odd("gy")
    first_ref[...] = jnp.where(is_odd, left, right)
    second_ref[...] = jnp.where(is_odd, right, left)
    top_ref[...] = top


def selected(values, select):
    rows = values.shape[0]
    parts = []
    for _ in range(3):
        parts.append(values.astype(jnp.bfloat16))
        values = values - parts[-1].astype(jnp.float32)
    found = jnp.dot(jnp.concatenate(parts, axis=0), select, preferred_element_type=jnp.float32)
    return (found[0:rows] + found[rows : 2 * rows]) + found[2 * rows :]


def minmod(first, second):
    low = jnp.minimum(first, second)
    high = jnp.maximum(first, second)
    return jnp.maximum(low, jnp.minimum(high, 0.0))


MOMENTUM = math.sqrt(0.5 * (GAMMA - 1.0))
SCALES = (1.0, MOMENTUM, MOMENTUM, GAMMA - 1.0)


def known(state):
    density, normal, tangent, energy = state
    inv = pl.reciprocal(density, approx=True)
    vel = normal * inv
    pressure = energy - (normal * normal + tangent * tangent) * inv
    square = jnp.maximum((GAMMA * MOMENTUM * MOMENTUM) * pressure * inv, TINY)
    return state, vel, pressure, pressure * vel, jnp.abs(vel) + square * lax.rsqrt(square)


def face(left, right):
    (left_state, left_vel, left_pressure, left_work, left_speed) = left
    (right_state, right_vel, right_pressure, right_work, right_speed) = right
    top = jnp.maximum(left_speed, right_speed)
    left_rate = left_vel + top
    right_rate = right_vel - top
    flux = [left_rate * left_state[comp] + right_rate * right_state[comp] for comp in range(4)]
    flux[1] = flux[1] + (MOMENTUM * MOMENTUM) * (left_pressure + right_pressure)
    flux[3] = flux[3] + (GAMMA - 1.0) * (left_work + right_work)
    return flux


def minus(first, second):
    return [first[comp] - second[comp] for comp in range(4)]


def rolled(tree, by, axis):
    return jax.tree.map(lambda value: pltpu.roll(value, by % value.shape[axis], axis=axis), tree)


def cell(whole, jump_before, jump_after):
    slope = [minmod(jump_before[comp], jump_after[comp]) for comp in range(4)]
    return known(minus(whole, slope)), known([whole[comp] + slope[comp] for comp in range(4)])


def row_changes(values, wholes):
    count = len(values)
    end_jump = minus(rolled(values[0], -1, 1), values[-1])
    jumps = [minus(values[at + 1], values[at]) for at in range(count - 1)] + [end_jump]
    faces, first_low, high = [], None, None
    for at in range(count):
        jump = jumps[at - 1] if at else minus(values[0], rolled(values[-1], 1, 1))
        low, next_high = cell(wholes[at], jump, jumps[at])
        if at:
            faces.append(face(high, low))
        else:
            first_low = low
        high = next_high
    faces.append(face(high, known(rolled(first_low[0], -1, 1))))
    return [minus(faces[at], faces[at - 1] if at else rolled(faces[-1], 1, 1)) for at in range(count)]


class Column:
    def __init__(self, count, begin, here, after):
        self.count, self.begin = count, begin
        self.jump = self.first_jump = minus(after, here)
        self.before = here
        self.first_low = self.first_flux = self.last_flux = self.high = None

    def feed(self, row, here, whole, after):
        next_row = (row + 1) % self.count
        if after is None:
            next_jump = self.first_jump
        else:
            next_jump = minus(rolled(after, -1, 0) if next_row == 0 else after, here)
        jump = minus(here, rolled(self.before, 1, 0)) if row == 0 else self.jump
        low, high = cell(whole, jump, next_jump)
        done = []
        if self.first_low is None:
            self.first_low = low
        else:
            flux = face(known(rolled(self.high[0], 1, 0)) if row == 0 else self.high, low)
            if self.last_flux is None:
                self.first_flux = flux
            else:
                seen = rolled(flux, -1, 0) if row == 0 else flux
                done.append(((row - 1) % self.count, minus(seen, self.last_flux)))
            self.last_flux = flux
        self.high, self.jump, self.before = high, next_jump, here
        if after is None:
            flux = face(high, self.first_low)
            done.append((row, minus(flux, self.last_flux)))
            done.append(((row + 1) % self.count, minus(self.first_flux, flux)))
        return done


Y_ORDER = (0, 2, 1, 3)


def changes(load, rows, cols, begin, store):
    along_y = {}
    values = {at: [load((begin + at) % rows, col) for col in range(cols)] for at in range(2)}
    columns = [Column(rows, begin, values[0][col], values[1][col]) for col in range(cols)]
    for at in range(1, rows + 1):
        row = (begin + at) % rows
        here = values.pop(at)
        if at < rows:
            values[at + 1] = [load((row + 1) % rows, col) for col in range(cols)]
        whole = [[part + part for part in value] for value in here]
        ready = []
        for col in range(cols):
            after = values[at + 1][col] if at < rows else None
            ready += [(col, *item) for item in columns[col].feed(row, here[col], whole[col], after)]
        along_y[row] = row_changes(*([[part[comp] for comp in Y_ORDER] for part in value] for value in (here, whole)))
        for col, done, parts in ready:
            other = along_y[done][col]
            store(done, col, [parts[comp] + other[Y_ORDER[comp]] for comp in range(4)])


def place_of(lane, group, groups):
    return groups * lane + group


def deal_kernel(state_ref, up_ref, down_ref, own_ref, dealt_ref, halo_select_ref, back_select_ref, top_ref, plain):
    top_ref[...] = own_ref[...]
    rows, cols = state_ref.shape[1:]
    tall = rows + 2 * HALO
    wide = dealt_ref.shape[1]
    groups = wide // LANES
    for comp in range(4):
        span = slice(comp * HALO, (comp + 1) * HALO)
        low = comp * tall
        plain[low : low + HALO, :] = up_ref[span, :]
        plain[low + HALO : low + HALO + rows, :] = state_ref[comp]
        plain[low + HALO + rows : low + tall, :] = down_ref[span, :]
    source = iota((wide, wide), 0)
    goal = iota((wide, wide), 1)
    place = place_of(goal % LANES, goal // LANES, groups)
    place = jnp.where(place < cols + 2 * HALO, (place + wide - HALO) % wide, 0)
    select = jnp.where(source == place, 1.0, 0.0).astype(jnp.bfloat16)
    dealt_ref[...] = selected(plain[...], select[0:cols])
    halo_select_ref[...] = select[cols:]
    source = iota((wide, cols), 0)
    goal = iota((wide, cols), 1)
    back = place_of(source % LANES, source // LANES, groups) == goal + HALO
    back_select_ref[...] = jnp.where(back, 1.0, 0.0).astype(jnp.bfloat16)


def join_kernel(next_ref, swap_ref, far_ref, own_ref, top_ref):
    speeds = jnp.maximum(next_ref[0:8, :], swap_ref[0:8, :])
    carried = (iota((8, LANES), 0) == 0) & (iota((8, LANES), 1) < LANES // 2)
    known_here = jnp.maximum(own_ref[...], far_ref[...])
    top_ref[...] = jnp.full((8, LANES), jnp.max(jnp.where(carried, speeds, known_here)))


def first_kernel(cells_ref, select_ref, next_ref, swap_ref, field_ref, change_ref, plain, dealt):
    half = next_ref.shape[0]
    tall = 2 * half
    groups = cells_ref.shape[1] // LANES
    lane = iota((half, LANES), 1)
    is_odd = odd("gy")
    from_swap = swap_ref[...]
    from_next = next_ref[...]
    from_before = jnp.where(is_odd, from_swap, from_next)
    from_after = jnp.where(is_odd, from_next, from_swap)
    for side in range(2):
        for comp in range(4):
            at = side * (LANES // 2) + comp * HALO
            left = pltpu.roll(from_before, (LANES - HALO - at) % LANES, axis=1)
            right = pltpu.roll(from_after, (-at) % LANES, axis=1)
            low = comp * tall + side * half
            plain[low : low + half, :] = jnp.where(lane < LANES // 2, right, left)
    found = cells_ref[...] + selected(plain[...], select_ref[...])
    for comp in range(4):
        for group in range(groups):
            cells = found[comp * tall : (comp + 1) * tall, group * LANES : (group + 1) * LANES]
            dealt[comp, group] = (0.5 * SCALES[comp]) * cells
    count = tall // 8
    for comp in range(4):
        for row in range(count):
            for group in range(groups):
                field_ref[comp, row, group] = dealt[comp, group, pl.ds(row, 8, stride=count), :]

    def store(row, col, parts):
        for comp in range(4):
            change_ref[comp, row, col] = parts[comp]

    def load(row, col):
        return [field_ref[comp, row, col] for comp in range(4)]

    changes(load, count, groups, 0, store)


def steps_kernel(field_ref, change_ref, select_ref, own_ref, mate_ref, out_ref, field, base, mid, dealt, result, sems):
    rows, cols = out_ref.shape[1:]
    tall = rows + 2 * HALO
    groups = field_ref.shape[2]
    scale = (0.125 * COURANT / MOMENTUM) / jnp.max(jnp.maximum(own_ref[...], mate_ref[...]))
    scales = (1.0, scale, scale, scale * scale)

    def one_step(start, count, old, first_changes):
        def to_mid(row, col, parts):
            for comp in range(4):
                cells, move = old[comp, row, col], parts[comp]
                if first_changes is not None:
                    cells, move = scales[comp] * cells, (scales[comp] * scale) * move
                moved = cells - move
                base[comp, row, col] = moved
                mid[comp, row, col] = moved - move

        def to_field(row, col, parts):
            for comp in range(4):
                new = base[comp, row, col] - parts[comp]
                dealt[comp, col, pl.ds(start + row, 8, stride=count), :] = new

        def load_from(ref):
            return lambda row, col: [ref[comp, row, col] for comp in range(4)]

        if first_changes is not None:
            for row in range(count):
                for col in range(groups):
                    to_mid(row, col, [first_changes[comp, row, col] for comp in range(4)])
        else:
            for comp in range(4):
                for row in range(count):
                    for col in range(groups):
                        old[comp, row, col] = dealt[comp, col, pl.ds(start + row, 8, stride=count), :]
            changes(load_from(old), count, groups, 0, to_mid)
        changes(load_from(mid), count, groups, count // 2, to_field)

    one_step(0, tall // 8, field_ref, change_ref)
    for index in range(1, STEPS):
        one_step(4 * index, (tall - 8 * index) // 8, field, None)

    wide = groups * LANES
    lane = iota((rows, LANES), 1)
    parts = []
    for comp in range(4):
        line = []
        for group in range(groups):
            place = place_of(lane, group, groups)
            inside = (place >= HALO) & (place < HALO + cols)
            line.append(jnp.where(inside, dealt[comp, group, HALO : HALO + rows, :], 0.0))
        parts.append(jnp.concatenate(line, axis=1))
    found = selected(jnp.concatenate(parts, axis=0), select_ref[...])
    copies = []
    for comp in range(4):
        result[comp] = ((2.0 / SCALES[comp]) / scales[comp]) * found[comp * rows : (comp + 1) * rows, :]
        copies.append(pltpu.make_async_copy(result.at[comp], out_ref.at[comp], sems.at[comp]))
        copies[-1].start()
    for copy in copies:
        copy.wait()


def local(state):
    parts, rows, cols = state.shape
    tall = rows + 2 * HALO
    groups = -(-(cols + 2 * HALO) // LANES)

    def sent(value, axis, by):
        count = lax.axis_size(axis)
        return lax.ppermute(value, axis, [(i, (i + by) % count) for i in range(count)])

    def swapped_bit(value, axis, by):
        return lax.ppermute(value, axis, [(i, i ^ by) for i in range(lax.axis_size(axis))])

    def swapped_pairs(value, axis, first):
        count = lax.axis_size(axis)
        pairs = []
        for low in range(first, count, 2):
            high = (low + 1) % count
            pairs += [(low, high), (high, low)]
        return lax.ppermute(value, axis, pairs)

    def swapped_threes(value, axis):
        count = lax.axis_size(axis)
        return lax.ppermute(value, axis, [(i, (i + 3 - 6 * (i % 2)) % count) for i in range(count)])

    edge_type = array(parts * HALO + 8, cols)
    first, second, top = pl.pallas_call(
        edge_kernel,
        out_shape=(edge_type, edge_type, array(8, LANES)),
        in_specs=[VMEM],
        out_specs=(VMEM,) * 3,
        compiler_params=params(4),
        name="edge",
    )(state)
    second = swapped_pairs(second, "gx", 1)
    first = swapped_pairs(first, "gx", 0)
    far = swapped_threes(top, "gx"), swapped_bit(top, "gx", 4)
    side_type = array(tall // 2, LANES)
    up, down, first, second, top = pl.pallas_call(
        pack_kernel,
        out_shape=(edge_type, edge_type, side_type, side_type, array(8, LANES)),
        in_specs=[VMEM] * 6,
        out_specs=(VMEM,) * 5,
        compiler_params=params(4),
        name="pack",
    )(state, second, *far, first, top)
    second = swapped_pairs(second, "gy", 1)
    first = swapped_pairs(first, "gy", 0)
    far = swapped_bit(top, "gy", 2)
    wide = groups * LANES
    cells, halo_select, back_select, top = pl.pallas_call(
        deal_kernel,
        out_shape=(
            array(parts * tall, wide),
            jax.ShapeDtypeStruct((wide - cols, wide), jnp.bfloat16),
            jax.ShapeDtypeStruct((wide, cols), jnp.bfloat16),
            array(8, LANES),
        ),
        in_specs=[VMEM] * 4,
        out_specs=(VMEM,) * 4,
        scratch_shapes=[pltpu.VMEM((parts * tall, cols), jnp.float32)],
        compiler_params=params(8),
        cost_estimate=pl.CostEstimate(flops=300_000_000, bytes_accessed=1_500_000, transcendentals=0),
        name="deal",
    )(state, up, down, top)
    top = pl.pallas_call(
        join_kernel,
        out_shape=array(8, LANES),
        in_specs=[VMEM] * 4,
        out_specs=VMEM,
        compiler_params=params(4),
        name="join",
    )(second, first, far, top)
    for axis, covered in (("gy", 4), ("gx", 8)):
        while covered < lax.axis_size(axis):
            top = jnp.maximum(top, sent(top, axis, covered))
            covered *= 2
    mate = swapped_bit(top, "gx", 1)
    dealt_type = array(parts, tall // 8, groups, 8, LANES)
    dealt = pltpu.VMEM(dealt_type.shape, jnp.float32)
    plain = pltpu.VMEM((parts, groups, tall, LANES), jnp.float32)
    field, change = pl.pallas_call(
        first_kernel,
        out_shape=(dealt_type, dealt_type),
        in_specs=[VMEM] * 4,
        out_specs=(VMEM,) * 2,
        scratch_shapes=[pltpu.VMEM((parts * tall, LANES), jnp.float32), plain],
        compiler_params=params(16),
        cost_estimate=pl.CostEstimate(flops=20_000_000, bytes_accessed=2_000_000, transcendentals=400_000),
        name="first",
    )(cells, halo_select, second, first)
    return pl.pallas_call(
        steps_kernel,
        out_shape=array(parts, rows, cols),
        in_specs=[VMEM] * 5,
        out_specs=pl.BlockSpec(memory_space=pl.ANY),
        scratch_shapes=[dealt] * 3
        + [plain, pltpu.VMEM((parts, rows, cols), jnp.float32), pltpu.SemaphoreType.DMA((parts,))],
        compiler_params=params(16),
        name="steps",
    )(field, change, back_select, top, mate)


def solution(mesh):
    in_specs = (P(None, "gx", "gy"),)
    out_specs = P(None, "gx", "gy")
    return jax.shard_map(local, mesh=mesh, in_specs=in_specs, out_specs=out_specs, check_vma=False)
```

```python
import functools
import math

import jax
import jax.numpy as jnp
from jax import lax
from jax.experimental import pallas as pl
from jax.experimental.pallas import tpu as pltpu
from jax.sharding import PartitionSpec as P

STEPS = 4
HALO = 4 * STEPS
LANES = 128
GAMMA = 1.4
COURANT = 0.35
TINY = 1e-30

VMEM = pl.BlockSpec(memory_space=pltpu.VMEM)


def params(limit):
    return pltpu.CompilerParams(vmem_limit_bytes=limit << 20)


def array(*shape):
    return jax.ShapeDtypeStruct(shape, jnp.float32)


def iota(shape, dim):
    return lax.broadcasted_iota(jnp.int32, shape, dim)


def odd(axis):
    return lax.rem(lax.axis_index(axis), 2) == 1


def edge_kernel(block_ref, first_ref, second_ref, top_ref):
    rows = block_ref.shape[1]
    density, mom_x, mom_y, energy = (block_ref[comp] for comp in range(4))
    inv = 1.0 / density
    pressure = (GAMMA - 1.0) * (energy - 0.5 * (mom_x * mom_x + mom_y * mom_y) * inv)
    speed = jnp.maximum(jnp.abs(mom_x * inv), jnp.abs(mom_y * inv)) + jnp.sqrt(GAMMA * pressure * inv)
    top = jnp.max(speed)
    is_odd = odd("gx")
    for comp in range(4):
        span = slice(comp * HALO, (comp + 1) * HALO)
        head = block_ref[comp, 0:HALO, :]
        tail = block_ref[comp, rows - HALO : rows, :]
        first_ref[span, :] = jnp.where(is_odd, head, tail)
        second_ref[span, :] = jnp.where(is_odd, tail, head)
    first_ref[4 * HALO :, :] = jnp.full((8, first_ref.shape[1]), top)
    second_ref[4 * HALO :, :] = jnp.full((8, second_ref.shape[1]), top)
    top_ref[...] = jnp.full(top_ref.shape, top)


def pack_kernel(state_ref, next_ref, three_ref, four_ref, swap_ref, own_ref, up_ref, down_ref, first_ref, second_ref, top_ref):
    rows = state_ref.shape[1]
    cols = state_ref.shape[2]
    half = rows // 2 + HALO
    lane = iota((half, LANES), 1)
    is_odd = odd("gx")
    up_ref[...] = jnp.where(is_odd, swap_ref[...], next_ref[...])
    down_ref[...] = jnp.where(is_odd, next_ref[...], swap_ref[...])
    top = jnp.maximum(jnp.maximum(own_ref[...], jnp.maximum(three_ref[...], four_ref[...])),
                      jnp.maximum(up_ref[4 * HALO :, 0:LANES], down_ref[4 * HALO :, 0:LANES]))

    def edge(low, at):
        lanes = slice(low, low + LANES)
        total = jnp.zeros((half, LANES), jnp.float32)
        for side in range(2):
            for comp in range(4):
                span = slice(comp * HALO, (comp + 1) * HALO)
                if side == 0:
                    cells = jnp.concatenate([up_ref[span, lanes], state_ref[comp, 0 : rows // 2, lanes]], axis=0)
                else:
                    cells = jnp.concatenate([state_ref[comp, rows // 2 : rows, lanes], down_ref[span, lanes]], axis=0)
                goal = side * (LANES // 2) + comp * HALO
                moved = pltpu.roll(cells, (goal - at) % LANES, axis=1)
                total = jnp.where((lane >= goal) & (lane < goal + HALO), moved, total)
        return total

    left = edge(0, 0)
    right = edge(cols - LANES, LANES - HALO)
    free = (iota((half, LANES), 0) == 0) & (lane < LANES // 2)
    under = jnp.concatenate([top] * (half // 8), axis=0)
    left = jnp.where(free, under, left)
    right = jnp.where(free, under, right)
    is_odd = odd("gy")
    first_ref[...] = jnp.where(is_odd, left, right)
    second_ref[...] = jnp.where(is_odd, right, left)
    top_ref[...] = top


def selected(values, select):
    rows = values.shape[0]
    parts = []
    for _ in range(3):
        parts.append(values.astype(jnp.bfloat16))
        values = values - parts[-1].astype(jnp.float32)
    found = jnp.dot(jnp.concatenate(parts, axis=0), select, preferred_element_type=jnp.float32)
    return (found[0:rows] + found[rows : 2 * rows]) + found[2 * rows :]


def minmod(first, second):
    low = jnp.minimum(first, second)
    high = jnp.maximum(first, second)
    return jnp.maximum(low, jnp.minimum(high, 0.0))


MOMENTUM = math.sqrt(0.5 * (GAMMA - 1.0))
SCALES = (1.0, MOMENTUM, MOMENTUM, GAMMA - 1.0)


def known(state):
    density, normal, tangent, energy = state
    inv = pl.reciprocal(density, approx=True)
    vel = normal * inv
    pressure = energy - (normal * normal + tangent * tangent) * inv
    square = jnp.maximum((GAMMA * MOMENTUM * MOMENTUM) * pressure * inv, TINY)
    return state, vel, pressure, pressure * vel, jnp.abs(vel) + square * lax.rsqrt(square)


def face(left, right):
    (left_state, left_vel, left_pressure, left_work, left_speed) = left
    (right_state, right_vel, right_pressure, right_work, right_speed) = right
    top = jnp.maximum(left_speed, right_speed)
    left_rate = left_vel + top
    right_rate = right_vel - top
    flux = [left_rate * left_state[comp] + right_rate * right_state[comp] for comp in range(4)]
    flux[1] = flux[1] + (MOMENTUM * MOMENTUM) * (left_pressure + right_pressure)
    flux[3] = flux[3] + (GAMMA - 1.0) * (left_work + right_work)
    return flux


def minus(first, second):
    return [first[comp] - second[comp] for comp in range(4)]


def rolled(tree, by, axis):
    return jax.tree.map(lambda value: pltpu.roll(value, by % value.shape[axis], axis=axis), tree)


def cell(whole, jump_before, jump_after):
    slope = [minmod(jump_before[comp], jump_after[comp]) for comp in range(4)]
    return known(minus(whole, slope)), known([whole[comp] + slope[comp] for comp in range(4)])


def row_changes(values, wholes):
    count = len(values)
    end_jump = minus(rolled(values[0], -1, 1), values[-1])
    jumps = [minus(values[at + 1], values[at]) for at in range(count - 1)] + [end_jump]
    faces, first_low, high = [], None, None
    for at in range(count):
        jump = jumps[at - 1] if at else minus(values[0], rolled(values[-1], 1, 1))
        low, next_high = cell(wholes[at], jump, jumps[at])
        if at:
            faces.append(face(high, low))
        else:
            first_low = low
        high = next_high
    faces.append(face(high, known(rolled(first_low[0], -1, 1))))
    return [minus(faces[at], faces[at - 1] if at else rolled(faces[-1], 1, 1)) for at in range(count)]


class Column:
    def __init__(self, count, begin, here, after):
        self.count, self.begin = count, begin
        self.jump = self.first_jump = minus(after, here)
        self.before = here
        self.first_low = self.first_flux = self.last_flux = self.high = None

    def feed(self, row, here, whole, after):
        next_row = (row + 1) % self.count
        if after is None:
            next_jump = self.first_jump
        else:
            next_jump = minus(rolled(after, -1, 0) if next_row == 0 else after, here)
        jump = minus(here, rolled(self.before, 1, 0)) if row == 0 else self.jump
        low, high = cell(whole, jump, next_jump)
        done = []
        if self.first_low is None:
            self.first_low = low
        else:
            flux = face(known(rolled(self.high[0], 1, 0)) if row == 0 else self.high, low)
            if self.last_flux is None:
                self.first_flux = flux
            else:
                seen = rolled(flux, -1, 0) if row == 0 else flux
                done.append(((row - 1) % self.count, minus(seen, self.last_flux)))
            self.last_flux = flux
        self.high, self.jump, self.before = high, next_jump, here
        if after is None:
            flux = face(high, self.first_low)
            done.append((row, minus(flux, self.last_flux)))
            done.append(((row + 1) % self.count, minus(self.first_flux, flux)))
        return done


Y_ORDER = (0, 2, 1, 3)


def changes(load, rows, cols, begin, store):
    along_y = {}
    values = {at: [load((begin + at) % rows, col) for col in range(cols)] for at in range(2)}
    columns = [Column(rows, begin, values[0][col], values[1][col]) for col in range(cols)]
    for at in range(1, rows + 1):
        row = (begin + at) % rows
        here = values.pop(at)
        if at < rows:
            values[at + 1] = [load((row + 1) % rows, col) for col in range(cols)]
        whole = [[part + part for part in value] for value in here]
        ready = []
        for col in range(cols):
            after = values[at + 1][col] if at < rows else None
            ready += [(col, *item) for item in columns[col].feed(row, here[col], whole[col], after)]
        along_y[row] = row_changes(*([[part[comp] for comp in Y_ORDER] for part in value] for value in (here, whole)))
        for col, done, parts in ready:
            other = along_y[done][col]
            store(done, col, [parts[comp] + other[Y_ORDER[comp]] for comp in range(4)])


def place_of(lane, group, groups):
    return groups * lane + group


def deal_kernel(state_ref, up_ref, down_ref, own_ref, dealt_ref, halo_select_ref, back_select_ref, top_ref, plain):
    top_ref[...] = own_ref[...]
    rows, cols = state_ref.shape[1:]
    tall = rows + 2 * HALO
    wide = dealt_ref.shape[1]
    groups = wide // LANES
    for comp in range(4):
        span = slice(comp * HALO, (comp + 1) * HALO)
        low = comp * tall
        plain[low : low + HALO, :] = up_ref[span, :]
        plain[low + HALO : low + HALO + rows, :] = state_ref[comp]
        plain[low + HALO + rows : low + tall, :] = down_ref[span, :]
    source = iota((wide, wide), 0)
    goal = iota((wide, wide), 1)
    place = place_of(goal % LANES, goal // LANES, groups)
    place = jnp.where(place < cols + 2 * HALO, (place + wide - HALO) % wide, 0)
    select = jnp.where(source == place, 1.0, 0.0).astype(jnp.bfloat16)
    dealt_ref[...] = selected(plain[...], select[0:cols])
    halo_select_ref[...] = select[cols:]
    source = iota((wide, cols), 0)
    goal = iota((wide, cols), 1)
    back = place_of(source % LANES, source // LANES, groups) == goal + HALO
    back_select_ref[...] = jnp.where(back, 1.0, 0.0).astype(jnp.bfloat16)


def join_kernel(next_ref, swap_ref, far_ref, own_ref, top_ref):
    speeds = jnp.maximum(next_ref[0:8, :], swap_ref[0:8, :])
    carried = (iota((8, LANES), 0) == 0) & (iota((8, LANES), 1) < LANES // 2)
    known_here = jnp.maximum(own_ref[...], far_ref[...])
    top_ref[...] = jnp.full((8, LANES), jnp.max(jnp.where(carried, speeds, known_here)))


def first_kernel(cells_ref, select_ref, next_ref, swap_ref, field_ref, change_ref, plain, dealt):
    half = next_ref.shape[0]
    tall = 2 * half
    groups = cells_ref.shape[1] // LANES
    lane = iota((half, LANES), 1)
    is_odd = odd("gy")
    from_swap = swap_ref[...]
    from_next = next_ref[...]
    from_before = jnp.where(is_odd, from_swap, from_next)
    from_after = jnp.where(is_odd, from_next, from_swap)
    for side in range(2):
        for comp in range(4):
            at = side * (LANES // 2) + comp * HALO
            left = pltpu.roll(from_before, (LANES - HALO - at) % LANES, axis=1)
            right = pltpu.roll(from_after, (-at) % LANES, axis=1)
            low = comp * tall + side * half
            plain[low : low + half, :] = jnp.where(lane < LANES // 2, right, left)
    found = cells_ref[...] + selected(plain[...], select_ref[...])
    for comp in range(4):
        for group in range(groups):
            cells = found[comp * tall : (comp + 1) * tall, group * LANES : (group + 1) * LANES]
            dealt[comp, group] = (0.5 * SCALES[comp]) * cells
    count = tall // 8
    for comp in range(4):
        for row in range(count):
            for group in range(groups):
                field_ref[comp, row, group] = dealt[comp, group, pl.ds(row, 8, stride=count), :]

    def store(row, col, parts):
        for comp in range(4):
            change_ref[comp, row, col] = parts[comp]

    def load(row, col):
        return [field_ref[comp, row, col] for comp in range(4)]

    changes(load, count, groups, 0, store)


def steps_kernel(field_ref, change_ref, select_ref, own_ref, mate_ref, out_ref, field, base, mid, dealt, result, sems):
    rows, cols = out_ref.shape[1:]
    tall = rows + 2 * HALO
    groups = field_ref.shape[2]
    scale = (0.125 * COURANT / MOMENTUM) / jnp.max(jnp.maximum(own_ref[...], mate_ref[...]))
    scales = (1.0, scale, scale, scale * scale)

    def one_step(start, count, old, first_changes, keep):
        def to_mid(row, col, parts):
            for comp in range(4):
                cells, move = old[comp, row, col], parts[comp]
                if first_changes is not None:
                    cells, move = scales[comp] * cells, (scales[comp] * scale) * move
                moved = cells - move
                base[comp, row, col] = moved
                mid[comp, row, col] = moved - move

        def to_field(row, col, parts):
            for comp in range(4):
                new = base[comp, row, col] - parts[comp]
                if keep:
                    field[comp, row, col] = new
                else:
                    dealt[comp, col, pl.ds(start + row, 8, stride=count), :] = new

        def load_from(ref):
            return lambda row, col: [ref[comp, row, col] for comp in range(4)]

        if first_changes is not None:
            for row in range(count):
                for col in range(groups):
                    to_mid(row, col, [first_changes[comp, row, col] for comp in range(4)])
        else:
            changes(load_from(old), count, groups, 0, to_mid)
        changes(load_from(mid), count, groups, count // 2, to_field)

    for index in range(STEPS):
        start = 8 * (index // 2)
        count = (tall - 2 * start) // 8
        if index and index % 2 == 0:
            for comp in range(4):
                for row in range(count):
                    for col in range(groups):
                        field[comp, row, col] = dealt[comp, col, pl.ds(start + row, 8, stride=count), :]
        keep = index % 2 == 0 and index + 1 < STEPS
        one_step(start, count, field if index else field_ref, None if index else change_ref, keep)

    wide = groups * LANES
    lane = iota((rows, LANES), 1)
    parts = []
    for comp in range(4):
        line = []
        for group in range(groups):
            place = place_of(lane, group, groups)
            inside = (place >= HALO) & (place < HALO + cols)
            line.append(jnp.where(inside, dealt[comp, group, HALO : HALO + rows, :], 0.0))
        parts.append(jnp.concatenate(line, axis=1))
    found = selected(jnp.concatenate(parts, axis=0), select_ref[...])
    copies = []
    for comp in range(4):
        result[comp] = ((2.0 / SCALES[comp]) / scales[comp]) * found[comp * rows : (comp + 1) * rows, :]
        copies.append(pltpu.make_async_copy(result.at[comp], out_ref.at[comp], sems.at[comp]))
        copies[-1].start()
    for copy in copies:
        copy.wait()


def local(state):
    parts, rows, cols = state.shape
    tall = rows + 2 * HALO
    groups = -(-(cols + 2 * HALO) // LANES)

    def sent(value, axis, by):
        count = lax.axis_size(axis)
        return lax.ppermute(value, axis, [(i, (i + by) % count) for i in range(count)])

    def swapped_bit(value, axis, by):
        return lax.ppermute(value, axis, [(i, i ^ by) for i in range(lax.axis_size(axis))])

    def swapped_pairs(value, axis, first):
        count = lax.axis_size(axis)
        pairs = []
        for low in range(first, count, 2):
            high = (low + 1) % count
            pairs += [(low, high), (high, low)]
        return lax.ppermute(value, axis, pairs)

    def swapped_threes(value, axis):
        count = lax.axis_size(axis)
        return lax.ppermute(value, axis, [(i, (i + 3 - 6 * (i % 2)) % count) for i in range(count)])

    edge_type = array(parts * HALO + 8, cols)
    first, second, top = pl.pallas_call(
        edge_kernel,
        out_shape=(edge_type, edge_type, array(8, LANES)),
        in_specs=[VMEM],
        out_specs=(VMEM,) * 3,
        compiler_params=params(4),
        name="edge",
    )(state)
    second = swapped_pairs(second, "gx", 1)
    first = swapped_pairs(first, "gx", 0)
    far = swapped_threes(top, "gx"), swapped_bit(top, "gx", 4)
    side_type = array(tall // 2, LANES)
    up, down, first, second, top = pl.pallas_call(
        pack_kernel,
        out_shape=(edge_type, edge_type, side_type, side_type, array(8, LANES)),
        in_specs=[VMEM] * 6,
        out_specs=(VMEM,) * 5,
        compiler_params=params(4),
        name="pack",
    )(state, second, *far, first, top)
    second = swapped_pairs(second, "gy", 1)
    first = swapped_pairs(first, "gy", 0)
    far = swapped_bit(top, "gy", 2)
    wide = groups * LANES
    cells, halo_select, back_select, top = pl.pallas_call(
        deal_kernel,
        out_shape=(
            array(parts * tall, wide),
            jax.ShapeDtypeStruct((wide - cols, wide), jnp.bfloat16),
            jax.ShapeDtypeStruct((wide, cols), jnp.bfloat16),
            array(8, LANES),
        ),
        in_specs=[VMEM] * 4,
        out_specs=(VMEM,) * 4,
        scratch_shapes=[pltpu.VMEM((parts * tall, cols), jnp.float32)],
        compiler_params=params(8),
        cost_estimate=pl.CostEstimate(flops=300_000_000, bytes_accessed=1_500_000, transcendentals=0),
        name="deal",
    )(state, up, down, top)
    top = pl.pallas_call(
        join_kernel,
        out_shape=array(8, LANES),
        in_specs=[VMEM] * 4,
        out_specs=VMEM,
        compiler_params=params(4),
        name="join",
    )(second, first, far, top)
    for axis, covered in (("gy", 4), ("gx", 8)):
        while covered < lax.axis_size(axis):
            top = jnp.maximum(top, sent(top, axis, covered))
            covered *= 2
    mate = swapped_bit(top, "gx", 1)
    dealt_type = array(parts, tall // 8, groups, 8, LANES)
    dealt = pltpu.VMEM(dealt_type.shape, jnp.float32)
    plain = pltpu.VMEM((parts, groups, tall, LANES), jnp.float32)
    field, change = pl.pallas_call(
        first_kernel,
        out_shape=(dealt_type, dealt_type),
        in_specs=[VMEM] * 4,
        out_specs=(VMEM,) * 2,
        scratch_shapes=[pltpu.VMEM((parts * tall, LANES), jnp.float32), plain],
        compiler_params=params(16),
        cost_estimate=pl.CostEstimate(flops=20_000_000, bytes_accessed=2_000_000, transcendentals=400_000),
        name="first",
    )(cells, halo_select, second, first)
    return pl.pallas_call(
        steps_kernel,
        out_shape=array(parts, rows, cols),
        in_specs=[VMEM] * 5,
        out_specs=pl.BlockSpec(memory_space=pl.ANY),
        scratch_shapes=[dealt] * 3
        + [plain, pltpu.VMEM((parts, rows, cols), jnp.float32), pltpu.SemaphoreType.DMA((parts,))],
        compiler_params=params(16),
        name="steps",
    )(field, change, back_select, top, mate)


def solution(mesh):
    in_specs = (P(None, "gx", "gy"),)
    out_specs = P(None, "gx", "gy")
    return jax.shard_map(local, mesh=mesh, in_specs=in_specs, out_specs=out_specs, check_vma=False)
```

```python
import functools
import math

import jax
import jax.numpy as jnp
from jax import lax
from jax.experimental import pallas as pl
from jax.experimental.pallas import tpu as pltpu
from jax.sharding import PartitionSpec as P

STEPS = 4
HALO = 4 * STEPS
LANES = 128
GAMMA = 1.4
COURANT = 0.35
TINY = 1e-30

VMEM = pl.BlockSpec(memory_space=pltpu.VMEM)


def params(limit):
    return pltpu.CompilerParams(vmem_limit_bytes=limit << 20)


def array(*shape):
    return jax.ShapeDtypeStruct(shape, jnp.float32)


def iota(shape, dim):
    return lax.broadcasted_iota(jnp.int32, shape, dim)


def odd(axis):
    return lax.rem(lax.axis_index(axis), 2) == 1


def edge_kernel(block_ref, first_ref, second_ref, top_ref):
    rows = block_ref.shape[1]
    density, mom_x, mom_y, energy = (block_ref[comp] for comp in range(4))
    inv = 1.0 / density
    pressure = (GAMMA - 1.0) * (energy - 0.5 * (mom_x * mom_x + mom_y * mom_y) * inv)
    speed = jnp.maximum(jnp.abs(mom_x * inv), jnp.abs(mom_y * inv)) + jnp.sqrt(GAMMA * pressure * inv)
    top = jnp.max(speed)
    is_odd = odd("gx")
    for comp in range(4):
        span = slice(comp * HALO, (comp + 1) * HALO)
        head = block_ref[comp, 0:HALO, :]
        tail = block_ref[comp, rows - HALO : rows, :]
        first_ref[span, :] = jnp.where(is_odd, head, tail)
        second_ref[span, :] = jnp.where(is_odd, tail, head)
    first_ref[4 * HALO :, :] = jnp.full((8, first_ref.shape[1]), top)
    second_ref[4 * HALO :, :] = jnp.full((8, second_ref.shape[1]), top)
    top_ref[...] = jnp.full(top_ref.shape, top)


def pack_kernel(state_ref, next_ref, three_ref, four_ref, swap_ref, own_ref, up_ref, down_ref, first_ref, second_ref, top_ref):
    rows = state_ref.shape[1]
    cols = state_ref.shape[2]
    half = rows // 2 + HALO
    lane = iota((half, LANES), 1)
    is_odd = odd("gx")
    up_ref[...] = jnp.where(is_odd, swap_ref[...], next_ref[...])
    down_ref[...] = jnp.where(is_odd, next_ref[...], swap_ref[...])
    top = jnp.maximum(jnp.maximum(own_ref[...], jnp.maximum(three_ref[...], four_ref[...])),
                      jnp.maximum(up_ref[4 * HALO :, 0:LANES], down_ref[4 * HALO :, 0:LANES]))

    def edge(low, at):
        lanes = slice(low, low + LANES)
        total = jnp.zeros((half, LANES), jnp.float32)
        for side in range(2):
            for comp in range(4):
                span = slice(comp * HALO, (comp + 1) * HALO)
                if side == 0:
                    cells = jnp.concatenate([up_ref[span, lanes], state_ref[comp, 0 : rows // 2, lanes]], axis=0)
                else:
                    cells = jnp.concatenate([state_ref[comp, rows // 2 : rows, lanes], down_ref[span, lanes]], axis=0)
                goal = side * (LANES // 2) + comp * HALO
                moved = pltpu.roll(cells, (goal - at) % LANES, axis=1)
                total = jnp.where((lane >= goal) & (lane < goal + HALO), moved, total)
        return total

    left = edge(0, 0)
    right = edge(cols - LANES, LANES - HALO)
    free = (iota((half, LANES), 0) == 0) & (lane < LANES // 2)
    under = jnp.concatenate([top] * (half // 8), axis=0)
    left = jnp.where(free, under, left)
    right = jnp.where(free, under, right)
    is_odd = odd("gy")
    first_ref[...] = jnp.where(is_odd, left, right)
    second_ref[...] = jnp.where(is_odd, right, left)
    top_ref[...] = top


def selected(values, select):
    rows = values.shape[0]
    parts = []
    for _ in range(3):
        parts.append(values.astype(jnp.bfloat16))
        values = values - parts[-1].astype(jnp.float32)
    found = jnp.dot(jnp.concatenate(parts, axis=0), select, preferred_element_type=jnp.float32)
    return (found[0:rows] + found[rows : 2 * rows]) + found[2 * rows :]


def minmod(first, second):
    low = jnp.minimum(first, second)
    high = jnp.maximum(first, second)
    return jnp.maximum(low, jnp.minimum(high, 0.0))


MOMENTUM = math.sqrt(0.5 * (GAMMA - 1.0))
SCALES = (1.0, MOMENTUM, MOMENTUM, GAMMA - 1.0)


def known(state):
    density, normal, tangent, energy = state
    inv = pl.reciprocal(density, approx=True)
    vel = normal * inv
    pressure = energy - (normal * normal + tangent * tangent) * inv
    square = jnp.maximum((GAMMA * MOMENTUM * MOMENTUM) * pressure * inv, TINY)
    return state, vel, pressure, pressure * vel, jnp.abs(vel) + square * lax.rsqrt(square)


def face(left, right):
    (left_state, left_vel, left_pressure, left_work, left_speed) = left
    (right_state, right_vel, right_pressure, right_work, right_speed) = right
    top = jnp.maximum(left_speed, right_speed)
    left_rate = left_vel + top
    right_rate = right_vel - top
    flux = [left_rate * left_state[comp] + right_rate * right_state[comp] for comp in range(4)]
    flux[1] = flux[1] + (MOMENTUM * MOMENTUM) * (left_pressure + right_pressure)
    flux[3] = flux[3] + (GAMMA - 1.0) * (left_work + right_work)
    return flux


def minus(first, second):
    return [first[comp] - second[comp] for comp in range(4)]


def rolled(tree, by, axis):
    return jax.tree.map(lambda value: pltpu.roll(value, by % value.shape[axis], axis=axis), tree)


class Slots:
    ROWS = 40

    def __init__(self, ref):
        self.ref, self.used = ref, 0

    def __call__(self, parts, by):
        return [self.move(part, by) for part in parts]

    def move(self, value, by):
        slot = self.used % self.ref.shape[0]
        self.used += 1
        self.ref[slot, pl.ds(8, 8, stride=3), :] = value
        return self.ref[slot, pl.ds(8 - 3 * by, 8, stride=3), :]


def turned(parts, by):
    return rolled(parts, by, 0)


def cell(whole, jump_before, jump_after):
    slope = [minmod(jump_before[comp], jump_after[comp]) for comp in range(4)]
    return known(minus(whole, slope)), known([whole[comp] + slope[comp] for comp in range(4)])


def row_changes(values, wholes):
    count = len(values)
    end_jump = minus(rolled(values[0], -1, 1), values[-1])
    jumps = [minus(values[at + 1], values[at]) for at in range(count - 1)] + [end_jump]
    faces, first_low, high = [], None, None
    for at in range(count):
        jump = jumps[at - 1] if at else minus(values[0], rolled(values[-1], 1, 1))
        low, next_high = cell(wholes[at], jump, jumps[at])
        if at:
            faces.append(face(high, low))
        else:
            first_low = low
        high = next_high
    faces.append(face(high, known(rolled(first_low[0], -1, 1))))
    return [minus(faces[at], faces[at - 1] if at else rolled(faces[-1], 1, 1)) for at in range(count)]


class Column:
    def __init__(self, count, here, after, shifted):
        self.count, self.shifted = count, shifted
        self.jump = self.first_jump = minus(after, here)
        self.before = here
        self.first_low = self.first_flux = self.last_flux = self.high = None

    def feed(self, row, here, whole, after):
        next_row = (row + 1) % self.count
        if after is None:
            next_jump = self.first_jump
        else:
            next_jump = minus(self.shifted(after, -1) if next_row == 0 else after, here)
        jump = minus(here, self.shifted(self.before, 1)) if row == 0 else self.jump
        low, high = cell(whole, jump, next_jump)
        done = []
        if self.first_low is None:
            self.first_low = low
        else:
            flux = face(known(self.shifted(self.high[0], 1)) if row == 0 else self.high, low)
            if self.last_flux is None:
                self.first_flux = flux
            else:
                seen = self.shifted(flux, -1) if row == 0 else flux
                done.append(((row - 1) % self.count, minus(seen, self.last_flux)))
            self.last_flux = flux
        self.high, self.jump, self.before = high, next_jump, here
        if after is None:
            flux = face(high, self.first_low)
            done.append((row, minus(flux, self.last_flux)))
            done.append(((row + 1) % self.count, minus(self.first_flux, flux)))
        return done


Y_ORDER = (0, 2, 1, 3)


def changes(load, rows, cols, begin, store, shifted=turned):
    along_y = {}
    values = {at: [load((begin + at) % rows, col) for col in range(cols)] for at in range(2)}
    columns = [Column(rows, values[0][col], values[1][col], shifted) for col in range(cols)]
    for at in range(1, rows + 1):
        row = (begin + at) % rows
        here = values.pop(at)
        if at < rows:
            values[at + 1] = [load((row + 1) % rows, col) for col in range(cols)]
        whole = [[part + part for part in value] for value in here]
        ready = []
        for col in range(cols):
            after = values[at + 1][col] if at < rows else None
            ready += [(col, *item) for item in columns[col].feed(row, here[col], whole[col], after)]
        along_y[row] = row_changes(*([[part[comp] for comp in Y_ORDER] for part in value] for value in (here, whole)))
        for col, done, parts in ready:
            other = along_y[done][col]
            store(done, col, [parts[comp] + other[Y_ORDER[comp]] for comp in range(4)])


def place_of(lane, group, groups):
    return groups * lane + group


def deal_kernel(state_ref, up_ref, down_ref, own_ref, dealt_ref, halo_select_ref, back_select_ref, top_ref, plain):
    top_ref[...] = own_ref[...]
    rows, cols = state_ref.shape[1:]
    tall = rows + 2 * HALO
    wide = dealt_ref.shape[1]
    groups = wide // LANES
    for comp in range(4):
        span = slice(comp * HALO, (comp + 1) * HALO)
        low = comp * tall
        plain[low : low + HALO, :] = up_ref[span, :]
        plain[low + HALO : low + HALO + rows, :] = state_ref[comp]
        plain[low + HALO + rows : low + tall, :] = down_ref[span, :]
    source = iota((wide, wide), 0)
    goal = iota((wide, wide), 1)
    place = place_of(goal % LANES, goal // LANES, groups)
    place = jnp.where(place < cols + 2 * HALO, (place + wide - HALO) % wide, 0)
    select = jnp.where(source == place, 1.0, 0.0).astype(jnp.bfloat16)
    dealt_ref[...] = selected(plain[...], select[0:cols])
    halo_select_ref[...] = select[cols:]
    source = iota((wide, cols), 0)
    goal = iota((wide, cols), 1)
    back = place_of(source % LANES, source // LANES, groups) == goal + HALO
    back_select_ref[...] = jnp.where(back, 1.0, 0.0).astype(jnp.bfloat16)


def join_kernel(next_ref, swap_ref, far_ref, own_ref, top_ref):
    speeds = jnp.maximum(next_ref[0:8, :], swap_ref[0:8, :])
    carried = (iota((8, LANES), 0) == 0) & (iota((8, LANES), 1) < LANES // 2)
    known_here = jnp.maximum(own_ref[...], far_ref[...])
    top_ref[...] = jnp.full((8, LANES), jnp.max(jnp.where(carried, speeds, known_here)))


def first_kernel(cells_ref, select_ref, next_ref, swap_ref, field_ref, change_ref, plain, dealt):
    half = next_ref.shape[0]
    tall = 2 * half
    groups = cells_ref.shape[1] // LANES
    lane = iota((half, LANES), 1)
    is_odd = odd("gy")
    from_swap = swap_ref[...]
    from_next = next_ref[...]
    from_before = jnp.where(is_odd, from_swap, from_next)
    from_after = jnp.where(is_odd, from_next, from_swap)
    for side in range(2):
        for comp in range(4):
            at = side * (LANES // 2) + comp * HALO
            left = pltpu.roll(from_before, (LANES - HALO - at) % LANES, axis=1)
            right = pltpu.roll(from_after, (-at) % LANES, axis=1)
            low = comp * tall + side * half
            plain[low : low + half, :] = jnp.where(lane < LANES // 2, right, left)
    found = cells_ref[...] + selected(plain[...], select_ref[...])
    for comp in range(4):
        for group in range(groups):
            cells = found[comp * tall : (comp + 1) * tall, group * LANES : (group + 1) * LANES]
            dealt[comp, group] = (0.5 * SCALES[comp]) * cells
    count = tall // 8
    for comp in range(4):
        for row in range(count):
            for group in range(groups):
                field_ref[comp, row, group] = dealt[comp, group, pl.ds(row, 8, stride=count), :]

    def store(row, col, parts):
        for comp in range(4):
            change_ref[comp, row, col] = parts[comp]

    def load(row, col):
        return [field_ref[comp, row, col] for comp in range(4)]

    changes(load, count, groups, 0, store)


def steps_kernel(field_ref, change_ref, select_ref, own_ref, mate_ref, out_ref, field, base, mid, dealt, result, slots, sems):
    rows, cols = out_ref.shape[1:]
    tall = rows + 2 * HALO
    groups = field_ref.shape[2]
    scale = (0.125 * COURANT / MOMENTUM) / jnp.max(jnp.maximum(own_ref[...], mate_ref[...]))
    scales = (1.0, scale, scale, scale * scale)

    shifted = Slots(slots)

    def one_step(start, count, old, first_changes):
        def to_mid(row, col, parts):
            for comp in range(4):
                cells, move = old[comp, row, col], parts[comp]
                if first_changes is not None:
                    cells, move = scales[comp] * cells, (scales[comp] * scale) * move
                moved = cells - move
                base[comp, row, col] = moved
                mid[comp, row, col] = moved - move

        def to_field(row, col, parts):
            for comp in range(4):
                new = base[comp, row, col] - parts[comp]
                dealt[comp, col, pl.ds(start + row, 8, stride=count), :] = new

        def load_from(ref):
            return lambda row, col: [ref[comp, row, col] for comp in range(4)]

        if first_changes is not None:
            for row in range(count):
                for col in range(groups):
                    to_mid(row, col, [first_changes[comp, row, col] for comp in range(4)])
        else:
            for comp in range(4):
                for row in range(count):
                    for col in range(groups):
                        old[comp, row, col] = dealt[comp, col, pl.ds(start + row, 8, stride=count), :]
            changes(load_from(old), count, groups, 0, to_mid, shifted)
        changes(load_from(mid), count, groups, count // 2, to_field, shifted)

    one_step(0, tall // 8, field_ref, change_ref)
    for index in range(1, STEPS):
        one_step(4 * index, (tall - 8 * index) // 8, field, None)

    wide = groups * LANES
    lane = iota((rows, LANES), 1)
    parts = []
    for comp in range(4):
        line = []
        for group in range(groups):
            place = place_of(lane, group, groups)
            inside = (place >= HALO) & (place < HALO + cols)
            line.append(jnp.where(inside, dealt[comp, group, HALO : HALO + rows, :], 0.0))
        parts.append(jnp.concatenate(line, axis=1))
    found = selected(jnp.concatenate(parts, axis=0), select_ref[...])
    copies = []
    for comp in range(4):
        result[comp] = ((2.0 / SCALES[comp]) / scales[comp]) * found[comp * rows : (comp + 1) * rows, :]
        copies.append(pltpu.make_async_copy(result.at[comp], out_ref.at[comp], sems.at[comp]))
        copies[-1].start()
    for copy in copies:
        copy.wait()


def local(state):
    parts, rows, cols = state.shape
    tall = rows + 2 * HALO
    groups = -(-(cols + 2 * HALO) // LANES)

    def sent(value, axis, by):
        count = lax.axis_size(axis)
        return lax.ppermute(value, axis, [(i, (i + by) % count) for i in range(count)])

    def swapped_bit(value, axis, by):
        return lax.ppermute(value, axis, [(i, i ^ by) for i in range(lax.axis_size(axis))])

    def swapped_pairs(value, axis, first):
        count = lax.axis_size(axis)
        pairs = []
        for low in range(first, count, 2):
            high = (low + 1) % count
            pairs += [(low, high), (high, low)]
        return lax.ppermute(value, axis, pairs)

    def swapped_threes(value, axis):
        count = lax.axis_size(axis)
        return lax.ppermute(value, axis, [(i, (i + 3 - 6 * (i % 2)) % count) for i in range(count)])

    edge_type = array(parts * HALO + 8, cols)
    first, second, top = pl.pallas_call(
        edge_kernel,
        out_shape=(edge_type, edge_type, array(8, LANES)),
        in_specs=[VMEM],
        out_specs=(VMEM,) * 3,
        compiler_params=params(4),
        name="edge",
    )(state)
    second = swapped_pairs(second, "gx", 1)
    first = swapped_pairs(first, "gx", 0)
    far = swapped_threes(top, "gx"), swapped_bit(top, "gx", 4)
    side_type = array(tall // 2, LANES)
    up, down, first, second, top = pl.pallas_call(
        pack_kernel,
        out_shape=(edge_type, edge_type, side_type, side_type, array(8, LANES)),
        in_specs=[VMEM] * 6,
        out_specs=(VMEM,) * 5,
        compiler_params=params(4),
        name="pack",
    )(state, second, *far, first, top)
    second = swapped_pairs(second, "gy", 1)
    first = swapped_pairs(first, "gy", 0)
    far = swapped_bit(top, "gy", 2)
    wide = groups * LANES
    cells, halo_select, back_select, top = pl.pallas_call(
        deal_kernel,
        out_shape=(
            array(parts * tall, wide),
            jax.ShapeDtypeStruct((wide - cols, wide), jnp.bfloat16),
            jax.ShapeDtypeStruct((wide, cols), jnp.bfloat16),
            array(8, LANES),
        ),
        in_specs=[VMEM] * 4,
        out_specs=(VMEM,) * 4,
        scratch_shapes=[pltpu.VMEM((parts * tall, cols), jnp.float32)],
        compiler_params=params(8),
        cost_estimate=pl.CostEstimate(flops=300_000_000, bytes_accessed=1_500_000, transcendentals=0),
        name="deal",
    )(state, up, down, top)
    top = pl.pallas_call(
        join_kernel,
        out_shape=array(8, LANES),
        in_specs=[VMEM] * 4,
        out_specs=VMEM,
        compiler_params=params(4),
        name="join",
    )(second, first, far, top)
    for axis, covered in (("gy", 4), ("gx", 8)):
        while covered < lax.axis_size(axis):
            top = jnp.maximum(top, sent(top, axis, covered))
            covered *= 2
    mate = swapped_bit(top, "gx", 1)
    dealt_type = array(parts, tall // 8, groups, 8, LANES)
    dealt = pltpu.VMEM(dealt_type.shape, jnp.float32)
    plain = pltpu.VMEM((parts, groups, tall, LANES), jnp.float32)
    field, change = pl.pallas_call(
        first_kernel,
        out_shape=(dealt_type, dealt_type),
        in_specs=[VMEM] * 4,
        out_specs=(VMEM,) * 2,
        scratch_shapes=[pltpu.VMEM((parts * tall, LANES), jnp.float32), plain],
        compiler_params=params(16),
        cost_estimate=pl.CostEstimate(flops=20_000_000, bytes_accessed=2_000_000, transcendentals=400_000),
        name="first",
    )(cells, halo_select, second, first)
    return pl.pallas_call(
        steps_kernel,
        out_shape=array(parts, rows, cols),
        in_specs=[VMEM] * 5,
        out_specs=pl.BlockSpec(memory_space=pl.ANY),
        scratch_shapes=[dealt] * 3
        + [
            plain,
            pltpu.VMEM((parts, rows, cols), jnp.float32),
            pltpu.VMEM((16 * groups * 2, Slots.ROWS, LANES), jnp.float32),
            pltpu.SemaphoreType.DMA((parts,)),
        ],
        compiler_params=params(16),
        name="steps",
    )(field, change, back_select, top, mate)


def solution(mesh):
    in_specs = (P(None, "gx", "gy"),)
    out_specs = P(None, "gx", "gy")
    return jax.shard_map(local, mesh=mesh, in_specs=in_specs, out_specs=out_specs, check_vma=False)
```

```python
import functools
import math

import jax
import jax.numpy as jnp
from jax import lax
from jax.experimental import pallas as pl
from jax.experimental.pallas import tpu as pltpu
from jax.sharding import PartitionSpec as P

STEPS = 4
HALO = 4 * STEPS
LANES = 128
GAMMA = 1.4
COURANT = 0.35
TINY = 1e-30

VMEM = pl.BlockSpec(memory_space=pltpu.VMEM)


def params(limit):
    return pltpu.CompilerParams(vmem_limit_bytes=limit << 20)


def array(*shape):
    return jax.ShapeDtypeStruct(shape, jnp.float32)


def iota(shape, dim):
    return lax.broadcasted_iota(jnp.int32, shape, dim)


def odd(axis):
    return lax.rem(lax.axis_index(axis), 2) == 1


def edge_kernel(block_ref, first_ref, second_ref, top_ref):
    rows = block_ref.shape[1]
    density, mom_x, mom_y, energy = (block_ref[comp] for comp in range(4))
    inv = 1.0 / density
    pressure = (GAMMA - 1.0) * (energy - 0.5 * (mom_x * mom_x + mom_y * mom_y) * inv)
    speed = jnp.maximum(jnp.abs(mom_x * inv), jnp.abs(mom_y * inv)) + jnp.sqrt(GAMMA * pressure * inv)
    top = jnp.max(speed)
    is_odd = odd("gx")
    for comp in range(4):
        span = slice(comp * HALO, (comp + 1) * HALO)
        head = block_ref[comp, 0:HALO, :]
        tail = block_ref[comp, rows - HALO : rows, :]
        first_ref[span, :] = jnp.where(is_odd, head, tail)
        second_ref[span, :] = jnp.where(is_odd, tail, head)
    first_ref[4 * HALO :, :] = jnp.full((8, first_ref.shape[1]), top)
    second_ref[4 * HALO :, :] = jnp.full((8, second_ref.shape[1]), top)
    top_ref[...] = jnp.full(top_ref.shape, top)


def pack_kernel(state_ref, next_ref, three_ref, four_ref, swap_ref, own_ref, up_ref, down_ref, first_ref, second_ref, top_ref):
    rows = state_ref.shape[1]
    cols = state_ref.shape[2]
    half = rows // 2 + HALO
    lane = iota((half, LANES), 1)
    is_odd = odd("gx")
    up_ref[...] = jnp.where(is_odd, swap_ref[...], next_ref[...])
    down_ref[...] = jnp.where(is_odd, next_ref[...], swap_ref[...])
    top = jnp.maximum(jnp.maximum(own_ref[...], jnp.maximum(three_ref[...], four_ref[...])),
                      jnp.maximum(up_ref[4 * HALO :, 0:LANES], down_ref[4 * HALO :, 0:LANES]))

    def edge(low, at):
        lanes = slice(low, low + LANES)
        total = jnp.zeros((half, LANES), jnp.float32)
        for side in range(2):
            for comp in range(4):
                span = slice(comp * HALO, (comp + 1) * HALO)
                if side == 0:
                    cells = jnp.concatenate([up_ref[span, lanes], state_ref[comp, 0 : rows // 2, lanes]], axis=0)
                else:
                    cells = jnp.concatenate([state_ref[comp, rows // 2 : rows, lanes], down_ref[span, lanes]], axis=0)
                goal = side * (LANES // 2) + comp * HALO
                moved = pltpu.roll(cells, (goal - at) % LANES, axis=1)
                total = jnp.where((lane >= goal) & (lane < goal + HALO), moved, total)
        return total

    left = edge(0, 0)
    right = edge(cols - LANES, LANES - HALO)
    free = (iota((half, LANES), 0) == 0) & (lane < LANES // 2)
    under = jnp.concatenate([top] * (half // 8), axis=0)
    left = jnp.where(free, under, left)
    right = jnp.where(free, under, right)
    is_odd = odd("gy")
    first_ref[...] = jnp.where(is_odd, left, right)
    second_ref[...] = jnp.where(is_odd, right, left)
    top_ref[...] = top


def selected(values, select):
    rows = values.shape[0]
    parts = []
    for _ in range(3):
        parts.append(values.astype(jnp.bfloat16))
        values = values - parts[-1].astype(jnp.float32)
    found = jnp.dot(jnp.concatenate(parts, axis=0), select, preferred_element_type=jnp.float32)
    return (found[0:rows] + found[rows : 2 * rows]) + found[2 * rows :]


def minmod(first, second):
    low = jnp.minimum(first, second)
    high = jnp.maximum(first, second)
    return jnp.maximum(low, jnp.minimum(high, 0.0))


MOMENTUM = math.sqrt(0.5 * (GAMMA - 1.0))
SCALES = (1.0, MOMENTUM, MOMENTUM, GAMMA - 1.0)


def known(state):
    density, normal, tangent, energy = state
    inv = pl.reciprocal(density, approx=True)
    vel = normal * inv
    pressure = energy - (normal * normal + tangent * tangent) * inv
    square = jnp.maximum((GAMMA * MOMENTUM * MOMENTUM) * pressure * inv, TINY)
    return state, vel, pressure, pressure * vel, jnp.abs(vel) + square * lax.rsqrt(square)


def face(left, right):
    (left_state, left_vel, left_pressure, left_work, left_speed) = left
    (right_state, right_vel, right_pressure, right_work, right_speed) = right
    top = jnp.maximum(left_speed, right_speed)
    left_rate = left_vel + top
    right_rate = right_vel - top
    flux = [left_rate * left_state[comp] + right_rate * right_state[comp] for comp in range(4)]
    flux[1] = flux[1] + (MOMENTUM * MOMENTUM) * (left_pressure + right_pressure)
    flux[3] = flux[3] + (GAMMA - 1.0) * (left_work + right_work)
    return flux


def minus(first, second):
    return [first[comp] - second[comp] for comp in range(4)]


def rolled(tree, by, axis):
    return jax.tree.map(lambda value: pltpu.roll(value, by % value.shape[axis], axis=axis), tree)


def cell(whole, jump_before, jump_after):
    slope = [minmod(jump_before[comp], jump_after[comp]) for comp in range(4)]
    return known(minus(whole, slope)), known([whole[comp] + slope[comp] for comp in range(4)])


def row_changes(values, wholes):
    count = len(values)
    end_jump = minus(rolled(values[0], -1, 1), values[-1])
    jumps = [minus(values[at + 1], values[at]) for at in range(count - 1)] + [end_jump]
    faces, first_low, high = [], None, None
    for at in range(count):
        jump = jumps[at - 1] if at else minus(values[0], rolled(values[-1], 1, 1))
        low, next_high = cell(wholes[at], jump, jumps[at])
        if at:
            faces.append(face(high, low))
        else:
            first_low = low
        high = next_high
    faces.append(face(high, known(rolled(first_low[0], -1, 1))))
    return [minus(faces[at], faces[at - 1] if at else rolled(faces[-1], 1, 1)) for at in range(count)]


class Column:
    def __init__(self, count, begin, here, after):
        self.count, self.begin = count, begin
        self.jump = self.first_jump = minus(after, here)
        self.before = here
        self.first_low = self.first_flux = self.last_flux = self.high = None

    def feed(self, row, here, whole, after):
        next_row = (row + 1) % self.count
        if after is None:
            next_jump = self.first_jump
        else:
            next_jump = minus(rolled(after, -1, 0) if next_row == 0 else after, here)
        jump = minus(here, rolled(self.before, 1, 0)) if row == 0 else self.jump
        low, high = cell(whole, jump, next_jump)
        done = []
        if self.first_low is None:
            self.first_low = low
        else:
            flux = face(known(rolled(self.high[0], 1, 0)) if row == 0 else self.high, low)
            if self.last_flux is None:
                self.first_flux = flux
            else:
                seen = rolled(flux, -1, 0) if row == 0 else flux
                done.append(((row - 1) % self.count, minus(seen, self.last_flux)))
            self.last_flux = flux
        self.high, self.jump, self.before = high, next_jump, here
        if after is None:
            flux = face(high, self.first_low)
            done.append((row, minus(flux, self.last_flux)))
            done.append(((row + 1) % self.count, minus(self.first_flux, flux)))
        return done


Y_ORDER = (0, 2, 1, 3)


def changes(load, rows, cols, begin, store):
    along_y = {}
    values = {at: [load((begin + at) % rows, col) for col in range(cols)] for at in range(2)}
    columns = [Column(rows, begin, values[0][col], values[1][col]) for col in range(cols)]
    for at in range(1, rows + 1):
        row = (begin + at) % rows
        here = values.pop(at)
        if at < rows:
            values[at + 1] = [load((row + 1) % rows, col) for col in range(cols)]
        whole = [[part + part for part in value] for value in here]
        ready = []
        for col in range(cols):
            after = values[at + 1][col] if at < rows else None
            ready += [(col, *item) for item in columns[col].feed(row, here[col], whole[col], after)]
        along_y[row] = row_changes(*([[part[comp] for comp in Y_ORDER] for part in value] for value in (here, whole)))
        for col, done, parts in ready:
            other = along_y[done][col]
            store(done, col, [parts[comp] + other[Y_ORDER[comp]] for comp in range(4)])


def place_of(lane, group, groups):
    return groups * lane + group


def deal_kernel(state_ref, up_ref, down_ref, own_ref, dealt_ref, halo_select_ref, back_select_ref, top_ref, plain):
    top_ref[...] = own_ref[...]
    rows, cols = state_ref.shape[1:]
    tall = rows + 2 * HALO
    wide = dealt_ref.shape[1]
    groups = wide // LANES
    for comp in range(4):
        span = slice(comp * HALO, (comp + 1) * HALO)
        low = comp * tall
        plain[low : low + HALO, :] = up_ref[span, :]
        plain[low + HALO : low + HALO + rows, :] = state_ref[comp]
        plain[low + HALO + rows : low + tall, :] = down_ref[span, :]
    source = iota((wide, wide), 0)
    goal = iota((wide, wide), 1)
    place = place_of(goal % LANES, goal // LANES, groups)
    place = jnp.where(place < cols + 2 * HALO, (place + wide - HALO) % wide, 0)
    select = jnp.where(source == place, 1.0, 0.0).astype(jnp.bfloat16)
    dealt_ref[...] = selected(plain[...], select[0:cols])
    halo_select_ref[...] = select[cols:]
    source = iota((wide, cols), 0)
    goal = iota((wide, cols), 1)
    back = place_of(source % LANES, source // LANES, groups) == goal + HALO
    back_select_ref[...] = jnp.where(back, 1.0, 0.0).astype(jnp.bfloat16)


def join_kernel(next_ref, swap_ref, far_ref, own_ref, top_ref):
    speeds = jnp.maximum(next_ref[0:8, :], swap_ref[0:8, :])
    carried = (iota((8, LANES), 0) == 0) & (iota((8, LANES), 1) < LANES // 2)
    known_here = jnp.maximum(own_ref[...], far_ref[...])
    top_ref[...] = jnp.full((8, LANES), jnp.max(jnp.where(carried, speeds, known_here)))


def first_kernel(cells_ref, select_ref, next_ref, swap_ref, field_ref, change_ref, plain, dealt):
    half = next_ref.shape[0]
    tall = 2 * half
    groups = cells_ref.shape[1] // LANES
    lane = iota((half, LANES), 1)
    is_odd = odd("gy")
    from_swap = swap_ref[...]
    from_next = next_ref[...]
    from_before = jnp.where(is_odd, from_swap, from_next)
    from_after = jnp.where(is_odd, from_next, from_swap)
    for side in range(2):
        for comp in range(4):
            at = side * (LANES // 2) + comp * HALO
            left = pltpu.roll(from_before, (LANES - HALO - at) % LANES, axis=1)
            right = pltpu.roll(from_after, (-at) % LANES, axis=1)
            low = comp * tall + side * half
            plain[low : low + half, :] = jnp.where(lane < LANES // 2, right, left)
    found = cells_ref[...] + selected(plain[...], select_ref[...])
    for comp in range(4):
        for group in range(groups):
            cells = found[comp * tall : (comp + 1) * tall, group * LANES : (group + 1) * LANES]
            dealt[comp, group] = (0.5 * SCALES[comp]) * cells
    count = tall // 8
    for comp in range(4):
        for row in range(count):
            for group in range(groups):
                field_ref[comp, row, group] = dealt[comp, group, pl.ds(row, 8, stride=count), :]

    def store(row, col, parts):
        for comp in range(4):
            change_ref[comp, row, col] = parts[comp]

    def load(row, col):
        return [field_ref[comp, row, col] for comp in range(4)]

    changes(load, count, groups, 0, store)


def steps_kernel(field_ref, change_ref, select_ref, own_ref, mate_ref, out_ref, mid, dealt, result, sems):
    rows, cols = out_ref.shape[1:]
    tall = rows + 2 * HALO
    groups = field_ref.shape[2]
    scale = (0.125 * COURANT / MOMENTUM) / jnp.max(jnp.maximum(own_ref[...], mate_ref[...]))
    scales = (1.0, scale, scale, scale * scale)

    def one_step(start, count, old, first_changes):
        def to_mid(row, col, parts):
            here = old(row, col)
            for comp in range(4):
                mid[comp, row, col] = (here[comp] - parts[comp]) - parts[comp]

        def to_dealt(row, col, parts):
            here = old(row, col)
            for comp in range(4):
                new = 0.5 * (here[comp] + mid[comp, row, col]) - parts[comp]
                dealt[comp, col, pl.ds(start + row, 8, stride=count), :] = new

        if first_changes is not None:
            for row in range(count):
                for col in range(groups):
                    to_mid(row, col, first_changes(row, col))
        else:
            changes(old, count, groups, 0, to_mid)
        changes(lambda row, col: [mid[comp, row, col] for comp in range(4)], count, groups, count // 2, to_dealt)

    def scaled_field(row, col):
        return [scales[comp] * field_ref[comp, row, col] for comp in range(4)]

    def scaled_change(row, col):
        return [(scales[comp] * scale) * change_ref[comp, row, col] for comp in range(4)]

    one_step(0, tall // 8, scaled_field, scaled_change)
    for index in range(1, STEPS):
        start = 4 * index
        count = (tall - 8 * index) // 8

        def from_dealt(row, col, start=start, count=count):
            return [dealt[comp, col, pl.ds(start + row, 8, stride=count), :] for comp in range(4)]

        one_step(start, count, from_dealt, None)

    wide = groups * LANES
    lane = iota((rows, LANES), 1)
    parts = []
    for comp in range(4):
        line = []
        for group in range(groups):
            place = place_of(lane, group, groups)
            inside = (place >= HALO) & (place < HALO + cols)
            line.append(jnp.where(inside, dealt[comp, group, HALO : HALO + rows, :], 0.0))
        parts.append(jnp.concatenate(line, axis=1))
    found = selected(jnp.concatenate(parts, axis=0), select_ref[...])
    copies = []
    for comp in range(4):
        result[comp] = ((2.0 / SCALES[comp]) / scales[comp]) * found[comp * rows : (comp + 1) * rows, :]
        copies.append(pltpu.make_async_copy(result.at[comp], out_ref.at[comp], sems.at[comp]))
        copies[-1].start()
    for copy in copies:
        copy.wait()


def local(state):
    parts, rows, cols = state.shape
    tall = rows + 2 * HALO
    groups = -(-(cols + 2 * HALO) // LANES)

    def sent(value, axis, by):
        count = lax.axis_size(axis)
        return lax.ppermute(value, axis, [(i, (i + by) % count) for i in range(count)])

    def swapped_bit(value, axis, by):
        return lax.ppermute(value, axis, [(i, i ^ by) for i in range(lax.axis_size(axis))])

    def swapped_pairs(value, axis, first):
        count = lax.axis_size(axis)
        pairs = []
        for low in range(first, count, 2):
            high = (low + 1) % count
            pairs += [(low, high), (high, low)]
        return lax.ppermute(value, axis, pairs)

    def swapped_threes(value, axis):
        count = lax.axis_size(axis)
        return lax.ppermute(value, axis, [(i, (i + 3 - 6 * (i % 2)) % count) for i in range(count)])

    edge_type = array(parts * HALO + 8, cols)
    first, second, top = pl.pallas_call(
        edge_kernel,
        out_shape=(edge_type, edge_type, array(8, LANES)),
        in_specs=[VMEM],
        out_specs=(VMEM,) * 3,
        compiler_params=params(4),
        name="edge",
    )(state)
    second = swapped_pairs(second, "gx", 1)
    first = swapped_pairs(first, "gx", 0)
    far = swapped_threes(top, "gx"), swapped_bit(top, "gx", 4)
    side_type = array(tall // 2, LANES)
    up, down, first, second, top = pl.pallas_call(
        pack_kernel,
        out_shape=(edge_type, edge_type, side_type, side_type, array(8, LANES)),
        in_specs=[VMEM] * 6,
        out_specs=(VMEM,) * 5,
        compiler_params=params(4),
        name="pack",
    )(state, second, *far, first, top)
    second = swapped_pairs(second, "gy", 1)
    first = swapped_pairs(first, "gy", 0)
    far = swapped_bit(top, "gy", 2)
    wide = groups * LANES
    cells, halo_select, back_select, top = pl.pallas_call(
        deal_kernel,
        out_shape=(
            array(parts * tall, wide),
            jax.ShapeDtypeStruct((wide - cols, wide), jnp.bfloat16),
            jax.ShapeDtypeStruct((wide, cols), jnp.bfloat16),
            array(8, LANES),
        ),
        in_specs=[VMEM] * 4,
        out_specs=(VMEM,) * 4,
        scratch_shapes=[pltpu.VMEM((parts * tall, cols), jnp.float32)],
        compiler_params=params(8),
        cost_estimate=pl.CostEstimate(flops=300_000_000, bytes_accessed=1_500_000, transcendentals=0),
        name="deal",
    )(state, up, down, top)
    top = pl.pallas_call(
        join_kernel,
        out_shape=array(8, LANES),
        in_specs=[VMEM] * 4,
        out_specs=VMEM,
        compiler_params=params(4),
        name="join",
    )(second, first, far, top)
    for axis, covered in (("gy", 4), ("gx", 8)):
        while covered < lax.axis_size(axis):
            top = jnp.maximum(top, sent(top, axis, covered))
            covered *= 2
    mate = swapped_bit(top, "gx", 1)
    dealt_type = array(parts, tall // 8, groups, 8, LANES)
    dealt = pltpu.VMEM(dealt_type.shape, jnp.float32)
    plain = pltpu.VMEM((parts, groups, tall, LANES), jnp.float32)
    field, change = pl.pallas_call(
        first_kernel,
        out_shape=(dealt_type, dealt_type),
        in_specs=[VMEM] * 4,
        out_specs=(VMEM,) * 2,
        scratch_shapes=[pltpu.VMEM((parts * tall, LANES), jnp.float32), plain],
        compiler_params=params(16),
        cost_estimate=pl.CostEstimate(flops=20_000_000, bytes_accessed=2_000_000, transcendentals=400_000),
        name="first",
    )(cells, halo_select, second, first)
    return pl.pallas_call(
        steps_kernel,
        out_shape=array(parts, rows, cols),
        in_specs=[VMEM] * 5,
        out_specs=pl.BlockSpec(memory_space=pl.ANY),
        scratch_shapes=[dealt]
        + [plain, pltpu.VMEM((parts, rows, cols), jnp.float32), pltpu.SemaphoreType.DMA((parts,))],
        compiler_params=params(16),
        name="steps",
    )(field, change, back_select, top, mate)


def solution(mesh):
    in_specs = (P(None, "gx", "gy"),)
    out_specs = P(None, "gx", "gy")
    return jax.shard_map(local, mesh=mesh, in_specs=in_specs, out_specs=out_specs, check_vma=False)
```

```python
import functools
import math

import jax
import jax.numpy as jnp
from jax import lax
from jax.experimental import pallas as pl
from jax.experimental.pallas import tpu as pltpu
from jax.sharding import PartitionSpec as P

STEPS = 4
HALO = 4 * STEPS
LANES = 128
GAMMA = 1.4
COURANT = 0.35
TINY = 1e-30

VMEM = pl.BlockSpec(memory_space=pltpu.VMEM)


def params(limit):
    return pltpu.CompilerParams(vmem_limit_bytes=limit << 20)


def array(*shape):
    return jax.ShapeDtypeStruct(shape, jnp.float32)


def iota(shape, dim):
    return lax.broadcasted_iota(jnp.int32, shape, dim)


def odd(axis):
    return lax.rem(lax.axis_index(axis), 2) == 1


def edge_kernel(block_ref, rows_ref, top_ref):
    rows = block_ref.shape[1]
    density, mom_x, mom_y, energy = (block_ref[comp] for comp in range(4))
    inv = 1.0 / density
    pressure = (GAMMA - 1.0) * (energy - 0.5 * (mom_x * mom_x + mom_y * mom_y) * inv)
    speed = jnp.maximum(jnp.abs(mom_x * inv), jnp.abs(mom_y * inv)) + jnp.sqrt(GAMMA * pressure * inv)
    top = jnp.max(speed)
    is_odd = odd("gx")
    for comp in range(4):
        head = block_ref[comp, 0:HALO, :]
        tail = block_ref[comp, rows - HALO : rows, :]
        rows_ref[comp * HALO : (comp + 1) * HALO, :] = jnp.where(is_odd, tail, head)
    rows_ref[4 * HALO :, :] = jnp.full((8, rows_ref.shape[1]), top)
    top_ref[...] = jnp.full(top_ref.shape, top)


def pack_kernel(state_ref, next_ref, three_ref, four_ref, mate_ref, own_ref, up_ref, down_ref, first_ref, second_ref, top_ref):
    rows = state_ref.shape[1]
    cols = state_ref.shape[2]
    half = rows // 2 + HALO
    lane = iota((half, LANES), 1)
    is_odd = odd("gx")
    for comp in range(4):
        span = slice(comp * HALO, (comp + 1) * HALO)
        up_ref[span, :] = jnp.where(is_odd, mate_ref[comp, rows - HALO : rows, :], next_ref[span, :])
        down_ref[span, :] = jnp.where(is_odd, next_ref[span, :], mate_ref[comp, 0:HALO, :])
    top = jnp.maximum(jnp.maximum(own_ref[...], next_ref[4 * HALO :, 0:LANES]), jnp.maximum(three_ref[...], four_ref[...]))

    def edge(low, at):
        lanes = slice(low, low + LANES)
        total = jnp.zeros((half, LANES), jnp.float32)
        for side in range(2):
            for comp in range(4):
                span = slice(comp * HALO, (comp + 1) * HALO)
                if side == 0:
                    cells = jnp.concatenate([up_ref[span, lanes], state_ref[comp, 0 : rows // 2, lanes]], axis=0)
                else:
                    cells = jnp.concatenate([state_ref[comp, rows // 2 : rows, lanes], down_ref[span, lanes]], axis=0)
                goal = side * (LANES // 2) + comp * HALO
                moved = pltpu.roll(cells, (goal - at) % LANES, axis=1)
                total = jnp.where((lane >= goal) & (lane < goal + HALO), moved, total)
        return total

    left = edge(0, 0)
    right = edge(cols - LANES, LANES - HALO)
    free = (iota((half, LANES), 0) == 0) & (lane < LANES // 2)
    under = jnp.concatenate([top] * (half // 8), axis=0)
    left = jnp.where(free, under, left)
    right = jnp.where(free, under, right)
    is_odd = odd("gy")
    first_ref[...] = jnp.where(is_odd, left, right)
    second_ref[...] = jnp.where(is_odd, right, left)
    top_ref[...] = top


def selected(values, select):
    rows = values.shape[0]
    parts = []
    for _ in range(3):
        parts.append(values.astype(jnp.bfloat16))
        values = values - parts[-1].astype(jnp.float32)
    found = jnp.dot(jnp.concatenate(parts, axis=0), select, preferred_element_type=jnp.float32)
    return (found[0:rows] + found[rows : 2 * rows]) + found[2 * rows :]


def minmod(first, second):
    low = jnp.minimum(first, second)
    high = jnp.maximum(first, second)
    return jnp.maximum(low, jnp.minimum(high, 0.0))


MOMENTUM = math.sqrt(0.5 * (GAMMA - 1.0))
SCALES = (1.0, MOMENTUM, MOMENTUM, GAMMA - 1.0)


def known(state):
    density, normal, tangent, energy = state
    inv = pl.reciprocal(density, approx=True)
    vel = normal * inv
    pressure = energy - (normal * normal + tangent * tangent) * inv
    square = jnp.maximum((GAMMA * MOMENTUM * MOMENTUM) * pressure * inv, TINY)
    return state, vel, pressure, pressure * vel, jnp.abs(vel) + square * lax.rsqrt(square)


def face(left, right):
    (left_state, left_vel, left_pressure, left_work, left_speed) = left
    (right_state, right_vel, right_pressure, right_work, right_speed) = right
    top = jnp.maximum(left_speed, right_speed)
    left_rate = left_vel + top
    right_rate = right_vel - top
    flux = [left_rate * left_state[comp] + right_rate * right_state[comp] for comp in range(4)]
    flux[1] = flux[1] + (MOMENTUM * MOMENTUM) * (left_pressure + right_pressure)
    flux[3] = flux[3] + (GAMMA - 1.0) * (left_work + right_work)
    return flux


def minus(first, second):
    return [first[comp] - second[comp] for comp in range(4)]


def rolled(tree, by, axis):
    return jax.tree.map(lambda value: pltpu.roll(value, by % value.shape[axis], axis=axis), tree)


def cell(whole, jump_before, jump_after):
    slope = [minmod(jump_before[comp], jump_after[comp]) for comp in range(4)]
    return known(minus(whole, slope)), known([whole[comp] + slope[comp] for comp in range(4)])


def row_changes(values, wholes):
    count = len(values)
    end_jump = minus(rolled(values[0], -1, 1), values[-1])
    jumps = [minus(values[at + 1], values[at]) for at in range(count - 1)] + [end_jump]
    faces, first_low, high = [], None, None
    for at in range(count):
        jump = jumps[at - 1] if at else minus(values[0], rolled(values[-1], 1, 1))
        low, next_high = cell(wholes[at], jump, jumps[at])
        if at:
            faces.append(face(high, low))
        else:
            first_low = low
        high = next_high
    faces.append(face(high, known(rolled(first_low[0], -1, 1))))
    return [minus(faces[at], faces[at - 1] if at else rolled(faces[-1], 1, 1)) for at in range(count)]


class Column:
    def __init__(self, count, begin, here, after):
        self.count, self.begin = count, begin
        self.jump = self.first_jump = minus(after, here)
        self.before = here
        self.first_low = self.first_flux = self.last_flux = self.high = None

    def feed(self, row, here, whole, after):
        next_row = (row + 1) % self.count
        if after is None:
            next_jump = self.first_jump
        else:
            next_jump = minus(rolled(after, -1, 0) if next_row == 0 else after, here)
        jump = minus(here, rolled(self.before, 1, 0)) if row == 0 else self.jump
        low, high = cell(whole, jump, next_jump)
        done = []
        if self.first_low is None:
            self.first_low = low
        else:
            flux = face(known(rolled(self.high[0], 1, 0)) if row == 0 else self.high, low)
            if self.last_flux is None:
                self.first_flux = flux
            else:
                seen = rolled(flux, -1, 0) if row == 0 else flux
                done.append(((row - 1) % self.count, minus(seen, self.last_flux)))
            self.last_flux = flux
        self.high, self.jump, self.before = high, next_jump, here
        if after is None:
            flux = face(high, self.first_low)
            done.append((row, minus(flux, self.last_flux)))
            done.append(((row + 1) % self.count, minus(self.first_flux, flux)))
        return done


Y_ORDER = (0, 2, 1, 3)


def changes(load, rows, cols, begin, store):
    along_y = {}
    values = {at: [load((begin + at) % rows, col) for col in range(cols)] for at in range(2)}
    columns = [Column(rows, begin, values[0][col], values[1][col]) for col in range(cols)]
    for at in range(1, rows + 1):
        row = (begin + at) % rows
        here = values.pop(at)
        if at < rows:
            values[at + 1] = [load((row + 1) % rows, col) for col in range(cols)]
        whole = [[part + part for part in value] for value in here]
        ready = []
        for col in range(cols):
            after = values[at + 1][col] if at < rows else None
            ready += [(col, *item) for item in columns[col].feed(row, here[col], whole[col], after)]
        along_y[row] = row_changes(*([[part[comp] for comp in Y_ORDER] for part in value] for value in (here, whole)))
        for col, done, parts in ready:
            other = along_y[done][col]
            store(done, col, [parts[comp] + other[Y_ORDER[comp]] for comp in range(4)])


def place_of(lane, group, groups):
    return groups * lane + group


def deal_kernel(state_ref, up_ref, down_ref, own_ref, dealt_ref, halo_select_ref, back_select_ref, top_ref, plain):
    top_ref[...] = own_ref[...]
    rows, cols = state_ref.shape[1:]
    tall = rows + 2 * HALO
    wide = dealt_ref.shape[1]
    groups = wide // LANES
    for comp in range(4):
        span = slice(comp * HALO, (comp + 1) * HALO)
        low = comp * tall
        plain[low : low + HALO, :] = up_ref[span, :]
        plain[low + HALO : low + HALO + rows, :] = state_ref[comp]
        plain[low + HALO + rows : low + tall, :] = down_ref[span, :]
    source = iota((wide, wide), 0)
    goal = iota((wide, wide), 1)
    place = place_of(goal % LANES, goal // LANES, groups)
    place = jnp.where(place < cols + 2 * HALO, (place + wide - HALO) % wide, 0)
    select = jnp.where(source == place, 1.0, 0.0).astype(jnp.bfloat16)
    dealt_ref[...] = selected(plain[...], select[0:cols])
    halo_select_ref[...] = select[cols:]
    source = iota((wide, cols), 0)
    goal = iota((wide, cols), 1)
    back = place_of(source % LANES, source // LANES, groups) == goal + HALO
    back_select_ref[...] = jnp.where(back, 1.0, 0.0).astype(jnp.bfloat16)


def join_kernel(next_ref, swap_ref, far_ref, own_ref, top_ref):
    speeds = jnp.maximum(next_ref[0:8, :], swap_ref[0:8, :])
    carried = (iota((8, LANES), 0) == 0) & (iota((8, LANES), 1) < LANES // 2)
    known_here = jnp.maximum(own_ref[...], far_ref[...])
    top_ref[...] = jnp.full((8, LANES), jnp.max(jnp.where(carried, speeds, known_here)))


def first_kernel(cells_ref, select_ref, next_ref, swap_ref, field_ref, change_ref, plain, dealt):
    half = next_ref.shape[0]
    tall = 2 * half
    groups = cells_ref.shape[1] // LANES
    lane = iota((half, LANES), 1)
    is_odd = odd("gy")
    from_swap = swap_ref[...]
    from_next = next_ref[...]
    from_before = jnp.where(is_odd, from_swap, from_next)
    from_after = jnp.where(is_odd, from_next, from_swap)
    for side in range(2):
        for comp in range(4):
            at = side * (LANES // 2) + comp * HALO
            left = pltpu.roll(from_before, (LANES - HALO - at) % LANES, axis=1)
            right = pltpu.roll(from_after, (-at) % LANES, axis=1)
            low = comp * tall + side * half
            plain[low : low + half, :] = jnp.where(lane < LANES // 2, right, left)
    found = cells_ref[...] + selected(plain[...], select_ref[...])
    for comp in range(4):
        for group in range(groups):
            cells = found[comp * tall : (comp + 1) * tall, group * LANES : (group + 1) * LANES]
            dealt[comp, group] = (0.5 * SCALES[comp]) * cells
    count = tall // 8
    for comp in range(4):
        for row in range(count):
            for group in range(groups):
                field_ref[comp, row, group] = dealt[comp, group, pl.ds(row, 8, stride=count), :]

    def store(row, col, parts):
        for comp in range(4):
            change_ref[comp, row, col] = parts[comp]

    def load(row, col):
        return [field_ref[comp, row, col] for comp in range(4)]

    changes(load, count, groups, 0, store)


def steps_kernel(field_ref, change_ref, select_ref, own_ref, mate_ref, out_ref, field, base, mid, dealt, result, sems):
    rows, cols = out_ref.shape[1:]
    tall = rows + 2 * HALO
    groups = field_ref.shape[2]
    scale = (0.125 * COURANT / MOMENTUM) / jnp.max(jnp.maximum(own_ref[...], mate_ref[...]))
    scales = (1.0, scale, scale, scale * scale)

    def one_step(start, count, old, first_changes):
        def to_mid(row, col, parts):
            for comp in range(4):
                cells, move = old[comp, row, col], parts[comp]
                if first_changes is not None:
                    cells, move = scales[comp] * cells, (scales[comp] * scale) * move
                moved = cells - move
                base[comp, row, col] = moved
                mid[comp, row, col] = moved - move

        def to_field(row, col, parts):
            for comp in range(4):
                new = base[comp, row, col] - parts[comp]
                dealt[comp, col, pl.ds(start + row, 8, stride=count), :] = new

        def load_from(ref):
            return lambda row, col: [ref[comp, row, col] for comp in range(4)]

        if first_changes is not None:
            for row in range(count):
                for col in range(groups):
                    to_mid(row, col, [first_changes[comp, row, col] for comp in range(4)])
        else:
            for comp in range(4):
                for row in range(count):
                    for col in range(groups):
                        old[comp, row, col] = dealt[comp, col, pl.ds(start + row, 8, stride=count), :]
            changes(load_from(old), count, groups, 0, to_mid)
        changes(load_from(mid), count, groups, count // 2, to_field)

    one_step(0, tall // 8, field_ref, change_ref)
    for index in range(1, STEPS):
        one_step(4 * index, (tall - 8 * index) // 8, field, None)

    wide = groups * LANES
    lane = iota((rows, LANES), 1)
    parts = []
    for comp in range(4):
        line = []
        for group in range(groups):
            place = place_of(lane, group, groups)
            inside = (place >= HALO) & (place < HALO + cols)
            line.append(jnp.where(inside, dealt[comp, group, HALO : HALO + rows, :], 0.0))
        parts.append(jnp.concatenate(line, axis=1))
    found = selected(jnp.concatenate(parts, axis=0), select_ref[...])
    copies = []
    for comp in range(4):
        result[comp] = ((2.0 / SCALES[comp]) / scales[comp]) * found[comp * rows : (comp + 1) * rows, :]
        copies.append(pltpu.make_async_copy(result.at[comp], out_ref.at[comp], sems.at[comp]))
        copies[-1].start()
    for copy in copies:
        copy.wait()


def local(state):
    parts, rows, cols = state.shape
    tall = rows + 2 * HALO
    groups = -(-(cols + 2 * HALO) // LANES)

    def sent(value, axis, by):
        count = lax.axis_size(axis)
        return lax.ppermute(value, axis, [(i, (i + by) % count) for i in range(count)])

    def swapped_bit(value, axis, by):
        return lax.ppermute(value, axis, [(i, i ^ by) for i in range(lax.axis_size(axis))])

    def swapped_pairs(value, axis, first):
        count = lax.axis_size(axis)
        pairs = []
        for low in range(first, count, 2):
            high = (low + 1) % count
            pairs += [(low, high), (high, low)]
        return lax.ppermute(value, axis, pairs)

    def swapped_threes(value, axis):
        count = lax.axis_size(axis)
        return lax.ppermute(value, axis, [(i, (i + 3 - 6 * (i % 2)) % count) for i in range(count)])

    edge_type = array(parts * HALO, cols)
    mate = swapped_pairs(state, "gx", 0)
    second, top = pl.pallas_call(
        edge_kernel,
        out_shape=(array(parts * HALO + 8, cols), array(8, LANES)),
        in_specs=[VMEM],
        out_specs=(VMEM,) * 2,
        compiler_params=params(4),
        name="edge",
    )(state)
    second = swapped_pairs(second, "gx", 1)
    far = swapped_threes(top, "gx"), swapped_bit(top, "gx", 4)
    side_type = array(tall // 2, LANES)
    up, down, first, second, top = pl.pallas_call(
        pack_kernel,
        out_shape=(edge_type, edge_type, side_type, side_type, array(8, LANES)),
        in_specs=[VMEM] * 6,
        out_specs=(VMEM,) * 5,
        compiler_params=params(4),
        name="pack",
    )(state, second, *far, mate, top)
    second = swapped_pairs(second, "gy", 1)
    first = swapped_pairs(first, "gy", 0)
    far = swapped_bit(top, "gy", 2)
    wide = groups * LANES
    cells, halo_select, back_select, top = pl.pallas_call(
        deal_kernel,
        out_shape=(
            array(parts * tall, wide),
            jax.ShapeDtypeStruct((wide - cols, wide), jnp.bfloat16),
            jax.ShapeDtypeStruct((wide, cols), jnp.bfloat16),
            array(8, LANES),
        ),
        in_specs=[VMEM] * 4,
        out_specs=(VMEM,) * 4,
        scratch_shapes=[pltpu.VMEM((parts * tall, cols), jnp.float32)],
        compiler_params=params(8),
        cost_estimate=pl.CostEstimate(flops=300_000_000, bytes_accessed=1_500_000, transcendentals=0),
        name="deal",
    )(state, up, down, top)
    top = pl.pallas_call(
        join_kernel,
        out_shape=array(8, LANES),
        in_specs=[VMEM] * 4,
        out_specs=VMEM,
        compiler_params=params(4),
        name="join",
    )(second, first, far, top)
    for axis, covered in (("gy", 4), ("gx", 8)):
        while covered < lax.axis_size(axis):
            top = jnp.maximum(top, sent(top, axis, covered))
            covered *= 2
    top_of_mate = swapped_bit(top, "gx", 1)
    dealt_type = array(parts, tall // 8, groups, 8, LANES)
    dealt = pltpu.VMEM(dealt_type.shape, jnp.float32)
    plain = pltpu.VMEM((parts, groups, tall, LANES), jnp.float32)
    field, change = pl.pallas_call(
        first_kernel,
        out_shape=(dealt_type, dealt_type),
        in_specs=[VMEM] * 4,
        out_specs=(VMEM,) * 2,
        scratch_shapes=[pltpu.VMEM((parts * tall, LANES), jnp.float32), plain],
        compiler_params=params(16),
        cost_estimate=pl.CostEstimate(flops=20_000_000, bytes_accessed=2_000_000, transcendentals=400_000),
        name="first",
    )(cells, halo_select, second, first)
    return pl.pallas_call(
        steps_kernel,
        out_shape=array(parts, rows, cols),
        in_specs=[VMEM] * 5,
        out_specs=pl.BlockSpec(memory_space=pl.ANY),
        scratch_shapes=[dealt] * 3
        + [plain, pltpu.VMEM((parts, rows, cols), jnp.float32), pltpu.SemaphoreType.DMA((parts,))],
        compiler_params=params(16),
        name="steps",
    )(field, change, back_select, top, top_of_mate)


def solution(mesh):
    in_specs = (P(None, "gx", "gy"),)
    out_specs = P(None, "gx", "gy")
    return jax.shard_map(local, mesh=mesh, in_specs=in_specs, out_specs=out_specs, check_vma=False)
```

```python
import functools
import math

import jax
import jax.numpy as jnp
from jax import lax
from jax.experimental import pallas as pl
from jax.experimental.pallas import tpu as pltpu
from jax.sharding import PartitionSpec as P

STEPS = 4
HALO = 4 * STEPS
LANES = 128
GAMMA = 1.4
COURANT = 0.35
TINY = 1e-30
MARGIN = 8

VMEM = pl.BlockSpec(memory_space=pltpu.VMEM)


def params(limit):
    return pltpu.CompilerParams(vmem_limit_bytes=limit << 20)


def array(*shape):
    return jax.ShapeDtypeStruct(shape, jnp.float32)


def iota(shape, dim):
    return lax.broadcasted_iota(jnp.int32, shape, dim)


def odd(axis):
    return lax.rem(lax.axis_index(axis), 2) == 1


def edge_kernel(block_ref, first_ref, second_ref, top_ref):
    rows = block_ref.shape[1]
    density, mom_x, mom_y, energy = (block_ref[comp] for comp in range(4))
    inv = 1.0 / density
    pressure = (GAMMA - 1.0) * (energy - 0.5 * (mom_x * mom_x + mom_y * mom_y) * inv)
    speed = jnp.maximum(jnp.abs(mom_x * inv), jnp.abs(mom_y * inv)) + jnp.sqrt(GAMMA * pressure * inv)
    top = jnp.max(speed)
    is_odd = odd("gx")
    for comp in range(4):
        span = slice(comp * HALO, (comp + 1) * HALO)
        head = block_ref[comp, 0:HALO, :]
        tail = block_ref[comp, rows - HALO : rows, :]
        first_ref[span, :] = jnp.where(is_odd, head, tail)
        second_ref[span, :] = jnp.where(is_odd, tail, head)
    first_ref[4 * HALO :, :] = jnp.full((8, first_ref.shape[1]), top)
    second_ref[4 * HALO :, :] = jnp.full((8, second_ref.shape[1]), top)
    top_ref[...] = jnp.full(top_ref.shape, top)


def pack_kernel(state_ref, next_ref, three_ref, four_ref, swap_ref, own_ref, up_ref, down_ref, first_ref, second_ref, top_ref):
    rows = state_ref.shape[1]
    cols = state_ref.shape[2]
    half = rows // 2 + HALO
    lane = iota((half, LANES), 1)
    is_odd = odd("gx")
    up_ref[...] = jnp.where(is_odd, swap_ref[...], next_ref[...])
    down_ref[...] = jnp.where(is_odd, next_ref[...], swap_ref[...])
    top = jnp.maximum(jnp.maximum(own_ref[...], jnp.maximum(three_ref[...], four_ref[...])),
                      jnp.maximum(up_ref[4 * HALO :, 0:LANES], down_ref[4 * HALO :, 0:LANES]))

    def edge(low, at):
        lanes = slice(low, low + LANES)
        total = jnp.zeros((half, LANES), jnp.float32)
        for side in range(2):
            for comp in range(4):
                span = slice(comp * HALO, (comp + 1) * HALO)
                if side == 0:
                    cells = jnp.concatenate([up_ref[span, lanes], state_ref[comp, 0 : rows // 2, lanes]], axis=0)
                else:
                    cells = jnp.concatenate([state_ref[comp, rows // 2 : rows, lanes], down_ref[span, lanes]], axis=0)
                goal = side * (LANES // 2) + comp * HALO
                moved = pltpu.roll(cells, (goal - at) % LANES, axis=1)
                total = jnp.where((lane >= goal) & (lane < goal + HALO), moved, total)
        return total

    left = edge(0, 0)
    right = edge(cols - LANES, LANES - HALO)
    free = (iota((half, LANES), 0) == 0) & (lane < LANES // 2)
    under = jnp.concatenate([top] * (half // 8), axis=0)
    left = jnp.where(free, under, left)
    right = jnp.where(free, under, right)
    is_odd = odd("gy")
    first_ref[...] = jnp.where(is_odd, left, right)
    second_ref[...] = jnp.where(is_odd, right, left)
    top_ref[...] = top


def selected(values, select):
    rows = values.shape[0]
    parts = []
    for _ in range(3):
        parts.append(values.astype(jnp.bfloat16))
        values = values - parts[-1].astype(jnp.float32)
    found = jnp.dot(jnp.concatenate(parts, axis=0), select, preferred_element_type=jnp.float32)
    return (found[0:rows] + found[rows : 2 * rows]) + found[2 * rows :]


def minmod(first, second):
    low = jnp.minimum(first, second)
    high = jnp.maximum(first, second)
    return jnp.maximum(low, jnp.minimum(high, 0.0))


MOMENTUM = math.sqrt(0.5 * (GAMMA - 1.0))
SCALES = (1.0, MOMENTUM, MOMENTUM, GAMMA - 1.0)


def known(state):
    density, normal, tangent, energy = state
    inv = pl.reciprocal(density, approx=True)
    vel = normal * inv
    pressure = energy - (normal * normal + tangent * tangent) * inv
    square = jnp.maximum((GAMMA * MOMENTUM * MOMENTUM) * pressure * inv, TINY)
    return state, vel, pressure, pressure * vel, jnp.abs(vel) + square * lax.rsqrt(square)


def face(left, right):
    (left_state, left_vel, left_pressure, left_work, left_speed) = left
    (right_state, right_vel, right_pressure, right_work, right_speed) = right
    top = jnp.maximum(left_speed, right_speed)
    left_rate = left_vel + top
    right_rate = right_vel - top
    flux = [left_rate * left_state[comp] + right_rate * right_state[comp] for comp in range(4)]
    flux[1] = flux[1] + (MOMENTUM * MOMENTUM) * (left_pressure + right_pressure)
    flux[3] = flux[3] + (GAMMA - 1.0) * (left_work + right_work)
    return flux


def minus(first, second):
    return [first[comp] - second[comp] for comp in range(4)]


def rolled(tree, by, axis):
    return jax.tree.map(lambda value: pltpu.roll(value, by % value.shape[axis], axis=axis), tree)


def cell(whole, jump_before, jump_after):
    slope = [minmod(jump_before[comp], jump_after[comp]) for comp in range(4)]
    return known(minus(whole, slope)), known([whole[comp] + slope[comp] for comp in range(4)])


def row_changes(values, wholes):
    count = len(values)
    end_jump = minus(rolled(values[0], -1, 1), values[-1])
    jumps = [minus(values[at + 1], values[at]) for at in range(count - 1)] + [end_jump]
    faces, first_low, high = [], None, None
    for at in range(count):
        jump = jumps[at - 1] if at else minus(values[0], rolled(values[-1], 1, 1))
        low, next_high = cell(wholes[at], jump, jumps[at])
        if at:
            faces.append(face(high, low))
        else:
            first_low = low
        high = next_high
    faces.append(face(high, known(rolled(first_low[0], -1, 1))))
    return [minus(faces[at], faces[at - 1] if at else rolled(faces[-1], 1, 1)) for at in range(count)]


class Column:
    def __init__(self, count, jump):
        self.count, self.jump, self.high, self.flux = count, jump, None, None

    def feed(self, row, whole, next_jump):
        slope = [minmod(self.jump[comp], next_jump[comp]) for comp in range(4)]
        done = None
        if row >= 0:
            flux = face(self.high, known(minus(whole, slope)))
            done = minus(flux, self.flux) if row else None
            self.flux = flux
        if row < self.count:
            self.high = known([whole[comp] + slope[comp] for comp in range(4)])
        self.jump = next_jump
        return done


Y_ORDER = (0, 2, 1, 3)


def changes(load, rows, cols, store):
    along_y = {}
    here = [load(-1, col) for col in range(cols)]
    columns = [Column(rows, minus(here[col], load(-2, col))) for col in range(cols)]
    for row in range(-1, rows + 1):
        after = [load(row + 1, col) for col in range(cols)]
        whole = [[part + part for part in value] for value in here]
        ready = [columns[col].feed(row, whole[col], minus(after[col], here[col])) for col in range(cols)]
        if row > 0:
            for col in range(cols):
                other = along_y[row - 1][col]
                store(row - 1, col, [ready[col][comp] + other[Y_ORDER[comp]] for comp in range(4)])
        if 0 <= row < rows:
            along_y[row] = row_changes(*([[part[comp] for comp in Y_ORDER] for part in value] for value in (here, whole)))
        here = after


def strips(start, count, row):
    return pl.ds(MARGIN + start + row, 8, stride=count)


def place_of(lane, group, groups):
    return groups * lane + group


def deal_kernel(state_ref, up_ref, down_ref, own_ref, dealt_ref, halo_select_ref, back_select_ref, top_ref, plain):
    top_ref[...] = own_ref[...]
    rows, cols = state_ref.shape[1:]
    tall = rows + 2 * HALO
    wide = dealt_ref.shape[1]
    groups = wide // LANES
    for comp in range(4):
        span = slice(comp * HALO, (comp + 1) * HALO)
        low = comp * tall
        plain[low : low + HALO, :] = up_ref[span, :]
        plain[low + HALO : low + HALO + rows, :] = state_ref[comp]
        plain[low + HALO + rows : low + tall, :] = down_ref[span, :]
    source = iota((wide, wide), 0)
    goal = iota((wide, wide), 1)
    place = place_of(goal % LANES, goal // LANES, groups)
    place = jnp.where(place < cols + 2 * HALO, (place + wide - HALO) % wide, 0)
    select = jnp.where(source == place, 1.0, 0.0).astype(jnp.bfloat16)
    dealt_ref[...] = selected(plain[...], select[0:cols])
    halo_select_ref[...] = select[cols:]
    source = iota((wide, cols), 0)
    goal = iota((wide, cols), 1)
    back = place_of(source % LANES, source // LANES, groups) == goal + HALO
    back_select_ref[...] = jnp.where(back, 1.0, 0.0).astype(jnp.bfloat16)


def join_kernel(next_ref, swap_ref, far_ref, own_ref, top_ref):
    speeds = jnp.maximum(next_ref[0:8, :], swap_ref[0:8, :])
    carried = (iota((8, LANES), 0) == 0) & (iota((8, LANES), 1) < LANES // 2)
    known_here = jnp.maximum(own_ref[...], far_ref[...])
    top_ref[...] = jnp.full((8, LANES), jnp.max(jnp.where(carried, speeds, known_here)))


def first_kernel(cells_ref, select_ref, next_ref, swap_ref, field_ref, change_ref, plain):
    half = next_ref.shape[0]
    tall = 2 * half
    groups = cells_ref.shape[1] // LANES
    lane = iota((half, LANES), 1)
    is_odd = odd("gy")
    from_swap = swap_ref[...]
    from_next = next_ref[...]
    from_before = jnp.where(is_odd, from_swap, from_next)
    from_after = jnp.where(is_odd, from_next, from_swap)
    for side in range(2):
        for comp in range(4):
            at = side * (LANES // 2) + comp * HALO
            left = pltpu.roll(from_before, (LANES - HALO - at) % LANES, axis=1)
            right = pltpu.roll(from_after, (-at) % LANES, axis=1)
            low = comp * tall + side * half
            plain[low : low + half, :] = jnp.where(lane < LANES // 2, right, left)
    found = cells_ref[...] + selected(plain[...], select_ref[...])
    for comp in range(4):
        for group in range(groups):
            cells = found[comp * tall : (comp + 1) * tall, group * LANES : (group + 1) * LANES]
            field_ref[comp, group, MARGIN : MARGIN + tall, :] = (0.5 * SCALES[comp]) * cells
    count = tall // 8

    def store(row, col, parts):
        for comp in range(4):
            change_ref[comp, row, col] = parts[comp]

    def load(row, col):
        return [field_ref[comp, col, strips(0, count, row), :] for comp in range(4)]

    changes(load, count, groups, store)


def steps_kernel(field_ref, change_ref, select_ref, own_ref, mate_ref, out_ref, field, base, mid, result, sems):
    rows, cols = out_ref.shape[1:]
    tall = rows + 2 * HALO
    groups = field_ref.shape[1]
    scale = (0.125 * COURANT / MOMENTUM) / jnp.max(jnp.maximum(own_ref[...], mate_ref[...]))
    scales = (1.0, scale, scale, scale * scale)

    for index in range(STEPS):
        start = 4 * index
        count = (tall - 2 * start) // 8

        def to_mid(row, col, parts):
            rows_of = strips(start, count, row)
            for comp in range(4):
                cells, move = field[comp, col, rows_of, :] if index else field_ref[comp, col, rows_of, :], parts[comp]
                if index == 0:
                    cells, move = scales[comp] * cells, (scales[comp] * scale) * move
                moved = cells - move
                base[comp, col, rows_of, :] = moved
                mid[comp, col, rows_of, :] = moved - move

        def to_field(row, col, parts):
            rows_of = strips(start + 4, count - 1, row)
            for comp in range(4):
                field[comp, col, rows_of, :] = base[comp, col, rows_of, :] - parts[comp]

        def from_field(row, col):
            return [field[comp, col, strips(start, count, row), :] for comp in range(4)]

        def from_mid(row, col):
            return [mid[comp, col, strips(start + 4, count - 1, row), :] for comp in range(4)]

        if index == 0:
            for row in range(count):
                for col in range(groups):
                    to_mid(row, col, [change_ref[comp, row, col] for comp in range(4)])
        else:
            changes(from_field, count, groups, to_mid)
        changes(from_mid, count - 1, groups, to_field)

    wide = groups * LANES
    lane = iota((rows, LANES), 1)
    parts = []
    for comp in range(4):
        line = []
        for group in range(groups):
            place = place_of(lane, group, groups)
            inside = (place >= HALO) & (place < HALO + cols)
            line.append(jnp.where(inside, field[comp, group, MARGIN + HALO : MARGIN + HALO + rows, :], 0.0))
        parts.append(jnp.concatenate(line, axis=1))
    found = selected(jnp.concatenate(parts, axis=0), select_ref[...])
    copies = []
    for comp in range(4):
        result[comp] = ((2.0 / SCALES[comp]) / scales[comp]) * found[comp * rows : (comp + 1) * rows, :]
        copies.append(pltpu.make_async_copy(result.at[comp], out_ref.at[comp], sems.at[comp]))
        copies[-1].start()
    for copy in copies:
        copy.wait()


def local(state):
    parts, rows, cols = state.shape
    tall = rows + 2 * HALO
    groups = -(-(cols + 2 * HALO) // LANES)

    def sent(value, axis, by):
        count = lax.axis_size(axis)
        return lax.ppermute(value, axis, [(i, (i + by) % count) for i in range(count)])

    def swapped_bit(value, axis, by):
        return lax.ppermute(value, axis, [(i, i ^ by) for i in range(lax.axis_size(axis))])

    def swapped_pairs(value, axis, first):
        count = lax.axis_size(axis)
        pairs = []
        for low in range(first, count, 2):
            high = (low + 1) % count
            pairs += [(low, high), (high, low)]
        return lax.ppermute(value, axis, pairs)

    def swapped_threes(value, axis):
        count = lax.axis_size(axis)
        return lax.ppermute(value, axis, [(i, (i + 3 - 6 * (i % 2)) % count) for i in range(count)])

    edge_type = array(parts * HALO + 8, cols)
    first, second, top = pl.pallas_call(
        edge_kernel,
        out_shape=(edge_type, edge_type, array(8, LANES)),
        in_specs=[VMEM],
        out_specs=(VMEM,) * 3,
        compiler_params=params(4),
        name="edge",
    )(state)
    second = swapped_pairs(second, "gx", 1)
    first = swapped_pairs(first, "gx", 0)
    far = swapped_threes(top, "gx"), swapped_bit(top, "gx", 4)
    side_type = array(tall // 2, LANES)
    up, down, first, second, top = pl.pallas_call(
        pack_kernel,
        out_shape=(edge_type, edge_type, side_type, side_type, array(8, LANES)),
        in_specs=[VMEM] * 6,
        out_specs=(VMEM,) * 5,
        compiler_params=params(4),
        name="pack",
    )(state, second, *far, first, top)
    second = swapped_pairs(second, "gy", 1)
    first = swapped_pairs(first, "gy", 0)
    far = swapped_bit(top, "gy", 2)
    wide = groups * LANES
    cells, halo_select, back_select, top = pl.pallas_call(
        deal_kernel,
        out_shape=(
            array(parts * tall, wide),
            jax.ShapeDtypeStruct((wide - cols, wide), jnp.bfloat16),
            jax.ShapeDtypeStruct((wide, cols), jnp.bfloat16),
            array(8, LANES),
        ),
        in_specs=[VMEM] * 4,
        out_specs=(VMEM,) * 4,
        scratch_shapes=[pltpu.VMEM((parts * tall, cols), jnp.float32)],
        compiler_params=params(8),
        cost_estimate=pl.CostEstimate(flops=300_000_000, bytes_accessed=1_500_000, transcendentals=0),
        name="deal",
    )(state, up, down, top)
    top = pl.pallas_call(
        join_kernel,
        out_shape=array(8, LANES),
        in_specs=[VMEM] * 4,
        out_specs=VMEM,
        compiler_params=params(4),
        name="join",
    )(second, first, far, top)
    for axis, covered in (("gy", 4), ("gx", 8)):
        while covered < lax.axis_size(axis):
            top = jnp.maximum(top, sent(top, axis, covered))
            covered *= 2
    mate = swapped_bit(top, "gx", 1)
    change_type = array(parts, tall // 8, groups, 8, LANES)
    field_type = array(parts, groups, tall + 2 * MARGIN, LANES)
    stage_array = pltpu.VMEM(field_type.shape, jnp.float32)
    field, change = pl.pallas_call(
        first_kernel,
        out_shape=(field_type, change_type),
        in_specs=[VMEM] * 4,
        out_specs=(VMEM,) * 2,
        scratch_shapes=[pltpu.VMEM((parts * tall, LANES), jnp.float32)],
        compiler_params=params(16),
        cost_estimate=pl.CostEstimate(flops=20_000_000, bytes_accessed=2_000_000, transcendentals=400_000),
        name="first",
    )(cells, halo_select, second, first)
    return pl.pallas_call(
        steps_kernel,
        out_shape=array(parts, rows, cols),
        in_specs=[VMEM] * 5,
        out_specs=pl.BlockSpec(memory_space=pl.ANY),
        scratch_shapes=[stage_array] * 3
        + [pltpu.VMEM((parts, rows, cols), jnp.float32), pltpu.SemaphoreType.DMA((parts,))],
        compiler_params=params(16),
        name="steps",
    )(field, change, back_select, top, mate)


def solution(mesh):
    in_specs = (P(None, "gx", "gy"),)
    out_specs = P(None, "gx", "gy")
    return jax.shard_map(local, mesh=mesh, in_specs=in_specs, out_specs=out_specs, check_vma=False)
```

```python
import functools
import math

import jax
import jax.numpy as jnp
from jax import lax
from jax.experimental import pallas as pl
from jax.experimental.pallas import tpu as pltpu
from jax.sharding import PartitionSpec as P

STEPS = 4
HALO = 4 * STEPS
LANES = 128
GAMMA = 1.4
COURANT = 0.35
TINY = 1e-30

VMEM = pl.BlockSpec(memory_space=pltpu.VMEM)


def params(limit):
    return pltpu.CompilerParams(vmem_limit_bytes=limit << 20)


def array(*shape):
    return jax.ShapeDtypeStruct(shape, jnp.float32)


def iota(shape, dim):
    return lax.broadcasted_iota(jnp.int32, shape, dim)


def odd(axis):
    return lax.rem(lax.axis_index(axis), 2) == 1


def edge_kernel(block_ref, first_ref, second_ref, top_ref):
    rows = block_ref.shape[1]
    density, mom_x, mom_y, energy = (block_ref[comp] for comp in range(4))
    inv = 1.0 / density
    pressure = (GAMMA - 1.0) * (energy - 0.5 * (mom_x * mom_x + mom_y * mom_y) * inv)
    speed = jnp.maximum(jnp.abs(mom_x * inv), jnp.abs(mom_y * inv)) + jnp.sqrt(GAMMA * pressure * inv)
    top = jnp.max(speed)
    is_odd = odd("gx")
    for comp in range(4):
        span = slice(comp * HALO, (comp + 1) * HALO)
        head = block_ref[comp, 0:HALO, :]
        tail = block_ref[comp, rows - HALO : rows, :]
        first_ref[span, :] = jnp.where(is_odd, head, tail)
        second_ref[span, :] = jnp.where(is_odd, tail, head)
    first_ref[4 * HALO :, :] = jnp.full((8, first_ref.shape[1]), top)
    second_ref[4 * HALO :, :] = jnp.full((8, second_ref.shape[1]), top)
    top_ref[...] = jnp.full(top_ref.shape, top)


def pack_kernel(state_ref, next_ref, three_ref, four_ref, swap_ref, own_ref, up_ref, down_ref, first_ref, second_ref, top_ref):
    rows = state_ref.shape[1]
    cols = state_ref.shape[2]
    half = rows // 2 + HALO
    lane = iota((half, LANES), 1)
    is_odd = odd("gx")
    up_ref[...] = jnp.where(is_odd, swap_ref[...], next_ref[...])
    down_ref[...] = jnp.where(is_odd, next_ref[...], swap_ref[...])
    top = jnp.maximum(jnp.maximum(own_ref[...], jnp.maximum(three_ref[...], four_ref[...])),
                      jnp.maximum(up_ref[4 * HALO :, 0:LANES], down_ref[4 * HALO :, 0:LANES]))

    def edge(low, at):
        lanes = slice(low, low + LANES)
        total = jnp.zeros((half, LANES), jnp.float32)
        for side in range(2):
            for comp in range(4):
                span = slice(comp * HALO, (comp + 1) * HALO)
                if side == 0:
                    cells = jnp.concatenate([up_ref[span, lanes], state_ref[comp, 0 : rows // 2, lanes]], axis=0)
                else:
                    cells = jnp.concatenate([state_ref[comp, rows // 2 : rows, lanes], down_ref[span, lanes]], axis=0)
                goal = side * (LANES // 2) + comp * HALO
                moved = pltpu.roll(cells, (goal - at) % LANES, axis=1)
                total = jnp.where((lane >= goal) & (lane < goal + HALO), moved, total)
        return total

    left = edge(0, 0)
    right = edge(cols - LANES, LANES - HALO)
    free = (iota((half, LANES), 0) == 0) & (lane < LANES // 2)
    under = jnp.concatenate([top] * (half // 8), axis=0)
    left = jnp.where(free, under, left)
    right = jnp.where(free, under, right)
    is_odd = odd("gy")
    first_ref[...] = jnp.where(is_odd, left, right)
    second_ref[...] = jnp.where(is_odd, right, left)
    top_ref[...] = top


def selected(lists, select):
    rows = lists[0].shape[0]
    parts = []
    for values in lists:
        for _ in range(3):
            parts.append(values.astype(jnp.bfloat16))
            values = values - parts[-1].astype(jnp.float32)
    found = jnp.dot(jnp.concatenate(parts, axis=0), select, preferred_element_type=jnp.float32)
    thirds = [found[at * rows : (at + 1) * rows] for at in range(len(parts))]
    return [(thirds[at] + thirds[at + 1]) + thirds[at + 2] for at in range(0, len(parts), 3)]


def minmod(first, second):
    low = jnp.minimum(first, second)
    high = jnp.maximum(first, second)
    return jnp.maximum(low, jnp.minimum(high, 0.0))


MOMENTUM = math.sqrt(0.5 * (GAMMA - 1.0))
SCALES = (1.0, MOMENTUM, MOMENTUM, GAMMA - 1.0)


def known(state):
    density, normal, tangent, energy = state
    inv = pl.reciprocal(density, approx=True)
    vel = normal * inv
    pressure = energy - (normal * normal + tangent * tangent) * inv
    square = jnp.maximum((GAMMA * MOMENTUM * MOMENTUM) * pressure * inv, TINY)
    return state, vel, pressure, pressure * vel, jnp.abs(vel) + square * lax.rsqrt(square)


def face(left, right):
    (left_state, left_vel, left_pressure, left_work, left_speed) = left
    (right_state, right_vel, right_pressure, right_work, right_speed) = right
    top = jnp.maximum(left_speed, right_speed)
    left_rate = left_vel + top
    right_rate = right_vel - top
    flux = [left_rate * left_state[comp] + right_rate * right_state[comp] for comp in range(4)]
    flux[1] = flux[1] + (MOMENTUM * MOMENTUM) * (left_pressure + right_pressure)
    flux[3] = flux[3] + (GAMMA - 1.0) * (left_work + right_work)
    return flux


def minus(first, second):
    return [first[comp] - second[comp] for comp in range(4)]


def rolled(tree, by, axis):
    return jax.tree.map(lambda value: pltpu.roll(value, by % value.shape[axis], axis=axis), tree)


def cell(whole, jump_before, jump_after):
    slope = [minmod(jump_before[comp], jump_after[comp]) for comp in range(4)]
    return known(minus(whole, slope)), known([whole[comp] + slope[comp] for comp in range(4)])


def row_changes(values, wholes):
    count = len(values)
    end_jump = minus(rolled(values[0], -1, 1), values[-1])
    jumps = [minus(values[at + 1], values[at]) for at in range(count - 1)] + [end_jump]
    faces, first_low, high = [], None, None
    for at in range(count):
        jump = jumps[at - 1] if at else minus(values[0], rolled(values[-1], 1, 1))
        low, next_high = cell(wholes[at], jump, jumps[at])
        if at:
            faces.append(face(high, low))
        else:
            first_low = low
        high = next_high
    faces.append(face(high, known(rolled(first_low[0], -1, 1))))
    return [minus(faces[at], faces[at - 1] if at else rolled(faces[-1], 1, 1)) for at in range(count)]


class Column:
    def __init__(self, count, begin, here, after):
        self.count, self.begin = count, begin
        self.jump = self.first_jump = minus(after, here)
        self.before = here
        self.first_low = self.first_flux = self.last_flux = self.high = None

    def feed(self, row, here, whole, after):
        next_row = (row + 1) % self.count
        if after is None:
            next_jump = self.first_jump
        else:
            next_jump = minus(rolled(after, -1, 0) if next_row == 0 else after, here)
        jump = minus(here, rolled(self.before, 1, 0)) if row == 0 else self.jump
        low, high = cell(whole, jump, next_jump)
        done = []
        if self.first_low is None:
            self.first_low = low
        else:
            flux = face(known(rolled(self.high[0], 1, 0)) if row == 0 else self.high, low)
            if self.last_flux is None:
                self.first_flux = flux
            else:
                seen = rolled(flux, -1, 0) if row == 0 else flux
                done.append(((row - 1) % self.count, minus(seen, self.last_flux)))
            self.last_flux = flux
        self.high, self.jump, self.before = high, next_jump, here
        if after is None:
            flux = face(high, self.first_low)
            done.append((row, minus(flux, self.last_flux)))
            done.append(((row + 1) % self.count, minus(self.first_flux, flux)))
        return done


Y_ORDER = (0, 2, 1, 3)


def changes(load, rows, cols, begin, store):
    along_y = {}
    values = {at: [load((begin + at) % rows, col) for col in range(cols)] for at in range(2)}
    columns = [Column(rows, begin, values[0][col], values[1][col]) for col in range(cols)]
    for at in range(1, rows + 1):
        row = (begin + at) % rows
        here = values.pop(at)
        if at < rows:
            values[at + 1] = [load((row + 1) % rows, col) for col in range(cols)]
        whole = [[part + part for part in value] for value in here]
        ready = []
        for col in range(cols):
            after = values[at + 1][col] if at < rows else None
            ready += [(col, *item) for item in columns[col].feed(row, here[col], whole[col], after)]
        along_y[row] = row_changes(*([[part[comp] for comp in Y_ORDER] for part in value] for value in (here, whole)))
        for col, done, parts in ready:
            other = along_y[done][col]
            store(done, col, [parts[comp] + other[Y_ORDER[comp]] for comp in range(4)])


def place_of(lane, group, groups):
    return groups * lane + group


def deal_kernel(state_ref, up_ref, down_ref, own_ref, dealt_ref, halo_select_ref, back_select_ref, top_ref, plain):
    top_ref[...] = own_ref[...]
    rows, cols = state_ref.shape[1:]
    tall = rows + 2 * HALO
    wide = dealt_ref.shape[1]
    groups = wide // LANES
    for comp in range(4):
        span = slice(comp * HALO, (comp + 1) * HALO)
        low = comp * tall
        plain[low : low + HALO, :] = up_ref[span, :]
        plain[low + HALO : low + HALO + rows, :] = state_ref[comp]
        plain[low + HALO + rows : low + tall, :] = down_ref[span, :]
    source = iota((wide, wide), 0)
    goal = iota((wide, wide), 1)
    place = place_of(goal % LANES, goal // LANES, groups)
    place = jnp.where(place < cols + 2 * HALO, (place + wide - HALO) % wide, 0)
    select = jnp.where(source == place, 1.0, 0.0).astype(jnp.bfloat16)
    dealt_ref[...] = selected([plain[...]], select[0:cols])[0]
    halo_select_ref[...] = select[cols:]
    source = iota((wide, cols), 0)
    goal = iota((wide, cols), 1)
    back = place_of(source % LANES, source // LANES, groups) == goal + HALO
    back_select_ref[...] = jnp.where(back, 1.0, 0.0).astype(jnp.bfloat16)


def join_kernel(next_ref, swap_ref, far_ref, own_ref, top_ref):
    speeds = jnp.maximum(next_ref[0:8, :], swap_ref[0:8, :])
    carried = (iota((8, LANES), 0) == 0) & (iota((8, LANES), 1) < LANES // 2)
    known_here = jnp.maximum(own_ref[...], far_ref[...])
    top_ref[...] = jnp.full((8, LANES), jnp.max(jnp.where(carried, speeds, known_here)))


def first_kernel(cells_ref, select_ref, next_ref, swap_ref, field_ref, change_ref, plain, dealt):
    half = next_ref.shape[0]
    tall = 2 * half
    groups = cells_ref.shape[1] // LANES
    lane = iota((half, LANES), 1)
    is_odd = odd("gy")
    from_swap = swap_ref[...]
    from_next = next_ref[...]
    from_before = jnp.where(is_odd, from_swap, from_next)
    from_after = jnp.where(is_odd, from_next, from_swap)
    for side in range(2):
        for comp in range(4):
            at = side * (LANES // 2) + comp * HALO
            left = pltpu.roll(from_before, (LANES - HALO - at) % LANES, axis=1)
            right = pltpu.roll(from_after, (-at) % LANES, axis=1)
            low = comp * tall + side * half
            plain[low : low + half, :] = jnp.where(lane < LANES // 2, right, left)
    found = cells_ref[...] + selected([plain[...]], select_ref[...])[0]
    for comp in range(4):
        for group in range(groups):
            cells = found[comp * tall : (comp + 1) * tall, group * LANES : (group + 1) * LANES]
            dealt[comp, group] = (0.5 * SCALES[comp]) * cells
    count = tall // 8
    for comp in range(4):
        for row in range(count):
            for group in range(groups):
                field_ref[comp, row, group] = dealt[comp, group, pl.ds(row, 8, stride=count), :]

    def store(row, col, parts):
        for comp in range(4):
            change_ref[comp, row, col] = parts[comp]

    def load(row, col):
        return [field_ref[comp, row, col] for comp in range(4)]

    changes(load, count, groups, 0, store)


def steps_kernel(field_ref, change_ref, select_ref, own_ref, mate_ref, out_ref, field, base, mid, dealt, result, sems):
    rows, cols = out_ref.shape[1:]
    tall = rows + 2 * HALO
    groups = field_ref.shape[2]
    scale = (0.125 * COURANT / MOMENTUM) / jnp.max(jnp.maximum(own_ref[...], mate_ref[...]))
    scales = (1.0, scale, scale, scale * scale)

    def one_step(start, count, old, first_changes):
        def to_mid(row, col, parts):
            for comp in range(4):
                cells, move = old[comp, row, col], parts[comp]
                if first_changes is not None:
                    cells, move = scales[comp] * cells, (scales[comp] * scale) * move
                moved = cells - move
                base[comp, row, col] = moved
                mid[comp, row, col] = moved - move

        def to_field(row, col, parts):
            for comp in range(4):
                new = base[comp, row, col] - parts[comp]
                dealt[comp, col, pl.ds(start + row, 8, stride=count), :] = new

        def load_from(ref):
            return lambda row, col: [ref[comp, row, col] for comp in range(4)]

        if first_changes is not None:
            for row in range(count):
                for col in range(groups):
                    to_mid(row, col, [first_changes[comp, row, col] for comp in range(4)])
        else:
            for comp in range(4):
                for row in range(count):
                    for col in range(groups):
                        old[comp, row, col] = dealt[comp, col, pl.ds(start + row, 8, stride=count), :]
            changes(load_from(old), count, groups, 0, to_mid)
        changes(load_from(mid), count, groups, count // 2, to_field)

    one_step(0, tall // 8, field_ref, change_ref)
    for index in range(1, STEPS):
        one_step(4 * index, (tall - 8 * index) // 8, field, None)

    wide = groups * LANES
    lane = iota((rows, LANES), 1)
    parts = []
    for comp in range(4):
        line = []
        for group in range(groups):
            place = place_of(lane, group, groups)
            inside = (place >= HALO) & (place < HALO + cols)
            line.append(jnp.where(inside, dealt[comp, group, HALO : HALO + rows, :], 0.0))
        parts.append(jnp.concatenate(line, axis=1))
    found = selected(parts, select_ref[...])
    copies = []
    for comp in range(4):
        result[comp] = ((2.0 / SCALES[comp]) / scales[comp]) * found[comp]
        copies.append(pltpu.make_async_copy(result.at[comp], out_ref.at[comp], sems.at[comp]))
        copies[-1].start()
    for copy in copies:
        copy.wait()


def local(state):
    parts, rows, cols = state.shape
    tall = rows + 2 * HALO
    groups = -(-(cols + 2 * HALO) // LANES)

    def sent(value, axis, by):
        count = lax.axis_size(axis)
        return lax.ppermute(value, axis, [(i, (i + by) % count) for i in range(count)])

    def swapped_bit(value, axis, by):
        return lax.ppermute(value, axis, [(i, i ^ by) for i in range(lax.axis_size(axis))])

    def swapped_pairs(value, axis, first):
        count = lax.axis_size(axis)
        pairs = []
        for low in range(first, count, 2):
            high = (low + 1) % count
            pairs += [(low, high), (high, low)]
        return lax.ppermute(value, axis, pairs)

    def swapped_threes(value, axis):
        count = lax.axis_size(axis)
        return lax.ppermute(value, axis, [(i, (i + 3 - 6 * (i % 2)) % count) for i in range(count)])

    edge_type = array(parts * HALO + 8, cols)
    first, second, top = pl.pallas_call(
        edge_kernel,
        out_shape=(edge_type, edge_type, array(8, LANES)),
        in_specs=[VMEM],
        out_specs=(VMEM,) * 3,
        compiler_params=params(4),
        name="edge",
    )(state)
    second = swapped_pairs(second, "gx", 1)
    first = swapped_pairs(first, "gx", 0)
    far = swapped_threes(top, "gx"), swapped_bit(top, "gx", 4)
    side_type = array(tall // 2, LANES)
    up, down, first, second, top = pl.pallas_call(
        pack_kernel,
        out_shape=(edge_type, edge_type, side_type, side_type, array(8, LANES)),
        in_specs=[VMEM] * 6,
        out_specs=(VMEM,) * 5,
        compiler_params=params(4),
        name="pack",
    )(state, second, *far, first, top)
    second = swapped_pairs(second, "gy", 1)
    first = swapped_pairs(first, "gy", 0)
    far = swapped_bit(top, "gy", 2)
    wide = groups * LANES
    cells, halo_select, back_select, top = pl.pallas_call(
        deal_kernel,
        out_shape=(
            array(parts * tall, wide),
            jax.ShapeDtypeStruct((wide - cols, wide), jnp.bfloat16),
            jax.ShapeDtypeStruct((wide, cols), jnp.bfloat16),
            array(8, LANES),
        ),
        in_specs=[VMEM] * 4,
        out_specs=(VMEM,) * 4,
        scratch_shapes=[pltpu.VMEM((parts * tall, cols), jnp.float32)],
        compiler_params=params(8),
        cost_estimate=pl.CostEstimate(flops=300_000_000, bytes_accessed=1_500_000, transcendentals=0),
        name="deal",
    )(state, up, down, top)
    top = pl.pallas_call(
        join_kernel,
        out_shape=array(8, LANES),
        in_specs=[VMEM] * 4,
        out_specs=VMEM,
        compiler_params=params(4),
        name="join",
    )(second, first, far, top)
    for axis, covered in (("gy", 4), ("gx", 8)):
        while covered < lax.axis_size(axis):
            top = jnp.maximum(top, sent(top, axis, covered))
            covered *= 2
    mate = swapped_bit(top, "gx", 1)
    dealt_type = array(parts, tall // 8, groups, 8, LANES)
    dealt = pltpu.VMEM(dealt_type.shape, jnp.float32)
    plain = pltpu.VMEM((parts, groups, tall, LANES), jnp.float32)
    field, change = pl.pallas_call(
        first_kernel,
        out_shape=(dealt_type, dealt_type),
        in_specs=[VMEM] * 4,
        out_specs=(VMEM,) * 2,
        scratch_shapes=[pltpu.VMEM((parts * tall, LANES), jnp.float32), plain],
        compiler_params=params(16),
        cost_estimate=pl.CostEstimate(flops=20_000_000, bytes_accessed=2_000_000, transcendentals=400_000),
        name="first",
    )(cells, halo_select, second, first)
    return pl.pallas_call(
        steps_kernel,
        out_shape=array(parts, rows, cols),
        in_specs=[VMEM] * 5,
        out_specs=pl.BlockSpec(memory_space=pl.ANY),
        scratch_shapes=[dealt] * 3
        + [plain, pltpu.VMEM((parts, rows, cols), jnp.float32), pltpu.SemaphoreType.DMA((parts,))],
        compiler_params=params(16),
        name="steps",
    )(field, change, back_select, top, mate)


def solution(mesh):
    in_specs = (P(None, "gx", "gy"),)
    out_specs = P(None, "gx", "gy")
    return jax.shard_map(local, mesh=mesh, in_specs=in_specs, out_specs=out_specs, check_vma=False)
```

```python
import functools
import math

import jax
import jax.numpy as jnp
from jax import lax
from jax.experimental import pallas as pl
from jax.experimental.pallas import tpu as pltpu
from jax.sharding import PartitionSpec as P

STEPS = 4
HALO = 4 * STEPS
LANES = 128
GAMMA = 1.4
COURANT = 0.35
TINY = 1e-30

VMEM = pl.BlockSpec(memory_space=pltpu.VMEM)


def params(limit):
    return pltpu.CompilerParams(vmem_limit_bytes=limit << 20)


def array(*shape):
    return jax.ShapeDtypeStruct(shape, jnp.float32)


def iota(shape, dim):
    return lax.broadcasted_iota(jnp.int32, shape, dim)


def odd(axis):
    return lax.rem(lax.axis_index(axis), 2) == 1


def edge_kernel(block_ref, first_ref, second_ref, top_ref):
    rows = block_ref.shape[1]
    density, mom_x, mom_y, energy = (block_ref[comp] for comp in range(4))
    inv = 1.0 / density
    pressure = (GAMMA - 1.0) * (energy - 0.5 * (mom_x * mom_x + mom_y * mom_y) * inv)
    speed = jnp.maximum(jnp.abs(mom_x * inv), jnp.abs(mom_y * inv)) + jnp.sqrt(GAMMA * pressure * inv)
    top = jnp.max(speed)
    is_odd = odd("gx")
    for comp in range(4):
        span = slice(comp * HALO, (comp + 1) * HALO)
        head = block_ref[comp, 0:HALO, :]
        tail = block_ref[comp, rows - HALO : rows, :]
        first_ref[span, :] = jnp.where(is_odd, head, tail)
        second_ref[span, :] = jnp.where(is_odd, tail, head)
    first_ref[4 * HALO :, :] = jnp.full((8, first_ref.shape[1]), top)
    second_ref[4 * HALO :, :] = jnp.full((8, second_ref.shape[1]), top)
    top_ref[...] = jnp.full(top_ref.shape, top)


def pack_kernel(state_ref, next_ref, three_ref, four_ref, swap_ref, own_ref, up_ref, down_ref, first_ref, second_ref, top_ref):
    rows = state_ref.shape[1]
    cols = state_ref.shape[2]
    half = rows // 2 + HALO
    lane = iota((half, LANES), 1)
    is_odd = odd("gx")
    up_ref[...] = jnp.where(is_odd, swap_ref[...], next_ref[...])
    down_ref[...] = jnp.where(is_odd, next_ref[...], swap_ref[...])
    top = jnp.maximum(jnp.maximum(own_ref[...], jnp.maximum(three_ref[...], four_ref[...])),
                      jnp.maximum(up_ref[4 * HALO :, 0:LANES], down_ref[4 * HALO :, 0:LANES]))

    def edge(low, at):
        lanes = slice(low, low + LANES)
        total = jnp.zeros((half, LANES), jnp.float32)
        for side in range(2):
            for comp in range(4):
                span = slice(comp * HALO, (comp + 1) * HALO)
                if side == 0:
                    cells = jnp.concatenate([up_ref[span, lanes], state_ref[comp, 0 : rows // 2, lanes]], axis=0)
                else:
                    cells = jnp.concatenate([state_ref[comp, rows // 2 : rows, lanes], down_ref[span, lanes]], axis=0)
                goal = side * (LANES // 2) + comp * HALO
                moved = pltpu.roll(cells, (goal - at) % LANES, axis=1)
                total = jnp.where((lane >= goal) & (lane < goal + HALO), moved, total)
        return total

    left = edge(0, 0)
    right = edge(cols - LANES, LANES - HALO)
    free = (iota((half, LANES), 0) == 0) & (lane < LANES // 2)
    under = jnp.concatenate([top] * (half // 8), axis=0)
    left = jnp.where(free, under, left)
    right = jnp.where(free, under, right)
    is_odd = odd("gy")
    first_ref[...] = jnp.where(is_odd, left, right)
    second_ref[...] = jnp.where(is_odd, right, left)
    top_ref[...] = top


def selected(values, select):
    rows = values.shape[0]
    parts = []
    for _ in range(3):
        parts.append(values.astype(jnp.bfloat16))
        values = values - parts[-1].astype(jnp.float32)
    found = jnp.dot(jnp.concatenate(parts, axis=0), select, preferred_element_type=jnp.float32)
    return (found[0:rows] + found[rows : 2 * rows]) + found[2 * rows :]


def minmod(first, second):
    low = jnp.minimum(first, second)
    high = jnp.maximum(first, second)
    return jnp.maximum(low, jnp.minimum(high, 0.0))


MOMENTUM = math.sqrt(0.5 * (GAMMA - 1.0))
SCALES = (1.0, MOMENTUM, MOMENTUM, GAMMA - 1.0)


def known(state):
    density, normal, tangent, energy = state
    inv = pl.reciprocal(density, approx=True)
    vel = normal * inv
    pressure = energy - (normal * normal + tangent * tangent) * inv
    square = jnp.maximum((GAMMA * MOMENTUM * MOMENTUM) * pressure * inv, TINY)
    return state, vel, pressure, pressure * vel, jnp.abs(vel) + square * lax.rsqrt(square)


def face(left, right):
    (left_state, left_vel, left_pressure, left_work, left_speed) = left
    (right_state, right_vel, right_pressure, right_work, right_speed) = right
    top = jnp.maximum(left_speed, right_speed)
    left_rate = left_vel + top
    right_rate = right_vel - top
    flux = [left_rate * left_state[comp] + right_rate * right_state[comp] for comp in range(4)]
    flux[1] = flux[1] + (MOMENTUM * MOMENTUM) * (left_pressure + right_pressure)
    flux[3] = flux[3] + (GAMMA - 1.0) * (left_work + right_work)
    return flux


def minus(first, second):
    return [first[comp] - second[comp] for comp in range(4)]


def rolled(tree, by, axis):
    return jax.tree.map(lambda value: pltpu.roll(value, by % value.shape[axis], axis=axis), tree)


def cell(whole, jump_before, jump_after):
    slope = [minmod(jump_before[comp], jump_after[comp]) for comp in range(4)]
    return known(minus(whole, slope)), known([whole[comp] + slope[comp] for comp in range(4)])


def row_changes(values, wholes):
    count = len(values)
    end_jump = minus(rolled(values[0], -1, 1), values[-1])
    jumps = [minus(values[at + 1], values[at]) for at in range(count - 1)] + [end_jump]
    faces, first_low, high = [], None, None
    for at in range(count):
        jump = jumps[at - 1] if at else minus(values[0], rolled(values[-1], 1, 1))
        low, next_high = cell(wholes[at], jump, jumps[at])
        if at:
            faces.append(face(high, low))
        else:
            first_low = low
        high = next_high
    faces.append(face(high, known(rolled(first_low[0], -1, 1))))
    return [minus(faces[at], faces[at - 1] if at else rolled(faces[-1], 1, 1)) for at in range(count)]


class Column:
    def __init__(self, count, begin, here, after):
        self.count, self.begin = count, begin
        self.jump = self.first_jump = minus(after, here)
        self.before = here
        self.first_low = self.first_flux = self.last_flux = self.high = None

    def feed(self, row, here, whole, after):
        next_row = (row + 1) % self.count
        if after is None:
            next_jump = self.first_jump
        else:
            next_jump = minus(rolled(after, -1, 0) if next_row == 0 else after, here)
        jump = minus(here, rolled(self.before, 1, 0)) if row == 0 else self.jump
        low, high = cell(whole, jump, next_jump)
        done = []
        if self.first_low is None:
            self.first_low = low
        else:
            flux = face(known(rolled(self.high[0], 1, 0)) if row == 0 else self.high, low)
            if self.last_flux is None:
                self.first_flux = flux
            else:
                seen = rolled(flux, -1, 0) if row == 0 else flux
                done.append(((row - 1) % self.count, minus(seen, self.last_flux)))
            self.last_flux = flux
        self.high, self.jump, self.before = high, next_jump, here
        if after is None:
            flux = face(high, self.first_low)
            done.append((row, minus(flux, self.last_flux)))
            done.append(((row + 1) % self.count, minus(self.first_flux, flux)))
        return done


Y_ORDER = (0, 2, 1, 3)


def changes(load, rows, cols, begin, store):
    along_y = {}
    values = {at: [load((begin + at) % rows, col) for col in range(cols)] for at in range(2)}
    columns = [Column(rows, begin, values[0][col], values[1][col]) for col in range(cols)]
    for at in range(1, rows + 1):
        row = (begin + at) % rows
        here = values.pop(at)
        if at < rows:
            values[at + 1] = [load((row + 1) % rows, col) for col in range(cols)]
        whole = [[part + part for part in value] for value in here]
        ready = []
        for col in range(cols):
            after = values[at + 1][col] if at < rows else None
            ready += [(col, *item) for item in columns[col].feed(row, here[col], whole[col], after)]
        along_y[row] = row_changes(*([[part[comp] for comp in Y_ORDER] for part in value] for value in (here, whole)))
        for col, done, parts in ready:
            other = along_y[done][col]
            store(done, col, [parts[comp] + other[Y_ORDER[comp]] for comp in range(4)])


def place_of(lane, group, groups):
    return groups * lane + group


def deal_kernel(state_ref, up_ref, down_ref, own_ref, dealt_ref, halo_select_ref, back_select_ref, top_ref, carried_ref, plain):
    top_ref[...] = own_ref[...]
    carried = (iota((8, LANES), 0) == 0) & (iota((8, LANES), 1) < LANES // 2)
    carried_ref[...] = jnp.where(carried, 1.0, 0.0)
    rows, cols = state_ref.shape[1:]
    tall = rows + 2 * HALO
    wide = dealt_ref.shape[1]
    groups = wide // LANES
    for comp in range(4):
        span = slice(comp * HALO, (comp + 1) * HALO)
        low = comp * tall
        plain[low : low + HALO, :] = up_ref[span, :]
        plain[low + HALO : low + HALO + rows, :] = state_ref[comp]
        plain[low + HALO + rows : low + tall, :] = down_ref[span, :]
    source = iota((wide, wide), 0)
    goal = iota((wide, wide), 1)
    place = place_of(goal % LANES, goal // LANES, groups)
    place = jnp.where(place < cols + 2 * HALO, (place + wide - HALO) % wide, 0)
    select = jnp.where(source == place, 1.0, 0.0).astype(jnp.bfloat16)
    dealt_ref[...] = selected(plain[...], select[0:cols])
    halo_select_ref[...] = select[cols:]
    source = iota((wide, cols), 0)
    goal = iota((wide, cols), 1)
    back = place_of(source % LANES, source // LANES, groups) == goal + HALO
    back_select_ref[...] = jnp.where(back, 1.0, 0.0).astype(jnp.bfloat16)


def first_kernel(cells_ref, select_ref, next_ref, swap_ref, field_ref, change_ref, plain, dealt):
    half = next_ref.shape[0]
    tall = 2 * half
    groups = cells_ref.shape[1] // LANES
    lane = iota((half, LANES), 1)
    is_odd = odd("gy")
    from_swap = swap_ref[...]
    from_next = next_ref[...]
    from_before = jnp.where(is_odd, from_swap, from_next)
    from_after = jnp.where(is_odd, from_next, from_swap)
    for side in range(2):
        for comp in range(4):
            at = side * (LANES // 2) + comp * HALO
            left = pltpu.roll(from_before, (LANES - HALO - at) % LANES, axis=1)
            right = pltpu.roll(from_after, (-at) % LANES, axis=1)
            low = comp * tall + side * half
            plain[low : low + half, :] = jnp.where(lane < LANES // 2, right, left)
    found = cells_ref[...] + selected(plain[...], select_ref[...])
    for comp in range(4):
        for group in range(groups):
            cells = found[comp * tall : (comp + 1) * tall, group * LANES : (group + 1) * LANES]
            dealt[comp, group] = (0.5 * SCALES[comp]) * cells
    count = tall // 8
    for comp in range(4):
        for row in range(count):
            for group in range(groups):
                field_ref[comp, row, group] = dealt[comp, group, pl.ds(row, 8, stride=count), :]

    def store(row, col, parts):
        for comp in range(4):
            change_ref[comp, row, col] = parts[comp]

    def load(row, col):
        return [field_ref[comp, row, col] for comp in range(4)]

    changes(load, count, groups, 0, store)


def steps_kernel(field_ref, change_ref, select_ref, own_ref, mate_ref, out_ref, field, base, mid, dealt, result, sems):
    rows, cols = out_ref.shape[1:]
    tall = rows + 2 * HALO
    groups = field_ref.shape[2]
    scale = (0.125 * COURANT / MOMENTUM) / jnp.max(jnp.maximum(own_ref[...], mate_ref[...]))
    scales = (1.0, scale, scale, scale * scale)

    def one_step(start, count, old, first_changes):
        def to_mid(row, col, parts):
            for comp in range(4):
                cells, move = old[comp, row, col], parts[comp]
                if first_changes is not None:
                    cells, move = scales[comp] * cells, (scales[comp] * scale) * move
                moved = cells - move
                base[comp, row, col] = moved
                mid[comp, row, col] = moved - move

        def to_field(row, col, parts):
            for comp in range(4):
                new = base[comp, row, col] - parts[comp]
                dealt[comp, col, pl.ds(start + row, 8, stride=count), :] = new

        def load_from(ref):
            return lambda row, col: [ref[comp, row, col] for comp in range(4)]

        if first_changes is not None:
            for row in range(count):
                for col in range(groups):
                    to_mid(row, col, [first_changes[comp, row, col] for comp in range(4)])
        else:
            for comp in range(4):
                for row in range(count):
                    for col in range(groups):
                        old[comp, row, col] = dealt[comp, col, pl.ds(start + row, 8, stride=count), :]
            changes(load_from(old), count, groups, 0, to_mid)
        changes(load_from(mid), count, groups, count // 2, to_field)

    one_step(0, tall // 8, field_ref, change_ref)
    for index in range(1, STEPS):
        one_step(4 * index, (tall - 8 * index) // 8, field, None)

    wide = groups * LANES
    lane = iota((rows, LANES), 1)
    parts = []
    for comp in range(4):
        line = []
        for group in range(groups):
            place = place_of(lane, group, groups)
            inside = (place >= HALO) & (place < HALO + cols)
            line.append(jnp.where(inside, dealt[comp, group, HALO : HALO + rows, :], 0.0))
        parts.append(jnp.concatenate(line, axis=1))
    found = selected(jnp.concatenate(parts, axis=0), select_ref[...])
    copies = []
    for comp in range(4):
        result[comp] = ((2.0 / SCALES[comp]) / scales[comp]) * found[comp * rows : (comp + 1) * rows, :]
        copies.append(pltpu.make_async_copy(result.at[comp], out_ref.at[comp], sems.at[comp]))
        copies[-1].start()
    for copy in copies:
        copy.wait()


def local(state):
    parts, rows, cols = state.shape
    tall = rows + 2 * HALO
    groups = -(-(cols + 2 * HALO) // LANES)

    def sent(value, axis, by):
        count = lax.axis_size(axis)
        return lax.ppermute(value, axis, [(i, (i + by) % count) for i in range(count)])

    def swapped_bit(value, axis, by):
        return lax.ppermute(value, axis, [(i, i ^ by) for i in range(lax.axis_size(axis))])

    def swapped_pairs(value, axis, first):
        count = lax.axis_size(axis)
        pairs = []
        for low in range(first, count, 2):
            high = (low + 1) % count
            pairs += [(low, high), (high, low)]
        return lax.ppermute(value, axis, pairs)

    def swapped_threes(value, axis):
        count = lax.axis_size(axis)
        return lax.ppermute(value, axis, [(i, (i + 3 - 6 * (i % 2)) % count) for i in range(count)])

    edge_type = array(parts * HALO + 8, cols)
    first, second, top = pl.pallas_call(
        edge_kernel,
        out_shape=(edge_type, edge_type, array(8, LANES)),
        in_specs=[VMEM],
        out_specs=(VMEM,) * 3,
        compiler_params=params(4),
        name="edge",
    )(state)
    second = swapped_pairs(second, "gx", 1)
    first = swapped_pairs(first, "gx", 0)
    far = swapped_threes(top, "gx"), swapped_bit(top, "gx", 4)
    side_type = array(tall // 2, LANES)
    up, down, first, second, top = pl.pallas_call(
        pack_kernel,
        out_shape=(edge_type, edge_type, side_type, side_type, array(8, LANES)),
        in_specs=[VMEM] * 6,
        out_specs=(VMEM,) * 5,
        compiler_params=params(4),
        name="pack",
    )(state, second, *far, first, top)
    second = swapped_pairs(second, "gy", 1)
    first = swapped_pairs(first, "gy", 0)
    far = swapped_bit(top, "gy", 2)
    wide = groups * LANES
    cells, halo_select, back_select, top, carried = pl.pallas_call(
        deal_kernel,
        out_shape=(
            array(parts * tall, wide),
            jax.ShapeDtypeStruct((wide - cols, wide), jnp.bfloat16),
            jax.ShapeDtypeStruct((wide, cols), jnp.bfloat16),
            array(8, LANES),
            array(8, LANES),
        ),
        in_specs=[VMEM] * 4,
        out_specs=(VMEM,) * 5,
        scratch_shapes=[pltpu.VMEM((parts * tall, cols), jnp.float32)],
        compiler_params=params(8),
        cost_estimate=pl.CostEstimate(flops=300_000_000, bytes_accessed=1_500_000, transcendentals=0),
        name="deal",
    )(state, up, down, top)
    top = jnp.maximum(jnp.maximum(top, far), carried * jnp.maximum(first[:8], second[:8]))
    for axis, covered in (("gy", 4), ("gx", 8)):
        while covered < lax.axis_size(axis):
            top = jnp.maximum(top, sent(top, axis, covered))
            covered *= 2
    mate = swapped_bit(top, "gx", 1)
    dealt_type = array(parts, tall // 8, groups, 8, LANES)
    dealt = pltpu.VMEM(dealt_type.shape, jnp.float32)
    plain = pltpu.VMEM((parts, groups, tall, LANES), jnp.float32)
    field, change = pl.pallas_call(
        first_kernel,
        out_shape=(dealt_type, dealt_type),
        in_specs=[VMEM] * 4,
        out_specs=(VMEM,) * 2,
        scratch_shapes=[pltpu.VMEM((parts * tall, LANES), jnp.float32), plain],
        compiler_params=params(16),
        cost_estimate=pl.CostEstimate(flops=20_000_000, bytes_accessed=2_000_000, transcendentals=400_000),
        name="first",
    )(cells, halo_select, second, first)
    return pl.pallas_call(
        steps_kernel,
        out_shape=array(parts, rows, cols),
        in_specs=[VMEM] * 5,
        out_specs=pl.BlockSpec(memory_space=pl.ANY),
        scratch_shapes=[dealt] * 3
        + [plain, pltpu.VMEM((parts, rows, cols), jnp.float32), pltpu.SemaphoreType.DMA((parts,))],
        compiler_params=params(16),
        name="steps",
    )(field, change, back_select, top, mate)


def solution(mesh):
    in_specs = (P(None, "gx", "gy"),)
    out_specs = P(None, "gx", "gy")
    return jax.shard_map(local, mesh=mesh, in_specs=in_specs, out_specs=out_specs, check_vma=False)
```

```python
import functools
import math

import jax
import jax.numpy as jnp
from jax import lax
from jax.experimental import pallas as pl
from jax.experimental.pallas import tpu as pltpu
from jax.sharding import PartitionSpec as P

STEPS = 4
HALO = 4 * STEPS
LANES = 128
GAMMA = 1.4
COURANT = 0.35
TINY = 1e-30

VMEM = pl.BlockSpec(memory_space=pltpu.VMEM)


def params(limit):
    return pltpu.CompilerParams(vmem_limit_bytes=limit << 20)


def array(*shape):
    return jax.ShapeDtypeStruct(shape, jnp.float32)


def iota(shape, dim):
    return lax.broadcasted_iota(jnp.int32, shape, dim)


def odd(axis):
    return lax.rem(lax.axis_index(axis), 2) == 1


def edge_kernel(block_ref, first_ref, second_ref, top_ref):
    rows = block_ref.shape[1]
    density, mom_x, mom_y, energy = (block_ref[comp] for comp in range(4))
    inv = 1.0 / density
    pressure = (GAMMA - 1.0) * (energy - 0.5 * (mom_x * mom_x + mom_y * mom_y) * inv)
    speed = jnp.maximum(jnp.abs(mom_x * inv), jnp.abs(mom_y * inv)) + jnp.sqrt(GAMMA * pressure * inv)
    top = jnp.max(speed)
    is_odd = odd("gx")
    for comp in range(4):
        span = slice(comp * HALO, (comp + 1) * HALO)
        head = block_ref[comp, 0:HALO, :]
        tail = block_ref[comp, rows - HALO : rows, :]
        first_ref[span, :] = jnp.where(is_odd, head, tail)
        second_ref[span, :] = jnp.where(is_odd, tail, head)
    first_ref[4 * HALO :, :] = jnp.full((8, first_ref.shape[1]), top)
    second_ref[4 * HALO :, :] = jnp.full((8, second_ref.shape[1]), top)
    top_ref[...] = jnp.full(top_ref.shape, top)


def pack_kernel(state_ref, next_ref, three_ref, four_ref, swap_ref, own_ref, first_ref, second_ref, top_ref):
    rows = state_ref.shape[1]
    cols = state_ref.shape[2]
    half = rows // 2 + HALO
    lane = iota((half, LANES), 1)
    is_odd = odd("gx")
    up = jnp.where(is_odd, swap_ref[...], next_ref[...])
    down = jnp.where(is_odd, next_ref[...], swap_ref[...])
    top = jnp.maximum(jnp.maximum(own_ref[...], jnp.maximum(three_ref[...], four_ref[...])),
                      jnp.maximum(up[4 * HALO :, 0:LANES], down[4 * HALO :, 0:LANES]))

    def edge(low, at):
        lanes = slice(low, low + LANES)
        total = jnp.zeros((half, LANES), jnp.float32)
        for side in range(2):
            for comp in range(4):
                span = slice(comp * HALO, (comp + 1) * HALO)
                if side == 0:
                    cells = jnp.concatenate([up[span, lanes], state_ref[comp, 0 : rows // 2, lanes]], axis=0)
                else:
                    cells = jnp.concatenate([state_ref[comp, rows // 2 : rows, lanes], down[span, lanes]], axis=0)
                goal = side * (LANES // 2) + comp * HALO
                moved = pltpu.roll(cells, (goal - at) % LANES, axis=1)
                total = jnp.where((lane >= goal) & (lane < goal + HALO), moved, total)
        return total

    left = edge(0, 0)
    right = edge(cols - LANES, LANES - HALO)
    free = (iota((half, LANES), 0) == 0) & (lane < LANES // 2)
    under = jnp.concatenate([top] * (half // 8), axis=0)
    left = jnp.where(free, under, left)
    right = jnp.where(free, under, right)
    is_odd = odd("gy")
    first_ref[...] = jnp.where(is_odd, left, right)
    second_ref[...] = jnp.where(is_odd, right, left)
    top_ref[...] = top


def selected(values, select):
    rows = values.shape[0]
    parts = []
    for _ in range(3):
        parts.append(values.astype(jnp.bfloat16))
        values = values - parts[-1].astype(jnp.float32)
    found = jnp.dot(jnp.concatenate(parts, axis=0), select, preferred_element_type=jnp.float32)
    return (found[0:rows] + found[rows : 2 * rows]) + found[2 * rows :]


def minmod(first, second):
    low = jnp.minimum(first, second)
    high = jnp.maximum(first, second)
    return jnp.maximum(low, jnp.minimum(high, 0.0))


MOMENTUM = math.sqrt(0.5 * (GAMMA - 1.0))
SCALES = (1.0, MOMENTUM, MOMENTUM, GAMMA - 1.0)


def known(state):
    density, normal, tangent, energy = state
    inv = pl.reciprocal(density, approx=True)
    vel = normal * inv
    pressure = energy - (normal * normal + tangent * tangent) * inv
    square = jnp.maximum((GAMMA * MOMENTUM * MOMENTUM) * pressure * inv, TINY)
    return state, vel, pressure, pressure * vel, jnp.abs(vel) + square * lax.rsqrt(square)


def face(left, right):
    (left_state, left_vel, left_pressure, left_work, left_speed) = left
    (right_state, right_vel, right_pressure, right_work, right_speed) = right
    top = jnp.maximum(left_speed, right_speed)
    left_rate = left_vel + top
    right_rate = right_vel - top
    flux = [left_rate * left_state[comp] + right_rate * right_state[comp] for comp in range(4)]
    flux[1] = flux[1] + (MOMENTUM * MOMENTUM) * (left_pressure + right_pressure)
    flux[3] = flux[3] + (GAMMA - 1.0) * (left_work + right_work)
    return flux


def minus(first, second):
    return [first[comp] - second[comp] for comp in range(4)]


def rolled(tree, by, axis):
    return jax.tree.map(lambda value: pltpu.roll(value, by % value.shape[axis], axis=axis), tree)


def cell(whole, jump_before, jump_after):
    slope = [minmod(jump_before[comp], jump_after[comp]) for comp in range(4)]
    return known(minus(whole, slope)), known([whole[comp] + slope[comp] for comp in range(4)])


def row_changes(values, wholes):
    count = len(values)
    end_jump = minus(rolled(values[0], -1, 1), values[-1])
    jumps = [minus(values[at + 1], values[at]) for at in range(count - 1)] + [end_jump]
    faces, first_low, high = [], None, None
    for at in range(count):
        jump = jumps[at - 1] if at else minus(values[0], rolled(values[-1], 1, 1))
        low, next_high = cell(wholes[at], jump, jumps[at])
        if at:
            faces.append(face(high, low))
        else:
            first_low = low
        high = next_high
    faces.append(face(high, known(rolled(first_low[0], -1, 1))))
    return [minus(faces[at], faces[at - 1] if at else rolled(faces[-1], 1, 1)) for at in range(count)]


class Column:
    def __init__(self, count, begin, here, after):
        self.count, self.begin = count, begin
        self.jump = self.first_jump = minus(after, here)
        self.before = here
        self.first_low = self.first_flux = self.last_flux = self.high = None

    def feed(self, row, here, whole, after):
        next_row = (row + 1) % self.count
        if after is None:
            next_jump = self.first_jump
        else:
            next_jump = minus(rolled(after, -1, 0) if next_row == 0 else after, here)
        jump = minus(here, rolled(self.before, 1, 0)) if row == 0 else self.jump
        low, high = cell(whole, jump, next_jump)
        done = []
        if self.first_low is None:
            self.first_low = low
        else:
            flux = face(known(rolled(self.high[0], 1, 0)) if row == 0 else self.high, low)
            if self.last_flux is None:
                self.first_flux = flux
            else:
                seen = rolled(flux, -1, 0) if row == 0 else flux
                done.append(((row - 1) % self.count, minus(seen, self.last_flux)))
            self.last_flux = flux
        self.high, self.jump, self.before = high, next_jump, here
        if after is None:
            flux = face(high, self.first_low)
            done.append((row, minus(flux, self.last_flux)))
            done.append(((row + 1) % self.count, minus(self.first_flux, flux)))
        return done


Y_ORDER = (0, 2, 1, 3)


def changes(load, rows, cols, begin, store):
    along_y = {}
    values = {at: [load((begin + at) % rows, col) for col in range(cols)] for at in range(2)}
    columns = [Column(rows, begin, values[0][col], values[1][col]) for col in range(cols)]
    for at in range(1, rows + 1):
        row = (begin + at) % rows
        here = values.pop(at)
        if at < rows:
            values[at + 1] = [load((row + 1) % rows, col) for col in range(cols)]
        whole = [[part + part for part in value] for value in here]
        ready = []
        for col in range(cols):
            after = values[at + 1][col] if at < rows else None
            ready += [(col, *item) for item in columns[col].feed(row, here[col], whole[col], after)]
        along_y[row] = row_changes(*([[part[comp] for comp in Y_ORDER] for part in value] for value in (here, whole)))
        for col, done, parts in ready:
            other = along_y[done][col]
            store(done, col, [parts[comp] + other[Y_ORDER[comp]] for comp in range(4)])


def place_of(lane, group, groups):
    return groups * lane + group


def deal_kernel(state_ref, next_ref, swap_ref, own_ref, dealt_ref, halo_select_ref, back_select_ref, top_ref, carried_ref, plain):
    top_ref[...] = own_ref[...]
    carried = (iota((8, LANES), 0) == 0) & (iota((8, LANES), 1) < LANES // 2)
    carried_ref[...] = jnp.where(carried, 1.0, 0.0)
    rows, cols = state_ref.shape[1:]
    tall = rows + 2 * HALO
    wide = dealt_ref.shape[1]
    groups = wide // LANES
    for comp in range(4):
        span = slice(comp * HALO, (comp + 1) * HALO)
        low = comp * tall
        plain[low : low + HALO, :] = jnp.where(odd("gx"), swap_ref[span, :], next_ref[span, :])
        plain[low + HALO : low + HALO + rows, :] = state_ref[comp]
        plain[low + HALO + rows : low + tall, :] = jnp.where(odd("gx"), next_ref[span, :], swap_ref[span, :])
    source = iota((wide, wide), 0)
    goal = iota((wide, wide), 1)
    place = place_of(goal % LANES, goal // LANES, groups)
    place = jnp.where(place < cols + 2 * HALO, (place + wide - HALO) % wide, 0)
    select = jnp.where(source == place, 1.0, 0.0).astype(jnp.bfloat16)
    dealt_ref[...] = selected(plain[...], select[0:cols])
    halo_select_ref[...] = select[cols:]
    source = iota((wide, cols), 0)
    goal = iota((wide, cols), 1)
    back = place_of(source % LANES, source // LANES, groups) == goal + HALO
    back_select_ref[...] = jnp.where(back, 1.0, 0.0).astype(jnp.bfloat16)


def first_kernel(cells_ref, select_ref, next_ref, swap_ref, field_ref, change_ref, plain, dealt):
    half = next_ref.shape[0]
    tall = 2 * half
    groups = cells_ref.shape[1] // LANES
    lane = iota((half, LANES), 1)
    is_odd = odd("gy")
    from_swap = swap_ref[...]
    from_next = next_ref[...]
    from_before = jnp.where(is_odd, from_swap, from_next)
    from_after = jnp.where(is_odd, from_next, from_swap)
    for side in range(2):
        for comp in range(4):
            at = side * (LANES // 2) + comp * HALO
            left = pltpu.roll(from_before, (LANES - HALO - at) % LANES, axis=1)
            right = pltpu.roll(from_after, (-at) % LANES, axis=1)
            low = comp * tall + side * half
            plain[low : low + half, :] = jnp.where(lane < LANES // 2, right, left)
    found = cells_ref[...] + selected(plain[...], select_ref[...])
    for comp in range(4):
        for group in range(groups):
            cells = found[comp * tall : (comp + 1) * tall, group * LANES : (group + 1) * LANES]
            dealt[comp, group] = (0.5 * SCALES[comp]) * cells
    count = tall // 8
    for comp in range(4):
        for row in range(count):
            for group in range(groups):
                field_ref[comp, row, group] = dealt[comp, group, pl.ds(row, 8, stride=count), :]

    def store(row, col, parts):
        for comp in range(4):
            change_ref[comp, row, col] = parts[comp]

    def load(row, col):
        return [field_ref[comp, row, col] for comp in range(4)]

    changes(load, count, groups, 0, store)


def steps_kernel(field_ref, change_ref, select_ref, own_ref, mate_ref, out_ref, field, base, mid, dealt, result, sems):
    rows, cols = out_ref.shape[1:]
    tall = rows + 2 * HALO
    groups = field_ref.shape[2]
    scale = (0.125 * COURANT / MOMENTUM) / jnp.max(jnp.maximum(own_ref[...], mate_ref[...]))
    scales = (1.0, scale, scale, scale * scale)

    def one_step(start, count, old, first_changes):
        def to_mid(row, col, parts):
            for comp in range(4):
                cells, move = old[comp, row, col], parts[comp]
                if first_changes is not None:
                    cells, move = scales[comp] * cells, (scales[comp] * scale) * move
                moved = cells - move
                base[comp, row, col] = moved
                mid[comp, row, col] = moved - move

        def to_field(row, col, parts):
            for comp in range(4):
                new = base[comp, row, col] - parts[comp]
                dealt[comp, col, pl.ds(start + row, 8, stride=count), :] = new

        def load_from(ref):
            return lambda row, col: [ref[comp, row, col] for comp in range(4)]

        if first_changes is not None:
            for row in range(count):
                for col in range(groups):
                    to_mid(row, col, [first_changes[comp, row, col] for comp in range(4)])
        else:
            for comp in range(4):
                for row in range(count):
                    for col in range(groups):
                        old[comp, row, col] = dealt[comp, col, pl.ds(start + row, 8, stride=count), :]
            changes(load_from(old), count, groups, 0, to_mid)
        changes(load_from(mid), count, groups, count // 2, to_field)

    one_step(0, tall // 8, field_ref, change_ref)
    for index in range(1, STEPS):
        one_step(4 * index, (tall - 8 * index) // 8, field, None)

    wide = groups * LANES
    lane = iota((rows, LANES), 1)
    parts = []
    for comp in range(4):
        line = []
        for group in range(groups):
            place = place_of(lane, group, groups)
            inside = (place >= HALO) & (place < HALO + cols)
            line.append(jnp.where(inside, dealt[comp, group, HALO : HALO + rows, :], 0.0))
        parts.append(jnp.concatenate(line, axis=1))
    found = selected(jnp.concatenate(parts, axis=0), select_ref[...])
    copies = []
    for comp in range(4):
        result[comp] = ((2.0 / SCALES[comp]) / scales[comp]) * found[comp * rows : (comp + 1) * rows, :]
        copies.append(pltpu.make_async_copy(result.at[comp], out_ref.at[comp], sems.at[comp]))
        copies[-1].start()
    for copy in copies:
        copy.wait()


def local(state):
    parts, rows, cols = state.shape
    tall = rows + 2 * HALO
    groups = -(-(cols + 2 * HALO) // LANES)

    def sent(value, axis, by):
        count = lax.axis_size(axis)
        return lax.ppermute(value, axis, [(i, (i + by) % count) for i in range(count)])

    def swapped_bit(value, axis, by):
        return lax.ppermute(value, axis, [(i, i ^ by) for i in range(lax.axis_size(axis))])

    def swapped_pairs(value, axis, first):
        count = lax.axis_size(axis)
        pairs = []
        for low in range(first, count, 2):
            high = (low + 1) % count
            pairs += [(low, high), (high, low)]
        return lax.ppermute(value, axis, pairs)

    def swapped_threes(value, axis):
        count = lax.axis_size(axis)
        return lax.ppermute(value, axis, [(i, (i + 3 - 6 * (i % 2)) % count) for i in range(count)])

    edge_type = array(parts * HALO + 8, cols)
    first, second, top = pl.pallas_call(
        edge_kernel,
        out_shape=(edge_type, edge_type, array(8, LANES)),
        in_specs=[VMEM],
        out_specs=(VMEM,) * 3,
        compiler_params=params(4),
        name="edge",
    )(state)
    second = swapped_pairs(second, "gx", 1)
    first = swapped_pairs(first, "gx", 0)
    far = swapped_threes(top, "gx"), swapped_bit(top, "gx", 4)
    side_type = array(tall // 2, LANES)
    row_halos = second, first
    first, second, top = pl.pallas_call(
        pack_kernel,
        out_shape=(side_type, side_type, array(8, LANES)),
        in_specs=[VMEM] * 6,
        out_specs=(VMEM,) * 3,
        compiler_params=params(4),
        name="pack",
    )(state, second, *far, first, top)
    second = swapped_pairs(second, "gy", 1)
    first = swapped_pairs(first, "gy", 0)
    far = swapped_bit(top, "gy", 2)
    wide = groups * LANES
    cells, halo_select, back_select, top, carried = pl.pallas_call(
        deal_kernel,
        out_shape=(
            array(parts * tall, wide),
            jax.ShapeDtypeStruct((wide - cols, wide), jnp.bfloat16),
            jax.ShapeDtypeStruct((wide, cols), jnp.bfloat16),
            array(8, LANES),
            array(8, LANES),
        ),
        in_specs=[VMEM] * 4,
        out_specs=(VMEM,) * 5,
        scratch_shapes=[pltpu.VMEM((parts * tall, cols), jnp.float32)],
        compiler_params=params(8),
        cost_estimate=pl.CostEstimate(flops=300_000_000, bytes_accessed=1_500_000, transcendentals=0),
        name="deal",
    )(state, *row_halos, top)
    top = jnp.maximum(jnp.maximum(top, far), carried * jnp.maximum(first[:8], second[:8]))
    for axis, covered in (("gy", 4), ("gx", 8)):
        while covered < lax.axis_size(axis):
            top = jnp.maximum(top, sent(top, axis, covered))
            covered *= 2
    mate = swapped_bit(top, "gx", 1)
    dealt_type = array(parts, tall // 8, groups, 8, LANES)
    dealt = pltpu.VMEM(dealt_type.shape, jnp.float32)
    plain = pltpu.VMEM((parts, groups, tall, LANES), jnp.float32)
    field, change = pl.pallas_call(
        first_kernel,
        out_shape=(dealt_type, dealt_type),
        in_specs=[VMEM] * 4,
        out_specs=(VMEM,) * 2,
        scratch_shapes=[pltpu.VMEM((parts * tall, LANES), jnp.float32), plain],
        compiler_params=params(16),
        cost_estimate=pl.CostEstimate(flops=20_000_000, bytes_accessed=2_000_000, transcendentals=400_000),
        name="first",
    )(cells, halo_select, second, first)
    return pl.pallas_call(
        steps_kernel,
        out_shape=array(parts, rows, cols),
        in_specs=[VMEM] * 5,
        out_specs=pl.BlockSpec(memory_space=pl.ANY),
        scratch_shapes=[dealt] * 3
        + [plain, pltpu.VMEM((parts, rows, cols), jnp.float32), pltpu.SemaphoreType.DMA((parts,))],
        compiler_params=params(16),
        name="steps",
    )(field, change, back_select, top, mate)


def solution(mesh):
    in_specs = (P(None, "gx", "gy"),)
    out_specs = P(None, "gx", "gy")
    return jax.shard_map(local, mesh=mesh, in_specs=in_specs, out_specs=out_specs, check_vma=False)
```

```python
import functools
import math

import jax
import jax.numpy as jnp
from jax import lax
from jax.experimental import pallas as pl
from jax.experimental.pallas import tpu as pltpu
from jax.sharding import PartitionSpec as P

STEPS = 4
HALO = 4 * STEPS
LANES = 128
GAMMA = 1.4
COURANT = 0.35
TINY = 1e-30

VMEM = pl.BlockSpec(memory_space=pltpu.VMEM)


def params(limit):
    return pltpu.CompilerParams(vmem_limit_bytes=limit << 20)


def array(*shape):
    return jax.ShapeDtypeStruct(shape, jnp.float32)


def iota(shape, dim):
    return lax.broadcasted_iota(jnp.int32, shape, dim)


def odd(axis):
    return lax.rem(lax.axis_index(axis), 2) == 1


def edge_kernel(block_ref, first_ref, second_ref, top_ref):
    rows = block_ref.shape[1]
    density, mom_x, mom_y, energy = (block_ref[comp] for comp in range(4))
    inv = 1.0 / density
    pressure = (GAMMA - 1.0) * (energy - 0.5 * (mom_x * mom_x + mom_y * mom_y) * inv)
    speed = jnp.maximum(jnp.abs(mom_x * inv), jnp.abs(mom_y * inv)) + jnp.sqrt(GAMMA * pressure * inv)
    top = jnp.max(speed)
    is_odd = odd("gx")
    for comp in range(4):
        span = slice(comp * HALO, (comp + 1) * HALO)
        head = block_ref[comp, 0:HALO, :]
        tail = block_ref[comp, rows - HALO : rows, :]
        first_ref[span, :] = jnp.where(is_odd, head, tail)
        second_ref[span, :] = jnp.where(is_odd, tail, head)
    first_ref[4 * HALO :, :] = jnp.full((8, first_ref.shape[1]), top)
    second_ref[4 * HALO :, :] = jnp.full((8, second_ref.shape[1]), top)
    top_ref[...] = jnp.full(top_ref.shape, top)


def pack_kernel(state_ref, next_ref, three_ref, four_ref, swap_ref, own_ref, first_ref, second_ref, top_ref):
    rows = state_ref.shape[1]
    cols = state_ref.shape[2]
    half = rows // 2 + HALO
    lane = iota((half, LANES), 1)
    is_odd = odd("gx")
    up = jnp.where(is_odd, swap_ref[...], next_ref[...])
    down = jnp.where(is_odd, next_ref[...], swap_ref[...])
    top = jnp.maximum(jnp.maximum(own_ref[...], jnp.maximum(three_ref[...], four_ref[...])),
                      jnp.maximum(up[4 * HALO :, 0:LANES], down[4 * HALO :, 0:LANES]))

    def edge(low, at):
        lanes = slice(low, low + LANES)
        total = jnp.zeros((half, LANES), jnp.float32)
        for side in range(2):
            for comp in range(4):
                span = slice(comp * HALO, (comp + 1) * HALO)
                if side == 0:
                    cells = jnp.concatenate([up[span, lanes], state_ref[comp, 0 : rows // 2, lanes]], axis=0)
                else:
                    cells = jnp.concatenate([state_ref[comp, rows // 2 : rows, lanes], down[span, lanes]], axis=0)
                goal = side * (LANES // 2) + comp * HALO
                moved = pltpu.roll(cells, (goal - at) % LANES, axis=1)
                total = jnp.where((lane >= goal) & (lane < goal + HALO), moved, total)
        return total

    left = edge(0, 0)
    right = edge(cols - LANES, LANES - HALO)
    free = (iota((half, LANES), 0) == 0) & (lane < LANES // 2)
    under = jnp.concatenate([top] * (half // 8), axis=0)
    left = jnp.where(free, under, left)
    right = jnp.where(free, under, right)
    is_odd = odd("gy")
    first_ref[...] = jnp.where(is_odd, left, right)
    second_ref[...] = jnp.where(is_odd, right, left)
    top_ref[...] = top


def selected(values, select):
    rows = values.shape[0]
    parts = []
    for _ in range(3):
        parts.append(values.astype(jnp.bfloat16))
        values = values - parts[-1].astype(jnp.float32)
    found = jnp.dot(jnp.concatenate(parts, axis=0), select, preferred_element_type=jnp.float32)
    return (found[0:rows] + found[rows : 2 * rows]) + found[2 * rows :]


def minmod(first, second):
    low = jnp.minimum(first, second)
    high = jnp.maximum(first, second)
    return jnp.maximum(low, jnp.minimum(high, 0.0))


MOMENTUM = math.sqrt(0.5 * (GAMMA - 1.0))
SCALES = (1.0, MOMENTUM, MOMENTUM, GAMMA - 1.0)


def known(state):
    density, normal, tangent, energy = state
    inv = pl.reciprocal(density, approx=True)
    vel = normal * inv
    pressure = energy - (normal * normal + tangent * tangent) * inv
    square = jnp.maximum((GAMMA * MOMENTUM * MOMENTUM) * pressure * inv, TINY)
    return state, vel, pressure, pressure * vel, jnp.abs(vel) + square * lax.rsqrt(square)


def face(left, right):
    (left_state, left_vel, left_pressure, left_work, left_speed) = left
    (right_state, right_vel, right_pressure, right_work, right_speed) = right
    top = jnp.maximum(left_speed, right_speed)
    left_rate = left_vel + top
    right_rate = right_vel - top
    flux = [left_rate * left_state[comp] + right_rate * right_state[comp] for comp in range(4)]
    flux[1] = flux[1] + (MOMENTUM * MOMENTUM) * (left_pressure + right_pressure)
    flux[3] = flux[3] + (GAMMA - 1.0) * (left_work + right_work)
    return flux


def minus(first, second):
    return [first[comp] - second[comp] for comp in range(4)]


def rolled(tree, by, axis):
    return jax.tree.map(lambda value: pltpu.roll(value, by % value.shape[axis], axis=axis), tree)


def cell(whole, jump_before, jump_after):
    slope = [minmod(jump_before[comp], jump_after[comp]) for comp in range(4)]
    return known(minus(whole, slope)), known([whole[comp] + slope[comp] for comp in range(4)])


def row_changes(values, wholes):
    count = len(values)
    end_jump = minus(rolled(values[0], -1, 1), values[-1])
    jumps = [minus(values[at + 1], values[at]) for at in range(count - 1)] + [end_jump]
    faces, first_low, high = [], None, None
    for at in range(count):
        jump = jumps[at - 1] if at else minus(values[0], rolled(values[-1], 1, 1))
        low, next_high = cell(wholes[at], jump, jumps[at])
        if at:
            faces.append(face(high, low))
        else:
            first_low = low
        high = next_high
    faces.append(face(high, known(rolled(first_low[0], -1, 1))))
    return [minus(faces[at], faces[at - 1] if at else rolled(faces[-1], 1, 1)) for at in range(count)]


class Column:
    def __init__(self, count, begin, here, after):
        self.count, self.begin = count, begin
        self.jump = self.first_jump = minus(after, here)
        self.before = here
        self.first_low = self.first_flux = self.last_flux = self.high = None

    def feed(self, row, here, whole, after):
        next_row = (row + 1) % self.count
        if after is None:
            next_jump = self.first_jump
        else:
            next_jump = minus(rolled(after, -1, 0) if next_row == 0 else after, here)
        jump = minus(here, rolled(self.before, 1, 0)) if row == 0 else self.jump
        low, high = cell(whole, jump, next_jump)
        done = []
        if self.first_low is None:
            self.first_low = low
        else:
            flux = face(known(rolled(self.high[0], 1, 0)) if row == 0 else self.high, low)
            if self.last_flux is None:
                self.first_flux = flux
            else:
                seen = rolled(flux, -1, 0) if row == 0 else flux
                done.append(((row - 1) % self.count, minus(seen, self.last_flux)))
            self.last_flux = flux
        self.high, self.jump, self.before = high, next_jump, here
        if after is None:
            flux = face(high, self.first_low)
            done.append((row, minus(flux, self.last_flux)))
            done.append(((row + 1) % self.count, minus(self.first_flux, flux)))
        return done


Y_ORDER = (0, 2, 1, 3)


def changes(load, rows, cols, begin, store):
    along_y = {}
    values = {at: [load((begin + at) % rows, col) for col in range(cols)] for at in range(2)}
    columns = [Column(rows, begin, values[0][col], values[1][col]) for col in range(cols)]
    for at in range(1, rows + 1):
        row = (begin + at) % rows
        here = values.pop(at)
        if at < rows:
            values[at + 1] = [load((row + 1) % rows, col) for col in range(cols)]
        whole = [[part + part for part in value] for value in here]
        ready = []
        for col in range(cols):
            after = values[at + 1][col] if at < rows else None
            ready += [(col, *item) for item in columns[col].feed(row, here[col], whole[col], after)]
        along_y[row] = row_changes(*([[part[comp] for comp in Y_ORDER] for part in value] for value in (here, whole)))
        for col, done, parts in ready:
            other = along_y[done][col]
            store(done, col, [parts[comp] + other[Y_ORDER[comp]] for comp in range(4)])


def place_of(lane, group, groups):
    return groups * lane + group


def deal_kernel(state_ref, next_ref, swap_ref, own_ref, dealt_ref, halo_select_ref, back_select_ref, top_ref, carried_ref, plain):
    top_ref[...] = own_ref[...]
    carried = (iota((8, LANES), 0) == 0) & (iota((8, LANES), 1) < LANES // 2)
    carried_ref[...] = jnp.where(carried, 1.0, 0.0)
    rows, cols = state_ref.shape[1:]
    tall = rows + 2 * HALO
    wide = dealt_ref.shape[1]
    groups = wide // LANES
    for comp in range(4):
        span = slice(comp * HALO, (comp + 1) * HALO)
        low = comp * tall
        plain[low : low + HALO, :] = jnp.where(odd("gx"), swap_ref[span, :], next_ref[span, :])
        plain[low + HALO : low + HALO + rows, :] = state_ref[comp]
        plain[low + HALO + rows : low + tall, :] = jnp.where(odd("gx"), next_ref[span, :], swap_ref[span, :])
    source = iota((wide, wide), 0)
    goal = iota((wide, wide), 1)
    place = place_of(goal % LANES, goal // LANES, groups)
    place = jnp.where(place < cols + 2 * HALO, (place + wide - HALO) % wide, 0)
    select = jnp.where(source == place, 1.0, 0.0).astype(jnp.bfloat16)
    dealt_ref[...] = selected(plain[...], select[0:cols])
    halo_select_ref[...] = select[cols:]
    source = iota((wide, cols), 0)
    goal = iota((wide, cols), 1)
    back = place_of(source % LANES, source // LANES, groups) == goal + HALO
    back_select_ref[...] = jnp.where(back, 1.0, 0.0).astype(jnp.bfloat16)


def first_kernel(cells_ref, select_ref, next_ref, swap_ref, field_ref, change_ref, plain, dealt):
    half = next_ref.shape[0]
    tall = 2 * half
    groups = cells_ref.shape[1] // LANES
    lane = iota((half, LANES), 1)
    is_odd = odd("gy")
    from_swap = swap_ref[...]
    from_next = next_ref[...]
    from_before = jnp.where(is_odd, from_swap, from_next)
    from_after = jnp.where(is_odd, from_next, from_swap)
    for side in range(2):
        for comp in range(4):
            at = side * (LANES // 2) + comp * HALO
            left = pltpu.roll(from_before, (LANES - HALO - at) % LANES, axis=1)
            right = pltpu.roll(from_after, (-at) % LANES, axis=1)
            low = comp * tall + side * half
            plain[low : low + half, :] = jnp.where(lane < LANES // 2, right, left)
    found = cells_ref[...] + selected(plain[...], select_ref[...])
    for comp in range(4):
        for group in range(groups):
            cells = found[comp * tall : (comp + 1) * tall, group * LANES : (group + 1) * LANES]
            dealt[comp, group] = (0.5 * SCALES[comp]) * cells
    count = tall // 8
    for comp in range(4):
        for row in range(count):
            for group in range(groups):
                field_ref[comp, row, group] = dealt[comp, group, pl.ds(row, 8, stride=count), :]

    def store(row, col, parts):
        for comp in range(4):
            change_ref[comp, row, col] = parts[comp]

    def load(row, col):
        return [field_ref[comp, row, col] for comp in range(4)]

    changes(load, count, groups, 0, store)


def steps_kernel(field_ref, change_ref, select_ref, own_ref, mate_ref, out_ref, field, base, mid, dealt, result, sems):
    rows, cols = out_ref.shape[1:]
    tall = rows + 2 * HALO
    groups = field_ref.shape[2]
    scale = (0.125 * COURANT / MOMENTUM) / jnp.max(jnp.maximum(own_ref[...], mate_ref[...]))
    scales = (1.0, scale, scale, scale * scale)

    def one_step(start, count, old, first_changes):
        def to_mid(row, col, parts):
            for comp in range(4):
                cells, move = old[comp, row, col], parts[comp]
                if first_changes is not None:
                    cells, move = scales[comp] * cells, (scales[comp] * scale) * move
                moved = cells - move
                base[comp, row, col] = moved
                mid[comp, row, col] = moved - move

        def to_field(row, col, parts):
            for comp in range(4):
                new = base[comp, row, col] - parts[comp]
                dealt[comp, col, pl.ds(start + row, 8, stride=count), :] = new

        def load_from(ref):
            return lambda row, col: [ref[comp, row, col] for comp in range(4)]

        if first_changes is not None:
            for row in range(count):
                for col in range(groups):
                    to_mid(row, col, [first_changes[comp, row, col] for comp in range(4)])
        else:
            for comp in range(4):
                for row in range(count):
                    for col in range(groups):
                        old[comp, row, col] = dealt[comp, col, pl.ds(start + row, 8, stride=count), :]
            changes(load_from(old), count, groups, 0, to_mid)
        changes(load_from(mid), count, groups, count // 2, to_field)

    one_step(0, tall // 8, field_ref, change_ref)
    for index in range(1, STEPS):
        one_step(4 * index, (tall - 8 * index) // 8, field, None)

    wide = groups * LANES
    lane = iota((rows, LANES), 1)
    parts = []
    for comp in range(4):
        line = []
        for group in range(groups):
            place = place_of(lane, group, groups)
            inside = (place >= HALO) & (place < HALO + cols)
            line.append(jnp.where(inside, dealt[comp, group, HALO : HALO + rows, :], 0.0))
        parts.append(jnp.concatenate(line, axis=1))
    found = selected(jnp.concatenate(parts, axis=0), select_ref[...])
    copies = []
    for comp in range(4):
        result[comp] = ((2.0 / SCALES[comp]) / scales[comp]) * found[comp * rows : (comp + 1) * rows, :]
        for side in range(2):
            part = (comp, pl.ds(side * (rows // 2), rows // 2))
            copies.append(pltpu.make_async_copy(result.at[part], out_ref.at[part], sems.at[comp, side]))
            copies[-1].start()
    for copy in copies:
        copy.wait()


def local(state):
    parts, rows, cols = state.shape
    tall = rows + 2 * HALO
    groups = -(-(cols + 2 * HALO) // LANES)

    def sent(value, axis, by):
        count = lax.axis_size(axis)
        return lax.ppermute(value, axis, [(i, (i + by) % count) for i in range(count)])

    def swapped_bit(value, axis, by):
        return lax.ppermute(value, axis, [(i, i ^ by) for i in range(lax.axis_size(axis))])

    def swapped_pairs(value, axis, first):
        count = lax.axis_size(axis)
        pairs = []
        for low in range(first, count, 2):
            high = (low + 1) % count
            pairs += [(low, high), (high, low)]
        return lax.ppermute(value, axis, pairs)

    def swapped_threes(value, axis):
        count = lax.axis_size(axis)
        return lax.ppermute(value, axis, [(i, (i + 3 - 6 * (i % 2)) % count) for i in range(count)])

    edge_type = array(parts * HALO + 8, cols)
    first, second, top = pl.pallas_call(
        edge_kernel,
        out_shape=(edge_type, edge_type, array(8, LANES)),
        in_specs=[VMEM],
        out_specs=(VMEM,) * 3,
        compiler_params=params(4),
        name="edge",
    )(state)
    second = swapped_pairs(second, "gx", 1)
    first = swapped_pairs(first, "gx", 0)
    far = swapped_threes(top, "gx"), swapped_bit(top, "gx", 4)
    side_type = array(tall // 2, LANES)
    row_halos = second, first
    first, second, top = pl.pallas_call(
        pack_kernel,
        out_shape=(side_type, side_type, array(8, LANES)),
        in_specs=[VMEM] * 6,
        out_specs=(VMEM,) * 3,
        compiler_params=params(4),
        name="pack",
    )(state, second, *far, first, top)
    second = swapped_pairs(second, "gy", 1)
    first = swapped_pairs(first, "gy", 0)
    far = swapped_bit(top, "gy", 2)
    wide = groups * LANES
    cells, halo_select, back_select, top, carried = pl.pallas_call(
        deal_kernel,
        out_shape=(
            array(parts * tall, wide),
            jax.ShapeDtypeStruct((wide - cols, wide), jnp.bfloat16),
            jax.ShapeDtypeStruct((wide, cols), jnp.bfloat16),
            array(8, LANES),
            array(8, LANES),
        ),
        in_specs=[VMEM] * 4,
        out_specs=(VMEM,) * 5,
        scratch_shapes=[pltpu.VMEM((parts * tall, cols), jnp.float32)],
        compiler_params=params(8),
        cost_estimate=pl.CostEstimate(flops=300_000_000, bytes_accessed=1_500_000, transcendentals=0),
        name="deal",
    )(state, *row_halos, top)
    top = jnp.maximum(jnp.maximum(top, far), carried * jnp.maximum(first[:8], second[:8]))
    for axis, covered in (("gy", 4), ("gx", 8)):
        while covered < lax.axis_size(axis):
            top = jnp.maximum(top, sent(top, axis, covered))
            covered *= 2
    mate = swapped_bit(top, "gx", 1)
    dealt_type = array(parts, tall // 8, groups, 8, LANES)
    dealt = pltpu.VMEM(dealt_type.shape, jnp.float32)
    plain = pltpu.VMEM((parts, groups, tall, LANES), jnp.float32)
    field, change = pl.pallas_call(
        first_kernel,
        out_shape=(dealt_type, dealt_type),
        in_specs=[VMEM] * 4,
        out_specs=(VMEM,) * 2,
        scratch_shapes=[pltpu.VMEM((parts * tall, LANES), jnp.float32), plain],
        compiler_params=params(16),
        cost_estimate=pl.CostEstimate(flops=20_000_000, bytes_accessed=2_000_000, transcendentals=400_000),
        name="first",
    )(cells, halo_select, second, first)
    return pl.pallas_call(
        steps_kernel,
        out_shape=array(parts, rows, cols),
        in_specs=[VMEM] * 5,
        out_specs=pl.BlockSpec(memory_space=pl.ANY),
        scratch_shapes=[dealt] * 3
        + [plain, pltpu.VMEM((parts, rows, cols), jnp.float32), pltpu.SemaphoreType.DMA((parts, 2))],
        compiler_params=params(16),
        name="steps",
    )(field, change, back_select, top, mate)


def solution(mesh):
    in_specs = (P(None, "gx", "gy"),)
    out_specs = P(None, "gx", "gy")
    return jax.shard_map(local, mesh=mesh, in_specs=in_specs, out_specs=out_specs, check_vma=False)
```
